32 devices in a mesh: group: 4 (over y, x), tile: 8 (over z, core).
Axes of the slice: x: 2, y: 2, z: 4, core: 2. Of those that a mesh axis runs over, the one named last changes fastest.
Arguments:
- points: float32 [7, 35, 16384], P(None, None, ('group', 'tile')), parts along dimension 2
- point_counts: int32 [16384], P(('group', 'tile')), parts along dimension 0, may hold values from 1 to 35, as said below
- voxel_cells: int32 [16384], P(('group', 'tile')), parts along dimension 0, may hold values from 0 to 131071, as said below
- anchor_labels: int32 [2, 1024, 128], P(None, ('group', 'tile')), parts along dimension 1, may hold values from -1 to 1, as said below
- box_targets: float32 [14, 1024, 128], P(None, ('group', 'tile')), parts along dimension 1, may hold values from -4 to 4
- weights: float32 [3297280], P(('group', 'tile')), parts along dimension 0
- adam_m: float32 [3297280], P(('group', 'tile')), parts along dimension 0
- adam_v: float32 [3297280], P(('group', 'tile')), parts along dimension 0, as said below
- outer_momentum: float32 [3297280], P(('group', 'tile')), parts along dimension 0, may hold values from -0.12 to 0.12
Outputs:
- adam_m_new: float32 [3297280], P(('group', 'tile')), parts along dimension 0
- adam_v_new: float32 [3297280], P(('group', 'tile')), parts along dimension 0
- outer_momentum_new: float32 [3297280], P(('group', 'tile')), parts along dimension 0
- weights_new: float32 [3297280], P(('group', 'tile')), parts along dimension 0
- loss_sum: float32 [4], P('group'), parts along dimension 0
- positives: float32 [4], P('group'), parts along dimension 0
The draws below stay inside these ranges and needn't reach their ends.
There are 4 independent parts, one for each index of `group`. The reference program is written for one: setup_inputs(seed, part) draws one part's arguments, and reference() takes and returns one part's arrays. A program takes and returns all parts, laid end to end along the dimension named above; each array names one. Nothing has to cross between parts.
Inputs may be any that keep to these rules, and one draw needn't show every extreme that they name: `point_counts`: some voxel holds 35 points in every draw. `voxel_cells`: the 512 slots of a device, devices in order, hold voxels in the rows of that device's block of 32 map rows; no two voxels share a cell; a cell number is (row * 128 + column) * 4 + height layer. `anchor_labels`: 1 marks positive anchors, 0 negative ones, -1 anchors left out of the loss. `adam_v`: every entry is positive.
All inputs are finite; a program needn't handle non-finite values.
Results may differ from the reference program's by a relative error of at most 0.0003.
The reference program's roundings to bfloat16 on the way count: a program that leaves them out, or rounds other values in their place, can miss the bound.
Values may be sent and summed in bfloat16 or wider, within the bound.
A program may use at most 192 MiB of HBM per device.

```python
import math
import jax
import jax.numpy as jnp
from jax import lax

C1 = 32
C2 = 128
CM = 64
CR1 = 128
CR2 = 128
CR3 = 256
ANCH = 2
P_SIZE = 35
ZD = 4
BW = 128
H_SCENE = 200
STEP = 10
V_DEV = 512
ROWS_DEV = 32
DO = 2
VOXELS = 4096
ROWS = 256
CELLS = 32768
NPARAM = 824320


def draw_points(key, part):
    key = jax.random.fold_in(key, 1)
    values = jax.random.normal(key, (7, P_SIZE, VOXELS), jnp.float32)
    return values


def draw_point_counts(key, part):
    key = jax.random.fold_in(key, 2)
    devices = VOXELS // V_DEV
    slot_device = jnp.arange(VOXELS) // V_DEV
    ceiling = P_SIZE // 3 + (P_SIZE - P_SIZE // 3) * slot_device // max(devices - 1, 1)
    raw_bits = jax.random.randint(key, (VOXELS,), 0, 1 << 20)
    counts = raw_bits % ceiling + 1
    return counts.at[VOXELS - V_DEV].set(P_SIZE).astype(jnp.int32)


def pick_cells(device_key, block_cells):
    inner_key, order_key = jax.random.split(device_key)
    middle = jax.random.permutation(inner_key, block_cells - 2)[:V_DEV - 2] + 1
    chosen = jnp.concatenate([jnp.array([0, block_cells - 1], jnp.int32), middle.astype(jnp.int32)])
    return chosen[jax.random.permutation(order_key, V_DEV)]


def draw_voxel_cells(key, part):
    key = jax.random.fold_in(key, 3)
    devices = VOXELS // V_DEV
    block_cells = ROWS_DEV * BW * ZD
    device_keys = jax.random.split(key, devices)
    chosen = jax.vmap(lambda k: pick_cells(k, block_cells))(device_keys)
    offsets = (jnp.arange(devices) * block_cells)[:, None]
    return (chosen + offsets).reshape(VOXELS).astype(jnp.int32)


def draw_anchor_labels(key, part):
    key = jax.random.fold_in(key, 4)
    devices = ROWS // ROWS_DEV
    row_device = jnp.arange(ROWS) // ROWS_DEV
    threshold = 20 + 40 * row_device // max(devices - 1, 1)
    ticket = jax.random.randint(key, (ANCH, ROWS, BW), 0, 1000)
    labels = jnp.where(ticket < threshold[None, :, None], 1, jnp.where(ticket >= 950, -1, 0))
    return labels.astype(jnp.int32)


def draw_weights(key, part):
    key = jax.random.fold_in(key, 5)
    segment_table = [((7, C1), 'normal', 7 ** (-0.5)), ((C1,), 'gain', 0.0), ((C1,), 'normal', 0.5), ((2 * C1, C2), 'normal', (2 * C1) ** (-0.5)), ((C2,), 'normal', 0.2), ((3, 3, 3, C2, CM), 'normal', 4.2 / math.sqrt(27 * C2)), ((CM,), 'normal', 0.2), ((3, 3, DO * CM, CR1), 'normal', 1.5 / math.sqrt(9 * DO * CM)), ((CR1,), 'normal', 0.2), ((3, 3, CR1, CR2), 'normal', 1.5 / math.sqrt(9 * CR1)), ((CR2,), 'normal', 0.2), ((3, 3, CR2, CR3), 'normal', 1.5 / math.sqrt(9 * CR2)), ((CR3,), 'normal', 0.2), ((CR3, ANCH * 8), 'normal', CR3 ** (-0.5)), ((ANCH * 8,), 'normal', 0.2)]
    pieces = []
    used = 0
    for position, (extent, draw_kind, spread) in enumerate(segment_table):
        sub_key = jax.random.fold_in(key, position + 10)
        length = math.prod(extent)
        used += length
        if draw_kind == 'gain':
            pieces.append(jax.random.uniform(sub_key, (length,), jnp.float32, 0.6, 1.4))
        else:
            pieces.append(spread * jax.random.normal(sub_key, (length,), jnp.float32))
    pieces.append(0.02 * jax.random.normal(jax.random.fold_in(key, 99), (NPARAM - used,), jnp.float32))
    return jnp.concatenate(pieces)


def draw_adam_m(key, part):
    key = jax.random.fold_in(key, 6)
    return jax.random.normal(key, (NPARAM,), jnp.float32) * (0.44 / math.sqrt(CELLS))


def draw_adam_v(key, part):
    key = jax.random.fold_in(key, 7)
    return jax.random.uniform(key, (NPARAM,), jnp.float32, 1.0, 4.0) * (0.016 / CELLS)


def levels(stream_key, shape, cuts, least, high):
    level = 1.0
    for dim, blocks in cuts:
        heights = jax.random.uniform(jax.random.fold_in(jax.random.fold_in(stream_key, 6), dim), (blocks,), jnp.float32, least / len(cuts), high / len(cuts))
        level = level * jnp.repeat(jnp.exp(heights), shape[dim] // blocks).reshape((-1,) + (1,) * (len(shape) - 1 - dim))
    return level


def centred(rng, shape, deviation, limit, cuts=(), dtype=jnp.bfloat16):
    values = jax.random.normal(rng, shape, jnp.float32) * deviation
    if len(cuts) > 0:
        values = levels(rng, shape, cuts, -0.22, 0.18) * values
    return jnp.clip(values, min=-limit, max=limit).astype(dtype)


def setup_inputs(seed: int = 0, part: int = 0) -> dict:
    seeds = jax.random.split(jax.random.key(seed), 10)
    part_splits = jax.random.split(jax.random.fold_in(seeds[9], part), 10)
    points = draw_points(jax.random.fold_in(jax.random.fold_in(seeds[9], part), 71), part)
    point_counts = draw_point_counts(jax.random.fold_in(jax.random.fold_in(seeds[9], part), 71), part)
    voxel_cells = draw_voxel_cells(jax.random.fold_in(jax.random.fold_in(seeds[9], part), 71), part)
    anchor_labels = draw_anchor_labels(jax.random.fold_in(jax.random.fold_in(seeds[9], part), 71), part)
    box_targets = centred(part_splits[4], (ANCH * 7, ROWS, BW), 1.0, 4.0, ((1, 8),), jnp.float32)
    weights = draw_weights(jax.random.fold_in(jax.random.fold_in(seeds[9], part), 71), part)
    adam_m = draw_adam_m(jax.random.fold_in(jax.random.fold_in(seeds[9], part), 71), part)
    adam_v = draw_adam_v(jax.random.fold_in(jax.random.fold_in(seeds[9], part), 71), part)
    outer_momentum = centred(part_splits[8], (NPARAM,), 0.02, 0.12, ((0, 8),), jnp.float32)
    return {"points": points, "point_counts": point_counts, "voxel_cells": voxel_cells, "anchor_labels": anchor_labels, "box_targets": box_targets, "weights": weights, "adam_m": adam_m, "adam_v": adam_v, "outer_momentum": outer_momentum}


PRECISE = lax.Precision.HIGHEST
FOCAL_ALPHA = 0.25
HUBER_BETA = 1.0 / 9.0
NORM_EPSILON = 1e-05
INNER_RATE = 0.05
FIRST_DECAY = 0.9
SECOND_DECAY = 0.999
ADAM_EPSILON = 1e-08
WEIGHT_DECAY = 0.01
OUTER_RATE = 0.7
OUTER_MOMENT = 0.9
LAYER_NAMES = ('mid', 'one', 'two', 'three')

@jax.custom_vjp
def low(v):
    return lax.optimization_barrier(v.astype(jnp.bfloat16)).astype(jnp.float32)

@jax.custom_vjp
def low_back(v):
    return v

def low_keep(v):
    return (low(v), None)

def low_pass(kept, grad):
    return (grad,)

def back_keep(v):
    return (v, None)

def back_low(kept, grad):
    return (low(grad),)
low.defvjp(low_keep, low_pass)
low_back.defvjp(back_keep, back_low)

def shapes():
    return [('w_vfe', (7, C1)), ('gamma', (C1,)), ('beta', (C1,)), ('w_fc', (2 * C1, C2)), ('b_fc', (C2,)), ('w_mid', (3, 3, 3, C2, CM)), ('b_mid', (CM,)), ('w_one', (3, 3, DO * CM, CR1)), ('b_one', (CR1,)), ('w_two', (3, 3, CR1, CR2)), ('b_two', (CR2,)), ('w_three', (3, 3, CR2, CR3)), ('b_three', (CR3,)), ('w_head', (CR3, ANCH * 8)), ('b_head', (ANCH * 8,))]

def unpack(flat_weights):
    params = {}
    offset = 0
    for entry_name, extent in shapes():
        length = math.prod(extent)
        params[entry_name] = flat_weights[offset:offset + length].reshape(extent)
        offset += length
    return params

def keep_rows(first_row, row_count, all_rows):
    global_row = first_row + jnp.arange(row_count)
    above = global_row % H_SCENE != 0
    below = ((global_row + 1) % H_SCENE != 0) & (global_row + 1 < all_rows)
    return jnp.stack([above, jnp.ones_like(above), below]).astype(jnp.float32)

def mid_taps():
    listing = []
    for out_depth in range(DO):
        first_z = max(0, 2 * out_depth - 1)
        last_z = min(ZD, 2 * out_depth + 2)
        listing.append((first_z, last_z, first_z - 2 * out_depth + 1))
    return listing

def conv_blocks(kernel, layer_name):
    if layer_name != 'mid':
        return [(0, kernel.shape[2], kernel)]
    blocks = []
    for first_z, last_z, first_tap in mid_taps():
        tap_block = kernel[first_tap:first_tap + last_z - first_z]
        blocks.append((first_z * C2, last_z * C2, tap_block.transpose(1, 2, 0, 3, 4).reshape(3, 3, (last_z - first_z) * C2, CM)))
    return blocks

def convolve(signal, kernel, row_keep):
    row_count, col_count = (signal.shape[1], signal.shape[2])
    padded = jnp.pad(signal, ((0, 0), (1, 1), (1, 1)))
    result = jnp.zeros((kernel.shape[3], row_count, col_count), jnp.float32)
    for i in range(3):
        for j in range(3):
            window = padded[:, i:i + row_count, j:j + col_count] * row_keep[i][None, :, None]
            result = result + jnp.einsum('co,crw->orw', kernel[i, j], window, precision=PRECISE)
    return result

def anchor_loss(logits, labels, targets):
    class_logits = logits[:ANCH]
    box_out = logits[ANCH:].reshape(ANCH, 7, logits.shape[1], logits.shape[2])
    positive = (labels == 1).astype(jnp.float32)
    negative = (labels == 0).astype(jnp.float32)
    chance = jax.nn.sigmoid(class_logits)
    focal_terms = -FOCAL_ALPHA * positive * (1.0 - chance) ** 2 * jax.nn.log_sigmoid(class_logits) - (1.0 - FOCAL_ALPHA) * negative * chance ** 2 * jax.nn.log_sigmoid(-class_logits)
    residual = box_out - targets.reshape(box_out.shape)
    magnitude = jnp.abs(residual)
    huber_terms = jnp.where(magnitude < HUBER_BETA, 0.5 * residual * residual / HUBER_BETA, magnitude - 0.5 * HUBER_BETA)
    return jnp.sum(focal_terms) + 2.0 * jnp.sum(huber_terms * positive[:, None])

def adam_outer(gradient, weight, moment, second, momentum):
    moment = FIRST_DECAY * moment + (1.0 - FIRST_DECAY) * gradient
    second = SECOND_DECAY * second + (1.0 - SECOND_DECAY) * gradient * gradient
    moment_fix = moment / (1.0 - FIRST_DECAY ** STEP)
    second_fix = second / (1.0 - SECOND_DECAY ** STEP)
    inner_weight = weight - INNER_RATE * (moment_fix / (jnp.sqrt(second_fix) + ADAM_EPSILON) + WEIGHT_DECAY * weight)
    inner_step = weight - inner_weight
    momentum = OUTER_MOMENT * momentum + inner_step
    updated = weight - OUTER_RATE * (inner_step + OUTER_MOMENT * momentum)
    return (moment, second, momentum, updated)

def forward(flat_weights, points, point_counts, voxel_cells, anchor_labels, box_targets):
    params = unpack(flat_weights)
    point_mask = (jnp.arange(P_SIZE)[:, None] < point_counts[None, :]).astype(jnp.float32)
    counts = point_counts.astype(jnp.float32)
    linear = jnp.einsum('ki,kpv->ipv', params['w_vfe'], points, precision=PRECISE)
    point_total = jnp.sum(point_mask)
    channel_mean = lax.optimization_barrier(jnp.sum(linear * point_mask, axis=(1, 2))) / point_total
    centered = linear - channel_mean[:, None, None]
    variance = lax.optimization_barrier(jnp.sum(centered * centered * point_mask, axis=(1, 2))) / point_total
    normed = centered * lax.rsqrt(variance + NORM_EPSILON)[:, None, None]
    act_in = params['gamma'][:, None, None] * normed + params['beta'][:, None, None]
    first_out = jax.nn.silu(act_in) * point_mask
    pooled = lax.optimization_barrier(jnp.sum(first_out, axis=1)) / counts
    joined = low(jnp.concatenate([first_out, pooled[:, None, :] * point_mask], axis=0))
    inner_pre = low_back(jnp.einsum('io,ipv->opv', low(params['w_fc']), joined, precision=PRECISE) + params['b_fc'][:, None, None])
    feature = lax.optimization_barrier(jnp.sum(jax.nn.silu(inner_pre) * point_mask, axis=1)) / counts
    canvas = jnp.zeros((ROWS * BW * ZD, C2), jnp.float32).at[voxel_cells].set(feature.T)
    canvas = canvas.reshape(ROWS, BW, ZD, C2).transpose(2, 3, 0, 1).reshape(ZD * C2, ROWS, BW)
    row_keep = keep_rows(0, ROWS, ROWS)
    signal = low(canvas)
    for layer_name in LAYER_NAMES:
        kernel = low(params['w_' + layer_name])
        pieces = [convolve(signal[first_channel:end_channel], block, row_keep) for first_channel, end_channel, block in conv_blocks(kernel, layer_name)]
        stacked = jnp.concatenate(pieces, axis=0)
        bias_vec = params['b_' + layer_name]
        bias_full = jnp.tile(bias_vec, stacked.shape[0] // bias_vec.shape[0])
        pre_act = low_back(stacked + bias_full[:, None, None])
        signal = low(jax.nn.silu(pre_act))
    logits = low_back(jnp.einsum('co,crw->orw', low(params['w_head']), signal, precision=PRECISE) + params['b_head'][:, None, None])
    return anchor_loss(logits, anchor_labels, box_targets)

def reference(points, point_counts, voxel_cells, anchor_labels, box_targets, weights, adam_m, adam_v, outer_momentum):
    positives = jnp.sum((anchor_labels == 1).astype(jnp.float32))
    divisor = jnp.maximum(positives, 1.0)

    def objective(flat_weights):
        return forward(flat_weights, points, point_counts, voxel_cells, anchor_labels, box_targets)
    loss_sum, pullback = jax.vjp(objective, weights)
    gradient, = pullback(1.0 / divisor)
    moment, second, momentum, updated = adam_outer(gradient, weights, adam_m, adam_v, outer_momentum)
    return (moment, second, momentum, updated, loss_sum.reshape(1), positives.reshape(1))
```

```python
import functools
import math

import jax
import jax.numpy as jnp
from jax import lax
from jax.experimental import pallas as pl
from jax.experimental.pallas import tpu as pltpu
from jax.sharding import PartitionSpec as P

MESH = pl.DeviceIdType.MESH
F32 = jnp.float32
BF16 = jnp.bfloat16
HIGH = lax.Precision.HIGHEST

C1, C2, CM, CR1, CR2, CR3, ANCH, ZD = 32, 128, 64, 128, 128, 256, 2, 4
H_SCENE = 200
STEP = 10
LANES = 128
NORM_EPSILON = 1e-05
INNER_RATE = 0.05
FIRST_DECAY = 0.9
SECOND_DECAY = 0.999
ADAM_EPSILON = 1e-08
WEIGHT_DECAY = 0.01
OUTER_RATE = 0.7
OUTER_MOMENT = 0.9
FOCAL_ALPHA = 0.25
HUBER_BETA = 1.0 / 9.0

SMALL = 80
FC_ROW, FC_LANE = 2, 32
BIAS_ROWS = (1795, 2947, 2948, 4100, 4101, 6405, 6406, 6407, 6439)
RUN_A = (2, 32)
RUN_B = (1795, 96)
A_MID = 65
B_ONE, B_TWO, B_THREE, B_HEAD = 0, 1153, 2306, 4612
MSG = 48


def vmem():
    return pl.BlockSpec(memory_space=pltpu.VMEM)


def anywhere():
    return pl.BlockSpec(memory_space=pl.ANY)


def smem():
    return pl.BlockSpec(memory_space=pltpu.SMEM)


def ceil_to(value, step):
    return (value + step - 1) // step * step


def sigmoid(value):
    return 0.5 * jnp.tanh(0.5 * value) + 0.5


def slope(value):
    s = sigmoid(value)
    return s * (1.0 + value * (1.0 - s))


def nt(a, b, precision=None):
    return lax.dot_general(a, b, (((1,), (1,)), ((), ())), precision=precision, preferred_element_type=F32)


def tn(a, b, precision=None):
    return lax.dot_general(a, b, (((0,), (0,)), ((), ())), precision=precision, preferred_element_type=F32)


def nn(a, b, precision=None):
    return lax.dot_general(a, b, (((1,), (0,)), ((), ())), precision=precision, preferred_element_type=F32)


def lane_of(shape):
    return lax.broadcasted_iota(jnp.int32, shape, len(shape) - 1)


def row_of(shape):
    return lax.broadcasted_iota(jnp.int32, shape, len(shape) - 2)


def enter(n, me):
    sem = pltpu.get_barrier_semaphore()

    def greet(k, carry):
        pl.semaphore_signal(
            sem, inc=1, device_id={"tile": lax.rem(me + k, n)}, device_id_type=MESH
        )
        return carry

    lax.fori_loop(1, n, greet, 0)
    pl.semaphore_wait(sem, n - 1)


def remote(src, dst, send, recv, peer):
    return pltpu.make_async_remote_copy(
        src_ref=src,
        dst_ref=dst,
        send_sem=send,
        recv_sem=recv,
        device_id={"tile": peer},
        device_id_type=MESH,
    )


def even_first():
    out = row_of((LANES, LANES))
    source = jnp.where(out < 64, 2 * out, 2 * out - 127)
    return lane_of((LANES, LANES)) == source


def first_layer(small_ref):
    turned = jnp.transpose(small_ref[0:LANES_PAD, :])
    columns = [turned[(k % 4) * 32 : (k % 4) * 32 + 32, k // 4 : k // 4 + 1] for k in range(7)]
    return columns, turned[96:128, 1:2], turned[0:32, 2:3]


LANES_PAD = 8


def voxel_rows(small_ref):
    here, after = small_ref[2:74, :], small_ref[3:75, :]
    mixed = jnp.where(lane_of((72, LANES)) >= FC_LANE, here, after)
    return pltpu.roll(mixed, LANES - FC_LANE, axis=1)


def front_kernel(
    n, points_hbm, counts_ref, labels_ref, shard_ref,
    wall, small, stat, linear, joined, feature,
    points, own, mine, msgs, sem_p, sem_small_s, sem_small_r, sem_msg_s, sem_msg_r, sem_w_s, sem_w_r, sem_f_s,
):
    me = lax.axis_index("tile")
    rows = shard_ref.shape[0]
    slots, voxels = points_hbm.shape[1], points_hbm.shape[2]
    sibling = me + 1 - 2 * lax.rem(me, 2)
    loads = [
        pltpu.make_async_copy(points_hbm.at[k], points.at[:, k, :], sem_p.at[k]) for k in range(7)
    ]
    for load in loads:
        load.start()
    own[...] = jnp.zeros_like(own)
    own[0:rows, :] = shard_ref[...].astype(BF16)
    enter(n, me)

    def small_copy(k):
        peer = lax.rem(me + k, n)
        return remote(small, small, sem_small_s.at[k], sem_small_r.at[0], peer)

    @pl.when(me == 0)
    def _():
        small[...] = shard_ref[0:SMALL, :]

        def send(k, carry):
            small_copy(k).start()
            return carry

        lax.fori_loop(1, n, send, 0)

    def shard_copy(k):
        return remote(own, wall.at[me], sem_w_s.at[k], sem_w_r.at[me], lax.rem(me + 2 * k, n))

    half = n // 2
    for k in range(1, half):
        shard_copy(k).start()
    to_sibling = remote(own, wall.at[me], sem_w_s.at[0], sem_w_r.at[me], sibling)
    to_sibling.start()
    wall[me] = own[...]

    counts = counts_ref[...]
    slot_no = row_of((slots, voxels))
    mask_all = (slot_no < counts).astype(F32)
    for load in loads:
        load.wait()
    point_sums = jnp.zeros((32, 1), F32)
    row32 = row_of((32, 1))
    for k in range(7):
        total = jnp.sum(jnp.sum(points[:, k, :] * mask_all, axis=1, keepdims=True), axis=0, keepdims=True)
        point_sums = point_sums + jnp.where(row32 == k, total, 0.0)
    positives = jnp.zeros((1, 1), F32)
    for a in range(ANCH):
        hits = (labels_ref[a] == 1).astype(F32)
        positives += jnp.sum(jnp.sum(hits, axis=1, keepdims=True), axis=0, keepdims=True)
    held = jnp.sum(jnp.sum(mask_all, axis=1, keepdims=True), axis=0, keepdims=True)
    for a, row in enumerate(BIAS_ROWS):
        owner, place = row // rows, row % rows
        mine[32 + a : 33 + a, :] = jnp.where(me == owner, shard_ref[place : place + 1, :], 0.0)
    for a in range(len(BIAS_ROWS), MSG - 32):
        mine[32 + a : 33 + a, :] = jnp.zeros((1, LANES), F32)

    @pl.when(me > 0)
    def _():
        small_copy(0).wait_recv()

    columns, gamma, beta = first_layer(small)
    wide = [jnp.broadcast_to(c, (32, voxels)) for c in columns]

    def pass_a(p, total):
        value = wide[0] * points[p, 0:1, :]
        for k in range(1, 7):
            value += wide[k] * points[p, k : k + 1, :]
        linear[p] = value
        return total + jnp.where(p < counts, value, 0.0)

    total = lax.fori_loop(0, slots, pass_a, jnp.zeros((32, voxels), F32), unroll=5)
    local_sum = jnp.sum(total, axis=1, keepdims=True)
    local_mean = local_sum / held

    def pass_b(p, total):
        off = linear[p] - local_mean
        return total + jnp.where(p < counts, off * off, 0.0)

    total = lax.fori_loop(0, slots, pass_b, jnp.zeros((32, voxels), F32), unroll=5)
    local_square = jnp.sum(total, axis=1, keepdims=True)
    lane = lane_of((32, LANES))
    packed = jnp.where(lane == 0, local_sum, 0.0)
    packed = jnp.where(lane == 1, local_square, packed)
    packed = jnp.where(lane == 2, held, packed)
    packed = jnp.where(lane == 3, positives, packed)
    packed = jnp.where(lane == 4, point_sums, packed)
    mine[0:32, :] = packed

    def message(k):
        return remote(mine, msgs.at[me], sem_msg_s.at[k], sem_msg_r.at[me], lax.rem(me + k, n))

    for k in range(1, n):
        message(k).start()
    msgs[me] = mine[...]
    for k in range(1, n):
        sender = lax.rem(me + n - k, n)
        remote(mine, msgs.at[sender], sem_msg_s.at[k], sem_msg_r.at[sender], sender).wait_recv()
    sums = msgs[0]
    for d in range(1, n):
        sums += msgs[d]
    held_all = sums[0:32, 2:3]
    mean = sums[0:32, 0:1] / held_all
    square = sums[0:32, 1:2]
    for d in range(n):
        held_d = msgs[d, 0:32, 2:3]
        off = msgs[d, 0:32, 0:1] / held_d - mean
        square += held_d * off * off
    inverse = lax.rsqrt(square / held_all + NORM_EPSILON)
    columns_out = jnp.where(lane == 0, mean, 0.0)
    columns_out = jnp.where(lane == 1, inverse, columns_out)
    columns_out = jnp.where(lane == 2, held_all, columns_out)
    columns_out = jnp.where(lane == 3, sums[0:32, 3:4], columns_out)
    columns_out = jnp.where(lane == 4, sums[0:32, 4:5] / held_all, columns_out)
    stat[0:32, :] = columns_out
    stat[32:MSG, :] = sums[32:MSG, :]

    inverse_counts = 1.0 / counts.astype(F32)

    def pass_c(p, pooled):
        act = gamma * ((linear[p] - mean) * inverse) + beta
        out = jnp.where(p < counts, act * sigmoid(act), 0.0)
        joined[p, 0:32, :] = out.astype(BF16)
        return pooled + out

    pooled = lax.fori_loop(0, slots, pass_c, jnp.zeros((32, voxels), F32), unroll=5)
    pooled = (pooled / counts.astype(F32)).astype(BF16)
    order = even_first()
    rows_fc = voxel_rows(small)
    kernel_t = nt(order.astype(BF16), rows_fc[0:64, :].astype(BF16)).astype(BF16)
    bias = jnp.sum(jnp.where(order, rows_fc[64:65, :], 0.0), axis=1, keepdims=True)
    tail = jnp.where(row_of((16, voxels)) == 0, 1.0, 0.0).astype(BF16)

    def pass_d(p, total):
        inside = p < counts
        joined[p, 32:64, :] = jnp.where(inside, pooled.astype(F32), 0.0).astype(BF16)
        joined[p, 64:80, :] = tail
        inner = nn(kernel_t, joined[p, 0:64, :]) + bias
        return total + jnp.where(inside, inner * sigmoid(inner), 0.0)

    total = lax.fori_loop(0, slots, pass_d, jnp.zeros((LANES, voxels), F32))
    feature[...] = jnp.transpose(total / counts.astype(F32))

    for k in range(1, half):
        source = lax.rem(me + n - 2 * k, n)
        remote(own, wall.at[source], sem_w_s.at[k], sem_w_r.at[source], source).wait_recv()
        remote(wall.at[source], wall.at[source], sem_f_s.at[k], sem_w_r.at[source], sibling).start()
    for k in range(half):
        source = lax.rem(sibling + n - 2 * k, n)
        remote(own, wall.at[source], sem_w_s.at[k], sem_w_r.at[source], source).wait_recv()
    for k in range(1, half):
        source = lax.rem(me + n - 2 * k, n)
        remote(wall.at[source], wall.at[source], sem_f_s.at[k], sem_w_r.at[source], sibling).wait_send()
        shard_copy(k).wait_send()
    to_sibling.wait_send()
    for k in range(1, n):
        message(k).wait_send()

    @pl.when(me == 0)
    def _():
        def done(k, carry):
            small_copy(k).wait_send()
            return carry

        lax.fori_loop(1, n, done, 0)


def front(n, points, counts, labels, shard):
    slots, voxels = points.shape[1:]
    rows = shard.shape[0]
    padded = ceil_to(rows, 16)
    shape = jax.ShapeDtypeStruct
    dma = pltpu.SemaphoreType.DMA
    return pl.pallas_call(
        functools.partial(front_kernel, n),
        name="front",
        out_shape=(
            shape((n, padded, LANES), BF16),
            shape((SMALL, LANES), F32),
            shape((MSG, LANES), F32),
            shape((slots, 32, voxels), F32),
            shape((slots, 80, voxels), BF16),
            shape((voxels, LANES), F32),
        ),
        in_specs=[anywhere(), vmem(), vmem(), vmem()],
        out_specs=(vmem(),) * 6,
        scratch_shapes=[
            pltpu.VMEM((slots, 8, voxels), F32),
            pltpu.VMEM((padded, LANES), BF16),
            pltpu.VMEM((MSG, LANES), F32),
            pltpu.VMEM((n, MSG, LANES), F32),
            dma((7,)), dma((n,)), dma((1,)), dma((n,)), dma((n,)), dma((n,)), dma((n,)), dma((n,)),
        ],
        compiler_params=pltpu.CompilerParams(
            collective_id=1, has_side_effects=True, vmem_limit_bytes=56 << 20
        ),
    )(points, counts, labels, shard)


def layout(n, row_count):
    first = lax.axis_index("tile") * row_count
    ahead = (first // H_SCENE + 1) * H_SCENE - first
    split = jnp.where(ahead < row_count, 1, 0)
    edge = jnp.where(ahead < row_count, ahead, row_count)
    top = jnp.where(lax.rem(first, H_SCENE) != 0, 1, 0)
    last = first + row_count
    bottom = jnp.where((lax.rem(last, H_SCENE) != 0) & (last < n * row_count), 1, 0)
    return edge, split, top, bottom


def place_ok(place, edge, split, row_count):
    return (place >= 1) & (place <= row_count + split) & ((place != edge + 1) | (split == 0))


def place_row(place, edge, row_count):
    row = jnp.where(place <= edge, place - 1, place - 2)
    return jnp.clip(row, 0, row_count - 1)


PITCH = 136


def voxel_base(cell, depth_cells, columns, edge, split):
    local = lax.rem(cell, depth_cells)
    spot = local // ZD
    row = spot // columns
    column = spot - row * columns
    place = row + 1 + jnp.where((row >= edge) & (split == 1), 1, 0)
    return place * PITCH + column + 7


def z_columns(cells_row):
    z = lax.rem(cells_row, ZD).astype(F32)
    return jnp.transpose(jnp.broadcast_to(z, (8, z.shape[1])))[:, 0:1]


def spread_z(feature, z_column, out_ref):
    for z in range(ZD):
        out_ref[:, z * C2 : (z + 1) * C2] = jnp.where(z_column == z, feature, 0.0).astype(BF16)


def middle_kernel(
    n, rows, row_count,
    cells_smem, cells_row, feature, wall,
    pre, w_mid, f_one, f_two, f_three, d_one, d_two, d_three, head_t,
    flat, run, spread, parts0, parts1, parts2, sum0, sum1, sum2,
):
    edge, split, _, _ = layout(n, row_count)
    voxels = feature.shape[0]
    columns = LANES
    parts, sums = (parts0, parts1, parts2), (sum0, sum1, sum2)
    for s in range(n):
        flat[s * rows : s * rows + wall.shape[1], :] = wall[s].astype(F32)

    def aligned(begin, start, count):
        row, lane = begin
        here = flat[pl.ds(row + start, count), :]
        after = flat[pl.ds(row + start + 1, count), :]
        mixed = jnp.where(lane_of((count, LANES)) >= lane, here, after)
        return pltpu.roll(mixed, LANES - lane, axis=1)

    low = lane_of((64, LANES)) < 64
    for ij in range(9):
        taps = [aligned(RUN_A, A_MID + (t * 9 + ij) * 64, 64) for t in range(3)]
        turned = [pltpu.roll(tap, 64, axis=1) for tap in taps]
        none = jnp.zeros((64, LANES), F32)
        for z in range(ZD):
            first, second = z + 1, z - 1
            a, a_t = (taps[first], turned[first]) if first < 3 else (none, none)
            b, b_t = (taps[second], turned[second]) if second >= 0 else (none, none)
            lanes = slice(ij * LANES, (ij + 1) * LANES)
            w_mid[z * C2 : z * C2 + 64, lanes] = jnp.where(low, a, b_t).astype(BF16)
            w_mid[z * C2 + 64 : (z + 1) * C2, lanes] = jnp.where(low, a_t, b).astype(BF16)

    spread_z(feature[...], z_columns(cells_row[...]), spread)
    for i in range(3):
        product = nn(spread[...], w_mid[:, i * 384 : (i + 1) * 384])
        for j in range(3):
            parts[i][pl.ds(2 - j, voxels, 4), :] = product[:, j * LANES : (j + 1) * LANES]
        sums[i][...] = jnp.zeros_like(sums[i])

    depth_cells = row_count * columns * ZD

    def add(v, carry):
        base = voxel_base(cells_smem[v], depth_cells, columns, edge, split)
        for i in range(3):
            spot = pl.ds(base + (1 - i) * PITCH, 3)
            sums[i][spot, :] = sums[i][spot, :] + parts[i][pl.ds(4 * v, 3), :]
        return carry

    lax.fori_loop(0, voxels, add, 0, unroll=4)

    def gather(p, carry):
        spot = pl.ds(pl.multiple_of(p * PITCH + 8, 8), columns)
        pre[p] = sum0[spot, :] + sum1[spot, :] + sum2[spot, :]
        return carry

    lax.fori_loop(0, row_count + 5, gather, 0)

    def zero_half(ref, row, column, height, width):
        ref[row : row + height, column : column + width] = jnp.zeros((height, width), BF16)

    for begin, f_ref, d_ref in ((B_ONE, f_one, d_one), (B_TWO, f_two, d_two)):
        for j in range(3):
            for e in range(2):
                outside = 3 if e == 0 else 0
                zero_half(f_ref, outside * 384 + j * LANES, e * LANES, LANES, LANES)
                zero_half(d_ref, e * LANES, outside * 384 + j * LANES, LANES, LANES)

        def tap(i, j, begin=begin, f_ref=f_ref, d_ref=d_ref):
            block = aligned(RUN_B, begin + (i * 3 + j) * LANES, LANES).astype(BF16)
            for e in range(2):
                t = i + e
                f_ref[t * 384 + j * LANES : t * 384 + (j + 1) * LANES, e * LANES : (e + 1) * LANES] = block
                t = 2 + e - i
                lane = t * 384 + (2 - j) * LANES
                d_ref[e * LANES : (e + 1) * LANES, lane : lane + LANES] = block

        for i in range(3):
            for j in range(3):
                tap(i, j)
    for j in range(3):
        for e in range(2):
            outside = 3 if e == 0 else 0
            zero_half(d_three, e * LANES, outside * 768 + j * 256, LANES, 256)
    for i in range(3):
        for j in range(3):
            run[...] = aligned(RUN_B, B_THREE + (i * 3 + j) * 256, 256)
            for h in range(2):
                block = run[pl.ds(h, LANES, 2), :].astype(BF16)
                row = (i * 3 + j) * LANES
                f_three[row : row + LANES, h * LANES : (h + 1) * LANES] = block
                for e in range(2):
                    lane = (2 + e - i) * 768 + (2 - j) * 256 + h * LANES
                    d_three[e * LANES : (e + 1) * LANES, lane : lane + LANES] = block
    head_rows = aligned(RUN_B, B_HEAD, 32).astype(BF16)
    chosen = nn(eighths(), head_rows)
    chosen = jnp.where(same_eighth(), chosen, 0.0).astype(BF16)
    head_t[...] = nt(fold16(), chosen).astype(BF16)


def eighths():
    return (row_of((CR3, 32)) // 8 == lane_of((CR3, 32))).astype(F32).astype(BF16)


def same_eighth():
    return lane_of((CR3, LANES)) // 16 == lax.rem(row_of((CR3, LANES)), 8)


def fold16():
    return (lax.rem(lane_of((16, LANES)), 16) == row_of((16, LANES))).astype(F32).astype(BF16)


def middle(n, rows, row_count, cells, feature, wall):
    shape = jax.ShapeDtypeStruct
    voxels = feature.shape[0]
    cells_all = (row_count + 6) * PITCH
    return pl.pallas_call(
        functools.partial(middle_kernel, n, rows, row_count),
        name="middle",
        out_shape=(
            shape((row_count + 5, LANES, LANES), F32),
            shape((512, 1152), BF16),
            shape((1536, 256), BF16),
            shape((1536, 256), BF16),
            shape((1152, 256), BF16),
            shape((256, 1536), BF16),
            shape((256, 1536), BF16),
            shape((256, 3072), BF16),
            shape((16, 256), BF16),
        ),
        in_specs=[smem(), vmem(), vmem(), vmem()],
        out_specs=(vmem(),) * 9,
        scratch_shapes=[
            pltpu.VMEM((n * rows + 24, LANES), F32),
            pltpu.VMEM((256, LANES), F32),
            pltpu.VMEM((voxels, ZD * C2), BF16),
            pltpu.VMEM((voxels * 4, LANES), F32),
            pltpu.VMEM((voxels * 4, LANES), F32),
            pltpu.VMEM((voxels * 4, LANES), F32),
            pltpu.VMEM((cells_all, LANES), F32),
            pltpu.VMEM((cells_all, LANES), F32),
            pltpu.VMEM((cells_all, LANES), F32),
        ],
        compiler_params=pltpu.CompilerParams(vmem_limit_bytes=56 << 20),
    )(cells, cells.reshape(1, -1), feature, wall)


PAIRS = 18
QB = 9
STEPS = PAIRS // QB
SPAN = QB * LANES
GRID = PAIRS * LANES
A_ROWS, B_ROWS = 1800, 4656


def conv_kernel(
    n, row_count,
    cells_smem, cells_row, feature, stat, pre_in, w_mid, f_one, f_two, f_three, d_one, d_two, d_three, head_t,
    labels_hbm, boxes_hbm,
    grad_a, grad_b, grad_feature, loss_out,
    x_one, x_two, x_three, pre_mid, pre_one, pre_two, back, spread,
    acc0, acc1, acc2,
    labels, boxes, logit_grads, loss_mine, loss_all,
    up_f, down_f, from_up_f, from_down_f, send_up, send_down, from_up, from_down,
    send_up_w, send_down_w, from_up_w, from_down_w,
    sem_t, sem_fs, sem_fr, sem_s, sem_r, sem_ws, sem_wr, sem_ls, sem_lr,
):
    me = lax.axis_index("tile")
    edge, split, top, bottom = layout(n, row_count)
    has_up, has_down = me > 0, me < n - 1
    above, below = jnp.maximum(me - 1, 0), jnp.minimum(me + 1, n - 1)
    loads = [pltpu.make_async_copy(labels_hbm.at[a], labels.at[:, a, :], sem_t.at[a]) for a in range(2)]
    loads += [
        pltpu.make_async_copy(boxes_hbm.at[a], boxes.at[:, 2 + a, :], sem_t.at[2 + a]) for a in range(14)
    ]
    for load in loads:
        load.start()
    enter(n, me)

    def ok(place):
        return place_ok(place, edge, split, row_count)

    def halo_copies(s, up_src, down_src, up_dst, down_dst, sem_send, sem_recv):
        up = remote(up_src, down_dst, sem_send.at[2 * s], sem_recv.at[2 * s], above)
        down = remote(down_src, up_dst, sem_send.at[2 * s + 1], sem_recv.at[2 * s + 1], below)
        return up, down

    def halo_start(copies):
        up, down = copies

        @pl.when(has_up)
        def _():
            up.start()

        @pl.when(has_down)
        def _():
            down.start()

    def halo_wait(copies):
        up, down = copies

        @pl.when(has_up)
        def _():
            up.wait_send()
            down.wait_recv()

        @pl.when(has_down)
        def _():
            down.wait_send()
            up.wait_recv()

    def thin(s):
        return halo_copies(
            s, send_up.at[s], send_down.at[s], from_up.at[s], from_down.at[s], sem_s, sem_r
        )

    def pick(condition, a, b):
        return jnp.where(condition, a, b)

    column = row_of((LANES, LANES))

    def shifted(value):
        left = jnp.where(column > 0, pltpu.roll(value, 1, axis=0), 0.0)
        right = jnp.where(column < LANES - 1, pltpu.roll(value, LANES - 1, axis=0), 0.0)
        return left.astype(BF16), value.astype(BF16), right.astype(BF16)

    def put(ref, pair, parity, value, part, parts):
        rows = pl.ds(pl.multiple_of(pair * LANES, LANES), LANES)
        width = 3 * parts * LANES
        for j, shift in enumerate(shifted(value)):
            lane = parity * width + (j * parts + part) * LANES
            ref[rows, lane : lane + LANES] = shift

    def put_edges(ref, s, parts, up_halo, down_halo):
        for part in range(parts):
            lanes = slice(part * LANES, (part + 1) * LANES)
            halo = pick((top == 1) & has_up, up_halo[:, lanes].astype(F32), 0.0)
            put(ref, 0, 0, halo, part, parts)
            halo = pick((bottom == 1) & has_down, down_halo[:, lanes].astype(F32), 0.0)
            width = 3 * parts * LANES
            row = pl.ds(16 * LANES, LANES)
            for j, shift in enumerate(shifted(halo)):
                lane = width + (j * parts + part) * LANES
                ref[row, lane : lane + LANES] = pick(split == 1, ref[row, lane : lane + LANES], shift)
            put(ref, 17, 0, pick(split == 1, halo, 0.0), part, parts)

    grad_b[B_HEAD + 32 :, :] = jnp.zeros((B_ROWS - B_HEAD - 32, LANES), F32)
    up_f[...] = pre_in[0]
    down_f[...] = pick(split == 1, pre_in[row_count + 2], pre_in[row_count + 1])
    copies = halo_copies(0, up_f, down_f, from_up_f, from_down_f, sem_fs, sem_fr)
    halo_start(copies)
    for ref, wide in ((x_one, 768), (x_two, 768), (x_three, 768)):
        ref[0:LANES, 0:384] = jnp.zeros((LANES, 384), BF16)
        ref[18 * LANES : 20 * LANES, :] = jnp.zeros((2 * LANES, wide), BF16)
    spread_z(feature[...], z_columns(cells_row[...]), spread)
    halo_wait(copies)

    bias_mid = stat[32:33, :]
    b_mid = jnp.concatenate([bias_mid[:, 32:96], bias_mid[:, 32:96]], axis=1)
    last = row_count

    def fold(q, carry):
        for e in range(2):
            p = 2 * q + 1 + e
            value = pre_in[p] + b_mid
            value += pick((p == 1) & (top == 1) & has_up, from_up_f[...], 0.0)
            value += pick((p == last + split) & (bottom == 1) & has_down, from_down_f[...], 0.0)
            pre_mid[pl.ds(pl.multiple_of(q * LANES, LANES), LANES), e * LANES : (e + 1) * LANES] = value
        return carry

    lax.fori_loop(0, PAIRS, fold, 0)

    def activate(pre_ref, x_ref, s):
        def step(q, carry):
            rows = pl.ds(pl.multiple_of(q * LANES, LANES), LANES)
            for e in range(2):
                value = pre_ref[rows, e * LANES : (e + 1) * LANES]
                value = pick(ok(2 * q + 1 + e), value * sigmoid(value), 0.0)
                put(x_ref, q + e, 1 - e, value, 0, 1)
            return carry

        lax.fori_loop(0, PAIRS, step, 0)
        exchange(x_ref, s)
        copies = thin(s)
        halo_wait(copies)
        put_edges(x_ref, s, 1, from_up[s], from_down[s])

    def exchange(x_ref, s):
        send_up[s] = x_ref[0:LANES, 512:640]
        send_down[s] = pick(split == 1, x_ref[16 * LANES : 17 * LANES, 512:640], x_ref[16 * LANES : 17 * LANES, 128:256])
        halo_start(thin(s))

    def banded(x_ref, f_ref, bias, out_ref):
        def step(b, carry):
            start = pl.multiple_of(b * SPAN, LANES)
            total = nn(x_ref[pl.ds(start, SPAN), :], f_ref[0:768, :])
            total += nn(x_ref[pl.ds(start + LANES, SPAN), :], f_ref[768:1536, :])
            out_ref[pl.ds(start, SPAN), :] = total + bias
            return carry

        lax.fori_loop(0, STEPS, step, 0)

    def banded_back(g_ref, d_ref, out_ref):
        width = g_ref.shape[1]

        def step(b, carry):
            start = pl.multiple_of(b * SPAN, LANES)
            total = nt(g_ref[pl.ds(start, SPAN), :], d_ref[:, 0:width])
            total += nt(g_ref[pl.ds(start + LANES, SPAN), :], d_ref[:, width : 2 * width])
            out_ref[pl.ds(start, SPAN), :] = total
            return carry

        lax.fori_loop(0, STEPS, step, 0)

    def bias_row(first, lane):
        mixed = jnp.where(lane_of((1, LANES)) >= lane, stat[first : first + 1, :], stat[first + 1 : first + 2, :])
        return pltpu.roll(jnp.broadcast_to(mixed, (8, LANES)), LANES - lane, axis=1)[0:1, :]

    def twice(row):
        return jnp.concatenate([row, row], axis=1)

    activate(pre_mid, x_one, 0)
    banded(x_one, f_one, twice(bias_row(33, 96)), pre_one)
    activate(pre_one, x_two, 1)
    banded(x_two, f_two, twice(bias_row(35, 96)), pre_two)
    activate(pre_two, x_three, 2)

    def weight_grads(g_ref, x_ref, parts, write):
        width, wide = parts * LANES, 3 * parts * LANES
        middle0 = slice(width, 2 * width)
        middle1 = slice(wide + width, wide + 2 * width)
        acc0[0 : 2 * width, :] = jnp.zeros((2 * width, 768), F32)
        acc1[0:width, :] = jnp.zeros((width, 384), F32)
        acc2[0:width, :] = jnp.zeros((width, 384), F32)

        def step(b, carry):
            start = pl.multiple_of(b * SPAN, LANES)
            rows = pl.ds(start, SPAN)
            g0, g1 = g_ref[rows, middle0], g_ref[rows, middle1]
            both = jnp.concatenate([g0, g1], axis=1)
            acc0[0 : 2 * width, :] += tn(both, x_ref[rows, :])
            acc2[0:width, :] += tn(g1, x_ref[pl.ds(start + LANES, SPAN), 0:384])
            after = g_ref[pl.ds(start + LANES, SPAN), middle0]
            acc1[0:width, :] += tn(after, x_ref[rows, 384:768])
            return carry

        lax.fori_loop(0, STEPS, step, 0)
        for i in range(3):
            if i == 0:
                total = acc0[width : 2 * width, 0:384] + acc1[0:width, :]
            elif i == 1:
                total = acc0[0:width, 0:384] + acc0[width : 2 * width, 384:768]
            else:
                total = acc0[0:width, 384:768] + acc2[0:width, :]
            for j in range(3):
                for part in range(parts):
                    block = total[part * LANES : (part + 1) * LANES, j * LANES : (j + 1) * LANES]
                    write(i, j, part, jnp.transpose(block))

    def bias_grads(g_ref, parts):
        width, wide = parts * LANES, 3 * parts * LANES
        ones = jnp.ones((16, SPAN), BF16)

        def step(b, total):
            rows = pl.ds(pl.multiple_of(b * SPAN, LANES), SPAN)
            total += nn(ones, g_ref[rows, width : 2 * width])
            return total + nn(ones, g_ref[rows, wide + width : wide + 2 * width])

        return lax.fori_loop(0, STEPS, step, jnp.zeros((16, width), F32))[0:1, :]

    def last_layers(pre_three, x_head, g_three):
        bias = jnp.concatenate([bias_row(37, 96), bias_row(38, 96)], axis=1)

        def conv_step(b, carry):
            start = pl.multiple_of(b * SPAN, LANES)
            rows, more = pl.ds(start, SPAN), pl.ds(start + LANES, SPAN)
            total = nn(x_ref3[rows, :], f_three[0:768, :]) + nn(x_ref3[more, 0:384], f_three[768:1152, :])
            pre_three[rows, 0:256] = total + bias
            total = nn(x_ref3[rows, 384:768], f_three[0:384, :]) + nn(x_ref3[more, :], f_three[384:1152, :])
            pre_three[rows, 256:512] = total + bias
            return carry

        x_ref3 = x_three
        lax.fori_loop(0, STEPS, conv_step, 0)

        def head_step(q, carry):
            rows = pl.ds(pl.multiple_of(q * LANES, LANES), LANES)
            value = pre_three[rows, :]
            x_head[rows, :] = (value * sigmoid(value)).astype(BF16)
            return carry

        lax.fori_loop(0, PAIRS, head_step, 0)
        for load in loads:
            load.wait()
        head_row = jnp.broadcast_to(stat[40:41, :], (LANES, LANES))
        b_head = jnp.sum(jnp.where(lane_of((16, LANES)) == row_of((16, LANES)) + 96, head_row[0:16, :], 0.0), axis=1, keepdims=True)
        divisor = jnp.maximum(stat[0:1, 3:4], 1.0)
        inverse = 1.0 / divisor
        row16 = row_of((16, LANES))

        def loss_tile(logits, place):
            row = place_row(place, edge, row_count)
            label = labels[row]
            kind = jnp.concatenate([label, jnp.zeros((14, LANES), jnp.int32)], axis=0)
            is_class = row16 < 2
            anchor0, anchor1 = label[0:1, :] == 1, label[1:2, :] == 1
            box_on = ((row16 < 9) & anchor0) | ((row16 >= 9) & anchor1)
            positive = (kind == 1).astype(F32)
            negative = (kind == 0).astype(F32)
            q = 1.0 / (1.0 + jnp.exp(-logits))
            rest = jnp.log(1.0 + jnp.exp(-jnp.abs(logits)))
            log_q = jnp.minimum(logits, 0.0) - rest
            log_not = jnp.minimum(-logits, 0.0) - rest
            short = 1.0 - q
            focal = -FOCAL_ALPHA * positive * short * short * log_q
            focal -= (1.0 - FOCAL_ALPHA) * negative * q * q * log_not
            slope_p = FOCAL_ALPHA * (2.0 * q * short * short * log_q - short * short * short)
            slope_n = (1.0 - FOCAL_ALPHA) * (q * q * q - 2.0 * q * q * short * log_not)
            residual = logits - boxes[row]
            size = jnp.abs(residual)
            huber = jnp.where(size < HUBER_BETA, (0.5 / HUBER_BETA) * residual * residual, size - 0.5 * HUBER_BETA)
            bent = jnp.clip(residual * (1.0 / HUBER_BETA), -1.0, 1.0)
            value = jnp.where(is_class, focal, jnp.where(box_on, 2.0 * huber, 0.0))
            grad = jnp.where(is_class, positive * slope_p + negative * slope_n, jnp.where(box_on, 2.0 * bent, 0.0))
            good = ok(place)
            return pick(good, value, 0.0), pick(good, grad * inverse, 0.0)

        def loss_step(q, total):
            rows = pl.ds(pl.multiple_of(q * LANES, LANES), LANES)
            for e in range(2):
                logits = nt(head_t[...], x_head[rows, e * 256 : (e + 1) * 256]) + b_head
                value, grad = loss_tile(logits, 2 * q + 1 + e)
                logit_grads[e, :, rows] = grad.astype(BF16)
                total = total + value
            return total

        total = lax.fori_loop(0, PAIRS, loss_step, jnp.zeros((16, LANES), F32), unroll=3)
        total = jnp.sum(jnp.sum(total, axis=1, keepdims=True), axis=0, keepdims=True)
        loss_mine[...] = jnp.broadcast_to(total, (8, LANES))
        for k in range(1, n):
            loss_copy(k).start()
        g_head = jnp.zeros((16, CR3), F32)
        g_bias = jnp.zeros((16, 1), F32)
        for e in range(2):
            g_head += nn(logit_grads[e], x_head[0:GRID, e * 256 : (e + 1) * 256])
            g_bias += jnp.sum(logit_grads[e].astype(F32), axis=1, keepdims=True)
        back_rows = jnp.where(same_eighth(), tn(g_head, fold16().astype(F32), HIGH), 0.0)
        grad_b[B_HEAD : B_HEAD + 32, :] = tn(eighths().astype(F32), back_rows, HIGH)
        spots = (lane_of((16, LANES)) == row_of((16, LANES))).astype(F32)
        grad_b[B_HEAD + 32 : B_HEAD + 33, :] = jnp.sum(spots * g_bias, axis=0, keepdims=True)

        def back_step(q, carry):
            rows = pl.ds(pl.multiple_of(q * LANES, LANES), LANES)
            for e in range(2):
                grad = tn(logit_grads[e, :, rows], head_t[...])
                grad = grad * slope(pre_three[rows, e * 256 : (e + 1) * 256])
                for part in range(2):
                    put(g_three, q + e, 1 - e, grad[:, part * LANES : (part + 1) * LANES], part, 2)
            return carry

        g_three[0:LANES, 0:768] = jnp.zeros((LANES, 768), BF16)
        g_three[18 * LANES : 20 * LANES, :] = jnp.zeros((2 * LANES, 1536), BF16)
        lax.fori_loop(0, PAIRS, back_step, 0)
        last_row = slice(16 * LANES, 17 * LANES)
        send_up_w[...] = g_three[0:LANES, 1024:1280]
        send_down_w[...] = pick(split == 1, g_three[last_row, 1024:1280], g_three[last_row, 256:512])
        copies = halo_copies(0, send_up_w, send_down_w, from_up_w, from_down_w, sem_ws, sem_wr)
        halo_start(copies)

        def write(i, j, part, block):
            start = B_THREE + 2 * (i * 3 + j) * LANES + part
            grad_b[pl.ds(start, LANES, 2), :] = block

        weight_grads(g_three, x_three, 2, write)
        sums = bias_grads(g_three, 2)
        grad_b[B_HEAD - 2 : B_HEAD - 1, :] = sums[:, 0:LANES]
        grad_b[B_HEAD - 1 : B_HEAD, :] = sums[:, LANES : 2 * LANES]
        halo_wait(copies)
        put_edges(g_three, 0, 2, from_up_w[...], from_down_w[...])
        banded_back(g_three, d_three, back)

    def loss_copy(k):
        return remote(loss_mine, loss_all.at[me], sem_ls.at[k], sem_lr.at[me], lax.rem(me + k, n))

    pl.run_scoped(
        last_layers,
        pltpu.VMEM((GRID, 512), F32),
        pltpu.VMEM((GRID, 512), BF16),
        pltpu.VMEM((20 * LANES, 1536), BF16),
    )

    def lower_layers(g_ref, g_map, win0, win1, win2, gathered):
        def grads_in(pre_ref):
            def step(q, carry):
                rows = pl.ds(pl.multiple_of(q * LANES, LANES), LANES)
                for e in range(2):
                    lanes = slice(e * LANES, (e + 1) * LANES)
                    value = back[rows, lanes] * slope(pre_ref[rows, lanes])
                    put(g_ref, q + e, 1 - e, pick(ok(2 * q + 1 + e), value, 0.0), 0, 1)
                return carry

            lax.fori_loop(0, PAIRS, step, 0)

        def layer(pre_ref, x_ref, d_ref, begin, s):
            g_ref[0:LANES, 0:384] = jnp.zeros((LANES, 384), BF16)
            grads_in(pre_ref)
            exchange(g_ref, s)

            def write(i, j, part, block):
                start = begin + (i * 3 + j) * LANES
                grad_b[start : start + LANES, :] = block

            weight_grads(g_ref, x_ref, 1, write)
            grad_b[begin + 1152 : begin + 1153, :] = bias_grads(g_ref, 1)
            halo_wait(thin(s))
            put_edges(g_ref, s, 1, from_up[s], from_down[s])
            banded_back(g_ref, d_ref, back)

        g_ref[18 * LANES : 20 * LANES, :] = jnp.zeros((2 * LANES, 768), BF16)
        layer(pre_two, x_two, d_two, B_TWO, 3)
        layer(pre_one, x_one, d_one, B_ONE, 4)

        g_map[...] = jnp.zeros_like(g_map)

        def to_map(q, total):
            rows = pl.ds(pl.multiple_of(q * LANES, LANES), LANES)
            for e in range(2):
                p = 2 * q + 1 + e
                lanes = slice(e * LANES, (e + 1) * LANES)
                value = back[rows, lanes] * slope(pre_mid[rows, lanes])
                value = pick(ok(p), value, 0.0).astype(BF16).astype(F32)
                g_map[pl.ds(pl.multiple_of(p * PITCH + 8, 8), LANES), :] = value
                total += jnp.sum(value, axis=0, keepdims=True)
            return total

        total = lax.fori_loop(0, PAIRS, to_map, jnp.zeros((1, LANES), F32))
        total = total[:, 0:CM] + total[:, CM : 2 * CM]
        grad_a[0:A_MID, :] = jnp.zeros((A_MID, LANES), F32)
        grad_a[A_MID + 1728 : A_ROWS, :] = jnp.zeros((A_ROWS - A_MID - 1728, LANES), F32)
        grad_a[A_MID + 1728 : A_MID + 1729, 0:CM] = total

        def map_row(place):
            return slice(place * PITCH + 8, place * PITCH + 8 + LANES)

        send_up[5] = g_map[map_row(1), :].astype(BF16)
        send_down[5] = pick(split == 1, g_map[map_row(row_count + 1), :], g_map[map_row(row_count), :]).astype(BF16)
        halo_start(thin(5))
        halo_wait(thin(5))
        g_map[map_row(0), :] = pick((top == 1) & has_up, from_up[5].astype(F32), 0.0)
        halo = pick((bottom == 1) & has_down, from_down[5].astype(F32), 0.0)
        g_map[map_row(row_count + 1), :] = pick(split == 1, g_map[map_row(row_count + 1), :], halo)
        g_map[map_row(row_count + 2), :] = pick(split == 1, halo, 0.0)

        wins = (win0, win1, win2)
        voxels = feature.shape[0]
        depth_cells = row_count * LANES * ZD

        def fetch(v, carry):
            base = voxel_base(cells_smem[v], depth_cells, LANES, edge, split)
            for i in range(3):
                wins[i][pl.ds(4 * v, 3), :] = g_map[pl.ds(base + (1 - i) * PITCH, 3), :]
            return carry

        lax.fori_loop(0, voxels, fetch, 0, unroll=8)
        for i in range(3):
            for j in range(3):
                lanes = slice((i * 3 + j) * LANES, (i * 3 + j + 1) * LANES)
                gathered[:, lanes] = wins[i][pl.ds(2 - j, voxels, 4), :].astype(BF16)
        low = lane_of((64, LANES)) < 64
        for i in range(3):
            block = tn(spread[...], gathered[:, i * 384 : (i + 1) * 384])
            for j in range(3):
                part = block[:, j * LANES : (j + 1) * LANES]
                even = [part[z * LANES : z * LANES + 64] for z in range(ZD)]
                odd = [part[z * LANES + 64 : (z + 1) * LANES] for z in range(ZD)]

                def flip(x):
                    return pltpu.roll(x, 64, axis=1)

                taps = (
                    jnp.where(low, flip(even[1]), odd[1]),
                    jnp.where(low, even[0] + flip(even[2]), flip(odd[0]) + odd[2]),
                    jnp.where(low, even[1] + flip(even[3]), flip(odd[1]) + odd[3]),
                )
                for t in range(3):
                    start = A_MID + (t * 9 + i * 3 + j) * 64
                    grad_a[start : start + 64, :] = taps[t]
        z_column = z_columns(cells_row[...])
        total = jnp.zeros((voxels, C2), F32)
        for z in range(ZD):
            total += jnp.where(z_column == z, nt(gathered[...], w_mid[z * C2 : (z + 1) * C2, :]), 0.0)
        grad_feature[...] = total

    voxels = feature.shape[0]
    pl.run_scoped(
        lower_layers,
        pltpu.VMEM((20 * LANES, 768), BF16),
        pltpu.VMEM(((row_count + 6) * PITCH, LANES), F32),
        pltpu.VMEM((voxels * 4, LANES), F32),
        pltpu.VMEM((voxels * 4, LANES), F32),
        pltpu.VMEM((voxels * 4, LANES), F32),
        pltpu.VMEM((voxels, 1152), BF16),
    )
    for k in range(1, n):
        sender = lax.rem(me + n - k, n)
        remote(loss_mine, loss_all.at[sender], sem_ls.at[k], sem_lr.at[sender], sender).wait_recv()
    loss_all[me] = loss_mine[...]
    total = loss_all[0]
    for d in range(1, n):
        total += loss_all[d]
    loss_out[...] = total
    for k in range(1, n):
        loss_copy(k).wait_send()


def convs(n, row_count, cells, feature, stat, middle_out, labels, boxes):
    shape = jax.ShapeDtypeStruct
    dma = pltpu.SemaphoreType.DMA
    voxels = feature.shape[0]
    row = (LANES, LANES)
    return pl.pallas_call(
        functools.partial(conv_kernel, n, row_count),
        name="convs",
        out_shape=(
            shape((A_ROWS, LANES), F32),
            shape((B_ROWS, LANES), F32),
            shape((voxels, LANES), F32),
            shape((8, LANES), F32),
        ),
        in_specs=[smem()] + [vmem()] * 12 + [anywhere()] * 2,
        out_specs=(vmem(),) * 4,
        scratch_shapes=[
            pltpu.VMEM((20 * LANES, 768), BF16),
            pltpu.VMEM((20 * LANES, 768), BF16),
            pltpu.VMEM((20 * LANES, 768), BF16),
            pltpu.VMEM((GRID, 256), F32),
            pltpu.VMEM((GRID, 256), F32),
            pltpu.VMEM((GRID, 256), F32),
            pltpu.VMEM((GRID, 256), F32),
            pltpu.VMEM((voxels, ZD * C2), BF16),
            pltpu.VMEM((512, 768), F32),
            pltpu.VMEM((256, 384), F32),
            pltpu.VMEM((256, 384), F32),
            pltpu.VMEM((row_count, 2, LANES), jnp.int32),
            pltpu.VMEM((row_count, 16, LANES), F32),
            pltpu.VMEM((2, 16, GRID), BF16),
            pltpu.VMEM((8, LANES), F32),
            pltpu.VMEM((n, 8, LANES), F32),
            pltpu.VMEM(row, F32),
            pltpu.VMEM(row, F32),
            pltpu.VMEM(row, F32),
            pltpu.VMEM(row, F32),
            pltpu.VMEM((6,) + row, BF16),
            pltpu.VMEM((6,) + row, BF16),
            pltpu.VMEM((6,) + row, BF16),
            pltpu.VMEM((6,) + row, BF16),
            pltpu.VMEM((LANES, 256), BF16),
            pltpu.VMEM((LANES, 256), BF16),
            pltpu.VMEM((LANES, 256), BF16),
            pltpu.VMEM((LANES, 256), BF16),
            dma((16,)), dma((2,)), dma((2,)), dma((12,)), dma((12,)), dma((2,)), dma((2,)), dma((n,)), dma((n,)),
        ],
        compiler_params=pltpu.CompilerParams(
            collective_id=2, has_side_effects=True, vmem_limit_bytes=62 << 20
        ),
    )(cells, cells.reshape(1, -1), feature, stat, *middle_out, labels, boxes)


def adam_outer(gradient, weight, moment, second, momentum):
    moment = FIRST_DECAY * moment + (1.0 - FIRST_DECAY) * gradient
    second = SECOND_DECAY * second + (1.0 - SECOND_DECAY) * gradient * gradient
    moment_fix = moment / (1.0 - FIRST_DECAY**STEP)
    second_fix = second / (1.0 - SECOND_DECAY**STEP)
    inner_weight = weight - INNER_RATE * (
        moment_fix / (jnp.sqrt(second_fix) + ADAM_EPSILON) + WEIGHT_DECAY * weight
    )
    inner_step = weight - inner_weight
    momentum = OUTER_MOMENT * momentum + inner_step
    updated = weight - OUTER_RATE * (inner_step + OUTER_MOMENT * momentum)
    return (moment, second, momentum, updated)


def flat_pieces(rows, slot):
    begin, end = slot * rows, (slot + 1) * rows
    spans = ((0, 67, None, 0), (67, 1795, "a", 2), (1795, 1796, "both", 0), (1796, 6440, "b", 1795), (6440, 1 << 30, None, 0))
    pieces = []
    for low, high, run, shift in spans:
        first, last = max(begin, low), min(end, high)
        if first < last:
            pieces.append((first - begin, last - first, run, first - shift))
    return pieces


NOTE = 112


def finish_kernel(
    n, points_hbm, counts_ref, small, stat, linear, joined, grad_feature, grad_a, grad_b,
    weight, moment, second, momentum,
    moment_out, second_out, momentum_out, weight_out,
    points, first, slots, pair, line, mine, notes, fc_rows, small_grad,
    sem_p, sem_ps, sem_pr, sem_zs, sem_zr, sem_ns, sem_nr,
):
    me = lax.axis_index("tile")
    rows = weight.shape[0]
    half = n // 2
    parity, chip = lax.rem(me, 2), me // 2
    sibling = me + 1 - 2 * parity
    count_p, voxels = points_hbm.shape[1], points_hbm.shape[2]
    points[...] = jnp.ones_like(points)
    loads = [
        pltpu.make_async_copy(points_hbm.at[k], points.at[:, k, :], sem_p.at[k]) for k in range(7)
    ]
    for load in loads:
        load.start()
    enter(n, me)

    def realigned(ref, start, count, lane):
        here, before = ref[pl.ds(start, count), :], ref[pl.ds(start - 1, count), :]
        mixed = jnp.where(lane_of((count, LANES)) >= LANES - lane, before, here)
        return pltpu.roll(mixed, lane, axis=1)

    for s in range(n):
        for row, count, run, start in flat_pieces(rows, s):
            if run is None:
                value = jnp.zeros((count, LANES), F32)
            elif run == "a":
                value = realigned(grad_a, start, count, 32)
            elif run == "b":
                value = realigned(grad_b, start, count, 96)
            else:
                lane = lane_of((8, LANES))
                part_a = jnp.where(lane[0:1] >= 96, grad_a[1792:1793, :], grad_a[1793:1794, :])
                part_b = jnp.where(lane[0:1] >= 32, 0.0, grad_b[0:1, :])
                part_a = pltpu.roll(jnp.broadcast_to(part_a, (8, LANES)), 32, axis=1)
                part_b = pltpu.roll(jnp.broadcast_to(part_b, (8, LANES)), 96, axis=1)
                value = (jnp.where(lane < 96, part_a, part_b))[0:1]
            slots[s, row : row + count, :] = value

    def pair_copy(k):
        return remote(slots.at[2 * k + 1 - parity], pair.at[k], sem_ps.at[k], sem_pr.at[k], sibling)

    for k in range(half):
        pair_copy(k).start()

    def line_copy(k):
        target = lax.rem(me + 2 * k, n)
        return remote(slots.at[target], line.at[chip], sem_zs.at[k], sem_zr.at[chip], target)

    for k in range(half):
        pair_copy(k).wait()
        slots[2 * k + parity] = slots[2 * k + parity] + pair[k]
    for k in range(1, half):
        line_copy(k).start()

    counts = counts_ref[...]
    columns, gamma, beta = first_layer(small)
    mean, scale, held = stat[0:32, 0:1], stat[0:32, 1:2], stat[0:32, 2:3]
    centre = stat[0:8, 4:5]
    order = even_first()
    rows_fc = voxel_rows(small)
    kernel = rows_fc[0:64, :].astype(BF16)
    kernel_t = nt(order.astype(BF16), kernel).astype(BF16)
    kernel = nt(kernel, order.astype(BF16)).astype(BF16)
    bias = jnp.sum(jnp.where(order, rows_fc[64:65, :], 0.0), axis=1, keepdims=True)
    counts_f = counts.astype(F32)
    grad_pre = jnp.transpose(grad_feature[...]) / counts_f

    def pass_e(p, carry):
        fc, pooled = carry
        inner = nn(kernel_t, joined[p, 0:64, :]) + bias
        grad = jnp.where(p < counts, grad_pre * slope(inner), 0.0).astype(BF16)
        fc += nt(joined[p], grad)
        down = nn(kernel, grad)
        first[p] = down[0:32]
        return fc, pooled + down[32:64]

    fc, pooled = lax.fori_loop(
        0, count_p, pass_e, (jnp.zeros((80, LANES), F32), jnp.zeros((32, voxels), F32))
    )
    pooled = pooled / counts_f
    for load in loads:
        load.wait()

    def halves(value):
        high = value.astype(BF16)
        return high, (value - high.astype(F32)).astype(BF16)

    def pass_f(p, carry):
        moments, g_gamma, centred = carry
        inside = p < counts
        normed = jnp.where(inside, (linear[p] - mean) * scale, 0.0)
        act = gamma * normed + beta
        grad = jnp.where(inside, (first[p] + pooled) * slope(act), 0.0)
        off = points[p] - centre
        off_high, off_low = halves(off)
        grad_high, grad_low = halves(grad)
        norm_high, norm_low = halves(normed)
        left = jnp.concatenate([grad_high, grad_low, norm_high, norm_low], axis=0)
        right = jnp.concatenate([off_high, off_low], axis=0)
        return (
            moments + nt(left, right),
            g_gamma + grad * normed,
            centred + jnp.where(inside, off, 0.0),
        )

    moments, g_gamma, centred = lax.fori_loop(
        0,
        count_p,
        pass_f,
        (jnp.zeros((LANES, 16), F32), jnp.zeros((32, voxels), F32), jnp.zeros((8, voxels), F32)),
    )
    by_grad = moments[0:32] + moments[32:64]
    by_grad = by_grad[:, 0:8] + by_grad[:, 8:16]
    by_norm = moments[64:96] + moments[96:128]
    by_norm = by_norm[:, 0:8] + by_norm[:, 8:16]
    mine[...] = jnp.zeros_like(mine)
    mine[0:72, :] = fc[0:72]
    mine[72:104, 0:8] = by_grad
    mine[72:104, 8:16] = by_norm
    mine[72:104, 16:17] = jnp.sum(g_gamma, axis=1, keepdims=True)
    mine[104:112, 0:1] = jnp.sum(centred, axis=1, keepdims=True)
    small_grad[...] = jnp.zeros_like(small_grad)

    def note(sender):
        return remote(mine, notes.at[sender], sem_ns.at[0], sem_nr.at[sender], 0)

    @pl.when(me > 0)
    def _():
        note(me).start()

    @pl.when(me == 0)
    def _():
        notes[0] = mine[...]
        for d in range(1, n):
            note(d).wait_recv()
        total = notes[0]
        for d in range(1, n):
            total += notes[d]
        by_grad, by_norm = total[72:104, 0:8], total[72:104, 8:16]
        g_gamma, g_beta = total[72:104, 16:17], total[72:104, 7:8]
        off_sums = jnp.transpose(jnp.broadcast_to(total[104:112, 0:1], (8, LANES)))[0:32, 0:8]
        g_vfe = scale * gamma * (
            by_grad - g_beta / held * off_sums - g_gamma / held * by_norm
        )
        tall0 = jnp.concatenate([g_vfe[:, k : k + 1] for k in range(4)], axis=0)
        tall1 = jnp.concatenate([g_vfe[:, 4:5], g_vfe[:, 5:6], g_vfe[:, 6:7], g_gamma], axis=0)
        tall2 = jnp.concatenate([g_beta, jnp.zeros((96, 1), F32)], axis=0)
        lane = lane_of((LANES, LANES))
        tall = jnp.where(lane == 0, tall0, 0.0) + jnp.where(lane == 1, tall1, 0.0) + jnp.where(lane == 2, tall2, 0.0)
        head = jnp.transpose(tall)[0:8]
        fc_rows[...] = jnp.zeros_like(fc_rows)
        fc_rows[8:80, :] = nn(total[0:72], order.astype(F32), HIGH)
        small_grad[2:74, :] = realigned(fc_rows, 8, 72, 32)
        small_grad[0:8, :] = small_grad[0:8, :] + head

    total = slots[me, 0:rows, :]
    for k in range(1, half):
        source = lax.rem(chip + half - k, half)
        remote(slots.at[0], line.at[source], sem_zs.at[k], sem_zr.at[source], sibling).wait_recv()
        total += line[source, 0:rows, :]
    slots[me, 0:rows, :] = total
    slots[me, 0:SMALL, :] = slots[me, 0:SMALL, :] + small_grad[...]
    outs = adam_outer(slots[me, 0:rows, :], weight[...], moment[...], second[...], momentum[...])
    moment_out[...], second_out[...], momentum_out[...], weight_out[...] = outs
    for k in range(1, half):
        line_copy(k).wait_send()

    @pl.when(me > 0)
    def _():
        note(me).wait_send()


def finish(n, points, counts, small, stat, linear, joined, grad_feature, grad_a, grad_b, shards):
    shape = jax.ShapeDtypeStruct
    dma = pltpu.SemaphoreType.DMA
    slots, voxels = points.shape[1:]
    rows = shards[0].shape[0]
    padded = ceil_to(rows, 8)
    half = n // 2
    return pl.pallas_call(
        functools.partial(finish_kernel, n),
        name="finish",
        out_shape=(shape((rows, LANES), F32),) * 4,
        in_specs=[anywhere()] + [vmem()] * 12,
        out_specs=(vmem(),) * 4,
        scratch_shapes=[
            pltpu.VMEM((slots, 8, voxels), F32),
            pltpu.VMEM((slots, 32, voxels), F32),
            pltpu.VMEM((n, padded, LANES), F32),
            pltpu.VMEM((half, padded, LANES), F32),
            pltpu.VMEM((half, padded, LANES), F32),
            pltpu.VMEM((NOTE, LANES), F32),
            pltpu.VMEM((n, NOTE, LANES), F32),
            pltpu.VMEM((88, LANES), F32),
            pltpu.VMEM((SMALL, LANES), F32),
            dma((7,)), dma((half,)), dma((half,)), dma((half,)), dma((half,)), dma((1,)), dma((n,)),
        ],
        compiler_params=pltpu.CompilerParams(
            collective_id=3, has_side_effects=True, vmem_limit_bytes=58 << 20
        ),
    )(points, counts, small, stat, linear, joined, grad_feature, grad_a, grad_b, *shards)


def shards(
    points, point_counts, voxel_cells, anchor_labels, box_targets, weights, adam_m, adam_v, outer_momentum
):
    n = lax.axis_size("tile")
    rows = weights.shape[0] // LANES
    row_count = anchor_labels.shape[1]
    held = [x.reshape(rows, LANES) for x in (weights, adam_m, adam_v, outer_momentum)]
    counts = point_counts.reshape(1, -1)
    wall, small, stat, linear, joined, feature = front(n, points, counts, anchor_labels, held[0])
    ready = middle(n, rows, row_count, voxel_cells, feature, wall)
    grad_a, grad_b, grad_feature, loss = convs(
        n, row_count, voxel_cells, feature, stat, ready, anchor_labels, box_targets
    )
    outs = finish(
        n, points, counts, small, stat, linear, joined, grad_feature, grad_a, grad_b, held
    )
    moment, second, momentum, updated = [x.reshape(weights.shape) for x in outs]
    return (moment, second, momentum, updated, loss[0, 0:1], stat[0, 3:4])


def solution(mesh):
    split = ("group", "tile")
    in_specs = (
        P(None, None, split), P(split), P(split), P(None, split, None), P(None, split, None),
        P(split), P(split), P(split), P(split),
    )
    out_specs = (P(split), P(split), P(split), P(split), P("group"), P("group"))
    return jax.shard_map(shards, mesh=mesh, in_specs=in_specs, out_specs=out_specs, check_vma=False)
```

```python
import functools
import math

import jax
import jax.numpy as jnp
from jax import lax
from jax.experimental import pallas as pl
from jax.experimental.pallas import tpu as pltpu
from jax.sharding import PartitionSpec as P

MESH = pl.DeviceIdType.MESH
F32 = jnp.float32
BF16 = jnp.bfloat16
HIGH = lax.Precision.HIGHEST

C1, C2, CM, CR1, CR2, CR3, ANCH, ZD = 32, 128, 64, 128, 128, 256, 2, 4
H_SCENE = 200
STEP = 10
LANES = 128
NORM_EPSILON = 1e-05
INNER_RATE = 0.05
FIRST_DECAY = 0.9
SECOND_DECAY = 0.999
ADAM_EPSILON = 1e-08
WEIGHT_DECAY = 0.01
OUTER_RATE = 0.7
OUTER_MOMENT = 0.9
FOCAL_ALPHA = 0.25
HUBER_BETA = 1.0 / 9.0

SMALL = 80
FC_ROW, FC_LANE = 2, 32
BIAS_ROWS = (1795, 2947, 2948, 4100, 4101, 6405, 6406, 6407, 6439)
RUN_A = (2, 32)
RUN_B = (1795, 96)
A_MID = 65
B_ONE, B_TWO, B_THREE, B_HEAD = 0, 1153, 2306, 4612
PAIRS_OF = tuple((a, b) for a in range(7) for b in range(a, 7))
DIAGONAL = tuple(r for r, (a, b) in enumerate(PAIRS_OF) if a == b)
CHUNK = 256


def vmem():
    return pl.BlockSpec(memory_space=pltpu.VMEM)


def anywhere():
    return pl.BlockSpec(memory_space=pl.ANY)


def smem():
    return pl.BlockSpec(memory_space=pltpu.SMEM)


def ceil_to(value, step):
    return (value + step - 1) // step * step


def sigmoid(value):
    return 0.5 * jnp.tanh(0.5 * value) + 0.5


def slope(value):
    s = sigmoid(value)
    return s * (1.0 + value * (1.0 - s))


def nt(a, b, precision=None):
    return lax.dot_general(a, b, (((1,), (1,)), ((), ())), precision=precision, preferred_element_type=F32)


def tn(a, b, precision=None):
    return lax.dot_general(a, b, (((0,), (0,)), ((), ())), precision=precision, preferred_element_type=F32)


def nn(a, b, precision=None):
    return lax.dot_general(a, b, (((1,), (0,)), ((), ())), precision=precision, preferred_element_type=F32)


def lane_of(shape):
    return lax.broadcasted_iota(jnp.int32, shape, len(shape) - 1)


def row_of(shape):
    return lax.broadcasted_iota(jnp.int32, shape, len(shape) - 2)


def enter(n, me, between=None):
    sem = pltpu.get_barrier_semaphore()

    def greet(k, carry):
        pl.semaphore_signal(
            sem, inc=1, device_id={"tile": lax.rem(me + k, n)}, device_id_type=MESH
        )
        return carry

    lax.fori_loop(1, n, greet, 0)
    if between is not None:
        between()
    pl.semaphore_wait(sem, n - 1)


def remote(src, dst, send, recv, peer):
    return pltpu.make_async_remote_copy(
        src_ref=src,
        dst_ref=dst,
        send_sem=send,
        recv_sem=recv,
        device_id={"tile": peer},
        device_id_type=MESH,
    )


def even_first():
    out = row_of((LANES, LANES))
    source = jnp.where(out < 64, 2 * out, 2 * out - 127)
    return lane_of((LANES, LANES)) == source


def first_layer(small_ref):
    turned = jnp.transpose(small_ref[0:LANES_PAD, :])
    columns = [turned[(k % 4) * 32 : (k % 4) * 32 + 32, k // 4 : k // 4 + 1] for k in range(7)]
    return columns, turned[96:128, 1:2], turned[0:32, 2:3]


LANES_PAD = 8


def voxel_rows(small_ref):
    here, after = small_ref[2:74, :], small_ref[3:75, :]
    mixed = jnp.where(lane_of((72, LANES)) >= FC_LANE, here, after)
    return pltpu.roll(mixed, LANES - FC_LANE, axis=1)


def linear_row(wide, points, p):
    value = wide[0] * points[0, pl.ds(p, 1), :]
    for k in range(1, 7):
        value += wide[k] * points[k, pl.ds(p, 1), :]
    return value


def local_moments(points, counts, labels_ref, sums, message):
    slots, voxels = points.shape[1:]
    inside = row_of((slots, voxels)) < counts

    def folded(value):
        total = value[:, 0:LANES]
        for c in range(1, voxels // LANES):
            total = total + value[:, c * LANES : (c + 1) * LANES]
        return jnp.sum(total, axis=0, keepdims=True)

    def whole(row):
        return jnp.sum(row, axis=1, keepdims=True)

    held = whole(folded(inside.astype(F32)))
    masked = [jnp.where(inside, points[k], 0.0) for k in range(7)]
    rows = [folded(value) for value in masked]
    means = [whole(row) / held for row in rows]
    centred = [jnp.where(inside, points[k] - means[k], 0.0) for k in range(7)]
    for r, (a, b) in enumerate(PAIRS_OF):
        sums[0, r : r + 1, :] = folded(centred[a] * centred[b])
        sums[1, r : r + 1, :] = rows[a]
        sums[2, r : r + 1, :] = rows[b]
    spare = len(PAIRS_OF)
    for c in range(3):
        sums[c, spare:LANES, :] = jnp.zeros((LANES - spare, LANES), F32)
    lane = lane_of((LANES, LANES))
    columns = jnp.zeros((LANES, LANES), F32)
    for c in range(3):
        columns = jnp.where(lane == c, jnp.sum(sums[c], axis=1, keepdims=True), columns)
    positives = jnp.zeros((1, 1), F32)
    for a in range(ANCH):
        positives += whole(jnp.sum((labels_ref[a] == 1).astype(F32), axis=0, keepdims=True))
    packed = jnp.transpose(columns)[0:8]
    row = row_of((8, LANES))
    packed = jnp.where(row == 3, held, packed)
    message[...] = jnp.where(row == 4, positives, packed)


def joint_moments(n, messages):
    total = messages[0]
    for d in range(1, n):
        total += messages[d]
    held = total[3:4]
    mean_a, mean_b = total[1:2] / held, total[2:3] / held
    product = total[0:1]
    for d in range(n):
        held_d = messages[d, 3:4, :]
        product += held_d * (messages[d, 1:2, :] / held_d - mean_a) * (messages[d, 2:3, :] / held_d - mean_b)
    return mean_a, product, held, total[4:5]


def channel_statistics(columns, mean_row, product, held):
    lane = lane_of((32, LANES))
    once, twice = jnp.zeros((32, LANES), F32), jnp.zeros((32, LANES), F32)
    for r, (a, b) in enumerate(PAIRS_OF):
        if a == b:
            once = jnp.where(lane == r, columns[a], once)
        twice = jnp.where(lane == r, (1.0 if a == b else 2.0) * columns[a] * columns[b], twice)
    mean = jnp.sum(once * mean_row, axis=1, keepdims=True)
    variance = jnp.sum(twice * (product / held), axis=1, keepdims=True)
    return mean, lax.rsqrt(variance + NORM_EPSILON)


def front_kernel(
    n, points, counts_ref, labels_ref, shard_ref,
    wall, small, stat, first_out, pooled_out, feature,
    own, sums, mine, messages, my_bias, biases,
    sem_small_s, sem_small_r, sem_msg_s, sem_msg_r, sem_b_s, sem_b_r, sem_w_s, sem_w_r, sem_f_s,
):
    me = lax.axis_index("tile")
    rows = shard_ref.shape[0]
    slots, voxels = points.shape[1:]
    sibling = me + 1 - 2 * lax.rem(me, 2)
    half = n // 2
    counts = counts_ref[...]

    def prepare():
        local_moments(points, counts, labels_ref, sums, mine)
        own[...] = jnp.zeros_like(own)
        own[0:rows, :] = shard_ref[...].astype(BF16)
        for a, row in enumerate(BIAS_ROWS):
            owner, place = row // rows, row % rows
            my_bias[a : a + 1, :] = jnp.where(me == owner, shard_ref[place : place + 1, :], 0.0)
        for a in range(len(BIAS_ROWS), 16):
            my_bias[a : a + 1, :] = jnp.zeros((1, LANES), F32)

    enter(n, me, prepare)

    def message(k):
        return remote(mine, messages.at[me], sem_msg_s.at[k], sem_msg_r.at[me], lax.rem(me + k, n))

    def bias_message(k):
        return remote(my_bias, biases.at[me], sem_b_s.at[k], sem_b_r.at[me], lax.rem(me + k, n))

    def small_copy(k):
        return remote(small, small, sem_small_s.at[k], sem_small_r.at[0], lax.rem(me + k, n))

    def shard_copy(k):
        return remote(own, wall.at[me], sem_w_s.at[k], sem_w_r.at[me], lax.rem(me + 2 * k, n))

    for k in range(1, n):
        message(k).start()

    @pl.when(me == 0)
    def _():
        small[...] = shard_ref[0:SMALL, :]

        def send(k, carry):
            small_copy(k).start()
            return carry

        lax.fori_loop(1, n, send, 0)

    for k in range(1, n):
        bias_message(k).start()
    for k in range(1, half):
        shard_copy(k).start()
    to_sibling = remote(own, wall.at[me], sem_w_s.at[0], sem_w_r.at[me], sibling)
    to_sibling.start()
    wall[me] = own[...]
    messages[me] = mine[...]
    biases[me] = my_bias[...]

    @pl.when(me > 0)
    def _():
        small_copy(0).wait_recv()

    columns, gamma, beta = first_layer(small)
    order = even_first()
    rows_fc = voxel_rows(small)
    kernel_t = nt(order.astype(BF16), rows_fc[0:64, :].astype(BF16)).astype(BF16)
    bias = jnp.sum(jnp.where(order, rows_fc[64:65, :], 0.0), axis=1, keepdims=True)
    for k in range(1, n):
        sender = lax.rem(me + n - k, n)
        remote(mine, messages.at[sender], sem_msg_s.at[k], sem_msg_r.at[sender], sender).wait_recv()
    mean_row, product, held, positives = joint_moments(n, messages)
    mean, inverse = channel_statistics(columns, mean_row, product, held)
    lane, row = lane_of((32, LANES)), row_of((32, LANES))
    columns_out = jnp.where(lane == 0, mean, 0.0)
    columns_out = jnp.where(lane == 1, inverse, columns_out)
    columns_out = jnp.where(lane == 2, held, columns_out)
    columns_out = jnp.where(lane == 3, positives, columns_out)
    for k, r in enumerate(DIAGONAL):
        columns_out = jnp.where((lane == 4) & (row == k), mean_row[:, r : r + 1], columns_out)
    stat[0:32, :] = columns_out

    for c in range(voxels // CHUNK):
        part = slice(c * CHUNK, (c + 1) * CHUNK)
        wide = [jnp.broadcast_to(column, (32, CHUNK)) for column in columns]
        held_c = counts[:, part]
        view = points.at[:, :, part]

        def pass_c(p, pooled, wide=wide, held_c=held_c, view=view, part=part):
            act = gamma * ((linear_row(wide, view, p) - mean) * inverse) + beta
            out = jnp.where(p < held_c, act * sigmoid(act), 0.0)
            first_out[p, :, part] = out.astype(BF16)
            return pooled + out

        pooled = lax.fori_loop(0, slots, pass_c, jnp.zeros((32, CHUNK), F32), unroll=5)
        pooled = (pooled / held_c.astype(F32)).astype(BF16)
        pooled_out[:, part] = pooled
        fixed = nn(kernel_t[:, 32:64], pooled) + bias

        def pass_d(p, total, fixed=fixed, held_c=held_c, part=part):
            inner = nn(kernel_t[:, 0:32], first_out[p, :, part]) + fixed
            return total + jnp.where(p < held_c, inner * sigmoid(inner), 0.0)

        total = lax.fori_loop(0, slots, pass_d, jnp.zeros((LANES, CHUNK), F32), unroll=5)
        feature[part, :] = jnp.transpose(total / held_c.astype(F32))

    for k in range(1, half):
        source = lax.rem(me + n - 2 * k, n)
        remote(own, wall.at[source], sem_w_s.at[k], sem_w_r.at[source], source).wait_recv()
        remote(wall.at[source], wall.at[source], sem_f_s.at[k], sem_w_r.at[source], sibling).start()
    for k in range(1, n):
        sender = lax.rem(me + n - k, n)
        remote(my_bias, biases.at[sender], sem_b_s.at[k], sem_b_r.at[sender], sender).wait_recv()
    total = biases[0]
    for d in range(1, n):
        total += biases[d]
    stat[32:48, :] = total
    for k in range(half):
        source = lax.rem(sibling + n - 2 * k, n)
        remote(own, wall.at[source], sem_w_s.at[k], sem_w_r.at[source], source).wait_recv()
    for k in range(1, half):
        source = lax.rem(me + n - 2 * k, n)
        remote(wall.at[source], wall.at[source], sem_f_s.at[k], sem_w_r.at[source], sibling).wait_send()
        shard_copy(k).wait_send()
    to_sibling.wait_send()
    for k in range(1, n):
        message(k).wait_send()
        bias_message(k).wait_send()

    @pl.when(me == 0)
    def _():
        def done(k, carry):
            small_copy(k).wait_send()
            return carry

        lax.fori_loop(1, n, done, 0)


def front(n, points, counts, labels, shard):
    slots, voxels = points.shape[1:]
    rows = shard.shape[0]
    padded = ceil_to(rows, 16)
    shape = jax.ShapeDtypeStruct
    dma = pltpu.SemaphoreType.DMA
    return pl.pallas_call(
        functools.partial(front_kernel, n),
        name="front",
        out_shape=(
            shape((n, padded, LANES), BF16),
            shape((SMALL, LANES), F32),
            shape((48, LANES), F32),
            shape((slots, 32, voxels), BF16),
            shape((32, voxels), BF16),
            shape((voxels, LANES), F32),
        ),
        in_specs=[vmem()] * 4,
        out_specs=(vmem(),) * 6,
        scratch_shapes=[
            pltpu.VMEM((padded, LANES), BF16),
            pltpu.VMEM((3, LANES, LANES), F32),
            pltpu.VMEM((8, LANES), F32),
            pltpu.VMEM((n, 8, LANES), F32),
            pltpu.VMEM((16, LANES), F32),
            pltpu.VMEM((n, 16, LANES), F32),
            dma((n,)), dma((1,)), dma((n,)), dma((n,)), dma((n,)), dma((n,)), dma((n,)), dma((n,)), dma((n,)),
        ],
        compiler_params=pltpu.CompilerParams(
            collective_id=1, has_side_effects=True, vmem_limit_bytes=56 << 20
        ),
    )(points, counts, labels, shard)


def layout(n, row_count):
    first = lax.axis_index("tile") * row_count
    ahead = (first // H_SCENE + 1) * H_SCENE - first
    split = jnp.where(ahead < row_count, 1, 0)
    edge = jnp.where(ahead < row_count, ahead, row_count)
    top = jnp.where(lax.rem(first, H_SCENE) != 0, 1, 0)
    last = first + row_count
    bottom = jnp.where((lax.rem(last, H_SCENE) != 0) & (last < n * row_count), 1, 0)
    return edge, split, top, bottom


def place_ok(place, edge, split, row_count):
    return (place >= 1) & (place <= row_count + split) & ((place != edge + 1) | (split == 0))


def place_row(place, edge, row_count):
    row = jnp.where(place <= edge, place - 1, place - 2)
    return jnp.clip(row, 0, row_count - 1)


PITCH = 136


def voxel_base(cell, depth_cells, columns, edge, split):
    local = lax.rem(cell, depth_cells)
    spot = local // ZD
    row = spot // columns
    column = spot - row * columns
    place = row + 1 + jnp.where((row >= edge) & (split == 1), 1, 0)
    return place * PITCH + column + 7


def z_columns(cells_row):
    z = lax.rem(cells_row, ZD).astype(F32)
    return jnp.transpose(jnp.broadcast_to(z, (8, z.shape[1])))[:, 0:1]


def spread_z(feature, z_column, out_ref):
    for z in range(ZD):
        out_ref[:, z * C2 : (z + 1) * C2] = jnp.where(z_column == z, feature, 0.0).astype(BF16)


def middle_kernel(
    n, rows, row_count,
    cells_smem, cells_row, feature, wall,
    pre, w_mid, f_one, f_two, f_three, d_one, d_two, d_three, head_t,
    flat, run, spread, parts0, parts1, parts2, sum0, sum1, sum2,
):
    edge, split, _, _ = layout(n, row_count)
    voxels = feature.shape[0]
    columns = LANES
    parts, sums = (parts0, parts1, parts2), (sum0, sum1, sum2)
    for s in range(n):
        flat[s * rows : s * rows + wall.shape[1], :] = wall[s].astype(F32)

    def aligned(begin, start, count):
        row, lane = begin
        here = flat[pl.ds(row + start, count), :]
        after = flat[pl.ds(row + start + 1, count), :]
        mixed = jnp.where(lane_of((count, LANES)) >= lane, here, after)
        return pltpu.roll(mixed, LANES - lane, axis=1)

    low = lane_of((64, LANES)) < 64
    for ij in range(9):
        taps = [aligned(RUN_A, A_MID + (t * 9 + ij) * 64, 64) for t in range(3)]
        turned = [pltpu.roll(tap, 64, axis=1) for tap in taps]
        none = jnp.zeros((64, LANES), F32)
        for z in range(ZD):
            first, second = z + 1, z - 1
            a, a_t = (taps[first], turned[first]) if first < 3 else (none, none)
            b, b_t = (taps[second], turned[second]) if second >= 0 else (none, none)
            lanes = slice(ij * LANES, (ij + 1) * LANES)
            w_mid[z * C2 : z * C2 + 64, lanes] = jnp.where(low, a, b_t).astype(BF16)
            w_mid[z * C2 + 64 : (z + 1) * C2, lanes] = jnp.where(low, a_t, b).astype(BF16)

    spread_z(feature[...], z_columns(cells_row[...]), spread)
    for i in range(3):
        product = nn(spread[...], w_mid[:, i * 384 : (i + 1) * 384])
        for j in range(3):
            parts[i][pl.ds(2 - j, voxels, 4), :] = product[:, j * LANES : (j + 1) * LANES]
        sums[i][...] = jnp.zeros_like(sums[i])

    depth_cells = row_count * columns * ZD

    def add(v, carry):
        base = voxel_base(cells_smem[v], depth_cells, columns, edge, split)
        for i in range(3):
            spot = pl.ds(base + (1 - i) * PITCH, 3)
            sums[i][spot, :] = sums[i][spot, :] + parts[i][pl.ds(4 * v, 3), :]
        return carry

    lax.fori_loop(0, voxels, add, 0, unroll=4)

    def gather(p, carry):
        spot = pl.ds(pl.multiple_of(p * PITCH + 8, 8), columns)
        pre[p] = sum0[spot, :] + sum1[spot, :] + sum2[spot, :]
        return carry

    lax.fori_loop(0, row_count + 5, gather, 0)

    def zero_half(ref, row, column, height, width):
        ref[row : row + height, column : column + width] = jnp.zeros((height, width), BF16)

    for begin, f_ref, d_ref in ((B_ONE, f_one, d_one), (B_TWO, f_two, d_two)):
        for j in range(3):
            for e in range(2):
                outside = 3 if e == 0 else 0
                zero_half(f_ref, outside * 384 + j * LANES, e * LANES, LANES, LANES)
                zero_half(d_ref, e * LANES, outside * 384 + j * LANES, LANES, LANES)

        def tap(i, j, begin=begin, f_ref=f_ref, d_ref=d_ref):
            block = aligned(RUN_B, begin + (i * 3 + j) * LANES, LANES).astype(BF16)
            for e in range(2):
                t = i + e
                f_ref[t * 384 + j * LANES : t * 384 + (j + 1) * LANES, e * LANES : (e + 1) * LANES] = block
                t = 2 + e - i
                lane = t * 384 + (2 - j) * LANES
                d_ref[e * LANES : (e + 1) * LANES, lane : lane + LANES] = block

        for i in range(3):
            for j in range(3):
                tap(i, j)
    for j in range(3):
        for e in range(2):
            outside = 3 if e == 0 else 0
            zero_half(d_three, e * LANES, outside * 768 + j * 256, LANES, 256)
    for i in range(3):
        for j in range(3):
            run[...] = aligned(RUN_B, B_THREE + (i * 3 + j) * 256, 256)
            for h in range(2):
                block = run[pl.ds(h, LANES, 2), :].astype(BF16)
                row = (i * 3 + j) * LANES
                f_three[row : row + LANES, h * LANES : (h + 1) * LANES] = block
                for e in range(2):
                    lane = (2 + e - i) * 768 + (2 - j) * 256 + h * LANES
                    d_three[e * LANES : (e + 1) * LANES, lane : lane + LANES] = block
    head_rows = aligned(RUN_B, B_HEAD, 32).astype(BF16)
    chosen = nn(eighths(), head_rows)
    chosen = jnp.where(same_eighth(), chosen, 0.0).astype(BF16)
    head_t[...] = nt(fold16(), chosen).astype(BF16)


def eighths():
    return (row_of((CR3, 32)) // 8 == lane_of((CR3, 32))).astype(F32).astype(BF16)


def same_eighth():
    return lane_of((CR3, LANES)) // 16 == lax.rem(row_of((CR3, LANES)), 8)


def fold16():
    return (lax.rem(lane_of((16, LANES)), 16) == row_of((16, LANES))).astype(F32).astype(BF16)


def middle(n, rows, row_count, cells, feature, wall):
    shape = jax.ShapeDtypeStruct
    voxels = feature.shape[0]
    cells_all = (row_count + 6) * PITCH
    return pl.pallas_call(
        functools.partial(middle_kernel, n, rows, row_count),
        name="middle",
        out_shape=(
            shape((row_count + 5, LANES, LANES), F32),
            shape((512, 1152), BF16),
            shape((1536, 256), BF16),
            shape((1536, 256), BF16),
            shape((1152, 256), BF16),
            shape((256, 1536), BF16),
            shape((256, 1536), BF16),
            shape((256, 3072), BF16),
            shape((16, 256), BF16),
        ),
        in_specs=[smem(), vmem(), vmem(), vmem()],
        out_specs=(vmem(),) * 9,
        scratch_shapes=[
            pltpu.VMEM((n * rows + 24, LANES), F32),
            pltpu.VMEM((256, LANES), F32),
            pltpu.VMEM((voxels, ZD * C2), BF16),
            pltpu.VMEM((voxels * 4, LANES), F32),
            pltpu.VMEM((voxels * 4, LANES), F32),
            pltpu.VMEM((voxels * 4, LANES), F32),
            pltpu.VMEM((cells_all, LANES), F32),
            pltpu.VMEM((cells_all, LANES), F32),
            pltpu.VMEM((cells_all, LANES), F32),
        ],
        compiler_params=pltpu.CompilerParams(vmem_limit_bytes=56 << 20),
    )(cells, cells.reshape(1, -1), feature, wall)


PAIRS = 18
QB = 9
STEPS = PAIRS // QB
SPAN = QB * LANES
GRID = PAIRS * LANES
A_ROWS, B_ROWS = 1800, 4656


def conv_kernel(
    n, row_count,
    cells_smem, cells_row, feature, stat, pre_in, w_mid, f_one, f_two, f_three, d_one, d_two, d_three, head_t,
    labels_hbm, boxes_hbm,
    grad_a, grad_b, grad_feature, loss_out,
    x_one, x_two, x_three, pre_mid, pre_one, pre_two, back, spread,
    acc0, acc1, acc2,
    labels, boxes, logit_grads, loss_mine, loss_all,
    up_f, down_f, from_up_f, from_down_f, send_up, send_down, from_up, from_down,
    send_up_w, send_down_w, from_up_w, from_down_w,
    sem_t, sem_fs, sem_fr, sem_s, sem_r, sem_ws, sem_wr, sem_ls, sem_lr,
):
    me = lax.axis_index("tile")
    edge, split, top, bottom = layout(n, row_count)
    has_up, has_down = me > 0, me < n - 1
    above, below = jnp.maximum(me - 1, 0), jnp.minimum(me + 1, n - 1)
    loads = [pltpu.make_async_copy(labels_hbm.at[a], labels.at[:, a, :], sem_t.at[a]) for a in range(2)]
    loads += [
        pltpu.make_async_copy(boxes_hbm.at[a], boxes.at[:, 2 + a, :], sem_t.at[2 + a]) for a in range(14)
    ]
    for load in loads:
        load.start()
    enter(n, me)

    def ok(place):
        return place_ok(place, edge, split, row_count)

    def halo_copies(s, up_src, down_src, up_dst, down_dst, sem_send, sem_recv):
        up = remote(up_src, down_dst, sem_send.at[2 * s], sem_recv.at[2 * s], above)
        down = remote(down_src, up_dst, sem_send.at[2 * s + 1], sem_recv.at[2 * s + 1], below)
        return up, down

    def halo_start(copies):
        up, down = copies

        @pl.when(has_up)
        def _():
            up.start()

        @pl.when(has_down)
        def _():
            down.start()

    def halo_wait(copies):
        up, down = copies

        @pl.when(has_up)
        def _():
            up.wait_send()
            down.wait_recv()

        @pl.when(has_down)
        def _():
            down.wait_send()
            up.wait_recv()

    def thin(s):
        return halo_copies(
            s, send_up.at[s], send_down.at[s], from_up.at[s], from_down.at[s], sem_s, sem_r
        )

    def pick(condition, a, b):
        return jnp.where(condition, a, b)

    column = row_of((LANES, LANES))

    def shifted(value):
        left = jnp.where(column > 0, pltpu.roll(value, 1, axis=0), 0.0)
        right = jnp.where(column < LANES - 1, pltpu.roll(value, LANES - 1, axis=0), 0.0)
        return left.astype(BF16), value.astype(BF16), right.astype(BF16)

    def put(ref, pair, parity, value, part, parts):
        rows = pl.ds(pl.multiple_of(pair * LANES, LANES), LANES)
        width = 3 * parts * LANES
        for j, shift in enumerate(shifted(value)):
            lane = parity * width + (j * parts + part) * LANES
            ref[rows, lane : lane + LANES] = shift

    def put_edges(ref, s, parts, up_halo, down_halo):
        for part in range(parts):
            lanes = slice(part * LANES, (part + 1) * LANES)
            halo = pick((top == 1) & has_up, up_halo[:, lanes].astype(F32), 0.0)
            put(ref, 0, 0, halo, part, parts)
            halo = pick((bottom == 1) & has_down, down_halo[:, lanes].astype(F32), 0.0)
            width = 3 * parts * LANES
            row = pl.ds(16 * LANES, LANES)
            for j, shift in enumerate(shifted(halo)):
                lane = width + (j * parts + part) * LANES
                ref[row, lane : lane + LANES] = pick(split == 1, ref[row, lane : lane + LANES], shift)
            put(ref, 17, 0, pick(split == 1, halo, 0.0), part, parts)

    grad_b[B_HEAD + 32 :, :] = jnp.zeros((B_ROWS - B_HEAD - 32, LANES), F32)
    up_f[...] = pre_in[0]
    down_f[...] = pick(split == 1, pre_in[row_count + 2], pre_in[row_count + 1])
    copies = halo_copies(0, up_f, down_f, from_up_f, from_down_f, sem_fs, sem_fr)
    halo_start(copies)
    for ref, wide in ((x_one, 768), (x_two, 768), (x_three, 768)):
        ref[0:LANES, 0:384] = jnp.zeros((LANES, 384), BF16)
        ref[18 * LANES : 20 * LANES, :] = jnp.zeros((2 * LANES, wide), BF16)
    spread_z(feature[...], z_columns(cells_row[...]), spread)
    halo_wait(copies)

    bias_mid = stat[32:33, :]
    b_mid = jnp.concatenate([bias_mid[:, 32:96], bias_mid[:, 32:96]], axis=1)
    last = row_count

    def fold(q, carry):
        for e in range(2):
            p = 2 * q + 1 + e
            value = pre_in[p] + b_mid
            value += pick((p == 1) & (top == 1) & has_up, from_up_f[...], 0.0)
            value += pick((p == last + split) & (bottom == 1) & has_down, from_down_f[...], 0.0)
            pre_mid[pl.ds(pl.multiple_of(q * LANES, LANES), LANES), e * LANES : (e + 1) * LANES] = value
        return carry

    lax.fori_loop(0, PAIRS, fold, 0)

    def activate(pre_ref, x_ref, s):
        def step(q, carry):
            rows = pl.ds(pl.multiple_of(q * LANES, LANES), LANES)
            for e in range(2):
                value = pre_ref[rows, e * LANES : (e + 1) * LANES]
                value = pick(ok(2 * q + 1 + e), value * sigmoid(value), 0.0)
                put(x_ref, q + e, 1 - e, value, 0, 1)
            return carry

        lax.fori_loop(0, PAIRS, step, 0)
        exchange(x_ref, s)
        copies = thin(s)
        halo_wait(copies)
        put_edges(x_ref, s, 1, from_up[s], from_down[s])

    def exchange(x_ref, s):
        send_up[s] = x_ref[0:LANES, 512:640]
        send_down[s] = pick(split == 1, x_ref[16 * LANES : 17 * LANES, 512:640], x_ref[16 * LANES : 17 * LANES, 128:256])
        halo_start(thin(s))

    def banded(x_ref, f_ref, bias, out_ref):
        def step(b, carry):
            start = pl.multiple_of(b * SPAN, LANES)
            total = nn(x_ref[pl.ds(start, SPAN), :], f_ref[0:768, :])
            total += nn(x_ref[pl.ds(start + LANES, SPAN), :], f_ref[768:1536, :])
            out_ref[pl.ds(start, SPAN), :] = total + bias
            return carry

        lax.fori_loop(0, STEPS, step, 0)

    def banded_back(g_ref, d_ref, out_ref):
        width = g_ref.shape[1]

        def step(b, carry):
            start = pl.multiple_of(b * SPAN, LANES)
            total = nt(g_ref[pl.ds(start, SPAN), :], d_ref[:, 0:width])
            total += nt(g_ref[pl.ds(start + LANES, SPAN), :], d_ref[:, width : 2 * width])
            out_ref[pl.ds(start, SPAN), :] = total
            return carry

        lax.fori_loop(0, STEPS, step, 0)

    def bias_row(first, lane):
        mixed = jnp.where(lane_of((1, LANES)) >= lane, stat[first : first + 1, :], stat[first + 1 : first + 2, :])
        return pltpu.roll(jnp.broadcast_to(mixed, (8, LANES)), LANES - lane, axis=1)[0:1, :]

    def twice(row):
        return jnp.concatenate([row, row], axis=1)

    activate(pre_mid, x_one, 0)
    banded(x_one, f_one, twice(bias_row(33, 96)), pre_one)
    activate(pre_one, x_two, 1)
    banded(x_two, f_two, twice(bias_row(35, 96)), pre_two)
    activate(pre_two, x_three, 2)

    def weight_grads(g_ref, x_ref, parts, write):
        width, wide = parts * LANES, 3 * parts * LANES
        middle0 = slice(width, 2 * width)
        middle1 = slice(wide + width, wide + 2 * width)
        acc0[0 : 2 * width, :] = jnp.zeros((2 * width, 768), F32)
        acc1[0:width, :] = jnp.zeros((width, 384), F32)
        acc2[0:width, :] = jnp.zeros((width, 384), F32)

        def step(b, carry):
            start = pl.multiple_of(b * SPAN, LANES)
            rows = pl.ds(start, SPAN)
            g0, g1 = g_ref[rows, middle0], g_ref[rows, middle1]
            both = jnp.concatenate([g0, g1], axis=1)
            acc0[0 : 2 * width, :] += tn(both, x_ref[rows, :])
            acc2[0:width, :] += tn(g1, x_ref[pl.ds(start + LANES, SPAN), 0:384])
            after = g_ref[pl.ds(start + LANES, SPAN), middle0]
            acc1[0:width, :] += tn(after, x_ref[rows, 384:768])
            return carry

        lax.fori_loop(0, STEPS, step, 0)
        for i in range(3):
            if i == 0:
                total = acc0[width : 2 * width, 0:384] + acc1[0:width, :]
            elif i == 1:
                total = acc0[0:width, 0:384] + acc0[width : 2 * width, 384:768]
            else:
                total = acc0[0:width, 384:768] + acc2[0:width, :]
            for j in range(3):
                for part in range(parts):
                    block = total[part * LANES : (part + 1) * LANES, j * LANES : (j + 1) * LANES]
                    write(i, j, part, jnp.transpose(block))

    def bias_grads(g_ref, parts):
        width, wide = parts * LANES, 3 * parts * LANES
        ones = jnp.ones((16, SPAN), BF16)

        def step(b, total):
            rows = pl.ds(pl.multiple_of(b * SPAN, LANES), SPAN)
            total += nn(ones, g_ref[rows, width : 2 * width])
            return total + nn(ones, g_ref[rows, wide + width : wide + 2 * width])

        return lax.fori_loop(0, STEPS, step, jnp.zeros((16, width), F32))[0:1, :]

    def last_layers(pre_three, x_head, g_three):
        bias = jnp.concatenate([bias_row(37, 96), bias_row(38, 96)], axis=1)

        def conv_step(b, carry):
            start = pl.multiple_of(b * SPAN, LANES)
            rows, more = pl.ds(start, SPAN), pl.ds(start + LANES, SPAN)
            total = nn(x_ref3[rows, :], f_three[0:768, :]) + nn(x_ref3[more, 0:384], f_three[768:1152, :])
            pre_three[rows, 0:256] = total + bias
            total = nn(x_ref3[rows, 384:768], f_three[0:384, :]) + nn(x_ref3[more, :], f_three[384:1152, :])
            pre_three[rows, 256:512] = total + bias
            return carry

        x_ref3 = x_three
        lax.fori_loop(0, STEPS, conv_step, 0)

        def head_step(q, carry):
            rows = pl.ds(pl.multiple_of(q * LANES, LANES), LANES)
            value = pre_three[rows, :]
            x_head[rows, :] = (value * sigmoid(value)).astype(BF16)
            return carry

        lax.fori_loop(0, PAIRS, head_step, 0)
        for load in loads:
            load.wait()
        head_row = jnp.broadcast_to(stat[40:41, :], (LANES, LANES))
        b_head = jnp.sum(jnp.where(lane_of((16, LANES)) == row_of((16, LANES)) + 96, head_row[0:16, :], 0.0), axis=1, keepdims=True)
        divisor = jnp.maximum(stat[0:1, 3:4], 1.0)
        inverse = 1.0 / divisor
        row16 = row_of((16, LANES))

        def loss_tile(logits, place):
            row = place_row(place, edge, row_count)
            label = labels[row]
            kind = jnp.concatenate([label, jnp.zeros((14, LANES), jnp.int32)], axis=0)
            is_class = row16 < 2
            anchor0, anchor1 = label[0:1, :] == 1, label[1:2, :] == 1
            box_on = ((row16 < 9) & anchor0) | ((row16 >= 9) & anchor1)
            positive = (kind == 1).astype(F32)
            negative = (kind == 0).astype(F32)
            q = 1.0 / (1.0 + jnp.exp(-logits))
            rest = jnp.log(1.0 + jnp.exp(-jnp.abs(logits)))
            log_q = jnp.minimum(logits, 0.0) - rest
            log_not = jnp.minimum(-logits, 0.0) - rest
            short = 1.0 - q
            focal = -FOCAL_ALPHA * positive * short * short * log_q
            focal -= (1.0 - FOCAL_ALPHA) * negative * q * q * log_not
            slope_p = FOCAL_ALPHA * (2.0 * q * short * short * log_q - short * short * short)
            slope_n = (1.0 - FOCAL_ALPHA) * (q * q * q - 2.0 * q * q * short * log_not)
            residual = logits - boxes[row]
            size = jnp.abs(residual)
            huber = jnp.where(size < HUBER_BETA, (0.5 / HUBER_BETA) * residual * residual, size - 0.5 * HUBER_BETA)
            bent = jnp.clip(residual * (1.0 / HUBER_BETA), -1.0, 1.0)
            value = jnp.where(is_class, focal, jnp.where(box_on, 2.0 * huber, 0.0))
            grad = jnp.where(is_class, positive * slope_p + negative * slope_n, jnp.where(box_on, 2.0 * bent, 0.0))
            good = ok(place)
            return pick(good, value, 0.0), pick(good, grad * inverse, 0.0)

        def loss_step(q, total):
            rows = pl.ds(pl.multiple_of(q * LANES, LANES), LANES)
            for e in range(2):
                logits = nt(head_t[...], x_head[rows, e * 256 : (e + 1) * 256]) + b_head
                value, grad = loss_tile(logits, 2 * q + 1 + e)
                logit_grads[e, :, rows] = grad.astype(BF16)
                total = total + value
            return total

        total = lax.fori_loop(0, PAIRS, loss_step, jnp.zeros((16, LANES), F32), unroll=3)
        total = jnp.sum(jnp.sum(total, axis=1, keepdims=True), axis=0, keepdims=True)
        loss_mine[...] = jnp.broadcast_to(total, (8, LANES))
        for k in range(1, n):
            loss_copy(k).start()
        g_head = jnp.zeros((16, CR3), F32)
        g_bias = jnp.zeros((16, 1), F32)
        for e in range(2):
            g_head += nn(logit_grads[e], x_head[0:GRID, e * 256 : (e + 1) * 256])
            g_bias += jnp.sum(logit_grads[e].astype(F32), axis=1, keepdims=True)
        back_rows = jnp.where(same_eighth(), tn(g_head, fold16().astype(F32), HIGH), 0.0)
        grad_b[B_HEAD : B_HEAD + 32, :] = tn(eighths().astype(F32), back_rows, HIGH)
        spots = (lane_of((16, LANES)) == row_of((16, LANES))).astype(F32)
        grad_b[B_HEAD + 32 : B_HEAD + 33, :] = jnp.sum(spots * g_bias, axis=0, keepdims=True)

        def back_step(q, carry):
            rows = pl.ds(pl.multiple_of(q * LANES, LANES), LANES)
            for e in range(2):
                grad = tn(logit_grads[e, :, rows], head_t[...])
                grad = grad * slope(pre_three[rows, e * 256 : (e + 1) * 256])
                for part in range(2):
                    put(g_three, q + e, 1 - e, grad[:, part * LANES : (part + 1) * LANES], part, 2)
            return carry

        g_three[0:LANES, 0:768] = jnp.zeros((LANES, 768), BF16)
        g_three[18 * LANES : 20 * LANES, :] = jnp.zeros((2 * LANES, 1536), BF16)
        lax.fori_loop(0, PAIRS, back_step, 0)
        last_row = slice(16 * LANES, 17 * LANES)
        send_up_w[...] = g_three[0:LANES, 1024:1280]
        send_down_w[...] = pick(split == 1, g_three[last_row, 1024:1280], g_three[last_row, 256:512])
        copies = halo_copies(0, send_up_w, send_down_w, from_up_w, from_down_w, sem_ws, sem_wr)
        halo_start(copies)

        def write(i, j, part, block):
            start = B_THREE + 2 * (i * 3 + j) * LANES + part
            grad_b[pl.ds(start, LANES, 2), :] = block

        weight_grads(g_three, x_three, 2, write)
        sums = bias_grads(g_three, 2)
        grad_b[B_HEAD - 2 : B_HEAD - 1, :] = sums[:, 0:LANES]
        grad_b[B_HEAD - 1 : B_HEAD, :] = sums[:, LANES : 2 * LANES]
        halo_wait(copies)
        put_edges(g_three, 0, 2, from_up_w[...], from_down_w[...])
        banded_back(g_three, d_three, back)

    def loss_copy(k):
        return remote(loss_mine, loss_all.at[me], sem_ls.at[k], sem_lr.at[me], lax.rem(me + k, n))

    pl.run_scoped(
        last_layers,
        pltpu.VMEM((GRID, 512), F32),
        pltpu.VMEM((GRID, 512), BF16),
        pltpu.VMEM((20 * LANES, 1536), BF16),
    )

    def lower_layers(g_ref, g_map, win0, win1, win2, gathered):
        def grads_in(pre_ref):
            def step(q, carry):
                rows = pl.ds(pl.multiple_of(q * LANES, LANES), LANES)
                for e in range(2):
                    lanes = slice(e * LANES, (e + 1) * LANES)
                    value = back[rows, lanes] * slope(pre_ref[rows, lanes])
                    put(g_ref, q + e, 1 - e, pick(ok(2 * q + 1 + e), value, 0.0), 0, 1)
                return carry

            lax.fori_loop(0, PAIRS, step, 0)

        def layer(pre_ref, x_ref, d_ref, begin, s):
            g_ref[0:LANES, 0:384] = jnp.zeros((LANES, 384), BF16)
            grads_in(pre_ref)
            exchange(g_ref, s)

            def write(i, j, part, block):
                start = begin + (i * 3 + j) * LANES
                grad_b[start : start + LANES, :] = block

            weight_grads(g_ref, x_ref, 1, write)
            grad_b[begin + 1152 : begin + 1153, :] = bias_grads(g_ref, 1)
            halo_wait(thin(s))
            put_edges(g_ref, s, 1, from_up[s], from_down[s])
            banded_back(g_ref, d_ref, back)

        g_ref[18 * LANES : 20 * LANES, :] = jnp.zeros((2 * LANES, 768), BF16)
        layer(pre_two, x_two, d_two, B_TWO, 3)
        layer(pre_one, x_one, d_one, B_ONE, 4)

        g_map[...] = jnp.zeros_like(g_map)

        def to_map(q, total):
            rows = pl.ds(pl.multiple_of(q * LANES, LANES), LANES)
            for e in range(2):
                p = 2 * q + 1 + e
                lanes = slice(e * LANES, (e + 1) * LANES)
                value = back[rows, lanes] * slope(pre_mid[rows, lanes])
                value = pick(ok(p), value, 0.0).astype(BF16).astype(F32)
                g_map[pl.ds(pl.multiple_of(p * PITCH + 8, 8), LANES), :] = value
                total += jnp.sum(value, axis=0, keepdims=True)
            return total

        total = lax.fori_loop(0, PAIRS, to_map, jnp.zeros((1, LANES), F32))
        total = total[:, 0:CM] + total[:, CM : 2 * CM]
        grad_a[0:A_MID, :] = jnp.zeros((A_MID, LANES), F32)
        grad_a[A_MID + 1728 : A_ROWS, :] = jnp.zeros((A_ROWS - A_MID - 1728, LANES), F32)
        grad_a[A_MID + 1728 : A_MID + 1729, 0:CM] = total

        def map_row(place):
            return slice(place * PITCH + 8, place * PITCH + 8 + LANES)

        send_up[5] = g_map[map_row(1), :].astype(BF16)
        send_down[5] = pick(split == 1, g_map[map_row(row_count + 1), :], g_map[map_row(row_count), :]).astype(BF16)
        halo_start(thin(5))
        halo_wait(thin(5))
        g_map[map_row(0), :] = pick((top == 1) & has_up, from_up[5].astype(F32), 0.0)
        halo = pick((bottom == 1) & has_down, from_down[5].astype(F32), 0.0)
        g_map[map_row(row_count + 1), :] = pick(split == 1, g_map[map_row(row_count + 1), :], halo)
        g_map[map_row(row_count + 2), :] = pick(split == 1, halo, 0.0)

        wins = (win0, win1, win2)
        voxels = feature.shape[0]
        depth_cells = row_count * LANES * ZD

        def fetch(v, carry):
            base = voxel_base(cells_smem[v], depth_cells, LANES, edge, split)
            for i in range(3):
                wins[i][pl.ds(4 * v, 3), :] = g_map[pl.ds(base + (1 - i) * PITCH, 3), :]
            return carry

        lax.fori_loop(0, voxels, fetch, 0, unroll=8)
        for i in range(3):
            for j in range(3):
                lanes = slice((i * 3 + j) * LANES, (i * 3 + j + 1) * LANES)
                gathered[:, lanes] = wins[i][pl.ds(2 - j, voxels, 4), :].astype(BF16)
        low = lane_of((64, LANES)) < 64
        for i in range(3):
            block = tn(spread[...], gathered[:, i * 384 : (i + 1) * 384])
            for j in range(3):
                part = block[:, j * LANES : (j + 1) * LANES]
                even = [part[z * LANES : z * LANES + 64] for z in range(ZD)]
                odd = [part[z * LANES + 64 : (z + 1) * LANES] for z in range(ZD)]

                def flip(x):
                    return pltpu.roll(x, 64, axis=1)

                taps = (
                    jnp.where(low, flip(even[1]), odd[1]),
                    jnp.where(low, even[0] + flip(even[2]), flip(odd[0]) + odd[2]),
                    jnp.where(low, even[1] + flip(even[3]), flip(odd[1]) + odd[3]),
                )
                for t in range(3):
                    start = A_MID + (t * 9 + i * 3 + j) * 64
                    grad_a[start : start + 64, :] = taps[t]
        z_column = z_columns(cells_row[...])
        total = jnp.zeros((voxels, C2), F32)
        for z in range(ZD):
            total += jnp.where(z_column == z, nt(gathered[...], w_mid[z * C2 : (z + 1) * C2, :]), 0.0)
        grad_feature[...] = total

    voxels = feature.shape[0]
    pl.run_scoped(
        lower_layers,
        pltpu.VMEM((20 * LANES, 768), BF16),
        pltpu.VMEM(((row_count + 6) * PITCH, LANES), F32),
        pltpu.VMEM((voxels * 4, LANES), F32),
        pltpu.VMEM((voxels * 4, LANES), F32),
        pltpu.VMEM((voxels * 4, LANES), F32),
        pltpu.VMEM((voxels, 1152), BF16),
    )
    for k in range(1, n):
        sender = lax.rem(me + n - k, n)
        remote(loss_mine, loss_all.at[sender], sem_ls.at[k], sem_lr.at[sender], sender).wait_recv()
    loss_all[me] = loss_mine[...]
    total = loss_all[0]
    for d in range(1, n):
        total += loss_all[d]
    loss_out[...] = total
    for k in range(1, n):
        loss_copy(k).wait_send()


def convs(n, row_count, cells, feature, stat, middle_out, labels, boxes):
    shape = jax.ShapeDtypeStruct
    dma = pltpu.SemaphoreType.DMA
    voxels = feature.shape[0]
    row = (LANES, LANES)
    return pl.pallas_call(
        functools.partial(conv_kernel, n, row_count),
        name="convs",
        out_shape=(
            shape((A_ROWS, LANES), F32),
            shape((B_ROWS, LANES), F32),
            shape((voxels, LANES), F32),
            shape((8, LANES), F32),
        ),
        in_specs=[smem()] + [vmem()] * 12 + [anywhere()] * 2,
        out_specs=(vmem(),) * 4,
        scratch_shapes=[
            pltpu.VMEM((20 * LANES, 768), BF16),
            pltpu.VMEM((20 * LANES, 768), BF16),
            pltpu.VMEM((20 * LANES, 768), BF16),
            pltpu.VMEM((GRID, 256), F32),
            pltpu.VMEM((GRID, 256), F32),
            pltpu.VMEM((GRID, 256), F32),
            pltpu.VMEM((GRID, 256), F32),
            pltpu.VMEM((voxels, ZD * C2), BF16),
            pltpu.VMEM((512, 768), F32),
            pltpu.VMEM((256, 384), F32),
            pltpu.VMEM((256, 384), F32),
            pltpu.VMEM((row_count, 2, LANES), jnp.int32),
            pltpu.VMEM((row_count, 16, LANES), F32),
            pltpu.VMEM((2, 16, GRID), BF16),
            pltpu.VMEM((8, LANES), F32),
            pltpu.VMEM((n, 8, LANES), F32),
            pltpu.VMEM(row, F32),
            pltpu.VMEM(row, F32),
            pltpu.VMEM(row, F32),
            pltpu.VMEM(row, F32),
            pltpu.VMEM((6,) + row, BF16),
            pltpu.VMEM((6,) + row, BF16),
            pltpu.VMEM((6,) + row, BF16),
            pltpu.VMEM((6,) + row, BF16),
            pltpu.VMEM((LANES, 256), BF16),
            pltpu.VMEM((LANES, 256), BF16),
            pltpu.VMEM((LANES, 256), BF16),
            pltpu.VMEM((LANES, 256), BF16),
            dma((16,)), dma((2,)), dma((2,)), dma((12,)), dma((12,)), dma((2,)), dma((2,)), dma((n,)), dma((n,)),
        ],
        compiler_params=pltpu.CompilerParams(
            collective_id=2, has_side_effects=True, vmem_limit_bytes=62 << 20
        ),
    )(cells, cells.reshape(1, -1), feature, stat, *middle_out, labels, boxes)


def adam_outer(gradient, weight, moment, second, momentum):
    moment = FIRST_DECAY * moment + (1.0 - FIRST_DECAY) * gradient
    second = SECOND_DECAY * second + (1.0 - SECOND_DECAY) * gradient * gradient
    moment_fix = moment / (1.0 - FIRST_DECAY**STEP)
    second_fix = second / (1.0 - SECOND_DECAY**STEP)
    inner_weight = weight - INNER_RATE * (
        moment_fix / (jnp.sqrt(second_fix) + ADAM_EPSILON) + WEIGHT_DECAY * weight
    )
    inner_step = weight - inner_weight
    momentum = OUTER_MOMENT * momentum + inner_step
    updated = weight - OUTER_RATE * (inner_step + OUTER_MOMENT * momentum)
    return (moment, second, momentum, updated)


def flat_pieces(rows, slot):
    begin, end = slot * rows, (slot + 1) * rows
    spans = ((0, 67, None, 0), (67, 1795, "a", 2), (1795, 1796, "both", 0), (1796, 6440, "b", 1795), (6440, 1 << 30, None, 0))
    pieces = []
    for low, high, run, shift in spans:
        first, last = max(begin, low), min(end, high)
        if first < last:
            pieces.append((first - begin, last - first, run, first - shift))
    return pieces


NOTE = 112


def finish_kernel(
    n, rows, points_hbm, points_in, counts_ref, small, stat, first_out, pooled_in, grad_feature, grad_a, grad_b,
    gradient,
    points, first, slots, pair, line, mine, notes, fc_rows, small_grad,
    sem_p, sem_ps, sem_pr, sem_zs, sem_zr, sem_ns, sem_nr,
):
    me = lax.axis_index("tile")
    half = n // 2
    parity, chip = lax.rem(me, 2), me // 2
    sibling = me + 1 - 2 * parity
    count_p, voxels = points_hbm.shape[1], points_hbm.shape[2]
    points[...] = jnp.ones_like(points)
    loads = [
        pltpu.make_async_copy(points_hbm.at[k], points.at[:, k, :], sem_p.at[k]) for k in range(7)
    ]
    for load in loads:
        load.start()
    enter(n, me)

    def realigned(ref, start, count, lane):
        here, before = ref[pl.ds(start, count), :], ref[pl.ds(start - 1, count), :]
        mixed = jnp.where(lane_of((count, LANES)) >= LANES - lane, before, here)
        return pltpu.roll(mixed, lane, axis=1)

    for s in range(n):
        for row, count, run, start in flat_pieces(rows, s):
            if run is None:
                value = jnp.zeros((count, LANES), F32)
            elif run == "a":
                value = realigned(grad_a, start, count, 32)
            elif run == "b":
                value = realigned(grad_b, start, count, 96)
            else:
                lane = lane_of((8, LANES))
                part_a = jnp.where(lane[0:1] >= 96, grad_a[1792:1793, :], grad_a[1793:1794, :])
                part_b = jnp.where(lane[0:1] >= 32, 0.0, grad_b[0:1, :])
                part_a = pltpu.roll(jnp.broadcast_to(part_a, (8, LANES)), 32, axis=1)
                part_b = pltpu.roll(jnp.broadcast_to(part_b, (8, LANES)), 96, axis=1)
                value = (jnp.where(lane < 96, part_a, part_b))[0:1]
            slots[s, row : row + count, :] = value

    def pair_copy(k):
        return remote(slots.at[2 * k + 1 - parity], pair.at[k], sem_ps.at[k], sem_pr.at[k], sibling)

    for k in range(half):
        pair_copy(k).start()

    def line_copy(k):
        target = lax.rem(me + 2 * k, n)
        return remote(slots.at[target], line.at[chip], sem_zs.at[k], sem_zr.at[chip], target)

    for k in range(half):
        pair_copy(k).wait()
        slots[2 * k + parity] = slots[2 * k + parity] + pair[k]
    for k in range(1, half):
        line_copy(k).start()

    counts = counts_ref[...]
    columns, gamma, beta = first_layer(small)
    mean, scale, held = stat[0:32, 0:1], stat[0:32, 1:2], stat[0:32, 2:3]
    centre = stat[0:8, 4:5]
    order = even_first()
    rows_fc = voxel_rows(small)
    kernel = rows_fc[0:64, :].astype(BF16)
    kernel_t = nt(order.astype(BF16), kernel).astype(BF16)
    kernel = nt(kernel, order.astype(BF16)).astype(BF16)
    bias = jnp.sum(jnp.where(order, rows_fc[64:65, :], 0.0), axis=1, keepdims=True)
    for load in loads:
        load.wait()

    def halves(value):
        high = value.astype(BF16)
        return high, (value - high.astype(F32)).astype(BF16)

    tail = jnp.where(row_of((16, CHUNK)) == 0, 1.0, 0.0).astype(BF16)
    fc = jnp.zeros((80, LANES), F32)
    moments, g_gamma, centred = jnp.zeros((LANES, 16), F32), jnp.zeros((32, CHUNK), F32), jnp.zeros((8, CHUNK), F32)
    for c in range(voxels // CHUNK):
        part = slice(c * CHUNK, (c + 1) * CHUNK)
        held_c = counts[:, part]
        counts_f = held_c.astype(F32)
        grad_pre = jnp.transpose(grad_feature[part, :]) / counts_f
        pooled_c = pooled_in[:, part]
        fixed = nn(kernel_t[:, 32:64], pooled_c) + bias

        def pass_e(p, carry, part=part, held_c=held_c, grad_pre=grad_pre, pooled_c=pooled_c, fixed=fixed):
            fc, pooled = carry
            start = first_out[p, :, part]
            inner = nn(kernel_t[:, 0:32], start) + fixed
            grad = jnp.where(p < held_c, grad_pre * slope(inner), 0.0).astype(BF16)
            fc += nt(jnp.concatenate([start, pooled_c, tail], axis=0), grad)
            down = nn(kernel, grad)
            first[p] = down[0:32]
            return fc, pooled + down[32:64]

        fc, pooled = lax.fori_loop(0, count_p, pass_e, (fc, jnp.zeros((32, CHUNK), F32)), unroll=5)
        pooled = pooled / counts_f
        wide = [jnp.broadcast_to(column, (32, CHUNK)) for column in columns]
        view = points_in.at[:, :, part]

        def pass_f(p, carry, part=part, held_c=held_c, pooled=pooled, wide=wide, view=view):
            moments, g_gamma, centred = carry
            inside = p < held_c
            normed = jnp.where(inside, (linear_row(wide, view, p) - mean) * scale, 0.0)
            act = gamma * normed + beta
            grad = jnp.where(inside, (first[p] + pooled) * slope(act), 0.0)
            off = points[p, :, part] - centre
            off_high, off_low = halves(off)
            grad_high, grad_low = halves(grad)
            norm_high, norm_low = halves(normed)
            left = jnp.concatenate([grad_high, grad_low, norm_high, norm_low], axis=0)
            right = jnp.concatenate([off_high, off_low], axis=0)
            return (
                moments + nt(left, right),
                g_gamma + grad * normed,
                centred + jnp.where(inside, off, 0.0),
            )

        moments, g_gamma, centred = lax.fori_loop(0, count_p, pass_f, (moments, g_gamma, centred), unroll=5)
    by_grad = moments[0:32] + moments[32:64]
    by_grad = by_grad[:, 0:8] + by_grad[:, 8:16]
    by_norm = moments[64:96] + moments[96:128]
    by_norm = by_norm[:, 0:8] + by_norm[:, 8:16]
    mine[...] = jnp.zeros_like(mine)
    mine[0:72, :] = fc[0:72]
    mine[72:104, 0:8] = by_grad
    mine[72:104, 8:16] = by_norm
    mine[72:104, 16:17] = jnp.sum(g_gamma, axis=1, keepdims=True)
    mine[104:112, 0:1] = jnp.sum(centred, axis=1, keepdims=True)
    small_grad[...] = jnp.zeros_like(small_grad)

    def note(sender):
        return remote(mine, notes.at[sender], sem_ns.at[0], sem_nr.at[sender], 0)

    @pl.when(me > 0)
    def _():
        note(me).start()

    @pl.when(me == 0)
    def _():
        notes[0] = mine[...]
        for d in range(1, n):
            note(d).wait_recv()
        total = notes[0]
        for d in range(1, n):
            total += notes[d]
        by_grad, by_norm = total[72:104, 0:8], total[72:104, 8:16]
        g_gamma, g_beta = total[72:104, 16:17], total[72:104, 7:8]
        off_sums = jnp.transpose(jnp.broadcast_to(total[104:112, 0:1], (8, LANES)))[0:32, 0:8]
        g_vfe = scale * gamma * (
            by_grad - g_beta / held * off_sums - g_gamma / held * by_norm
        )
        tall0 = jnp.concatenate([g_vfe[:, k : k + 1] for k in range(4)], axis=0)
        tall1 = jnp.concatenate([g_vfe[:, 4:5], g_vfe[:, 5:6], g_vfe[:, 6:7], g_gamma], axis=0)
        tall2 = jnp.concatenate([g_beta, jnp.zeros((96, 1), F32)], axis=0)
        lane = lane_of((LANES, LANES))
        tall = jnp.where(lane == 0, tall0, 0.0) + jnp.where(lane == 1, tall1, 0.0) + jnp.where(lane == 2, tall2, 0.0)
        head = jnp.transpose(tall)[0:8]
        fc_rows[...] = jnp.zeros_like(fc_rows)
        fc_rows[8:80, :] = nn(total[0:72], order.astype(F32), HIGH)
        small_grad[2:74, :] = realigned(fc_rows, 8, 72, 32)
        small_grad[0:8, :] = small_grad[0:8, :] + head

    total = slots[me, 0:rows, :]
    for k in range(1, half):
        source = lax.rem(chip + half - k, half)
        remote(slots.at[0], line.at[source], sem_zs.at[k], sem_zr.at[source], sibling).wait_recv()
        total += line[source, 0:rows, :]
    gradient[...] = total
    gradient[0:SMALL, :] = total[0:SMALL, :] + small_grad[...]
    for k in range(1, half):
        line_copy(k).wait_send()

    @pl.when(me > 0)
    def _():
        note(me).wait_send()


def finish(n, rows, points, counts, small, stat, first_out, pooled, grad_feature, grad_a, grad_b):
    shape = jax.ShapeDtypeStruct
    dma = pltpu.SemaphoreType.DMA
    slots, voxels = points.shape[1:]
    padded = ceil_to(rows, 8)
    half = n // 2
    return pl.pallas_call(
        functools.partial(finish_kernel, n, rows),
        name="finish",
        out_shape=shape((rows, LANES), F32),
        in_specs=[anywhere()] + [vmem()] * 9,
        out_specs=vmem(),
        scratch_shapes=[
            pltpu.VMEM((slots, 8, voxels), F32),
            pltpu.VMEM((slots, 32, CHUNK), F32),
            pltpu.VMEM((n, padded, LANES), F32),
            pltpu.VMEM((half, padded, LANES), F32),
            pltpu.VMEM((half, padded, LANES), F32),
            pltpu.VMEM((NOTE, LANES), F32),
            pltpu.VMEM((n, NOTE, LANES), F32),
            pltpu.VMEM((88, LANES), F32),
            pltpu.VMEM((SMALL, LANES), F32),
            dma((7,)), dma((half,)), dma((half,)), dma((half,)), dma((half,)), dma((1,)), dma((n,)),
        ],
        compiler_params=pltpu.CompilerParams(
            collective_id=3, has_side_effects=True, vmem_limit_bytes=58 << 20
        ),
    )(points, points, counts, small, stat, first_out, pooled, grad_feature, grad_a, grad_b)


def update_kernel(
    gradient, weight, moment, second, momentum, loss, stat,
    moment_out, second_out, momentum_out, weight_out, loss_out, positives_out,
):
    outs = adam_outer(gradient[...], weight[...], moment[...], second[...], momentum[...])
    moment_out[...], second_out[...], momentum_out[...], weight_out[...] = outs
    loss_out[0] = loss[0, 0]
    positives_out[0] = stat[0, 3]


def update(gradient, held, loss, stat):
    shape = jax.ShapeDtypeStruct
    return pl.pallas_call(
        update_kernel,
        name="update",
        out_shape=(shape(gradient.shape, F32),) * 4 + (shape((1,), F32),) * 2,
        in_specs=[vmem()] * 7,
        out_specs=(vmem(),) * 4 + (smem(),) * 2,
        compiler_params=pltpu.CompilerParams(vmem_limit_bytes=32 << 20),
    )(gradient, *held, loss, stat)


def shards(
    points, point_counts, voxel_cells, anchor_labels, box_targets, weights, adam_m, adam_v, outer_momentum
):
    n = lax.axis_size("tile")
    rows = weights.shape[0] // LANES
    row_count = anchor_labels.shape[1]
    held = [x.reshape(rows, LANES) for x in (weights, adam_m, adam_v, outer_momentum)]
    counts = point_counts.reshape(1, -1)
    wall, small, stat, first_out, pooled, feature = front(n, points, counts, anchor_labels, held[0])
    ready = middle(n, rows, row_count, voxel_cells, feature, wall)
    grad_a, grad_b, grad_feature, loss = convs(
        n, row_count, voxel_cells, feature, stat, ready, anchor_labels, box_targets
    )
    gradient = finish(
        n, rows, points, counts, small, stat, first_out, pooled, grad_feature, grad_a, grad_b
    )
    *outs, loss_sum, positives = update(gradient, held, loss, stat)
    moment, second, momentum, updated = [x.reshape(weights.shape) for x in outs]
    return (moment, second, momentum, updated, loss_sum, positives)


def solution(mesh):
    split = ("group", "tile")
    in_specs = (
        P(None, None, split), P(split), P(split), P(None, split, None), P(None, split, None),
        P(split), P(split), P(split), P(split),
    )
    out_specs = (P(split), P(split), P(split), P(split), P("group"), P("group"))
    return jax.shard_map(shards, mesh=mesh, in_specs=in_specs, out_specs=out_specs, check_vma=False)
```

```python
import functools
import math

import jax
import jax.numpy as jnp
from jax import lax
from jax.experimental import pallas as pl
from jax.experimental.pallas import tpu as pltpu
from jax.sharding import PartitionSpec as P

MESH = pl.DeviceIdType.MESH
F32 = jnp.float32
BF16 = jnp.bfloat16
HIGH = lax.Precision.HIGHEST

C1, C2, CM, CR1, CR2, CR3, ANCH, ZD = 32, 128, 64, 128, 128, 256, 2, 4
H_SCENE = 200
STEP = 10
LANES = 128
NORM_EPSILON = 1e-05
INNER_RATE = 0.05
FIRST_DECAY = 0.9
SECOND_DECAY = 0.999
ADAM_EPSILON = 1e-08
WEIGHT_DECAY = 0.01
OUTER_RATE = 0.7
OUTER_MOMENT = 0.9
FOCAL_ALPHA = 0.25
HUBER_BETA = 1.0 / 9.0

SMALL = 80
FC_ROW, FC_LANE = 2, 32
BIAS_ROWS = (1795, 2947, 2948, 4100, 4101, 6405, 6406, 6407, 6439)
RUN_A = (2, 32)
RUN_B = (1795, 96)
A_MID = 65
B_ONE, B_TWO, B_THREE, B_HEAD = 0, 1153, 2306, 4612
PAIRS_OF = tuple((a, b) for a in range(7) for b in range(a, 7))
DIAGONAL = tuple(r for r, (a, b) in enumerate(PAIRS_OF) if a == b)
CHUNK = 256


def vmem():
    return pl.BlockSpec(memory_space=pltpu.VMEM)


def anywhere():
    return pl.BlockSpec(memory_space=pl.ANY)


def smem():
    return pl.BlockSpec(memory_space=pltpu.SMEM)


def ceil_to(value, step):
    return (value + step - 1) // step * step


def sigmoid(value):
    return 0.5 * jnp.tanh(0.5 * value) + 0.5


def slope(value):
    s = sigmoid(value)
    return s * (1.0 + value * (1.0 - s))


def half_silu(half):
    return half * (1.0 + jnp.tanh(half))


def half_slope(half):
    t = jnp.tanh(half)
    return (1.0 + t) * (1.0 + half * (1.0 - t))


def nt(a, b, precision=None):
    return lax.dot_general(a, b, (((1,), (1,)), ((), ())), precision=precision, preferred_element_type=F32)


def tn(a, b, precision=None):
    return lax.dot_general(a, b, (((0,), (0,)), ((), ())), precision=precision, preferred_element_type=F32)


def nn(a, b, precision=None):
    return lax.dot_general(a, b, (((1,), (0,)), ((), ())), precision=precision, preferred_element_type=F32)


def lane_of(shape):
    return lax.broadcasted_iota(jnp.int32, shape, len(shape) - 1)


def row_of(shape):
    return lax.broadcasted_iota(jnp.int32, shape, len(shape) - 2)


def enter(n, me, between=None):
    sem = pltpu.get_barrier_semaphore()

    def greet(k, carry):
        pl.semaphore_signal(
            sem, inc=1, device_id={"tile": lax.rem(me + k, n)}, device_id_type=MESH
        )
        return carry

    lax.fori_loop(1, n, greet, 0)
    if between is not None:
        between()
    pl.semaphore_wait(sem, n - 1)


def remote(src, dst, send, recv, peer):
    return pltpu.make_async_remote_copy(
        src_ref=src,
        dst_ref=dst,
        send_sem=send,
        recv_sem=recv,
        device_id={"tile": peer},
        device_id_type=MESH,
    )


def even_first():
    out = row_of((LANES, LANES))
    source = jnp.where(out < 64, 2 * out, 2 * out - 127)
    return lane_of((LANES, LANES)) == source


def first_layer(small_ref):
    turned = jnp.transpose(small_ref[0:LANES_PAD, :])
    columns = [turned[(k % 4) * 32 : (k % 4) * 32 + 32, k // 4 : k // 4 + 1] for k in range(7)]
    return columns, turned[96:128, 1:2], turned[0:32, 2:3]


LANES_PAD = 8


def voxel_rows(small_ref):
    here, after = small_ref[2:74, :], small_ref[3:75, :]
    mixed = jnp.where(lane_of((72, LANES)) >= FC_LANE, here, after)
    return pltpu.roll(mixed, LANES - FC_LANE, axis=1)


def layout(n, row_count):
    first = lax.axis_index("tile") * row_count
    ahead = (first // H_SCENE + 1) * H_SCENE - first
    split = jnp.where(ahead < row_count, 1, 0)
    edge = jnp.where(ahead < row_count, ahead, row_count)
    top = jnp.where(lax.rem(first, H_SCENE) != 0, 1, 0)
    last = first + row_count
    bottom = jnp.where((lax.rem(last, H_SCENE) != 0) & (last < n * row_count), 1, 0)
    return edge, split, top, bottom


def place_ok(place, edge, split, row_count):
    return (place >= 1) & (place <= row_count + split) & ((place != edge + 1) | (split == 0))


def place_row(place, edge, row_count):
    row = jnp.where(place <= edge, place - 1, place - 2)
    return jnp.clip(row, 0, row_count - 1)


PITCH = 136


def voxel_bases(cells, n, row_count, columns):
    edge, split, _, _ = layout(n, row_count)
    local = lax.rem(cells, row_count * columns * ZD)
    row = local // (columns * ZD)
    column = lax.rem(local, columns * ZD) // ZD
    place = row + 1 + jnp.where((row >= edge) & (split == 1), 1, 0)
    return (place - 1) * PITCH + column + 7


def linear_row(wide, points, p):
    value = wide[0] * points[0, pl.ds(p, 1), :]
    for k in range(1, 7):
        value += wide[k] * points[k, pl.ds(p, 1), :]
    return value


def local_moments(points, counts, labels_ref, sums, message):
    slots, voxels = points.shape[1:]
    inside = row_of((slots, voxels)) < counts

    def folded(value):
        total = value[:, 0:LANES]
        for c in range(1, voxels // LANES):
            total = total + value[:, c * LANES : (c + 1) * LANES]
        return jnp.sum(total, axis=0, keepdims=True)

    def whole(row):
        return jnp.sum(row, axis=1, keepdims=True)

    held = whole(folded(inside.astype(F32)))
    masked = [jnp.where(inside, points[k], 0.0) for k in range(7)]
    rows = [folded(value) for value in masked]
    means = [whole(row) / held for row in rows]
    centred = [jnp.where(inside, points[k] - means[k], 0.0) for k in range(7)]
    for r, (a, b) in enumerate(PAIRS_OF):
        sums[0, r : r + 1, :] = folded(centred[a] * centred[b])
        sums[1, r : r + 1, :] = rows[a]
        sums[2, r : r + 1, :] = rows[b]
    spare = len(PAIRS_OF)
    for c in range(3):
        sums[c, spare:LANES, :] = jnp.zeros((LANES - spare, LANES), F32)
    lane = lane_of((LANES, LANES))
    columns = jnp.zeros((LANES, LANES), F32)
    for c in range(3):
        columns = jnp.where(lane == c, jnp.sum(sums[c], axis=1, keepdims=True), columns)
    positives = jnp.zeros((1, 1), F32)
    for a in range(ANCH):
        positives += whole(jnp.sum((labels_ref[a] == 1).astype(F32), axis=0, keepdims=True))
    packed = jnp.transpose(columns)[0:8]
    row = row_of((8, LANES))
    packed = jnp.where(row == 3, held, packed)
    message[...] = jnp.where(row == 4, positives, packed)


def joint_moments(n, messages):
    total = messages[0]
    for d in range(1, n):
        total += messages[d]
    held = total[3:4]
    mean_a, mean_b = total[1:2] / held, total[2:3] / held
    product = total[0:1]
    for d in range(n):
        held_d = messages[d, 3:4, :]
        product += held_d * (messages[d, 1:2, :] / held_d - mean_a) * (messages[d, 2:3, :] / held_d - mean_b)
    return mean_a, product, held, total[4:5]


def channel_statistics(columns, mean_row, product, held):
    lane = lane_of((32, LANES))
    once, twice = jnp.zeros((32, LANES), F32), jnp.zeros((32, LANES), F32)
    for r, (a, b) in enumerate(PAIRS_OF):
        if a == b:
            once = jnp.where(lane == r, columns[a], once)
        twice = jnp.where(lane == r, (1.0 if a == b else 2.0) * columns[a] * columns[b], twice)
    mean = jnp.sum(once * mean_row, axis=1, keepdims=True)
    variance = jnp.sum(twice * (product / held), axis=1, keepdims=True)
    return mean, lax.rsqrt(variance + NORM_EPSILON)


def front_kernel(
    n, points, counts_ref, cells_ref, labels_ref, shard_ref,
    wall, small, stat, first_out, pooled_out, feature, bases,
    own, sums, mine, messages, my_bias, biases,
    sem_small_s, sem_small_r, sem_msg_s, sem_msg_r, sem_b_s, sem_b_r, sem_w_s, sem_w_r, sem_f_s,
):
    me = lax.axis_index("tile")
    rows = shard_ref.shape[0]
    slots, voxels = points.shape[1:]
    sibling = me + 1 - 2 * lax.rem(me, 2)
    half = n // 2
    counts = counts_ref[...]

    def prepare():
        local_moments(points, counts, labels_ref, sums, mine)
        bases[...] = voxel_bases(cells_ref[...], n, labels_ref.shape[1], labels_ref.shape[2])
        own[...] = jnp.zeros_like(own)
        own[0:rows, :] = shard_ref[...].astype(BF16)
        for a, row in enumerate(BIAS_ROWS):
            owner, place = row // rows, row % rows
            my_bias[a : a + 1, :] = jnp.where(me == owner, shard_ref[place : place + 1, :], 0.0)
        for a in range(len(BIAS_ROWS), 16):
            my_bias[a : a + 1, :] = jnp.zeros((1, LANES), F32)

    enter(n, me, prepare)

    def message(k):
        return remote(mine, messages.at[me], sem_msg_s.at[k], sem_msg_r.at[me], lax.rem(me + k, n))

    def bias_message(k):
        return remote(my_bias, biases.at[me], sem_b_s.at[k], sem_b_r.at[me], lax.rem(me + k, n))

    def small_copy(k):
        return remote(small, small, sem_small_s.at[k], sem_small_r.at[0], lax.rem(me + k, n))

    def shard_copy(k):
        return remote(own, wall.at[me], sem_w_s.at[k], sem_w_r.at[me], lax.rem(me + 2 * k, n))

    for k in range(1, n):
        message(k).start()

    @pl.when(me == 0)
    def _():
        small[...] = shard_ref[0:SMALL, :]

        def send(k, carry):
            small_copy(k).start()
            return carry

        lax.fori_loop(1, n, send, 0)

    for k in range(1, n):
        bias_message(k).start()
    for k in range(1, half):
        shard_copy(k).start()
    to_sibling = remote(own, wall.at[me], sem_w_s.at[0], sem_w_r.at[me], sibling)
    to_sibling.start()
    wall[me] = own[...]
    messages[me] = mine[...]
    biases[me] = my_bias[...]

    @pl.when(me > 0)
    def _():
        small_copy(0).wait_recv()

    columns, gamma, beta = first_layer(small)
    order = even_first()
    rows_fc = voxel_rows(small)
    kernel_t = (0.5 * nt(order.astype(BF16), rows_fc[0:64, :].astype(BF16))).astype(BF16)
    bias = 0.5 * jnp.sum(jnp.where(order, rows_fc[64:65, :], 0.0), axis=1, keepdims=True)
    for k in range(1, n):
        sender = lax.rem(me + n - k, n)
        remote(mine, messages.at[sender], sem_msg_s.at[k], sem_msg_r.at[sender], sender).wait_recv()
    mean_row, product, held, positives = joint_moments(n, messages)
    mean, inverse = channel_statistics(columns, mean_row, product, held)
    lane, row = lane_of((32, LANES)), row_of((32, LANES))
    columns_out = jnp.where(lane == 0, mean, 0.0)
    columns_out = jnp.where(lane == 1, inverse, columns_out)
    columns_out = jnp.where(lane == 2, held, columns_out)
    columns_out = jnp.where(lane == 3, positives, columns_out)
    for k, r in enumerate(DIAGONAL):
        columns_out = jnp.where((lane == 4) & (row == k), mean_row[:, r : r + 1], columns_out)
    stat[0:32, :] = columns_out

    half_gamma, half_beta = 0.5 * gamma, 0.5 * beta
    for c in range(voxels // CHUNK):
        part = slice(c * CHUNK, (c + 1) * CHUNK)
        wide = [jnp.broadcast_to(column, (32, CHUNK)) for column in columns]
        held_c = counts[:, part]
        view = points.at[:, :, part]

        def pass_c(p, pooled, wide=wide, held_c=held_c, view=view, part=part):
            half_act = half_gamma * ((linear_row(wide, view, p) - mean) * inverse) + half_beta
            out = jnp.where(p < held_c, half_silu(half_act), 0.0)
            first_out[p, :, part] = out.astype(BF16)
            return pooled + out

        pooled = lax.fori_loop(0, slots, pass_c, jnp.zeros((32, CHUNK), F32), unroll=5)
        pooled = (pooled / held_c.astype(F32)).astype(BF16)
        pooled_out[:, part] = pooled
        fixed = nn(kernel_t[:, 32:64], pooled) + bias

        def pass_d(p, total, fixed=fixed, held_c=held_c, part=part):
            half_inner = nn(kernel_t[:, 0:32], first_out[p, :, part]) + fixed
            return total + jnp.where(p < held_c, half_silu(half_inner), 0.0)

        total = lax.fori_loop(0, slots, pass_d, jnp.zeros((LANES, CHUNK), F32), unroll=7)
        feature[part, :] = jnp.transpose(total / held_c.astype(F32))

    for k in range(1, half):
        source = lax.rem(me + n - 2 * k, n)
        remote(own, wall.at[source], sem_w_s.at[k], sem_w_r.at[source], source).wait_recv()
        remote(wall.at[source], wall.at[source], sem_f_s.at[k], sem_w_r.at[source], sibling).start()
    for k in range(1, n):
        sender = lax.rem(me + n - k, n)
        remote(my_bias, biases.at[sender], sem_b_s.at[k], sem_b_r.at[sender], sender).wait_recv()
    total = biases[0]
    for d in range(1, n):
        total += biases[d]
    stat[32:48, :] = total
    for k in range(half):
        source = lax.rem(sibling + n - 2 * k, n)
        remote(own, wall.at[source], sem_w_s.at[k], sem_w_r.at[source], source).wait_recv()
    for k in range(1, half):
        source = lax.rem(me + n - 2 * k, n)
        remote(wall.at[source], wall.at[source], sem_f_s.at[k], sem_w_r.at[source], sibling).wait_send()
        shard_copy(k).wait_send()
    to_sibling.wait_send()
    for k in range(1, n):
        message(k).wait_send()
        bias_message(k).wait_send()

    @pl.when(me == 0)
    def _():
        def done(k, carry):
            small_copy(k).wait_send()
            return carry

        lax.fori_loop(1, n, done, 0)


def front(n, points, counts, cells, labels, shard):
    slots, voxels = points.shape[1:]
    rows = shard.shape[0]
    padded = ceil_to(rows, 16)
    shape = jax.ShapeDtypeStruct
    dma = pltpu.SemaphoreType.DMA
    return pl.pallas_call(
        functools.partial(front_kernel, n),
        name="front",
        out_shape=(
            shape((n, padded, LANES), BF16),
            shape((SMALL, LANES), F32),
            shape((48, LANES), F32),
            shape((slots, 32, voxels), BF16),
            shape((32, voxels), BF16),
            shape((voxels, LANES), F32),
            shape((1, voxels), jnp.int32),
        ),
        in_specs=[vmem()] * 5,
        out_specs=(vmem(),) * 7,
        scratch_shapes=[
            pltpu.VMEM((padded, LANES), BF16),
            pltpu.VMEM((3, LANES, LANES), F32),
            pltpu.VMEM((8, LANES), F32),
            pltpu.VMEM((n, 8, LANES), F32),
            pltpu.VMEM((16, LANES), F32),
            pltpu.VMEM((n, 16, LANES), F32),
            dma((n,)), dma((1,)), dma((n,)), dma((n,)), dma((n,)), dma((n,)), dma((n,)), dma((n,)), dma((n,)),
        ],
        compiler_params=pltpu.CompilerParams(
            collective_id=1, has_side_effects=True, vmem_limit_bytes=56 << 20
        ),
    )(points, counts, cells, labels, shard)


def flat_pieces(rows, slot):
    begin, end = slot * rows, (slot + 1) * rows
    spans = ((0, 67, None, 0), (67, 1795, "a", 2), (1795, 1796, "both", 0), (1796, 6440, "b", 1795), (6440, 1 << 30, None, 0))
    pieces = []
    for low, high, run, shift in spans:
        first, last = max(begin, low), min(end, high)
        if first < last:
            pieces.append((first - begin, last - first, run, first - shift))
    return pieces


def flat_slot(slot, rows, low, high, grad_a, grad_b, out_ref):
    def realigned(ref, start, count, lane):
        here, before = ref[pl.ds(start, count), :], ref[pl.ds(start - 1, count), :]
        mixed = jnp.where(lane_of((count, LANES)) >= LANES - lane, before, here)
        return pltpu.roll(mixed, lane, axis=1)

    for row, count, run, start in flat_pieces(rows, slot):
        first, last = max(row, low), min(row + count, high)
        if first >= last:
            continue
        start, row, count = start + first - row, first, last - first
        if run is None:
            value = jnp.zeros((count, LANES), F32)
        elif run == "a":
            value = realigned(grad_a, start, count, 32)
        elif run == "b":
            value = realigned(grad_b, start, count, 96)
        else:
            lane = lane_of((1, LANES))
            part_a = jnp.where(lane >= 96, grad_a[1792:1793, :], grad_a[1793:1794, :])
            part_b = jnp.where(lane >= 32, 0.0, grad_b[0:1, :])
            part_a = pltpu.roll(jnp.broadcast_to(part_a, (8, LANES)), 32, axis=1)
            part_b = pltpu.roll(jnp.broadcast_to(part_b, (8, LANES)), 96, axis=1)
            value = jnp.where(lane < 96, part_a[0:1], part_b[0:1])
        out_ref[row : row + count, :] = value


class Piece:
    def __init__(self, chip, row, count, stage, order):
        self.chip, self.group, self.side = chip, chip // 2, chip % 2
        self.row, self.count, self.stage, self.order = row, count, stage, order
        self.rows = pl.ds(row, count)


def shard_pieces(n, rows):
    padded = ceil_to(rows, 8)
    early, late = [], []
    for chip in range(n // 2):
        first = 2 * chip * rows
        cut = min(ceil_to(min(max(1796 - first, 0), rows), 8), padded)
        spans = [(0, cut)] if cut else []
        if cut >= 400:
            half = ceil_to(cut // 2, 8)
            spans = [(0, half), (half, cut)]
        for order, (low, high) in enumerate(spans):
            late.append(Piece(chip, low, high - low, 3, order))
        if cut < padded:
            begin = first + cut
            stage = 0 if begin >= 4102 else 1 if begin >= 2949 else 2
            early.append(Piece(chip, cut, padded - cut, stage, 2))
    return early, late


def late_chips(n, rows):
    return max(piece.chip for piece in shard_pieces(n, rows)[1]) + 1


def z_columns(cells_row):
    z = lax.rem(cells_row, ZD).astype(F32)
    return jnp.transpose(jnp.broadcast_to(z, (8, z.shape[1])))[:, 0:1]


def spread_z(feature, z_column, out_ref):
    for z in range(ZD):
        out_ref[:, z * C2 : (z + 1) * C2] = jnp.where(z_column == z, feature, 0.0).astype(BF16)


def middle_kernel(
    n, rows, row_count,
    bases, cells_row, feature, wall,
    pre, w_mid, f_one, f_two, f_three, d_one, d_two, d_three, head_t,
    flat, run, spread, parts0, parts1, parts2, sum0, sum1, sum2,
):
    voxels = feature.shape[0]
    columns = LANES
    parts, sums = (parts0, parts1, parts2), (sum0, sum1, sum2)
    for s in range(n):
        flat[s * rows : s * rows + wall.shape[1], :] = wall[s].astype(F32)

    def aligned(begin, start, count):
        row, lane = begin
        here = flat[pl.ds(row + start, count), :]
        after = flat[pl.ds(row + start + 1, count), :]
        mixed = jnp.where(lane_of((count, LANES)) >= lane, here, after)
        return pltpu.roll(mixed, LANES - lane, axis=1)

    low = lane_of((64, LANES)) < 64
    for ij in range(9):
        taps = [aligned(RUN_A, A_MID + (t * 9 + ij) * 64, 64) for t in range(3)]
        turned = [pltpu.roll(tap, 64, axis=1) for tap in taps]
        none = jnp.zeros((64, LANES), F32)
        for z in range(ZD):
            first, second = z + 1, z - 1
            a, a_t = (taps[first], turned[first]) if first < 3 else (none, none)
            b, b_t = (taps[second], turned[second]) if second >= 0 else (none, none)
            lanes = slice(ij * LANES, (ij + 1) * LANES)
            w_mid[z * C2 : z * C2 + 64, lanes] = jnp.where(low, a, b_t).astype(BF16)
            w_mid[z * C2 + 64 : (z + 1) * C2, lanes] = jnp.where(low, a_t, b).astype(BF16)

    spread_z(feature[...], z_columns(cells_row[...]), spread)
    for i in range(3):
        product = nn(spread[...], w_mid[:, i * 384 : (i + 1) * 384])
        for j in range(3):
            parts[i][pl.ds(2 - j, voxels, 4), :] = product[:, j * LANES : (j + 1) * LANES]
        sums[i][...] = jnp.zeros_like(sums[i])

    def add(v, carry):
        base = bases[0, v]
        for i in range(3):
            spot = pl.ds(base + (2 - i) * PITCH, 3)
            sums[i][spot, :] = sums[i][spot, :] + parts[i][pl.ds(4 * v, 3), :]
        return carry

    lax.fori_loop(0, voxels, add, 0, unroll=8)

    def gather(p, carry):
        spot = pl.ds(pl.multiple_of(p * PITCH + 8, 8), columns)
        pre[p] = sum0[spot, :] + sum1[spot, :] + sum2[spot, :]
        return carry

    lax.fori_loop(0, row_count + 5, gather, 0)

    def zero_half(ref, row, column, height, width):
        ref[row : row + height, column : column + width] = jnp.zeros((height, width), BF16)

    for begin, f_ref, d_ref in ((B_ONE, f_one, d_one), (B_TWO, f_two, d_two)):
        for j in range(3):
            for e in range(2):
                outside = 3 if e == 0 else 0
                zero_half(f_ref, outside * 384 + j * LANES, e * LANES, LANES, LANES)
                zero_half(d_ref, e * LANES, outside * 384 + j * LANES, LANES, LANES)

        def tap(i, j, begin=begin, f_ref=f_ref, d_ref=d_ref):
            block = aligned(RUN_B, begin + (i * 3 + j) * LANES, LANES).astype(BF16)
            for e in range(2):
                t = i + e
                f_ref[t * 384 + j * LANES : t * 384 + (j + 1) * LANES, e * LANES : (e + 1) * LANES] = block
                t = 2 + e - i
                lane = t * 384 + (2 - j) * LANES
                d_ref[e * LANES : (e + 1) * LANES, lane : lane + LANES] = block

        for i in range(3):
            for j in range(3):
                tap(i, j)
    for j in range(3):
        for e in range(2):
            outside = 3 if e == 0 else 0
            zero_half(d_three, e * LANES, outside * 768 + j * 256, LANES, 256)
    for i in range(3):
        for j in range(3):
            run[...] = aligned(RUN_B, B_THREE + (i * 3 + j) * 256, 256)
            for h in range(2):
                block = run[pl.ds(h, LANES, 2), :].astype(BF16)
                row = (i * 3 + j) * LANES
                f_three[row : row + LANES, h * LANES : (h + 1) * LANES] = block
                for e in range(2):
                    lane = (2 + e - i) * 768 + (2 - j) * 256 + h * LANES
                    d_three[e * LANES : (e + 1) * LANES, lane : lane + LANES] = block
    head_rows = aligned(RUN_B, B_HEAD, 32).astype(BF16)
    chosen = nn(eighths(), head_rows)
    chosen = jnp.where(same_eighth(), chosen, 0.0).astype(BF16)
    head_t[...] = nt(fold16(), chosen).astype(BF16)


def eighths():
    return (row_of((CR3, 32)) // 8 == lane_of((CR3, 32))).astype(F32).astype(BF16)


def same_eighth():
    return lane_of((CR3, LANES)) // 16 == lax.rem(row_of((CR3, LANES)), 8)


def fold16():
    return (lax.rem(lane_of((16, LANES)), 16) == row_of((16, LANES))).astype(F32).astype(BF16)


def middle(n, rows, row_count, bases, cells, feature, wall):
    shape = jax.ShapeDtypeStruct
    voxels = feature.shape[0]
    cells_all = (row_count + 6) * PITCH
    return pl.pallas_call(
        functools.partial(middle_kernel, n, rows, row_count),
        name="middle",
        out_shape=(
            shape((row_count + 5, LANES, LANES), F32),
            shape((512, 1152), BF16),
            shape((1536, 256), BF16),
            shape((1536, 256), BF16),
            shape((1152, 256), BF16),
            shape((256, 1536), BF16),
            shape((256, 1536), BF16),
            shape((256, 3072), BF16),
            shape((16, 256), BF16),
        ),
        in_specs=[smem(), vmem(), vmem(), vmem()],
        out_specs=(vmem(),) * 9,
        scratch_shapes=[
            pltpu.VMEM((n * rows + 24, LANES), F32),
            pltpu.VMEM((256, LANES), F32),
            pltpu.VMEM((voxels, ZD * C2), BF16),
            pltpu.VMEM((voxels * 4, LANES), F32),
            pltpu.VMEM((voxels * 4, LANES), F32),
            pltpu.VMEM((voxels * 4, LANES), F32),
            pltpu.VMEM((cells_all, LANES), F32),
            pltpu.VMEM((cells_all, LANES), F32),
            pltpu.VMEM((cells_all, LANES), F32),
        ],
        compiler_params=pltpu.CompilerParams(vmem_limit_bytes=56 << 20),
    )(bases, cells, feature, wall)


PAIRS = 18
QB = 9
STEPS = PAIRS // QB
SPAN = QB * LANES
GRID = PAIRS * LANES
A_ROWS, B_ROWS = 1800, 4656


def conv_kernel(
    n, rows_dev, row_count,
    bases, cells_row, feature, stat, pre_in, w_mid, f_one, f_two, f_three, d_one, d_two, d_three, head_t,
    labels_hbm, boxes_hbm,
    late, early_part, grad_feature, loss_out,
    grad_a, grad_b, slots, core_in, chip_in,
    x_one, x_two, x_three, pre_mid, pre_one, pre_two, back, spread,
    acc0, acc1, acc2,
    labels, boxes, logit_grads, loss_mine, loss_all,
    up_f, down_f, from_up_f, from_down_f, send_up, send_down, from_up, from_down,
    send_up_w, send_down_w, from_up_w, from_down_w,
    sem_t, sem_fs, sem_fr, sem_s, sem_r, sem_ws, sem_wr, sem_ls, sem_lr, sem_cs, sem_cr, sem_zs, sem_zr,
):
    me = lax.axis_index("tile")
    edge, split, top, bottom = layout(n, row_count)
    has_up, has_down = me > 0, me < n - 1
    above, below = jnp.maximum(me - 1, 0), jnp.minimum(me + 1, n - 1)
    loads = [pltpu.make_async_copy(labels_hbm.at[a], labels.at[:, a, :], sem_t.at[a]) for a in range(2)]
    loads += [
        pltpu.make_async_copy(boxes_hbm.at[a], boxes.at[:, 2 + a, :], sem_t.at[2 + a]) for a in range(14)
    ]
    for load in loads:
        load.start()
    enter(n, me)

    early, late_list = shard_pieces(n, rows_dev)
    core, side = lax.rem(me, 2), lax.rem(me // 2, 2)
    sibling, other = me + 1 - 2 * core, me + 2 - 4 * side

    def core_copy(i):
        piece = early[i]
        return remote(
            slots.at[2 * piece.chip + 1 - core, piece.rows],
            core_in.at[piece.chip, piece.rows],
            sem_cs.at[i], sem_cr.at[i], sibling,
        )

    def chip_copy(i):
        piece = early[i]
        return remote(
            slots.at[2 * piece.chip + core, piece.rows],
            chip_in.at[piece.group, piece.rows],
            sem_zs.at[i], sem_zr.at[i], other,
        )

    def ship(stage):
        for i, piece in enumerate(early):
            if piece.stage == stage:
                for s in (2 * piece.chip, 2 * piece.chip + 1):
                    flat_slot(s, rows_dev, piece.row, piece.row + piece.count, grad_a, grad_b, slots.at[s])
                core_copy(i).start()

    def ship_on(stage):
        for i, piece in enumerate(early):
            if piece.stage == stage:
                core_copy(i).wait()
                spot = 2 * piece.chip + core
                slots[spot, piece.rows, :] = slots[spot, piece.rows, :] + core_in[piece.chip, piece.rows, :]

                @pl.when(side != piece.side)
                def _(i=i):
                    chip_copy(i).start()

    def ship_end():
        for i, piece in enumerate(early):

            @pl.when(side != piece.side)
            def _(i=i):
                chip_copy(i).wait_send()

            @pl.when(side == piece.side)
            def _(i=i, piece=piece):
                chip_copy(i).wait_recv()
                own = slots[2 * piece.chip + core, piece.rows, :]
                early_part[piece.group, piece.rows, :] = own + chip_in[piece.group, piece.rows, :]

    def ok(place):
        return place_ok(place, edge, split, row_count)

    def halo_copies(s, up_src, down_src, up_dst, down_dst, sem_send, sem_recv):
        up = remote(up_src, down_dst, sem_send.at[2 * s], sem_recv.at[2 * s], above)
        down = remote(down_src, up_dst, sem_send.at[2 * s + 1], sem_recv.at[2 * s + 1], below)
        return up, down

    def halo_start(copies):
        up, down = copies

        @pl.when(has_up)
        def _():
            up.start()

        @pl.when(has_down)
        def _():
            down.start()

    def halo_wait(copies):
        up, down = copies

        @pl.when(has_up)
        def _():
            up.wait_send()
            down.wait_recv()

        @pl.when(has_down)
        def _():
            down.wait_send()
            up.wait_recv()

    def thin(s):
        return halo_copies(
            s, send_up.at[s], send_down.at[s], from_up.at[s], from_down.at[s], sem_s, sem_r
        )

    def pick(condition, a, b):
        return jnp.where(condition, a, b)

    column = row_of((LANES, LANES))

    def shifted(value):
        left = jnp.where(column > 0, pltpu.roll(value, 1, axis=0), 0.0)
        right = jnp.where(column < LANES - 1, pltpu.roll(value, LANES - 1, axis=0), 0.0)
        return left.astype(BF16), value.astype(BF16), right.astype(BF16)

    def put(ref, pair, parity, value, part, parts):
        rows = pl.ds(pl.multiple_of(pair * LANES, LANES), LANES)
        width = 3 * parts * LANES
        for j, shift in enumerate(shifted(value)):
            lane = parity * width + (j * parts + part) * LANES
            ref[rows, lane : lane + LANES] = shift

    def edges(parts, up_halo, down_halo):
        rows = []
        for good, halo in (((top == 1) & has_up, up_halo), ((bottom == 1) & has_down, down_halo)):
            pieces = [shifted(pick(good, halo[:, p * LANES : (p + 1) * LANES].astype(F32), 0.0)) for p in range(parts)]
            rows.append(jnp.concatenate([pieces[p][j] for j in range(3) for p in range(parts)], axis=1))
        return rows

    def put_edges(ref, top_row, bottom_row):
        width = top_row.shape[1]
        ref[0:LANES, 0:width] = top_row
        rows = slice(16 * LANES, 17 * LANES)
        ref[rows, width : 2 * width] = pick(split == 1, ref[rows, width : 2 * width], bottom_row)
        rows = slice(17 * LANES, 18 * LANES)
        ref[rows, 0:width] = pick(split == 1, bottom_row, jnp.zeros_like(bottom_row))

    def add_edges(ref, at_top, at_bottom):
        width = at_top.shape[1]
        ref[0:LANES, 0:width] += at_top
        rows = slice(15 * LANES, 16 * LANES)
        ref[rows, width : 2 * width] += pick(split == 1, 0.0, at_bottom)
        rows = slice(16 * LANES, 17 * LANES)
        ref[rows, 0:width] += pick(split == 1, at_bottom, 0.0)

    up_f[...] = pre_in[0]
    down_f[...] = pick(split == 1, pre_in[row_count + 2], pre_in[row_count + 1])
    copies = halo_copies(0, up_f, down_f, from_up_f, from_down_f, sem_fs, sem_fr)
    halo_start(copies)
    for ref, wide in ((x_one, 768), (x_two, 768), (x_three, 768)):
        ref[0:LANES, 0:384] = jnp.zeros((LANES, 384), BF16)
        ref[18 * LANES : 20 * LANES, :] = jnp.zeros((2 * LANES, wide), BF16)
    spread_z(feature[...], z_columns(cells_row[...]), spread)
    bias_mid = stat[32:33, :]
    b_mid = jnp.concatenate([bias_mid[:, 32:96], bias_mid[:, 32:96]], axis=1)

    def activated(value, x_ref, q, e):
        value = pick(ok(2 * q + 1 + e), value * sigmoid(value), 0.0)
        put(x_ref, q + e, 1 - e, value, 0, 1)

    def mid_step(q, carry):
        rows = pl.ds(pl.multiple_of(q * LANES, LANES), LANES)
        for e in range(2):
            value = pre_in[2 * q + 1 + e] + b_mid
            pre_mid[rows, e * LANES : (e + 1) * LANES] = value
            activated(value, x_one, q, e)
        return carry

    lax.fori_loop(0, PAIRS, mid_step, 0)
    halo_wait(copies)
    at_top = pick((top == 1) & has_up, from_up_f[...], 0.0)
    at_bottom = pick((bottom == 1) & has_down, from_down_f[...], 0.0)
    add_edges(pre_mid, at_top, at_bottom)
    for q, e in ((0, 0), (15, 1), (16, 0)):
        activated(pre_mid[q * LANES : (q + 1) * LANES, e * LANES : (e + 1) * LANES], x_one, q, e)

    def activate(pre_ref, x_ref):
        def step(q, carry):
            rows = pl.ds(pl.multiple_of(q * LANES, LANES), LANES)
            for e in range(2):
                activated(pre_ref[rows, e * LANES : (e + 1) * LANES], x_ref, q, e)
            return carry

        lax.fori_loop(0, PAIRS, step, 0)

    def exchange(x_ref, s):
        send_up[s] = x_ref[0:LANES, 512:640]
        send_down[s] = pick(split == 1, x_ref[16 * LANES : 17 * LANES, 512:640], x_ref[16 * LANES : 17 * LANES, 128:256])
        halo_start(thin(s))

    def banded(x_ref, f_ref, bias, out_ref):
        def step(b, carry):
            start = pl.multiple_of(b * SPAN, LANES)
            total = nn(x_ref[pl.ds(start, SPAN), :], f_ref[0:768, :])
            total += nn(x_ref[pl.ds(start + LANES, SPAN), :], f_ref[768:1536, :])
            out_ref[pl.ds(start, SPAN), :] = total + bias
            return carry

        lax.fori_loop(0, STEPS, step, 0)

    def banded_back(g_ref, d_ref, out_ref):
        width = g_ref.shape[1]

        def step(b, carry):
            start = pl.multiple_of(b * SPAN, LANES)
            total = nt(g_ref[pl.ds(start, SPAN), :], d_ref[:, 0:width])
            total += nt(g_ref[pl.ds(start + LANES, SPAN), :], d_ref[:, width : 2 * width])
            out_ref[pl.ds(start, SPAN), :] = total
            return carry

        lax.fori_loop(0, STEPS, step, 0)

    def bias_row(first, lane):
        mixed = jnp.where(lane_of((1, LANES)) >= lane, stat[first : first + 1, :], stat[first + 1 : first + 2, :])
        return pltpu.roll(jnp.broadcast_to(mixed, (8, LANES)), LANES - lane, axis=1)[0:1, :]

    def twice(row):
        return jnp.concatenate([row, row], axis=1)

    def layer_forward(x_ref, f_ref, bias, out_ref, s):
        exchange(x_ref, s)
        banded(x_ref, f_ref, twice(bias), out_ref)
        halo_wait(thin(s))
        top_row, bottom_row = edges(1, from_up[s], from_down[s])
        put_edges(x_ref, top_row, bottom_row)
        add_edges(out_ref, nn(top_row, f_ref[0:384, 0:LANES]), nn(bottom_row, f_ref[768:1152, 0:LANES]))

    layer_forward(x_one, f_one, bias_row(33, 96), pre_one, 0)
    activate(pre_one, x_two)
    layer_forward(x_two, f_two, bias_row(35, 96), pre_two, 1)
    activate(pre_two, x_three)

    def weight_grads(g_ref, x_ref, parts, write):
        width, wide = parts * LANES, 3 * parts * LANES
        middle0 = slice(width, 2 * width)
        middle1 = slice(wide + width, wide + 2 * width)
        acc0[0 : 2 * width, :] = jnp.zeros((2 * width, 768), F32)
        acc1[0:width, :] = jnp.zeros((width, 384), F32)
        acc2[0:width, :] = jnp.zeros((width, 384), F32)

        def step(b, carry):
            start = pl.multiple_of(b * SPAN, LANES)
            rows = pl.ds(start, SPAN)
            g0, g1 = g_ref[rows, middle0], g_ref[rows, middle1]
            both = jnp.concatenate([g0, g1], axis=1)
            acc0[0 : 2 * width, :] += tn(both, x_ref[rows, :])
            acc2[0:width, :] += tn(g1, x_ref[pl.ds(start + LANES, SPAN), 0:384])
            after = g_ref[pl.ds(start + LANES, SPAN), middle0]
            acc1[0:width, :] += tn(after, x_ref[rows, 384:768])
            return carry

        lax.fori_loop(0, STEPS, step, 0)
        for i in range(3):
            if i == 0:
                total = acc0[width : 2 * width, 0:384] + acc1[0:width, :]
            elif i == 1:
                total = acc0[0:width, 0:384] + acc0[width : 2 * width, 384:768]
            else:
                total = acc0[0:width, 384:768] + acc2[0:width, :]
            for j in range(3):
                for part in range(parts):
                    block = total[part * LANES : (part + 1) * LANES, j * LANES : (j + 1) * LANES]
                    write(i, j, part, jnp.transpose(block))

    def bias_grads(g_ref, parts):
        width, wide = parts * LANES, 3 * parts * LANES
        ones = jnp.ones((16, SPAN), BF16)

        def step(b, total):
            rows = pl.ds(pl.multiple_of(b * SPAN, LANES), SPAN)
            total += nn(ones, g_ref[rows, width : 2 * width])
            return total + nn(ones, g_ref[rows, wide + width : wide + 2 * width])

        return lax.fori_loop(0, STEPS, step, jnp.zeros((16, width), F32))[0:1, :]

    def last_layers(pre_three, x_head, g_three):
        bias = jnp.concatenate([bias_row(37, 96), bias_row(38, 96)], axis=1)

        def conv_step(b, carry):
            start = pl.multiple_of(b * SPAN, LANES)
            rows, more = pl.ds(start, SPAN), pl.ds(start + LANES, SPAN)
            total = nn(x_ref3[rows, :], f_three[0:768, :]) + nn(x_ref3[more, 0:384], f_three[768:1152, :])
            pre_three[rows, 0:256] = total + bias
            total = nn(x_ref3[rows, 384:768], f_three[0:384, :]) + nn(x_ref3[more, :], f_three[384:1152, :])
            pre_three[rows, 256:512] = total + bias
            return carry

        x_ref3 = x_three
        exchange(x_three, 2)
        lax.fori_loop(0, STEPS, conv_step, 0)
        halo_wait(thin(2))
        top_row, bottom_row = edges(1, from_up[2], from_down[2])
        put_edges(x_three, top_row, bottom_row)
        add_edges(pre_three, nn(top_row, f_three[0:384, :]), nn(bottom_row, f_three[768:1152, :]))

        def head_step(q, carry):
            rows = pl.ds(pl.multiple_of(q * LANES, LANES), LANES)
            value = pre_three[rows, :]
            x_head[rows, :] = (value * sigmoid(value)).astype(BF16)
            return carry

        lax.fori_loop(0, PAIRS, head_step, 0)
        for load in loads:
            load.wait()
        head_row = jnp.broadcast_to(stat[40:41, :], (LANES, LANES))
        b_head = jnp.sum(jnp.where(lane_of((16, LANES)) == row_of((16, LANES)) + 96, head_row[0:16, :], 0.0), axis=1, keepdims=True)
        divisor = jnp.maximum(stat[0:1, 3:4], 1.0)
        inverse = 1.0 / divisor
        row16 = row_of((16, LANES))

        def loss_tile(logits, place):
            row = place_row(place, edge, row_count)
            label = labels[row]
            kind = jnp.concatenate([label, jnp.zeros((14, LANES), jnp.int32)], axis=0)
            is_class = row16 < 2
            anchor0, anchor1 = label[0:1, :] == 1, label[1:2, :] == 1
            box_on = ((row16 < 9) & anchor0) | ((row16 >= 9) & anchor1)
            positive = (kind == 1).astype(F32)
            negative = (kind == 0).astype(F32)
            q = 1.0 / (1.0 + jnp.exp(-logits))
            rest = jnp.log(1.0 + jnp.exp(-jnp.abs(logits)))
            log_q = jnp.minimum(logits, 0.0) - rest
            log_not = jnp.minimum(-logits, 0.0) - rest
            short = 1.0 - q
            focal = -FOCAL_ALPHA * positive * short * short * log_q
            focal -= (1.0 - FOCAL_ALPHA) * negative * q * q * log_not
            slope_p = FOCAL_ALPHA * (2.0 * q * short * short * log_q - short * short * short)
            slope_n = (1.0 - FOCAL_ALPHA) * (q * q * q - 2.0 * q * q * short * log_not)
            residual = logits - boxes[row]
            size = jnp.abs(residual)
            huber = jnp.where(size < HUBER_BETA, (0.5 / HUBER_BETA) * residual * residual, size - 0.5 * HUBER_BETA)
            bent = jnp.clip(residual * (1.0 / HUBER_BETA), -1.0, 1.0)
            value = jnp.where(is_class, focal, jnp.where(box_on, 2.0 * huber, 0.0))
            grad = jnp.where(is_class, positive * slope_p + negative * slope_n, jnp.where(box_on, 2.0 * bent, 0.0))
            good = ok(place)
            return pick(good, value, 0.0), pick(good, grad * inverse, 0.0)

        def loss_step(q, total):
            rows = pl.ds(pl.multiple_of(q * LANES, LANES), LANES)
            for e in range(2):
                logits = nt(head_t[...], x_head[rows, e * 256 : (e + 1) * 256]) + b_head
                value, grad = loss_tile(logits, 2 * q + 1 + e)
                logit_grads[e, :, rows] = grad.astype(BF16)
                total = total + value
            return total

        total = lax.fori_loop(0, PAIRS, loss_step, jnp.zeros((16, LANES), F32), unroll=3)
        total = jnp.sum(jnp.sum(total, axis=1, keepdims=True), axis=0, keepdims=True)
        loss_mine[...] = jnp.broadcast_to(total, (8, LANES))
        for k in range(1, n):
            loss_copy(k).start()
        g_head = jnp.zeros((16, CR3), F32)
        g_bias = jnp.zeros((16, 1), F32)
        for e in range(2):
            g_head += nn(logit_grads[e], x_head[0:GRID, e * 256 : (e + 1) * 256])
            g_bias += jnp.sum(logit_grads[e].astype(F32), axis=1, keepdims=True)
        back_rows = jnp.where(same_eighth(), tn(g_head, fold16().astype(F32), HIGH), 0.0)
        grad_b[B_HEAD : B_HEAD + 32, :] = tn(eighths().astype(F32), back_rows, HIGH)
        spots = (lane_of((16, LANES)) == row_of((16, LANES))).astype(F32)
        grad_b[B_HEAD + 32 : B_HEAD + 33, :] = jnp.sum(spots * g_bias, axis=0, keepdims=True)

        def back_step(q, carry):
            rows = pl.ds(pl.multiple_of(q * LANES, LANES), LANES)
            for e in range(2):
                grad = tn(logit_grads[e, :, rows], head_t[...])
                grad = grad * slope(pre_three[rows, e * 256 : (e + 1) * 256])
                for part in range(2):
                    put(g_three, q + e, 1 - e, grad[:, part * LANES : (part + 1) * LANES], part, 2)
            return carry

        g_three[0:LANES, 0:768] = jnp.zeros((LANES, 768), BF16)
        g_three[18 * LANES : 20 * LANES, :] = jnp.zeros((2 * LANES, 1536), BF16)
        lax.fori_loop(0, PAIRS, back_step, 0)
        last_row = slice(16 * LANES, 17 * LANES)
        send_up_w[...] = g_three[0:LANES, 1024:1280]
        send_down_w[...] = pick(split == 1, g_three[last_row, 1024:1280], g_three[last_row, 256:512])
        copies = halo_copies(0, send_up_w, send_down_w, from_up_w, from_down_w, sem_ws, sem_wr)
        halo_start(copies)

        def write(i, j, part, block):
            start = B_THREE + 2 * (i * 3 + j) * LANES + part
            grad_b[pl.ds(start, LANES, 2), :] = block

        banded_back(g_three, d_three, back)
        weight_grads(g_three, x_three, 2, write)
        sums = bias_grads(g_three, 2)
        grad_b[B_HEAD - 2 : B_HEAD - 1, :] = sums[:, 0:LANES]
        grad_b[B_HEAD - 1 : B_HEAD, :] = sums[:, LANES : 2 * LANES]
        ship(0)
        halo_wait(copies)
        add_back(d_three, *edges(2, from_up_w[...], from_down_w[...]))

    def add_back(d_ref, top_row, bottom_row):
        width = top_row.shape[1]
        add_edges(back, nt(top_row, d_ref[0:LANES, 0:width]), nt(bottom_row, d_ref[0:LANES, 2 * width : 3 * width]))

    def loss_copy(k):
        return remote(loss_mine, loss_all.at[me], sem_ls.at[k], sem_lr.at[me], lax.rem(me + k, n))

    pl.run_scoped(
        last_layers,
        pltpu.VMEM((GRID, 512), F32),
        pltpu.VMEM((GRID, 512), BF16),
        pltpu.VMEM((20 * LANES, 1536), BF16),
    )

    def lower_layers(g_ref, g_map, win0, win1, win2, gathered):
        def grads_in(pre_ref):
            def step(q, carry):
                rows = pl.ds(pl.multiple_of(q * LANES, LANES), LANES)
                for e in range(2):
                    lanes = slice(e * LANES, (e + 1) * LANES)
                    value = back[rows, lanes] * slope(pre_ref[rows, lanes])
                    put(g_ref, q + e, 1 - e, pick(ok(2 * q + 1 + e), value, 0.0), 0, 1)
                return carry

            lax.fori_loop(0, PAIRS, step, 0)

        def weights_of(x_ref, begin):
            def write(i, j, part, block):
                start = begin + (i * 3 + j) * LANES
                grad_b[start : start + LANES, :] = block

            weight_grads(g_ref, x_ref, 1, write)
            grad_b[begin + 1152 : begin + 1153, :] = bias_grads(g_ref, 1)

        def from_edges(d_ref, s):
            halo_wait(thin(s))
            add_back(d_ref, *edges(1, from_up[s], from_down[s]))

        g_ref[0:LANES, 0:384] = jnp.zeros((LANES, 384), BF16)
        g_ref[18 * LANES : 20 * LANES, :] = jnp.zeros((2 * LANES, 768), BF16)
        grads_in(pre_two)
        exchange(g_ref, 3)
        ship_on(0)
        banded_back(g_ref, d_two, back)
        weights_of(x_two, B_TWO)
        ship(1)
        from_edges(d_two, 3)
        grads_in(pre_one)
        exchange(g_ref, 4)
        ship_on(1)
        banded_back(g_ref, d_one, back)
        from_edges(d_one, 4)

        g_map[...] = jnp.zeros_like(g_map)

        def to_map(q, total):
            rows = pl.ds(pl.multiple_of(q * LANES, LANES), LANES)
            for e in range(2):
                p = 2 * q + 1 + e
                lanes = slice(e * LANES, (e + 1) * LANES)
                value = back[rows, lanes] * slope(pre_mid[rows, lanes])
                value = pick(ok(p), value, 0.0).astype(BF16).astype(F32)
                g_map[pl.ds(pl.multiple_of(p * PITCH + 8, 8), LANES), :] = value
                total += jnp.sum(value, axis=0, keepdims=True)
            return total

        total = lax.fori_loop(0, PAIRS, to_map, jnp.zeros((1, LANES), F32))
        total = total[:, 0:CM] + total[:, CM : 2 * CM]
        grad_a[0:A_MID, :] = jnp.zeros((A_MID, LANES), F32)
        grad_a[A_MID + 1728 : A_ROWS, :] = jnp.zeros((A_ROWS - A_MID - 1728, LANES), F32)
        grad_a[A_MID + 1728 : A_MID + 1729, 0:CM] = total

        def map_row(place):
            return slice(place * PITCH + 8, place * PITCH + 8 + LANES)

        send_up[5] = g_map[map_row(1), :].astype(BF16)
        send_down[5] = pick(split == 1, g_map[map_row(row_count + 1), :], g_map[map_row(row_count), :]).astype(BF16)
        halo_start(thin(5))
        weights_of(x_one, B_ONE)
        ship(2)
        halo_wait(thin(5))
        g_map[map_row(0), :] = pick((top == 1) & has_up, from_up[5].astype(F32), 0.0)
        halo = pick((bottom == 1) & has_down, from_down[5].astype(F32), 0.0)
        g_map[map_row(row_count + 1), :] = pick(split == 1, g_map[map_row(row_count + 1), :], halo)
        g_map[map_row(row_count + 2), :] = pick(split == 1, halo, 0.0)

        wins = (win0, win1, win2)
        voxels = feature.shape[0]

        def fetch(v, carry):
            base = bases[0, v]
            for i in range(3):
                wins[i][pl.ds(4 * v, 3), :] = g_map[pl.ds(base + (2 - i) * PITCH, 3), :]
            return carry

        lax.fori_loop(0, voxels, fetch, 0, unroll=8)
        ship_on(2)
        for i in range(3):
            for j in range(3):
                lanes = slice((i * 3 + j) * LANES, (i * 3 + j + 1) * LANES)
                gathered[:, lanes] = wins[i][pl.ds(2 - j, voxels, 4), :].astype(BF16)
        low = lane_of((64, LANES)) < 64
        for i in range(3):
            block = tn(spread[...], gathered[:, i * 384 : (i + 1) * 384])
            for j in range(3):
                part = block[:, j * LANES : (j + 1) * LANES]
                even = [part[z * LANES : z * LANES + 64] for z in range(ZD)]
                odd = [part[z * LANES + 64 : (z + 1) * LANES] for z in range(ZD)]

                def flip(x):
                    return pltpu.roll(x, 64, axis=1)

                taps = (
                    jnp.where(low, flip(even[1]), odd[1]),
                    jnp.where(low, even[0] + flip(even[2]), flip(odd[0]) + odd[2]),
                    jnp.where(low, even[1] + flip(even[3]), flip(odd[1]) + odd[3]),
                )
                for t in range(3):
                    start = A_MID + (t * 9 + i * 3 + j) * 64
                    grad_a[start : start + 64, :] = taps[t]
        z_column = z_columns(cells_row[...])
        total = jnp.zeros((voxels, C2), F32)
        for z in range(ZD):
            total += jnp.where(z_column == z, nt(gathered[...], w_mid[z * C2 : (z + 1) * C2, :]), 0.0)
        grad_feature[...] = total

    voxels = feature.shape[0]
    pl.run_scoped(
        lower_layers,
        pltpu.VMEM((20 * LANES, 768), BF16),
        pltpu.VMEM(((row_count + 6) * PITCH, LANES), F32),
        pltpu.VMEM((voxels * 4, LANES), F32),
        pltpu.VMEM((voxels * 4, LANES), F32),
        pltpu.VMEM((voxels * 4, LANES), F32),
        pltpu.VMEM((voxels, 1152), BF16),
    )
    for piece in late_list:
        for s in (2 * piece.chip, 2 * piece.chip + 1):
            flat_slot(s, rows_dev, piece.row, piece.row + piece.count, grad_a, grad_b, late.at[s])
    ship_end()
    for k in range(1, n):
        sender = lax.rem(me + n - k, n)
        remote(loss_mine, loss_all.at[sender], sem_ls.at[k], sem_lr.at[sender], sender).wait_recv()
    loss_all[me] = loss_mine[...]
    total = loss_all[0]
    for d in range(1, n):
        total += loss_all[d]
    loss_out[...] = total
    for k in range(1, n):
        loss_copy(k).wait_send()


def convs(n, rows_dev, row_count, bases, cells, feature, stat, middle_out, labels, boxes):
    shape = jax.ShapeDtypeStruct
    dma = pltpu.SemaphoreType.DMA
    voxels = feature.shape[0]
    row = (LANES, LANES)
    padded = ceil_to(rows_dev, 8)
    early = len(shard_pieces(n, rows_dev)[0])
    late = 2 * late_chips(n, rows_dev)
    return pl.pallas_call(
        functools.partial(conv_kernel, n, rows_dev, row_count),
        name="convs",
        out_shape=(
            shape((late, padded, LANES), F32),
            shape((n // 4, padded, LANES), F32),
            shape((voxels, LANES), F32),
            shape((8, LANES), F32),
        ),
        in_specs=[smem()] + [vmem()] * 12 + [anywhere()] * 2,
        out_specs=(vmem(),) * 4,
        scratch_shapes=[
            pltpu.VMEM((A_ROWS, LANES), F32),
            pltpu.VMEM((B_ROWS, LANES), F32),
            pltpu.VMEM((n, padded, LANES), F32),
            pltpu.VMEM((n // 2, padded, LANES), F32),
            pltpu.VMEM((n // 4, padded, LANES), F32),
            pltpu.VMEM((20 * LANES, 768), BF16),
            pltpu.VMEM((20 * LANES, 768), BF16),
            pltpu.VMEM((20 * LANES, 768), BF16),
            pltpu.VMEM((GRID, 256), F32),
            pltpu.VMEM((GRID, 256), F32),
            pltpu.VMEM((GRID, 256), F32),
            pltpu.VMEM((GRID, 256), F32),
            pltpu.VMEM((voxels, ZD * C2), BF16),
            pltpu.VMEM((512, 768), F32),
            pltpu.VMEM((256, 384), F32),
            pltpu.VMEM((256, 384), F32),
            pltpu.VMEM((row_count, 2, LANES), jnp.int32),
            pltpu.VMEM((row_count, 16, LANES), F32),
            pltpu.VMEM((2, 16, GRID), BF16),
            pltpu.VMEM((8, LANES), F32),
            pltpu.VMEM((n, 8, LANES), F32),
            pltpu.VMEM(row, F32),
            pltpu.VMEM(row, F32),
            pltpu.VMEM(row, F32),
            pltpu.VMEM(row, F32),
            pltpu.VMEM((6,) + row, BF16),
            pltpu.VMEM((6,) + row, BF16),
            pltpu.VMEM((6,) + row, BF16),
            pltpu.VMEM((6,) + row, BF16),
            pltpu.VMEM((LANES, 256), BF16),
            pltpu.VMEM((LANES, 256), BF16),
            pltpu.VMEM((LANES, 256), BF16),
            pltpu.VMEM((LANES, 256), BF16),
            dma((16,)), dma((2,)), dma((2,)), dma((12,)), dma((12,)), dma((2,)), dma((2,)), dma((n,)), dma((n,)),
            dma((early,)), dma((early,)), dma((early,)), dma((early,)),
        ],
        compiler_params=pltpu.CompilerParams(
            collective_id=2, has_side_effects=True, vmem_limit_bytes=62 << 20
        ),
    )(bases, cells, feature, stat, *middle_out, labels, boxes)


def adam_outer(gradient, weight, moment, second, momentum):
    moment = FIRST_DECAY * moment + (1.0 - FIRST_DECAY) * gradient
    second = SECOND_DECAY * second + (1.0 - SECOND_DECAY) * gradient * gradient
    moment_fix = moment / (1.0 - FIRST_DECAY**STEP)
    second_fix = second / (1.0 - SECOND_DECAY**STEP)
    inner_weight = weight - INNER_RATE * (
        moment_fix / (jnp.sqrt(second_fix) + ADAM_EPSILON) + WEIGHT_DECAY * weight
    )
    inner_step = weight - inner_weight
    momentum = OUTER_MOMENT * momentum + inner_step
    updated = weight - OUTER_RATE * (inner_step + OUTER_MOMENT * momentum)
    return (moment, second, momentum, updated)


NOTE_A, NOTE_B = 72, 40


def finish_kernel(
    n, rows, points_hbm, points_in, counts_ref, small, stat, first_out, pooled_in, grad_feature, late, early_part,
    gradient,
    points, first, inner_grads, core_in, chip_in, parts, far_in, mine_a, mine_b, notes_a, notes_b, fc_rows, small_grad,
    sem_p, sem_cs, sem_cr, sem_zs, sem_zr, sem_fs, sem_fr, sem_ns, sem_nar, sem_nbr,
):
    me = lax.axis_index("tile")
    early_list, late_list = shard_pieces(n, rows)
    core, side, my_group = lax.rem(me, 2), lax.rem(me // 2, 2), me // 4
    sibling, other = me + 1 - 2 * core, me + 2 - 4 * side
    count_p, voxels = points_hbm.shape[1], points_hbm.shape[2]
    points[...] = jnp.ones_like(points)
    loads = [
        pltpu.make_async_copy(points_hbm.at[k], points.at[:, k, :], sem_p.at[k]) for k in range(7)
    ]
    for load in loads:
        load.start()
    enter(n, me)

    def core_copy(i):
        piece = late_list[i]
        return remote(
            late.at[2 * piece.chip + 1 - core, piece.rows],
            core_in.at[piece.chip, piece.rows],
            sem_cs.at[i], sem_cr.at[i], sibling,
        )

    def chip_copy(i):
        piece = late_list[i]
        return remote(
            core_in.at[piece.chip, piece.rows],
            chip_in.at[piece.group, piece.rows],
            sem_zs.at[i], sem_zr.at[i], other,
        )

    def far_copy(source, piece, sender, send):
        owner = 4 * piece.group + 2 * side + core
        received = sem_fr.at[3 * sender + piece.order]
        return remote(source.at[piece.group, piece.rows], far_in.at[sender, piece.rows], send, received, owner)

    def far_start(source, piece, i):
        @pl.when((side == piece.side) & (my_group != piece.group))
        def _():
            far_copy(source, piece, my_group, sem_fs.at[i]).start()

    for i in range(len(late_list)):
        core_copy(i).start()
    late_count = len(late_list)
    for i, piece in enumerate(early_list):
        far_start(early_part, piece, late_count + i)

    counts = counts_ref[...]
    columns, gamma, beta = first_layer(small)
    mean, scale, held = stat[0:32, 0:1], stat[0:32, 1:2], stat[0:32, 2:3]
    centre = stat[0:8, 4:5]
    order = even_first()
    rows_fc = voxel_rows(small)
    kernel = rows_fc[0:64, :].astype(BF16)
    kernel_t = (0.5 * nt(order.astype(BF16), kernel)).astype(BF16)
    kernel = nt(kernel, order.astype(BF16)).astype(BF16)
    bias = 0.5 * jnp.sum(jnp.where(order, rows_fc[64:65, :], 0.0), axis=1, keepdims=True)
    half_gamma, half_beta = 0.5 * gamma, 0.5 * beta

    def sums_of_cores():
        for i, piece in enumerate(late_list):
            core_copy(i).wait()
            core_in[piece.chip, piece.rows, :] = (
                core_in[piece.chip, piece.rows, :] + late[2 * piece.chip + core, piece.rows, :]
            )

            @pl.when(side != piece.side)
            def _(i=i):
                chip_copy(i).start()

    def sums_of_chips(i):
        piece = late_list[i]

        @pl.when(side == piece.side)
        def _():
            chip_copy(i).wait_recv()
            own = core_in[piece.chip, piece.rows, :]
            parts[piece.group, piece.rows, :] = own + chip_in[piece.group, piece.rows, :]

        far_start(parts, piece, i)

    def halves(value):
        high = value.astype(BF16)
        return high, (value - high.astype(F32)).astype(BF16)

    def note(ref, notes, sender, s, received):
        return remote(ref, notes.at[sender], sem_ns.at[s], received.at[sender], 0)

    def send_note(s):
        @pl.when(me > 0)
        def _():
            (note(mine_a, notes_a, me, 0, sem_nar) if s == 0 else note(mine_b, notes_b, me, 1, sem_nbr)).start()

    tail = jnp.where(row_of((16, CHUNK)) == 0, 1.0, 0.0).astype(BF16)
    fc = jnp.zeros((80, LANES), F32)
    moments, g_gamma, centred = jnp.zeros((LANES, 16), F32), jnp.zeros((32, CHUNK), F32), jnp.zeros((8, CHUNK), F32)
    chunks = voxels // CHUNK
    for c in range(chunks):
        part = slice(c * CHUNK, (c + 1) * CHUNK)
        held_c = counts[:, part]
        counts_f = held_c.astype(F32)
        grad_pre = (0.5 * jnp.transpose(grad_feature[part, :])) / counts_f
        pooled_c = pooled_in[:, part]
        fixed = nn(kernel_t[:, 32:64], pooled_c) + bias

        def spot(p):
            return pl.ds(pl.multiple_of(p * CHUNK, LANES), CHUNK)

        def pass_e(p, carry, part=part, held_c=held_c, grad_pre=grad_pre, fixed=fixed):
            half_inner = nn(kernel_t[:, 0:32], first_out[p, :, part]) + fixed
            grad = jnp.where(p < held_c, grad_pre * half_slope(half_inner), 0.0)
            inner_grads[:, spot(p)] = grad.astype(BF16)
            return carry

        lax.fori_loop(0, count_p, pass_e, 0, unroll=7)
        if c == 0:
            sums_of_cores()

        def pass_g(p, carry, part=part, pooled_c=pooled_c):
            fc, pooled = carry
            grad = inner_grads[:, spot(p)]
            fc += nt(jnp.concatenate([first_out[p, :, part], pooled_c, tail], axis=0), grad)
            down = nn(kernel, grad)
            first[p] = down[0:32]
            return fc, pooled + down[32:64]

        fc, pooled = lax.fori_loop(0, count_p, pass_g, (fc, jnp.zeros((32, CHUNK), F32)), unroll=5)
        if c == 0:
            for load in loads:
                load.wait()
            sums_of_chips(0)
        if c == chunks - 1:
            mine_a[...] = fc[0:NOTE_A]
            send_note(0)
            for i in range(2 if chunks > 1 else 1, late_count):
                sums_of_chips(i)
        pooled = pooled / counts_f
        wide = [jnp.broadcast_to(column, (32, CHUNK)) for column in columns]
        view = points_in.at[:, :, part]

        def pass_f(p, carry, part=part, held_c=held_c, pooled=pooled, wide=wide, view=view):
            moments, g_gamma, centred = carry
            inside = p < held_c
            normed = jnp.where(inside, (linear_row(wide, view, p) - mean) * scale, 0.0)
            slopes = half_slope(half_gamma * normed + half_beta)
            grad = jnp.where(inside, (0.5 * (first[p] + pooled)) * slopes, 0.0)
            off = points[p, :, part] - centre
            off_high, off_low = halves(off)
            grad_high, grad_low = halves(grad)
            norm_high, norm_low = halves(normed)
            left = jnp.concatenate([grad_high, grad_low, norm_high, norm_low], axis=0)
            right = jnp.concatenate([off_high, off_low], axis=0)
            return (
                moments + nt(left, right),
                g_gamma + grad * normed,
                centred + jnp.where(inside, off, 0.0),
            )

        moments, g_gamma, centred = lax.fori_loop(0, count_p, pass_f, (moments, g_gamma, centred), unroll=5)
        if c == 0 and chunks > 1 and late_count > 1:
            sums_of_chips(1)
    by_grad = moments[0:32] + moments[32:64]
    by_grad = by_grad[:, 0:8] + by_grad[:, 8:16]
    by_norm = moments[64:96] + moments[96:128]
    by_norm = by_norm[:, 0:8] + by_norm[:, 8:16]
    mine_b[...] = jnp.zeros_like(mine_b)
    mine_b[0:32, 0:8] = by_grad
    mine_b[0:32, 8:16] = by_norm
    mine_b[0:32, 16:17] = jnp.sum(g_gamma, axis=1, keepdims=True)
    mine_b[32:40, 0:1] = jnp.sum(centred, axis=1, keepdims=True)
    send_note(1)
    small_grad[...] = jnp.zeros_like(small_grad)

    @pl.when(me == 0)
    def _():
        notes_a[0] = mine_a[...]
        notes_b[0] = mine_b[...]
        for d in range(1, n):
            note(mine_a, notes_a, d, 0, sem_nar).wait_recv()
            note(mine_b, notes_b, d, 1, sem_nbr).wait_recv()
        fc_total, total = notes_a[0], notes_b[0]
        for d in range(1, n):
            fc_total += notes_a[d]
            total += notes_b[d]
        by_grad, by_norm = total[0:32, 0:8], total[0:32, 8:16]
        g_gamma, g_beta = total[0:32, 16:17], total[0:32, 7:8]
        off_sums = jnp.transpose(jnp.broadcast_to(total[32:40, 0:1], (8, LANES)))[0:32, 0:8]
        g_vfe = scale * gamma * (
            by_grad - g_beta / held * off_sums - g_gamma / held * by_norm
        )
        tall0 = jnp.concatenate([g_vfe[:, k : k + 1] for k in range(4)], axis=0)
        tall1 = jnp.concatenate([g_vfe[:, 4:5], g_vfe[:, 5:6], g_vfe[:, 6:7], g_gamma], axis=0)
        tall2 = jnp.concatenate([g_beta, jnp.zeros((96, 1), F32)], axis=0)
        lane = lane_of((LANES, LANES))
        tall = jnp.where(lane == 0, tall0, 0.0) + jnp.where(lane == 1, tall1, 0.0) + jnp.where(lane == 2, tall2, 0.0)
        head = jnp.transpose(tall)[0:8]
        fc_rows[...] = jnp.zeros_like(fc_rows)
        fc_rows[8:80, :] = nn(fc_total, order.astype(F32), HIGH)
        here, before = fc_rows[8:80, :], fc_rows[7:79, :]
        mixed = jnp.where(lane_of((72, LANES)) >= LANES - FC_LANE, before, here)
        small_grad[2:74, :] = pltpu.roll(mixed, FC_LANE, axis=1)
        small_grad[0:8, :] = small_grad[0:8, :] + head

    for i, piece in enumerate(late_list + early_list):
        source = parts if i < late_count else early_part
        count = min(piece.count, rows - piece.row)
        taken = pl.ds(piece.row, count)
        here = side == piece.side

        @pl.when(here & (my_group == piece.group))
        def _(source=source, piece=piece, taken=taken):
            gradient[taken, :] = source[piece.group, taken, :]
            for k in range(1, n // 4):
                sender = lax.rem(my_group + n // 4 - k, n // 4)
                far_copy(source, piece, sender, sem_fs.at[0]).wait_recv()
                gradient[taken, :] = gradient[taken, :] + far_in[sender, taken, :]

        @pl.when(here & (my_group != piece.group))
        def _(source=source, piece=piece, i=i):
            far_copy(source, piece, my_group, sem_fs.at[i]).wait_send()

        if i < late_count:

            @pl.when(side != piece.side)
            def _(i=i):
                chip_copy(i).wait_send()

    gradient[0:SMALL, :] = gradient[0:SMALL, :] + small_grad[...]

    @pl.when(me > 0)
    def _():
        note(mine_a, notes_a, me, 0, sem_nar).wait_send()
        note(mine_b, notes_b, me, 1, sem_nbr).wait_send()


def finish(n, rows, points, counts, small, stat, first_out, pooled, grad_feature, late, early_part):
    shape = jax.ShapeDtypeStruct
    dma = pltpu.SemaphoreType.DMA
    slots, voxels = points.shape[1:]
    padded = ceil_to(rows, 8)
    fours = n // 4
    chips, count = late.shape[0] // 2, len(shard_pieces(n, rows)[1])
    everything = count + len(shard_pieces(n, rows)[0])
    return pl.pallas_call(
        functools.partial(finish_kernel, n, rows),
        name="finish",
        out_shape=shape((rows, LANES), F32),
        in_specs=[anywhere()] + [vmem()] * 9,
        out_specs=vmem(),
        scratch_shapes=[
            pltpu.VMEM((slots, 8, voxels), F32),
            pltpu.VMEM((slots, 32, CHUNK), F32),
            pltpu.VMEM((LANES, slots * CHUNK), BF16),
            pltpu.VMEM((chips, padded, LANES), F32),
            pltpu.VMEM((fours, padded, LANES), F32),
            pltpu.VMEM((fours, padded, LANES), F32),
            pltpu.VMEM((fours, padded, LANES), F32),
            pltpu.VMEM((NOTE_A, LANES), F32),
            pltpu.VMEM((NOTE_B, LANES), F32),
            pltpu.VMEM((n, NOTE_A, LANES), F32),
            pltpu.VMEM((n, NOTE_B, LANES), F32),
            pltpu.VMEM((88, LANES), F32),
            pltpu.VMEM((SMALL, LANES), F32),
            dma((7,)), dma((count,)), dma((count,)), dma((count,)), dma((count,)),
            dma((everything,)), dma((3 * fours,)), dma((2,)), dma((n,)), dma((n,)),
        ],
        compiler_params=pltpu.CompilerParams(
            collective_id=3, has_side_effects=True, vmem_limit_bytes=58 << 20
        ),
    )(points, points, counts, small, stat, first_out, pooled, grad_feature, late, early_part)


def update_kernel(
    gradient, weight, moment, second, momentum, loss, stat,
    moment_out, second_out, momentum_out, weight_out, loss_out, positives_out,
):
    outs = adam_outer(gradient[...], weight[...], moment[...], second[...], momentum[...])
    moment_out[...], second_out[...], momentum_out[...], weight_out[...] = outs
    loss_out[0] = loss[0, 0]
    positives_out[0] = stat[0, 3]


def update(gradient, held, loss, stat):
    shape = jax.ShapeDtypeStruct
    return pl.pallas_call(
        update_kernel,
        name="update",
        out_shape=(shape(gradient.shape, F32),) * 4 + (shape((1,), F32),) * 2,
        in_specs=[vmem()] * 7,
        out_specs=(vmem(),) * 4 + (smem(),) * 2,
        compiler_params=pltpu.CompilerParams(vmem_limit_bytes=32 << 20),
    )(gradient, *held, loss, stat)


def shards(
    points, point_counts, voxel_cells, anchor_labels, box_targets, weights, adam_m, adam_v, outer_momentum
):
    n = lax.axis_size("tile")
    rows = weights.shape[0] // LANES
    row_count = anchor_labels.shape[1]
    held = [x.reshape(rows, LANES) for x in (weights, adam_m, adam_v, outer_momentum)]
    counts = point_counts.reshape(1, -1)
    cells = voxel_cells.reshape(1, -1)
    wall, small, stat, first_out, pooled, feature, bases = front(
        n, points, counts, cells, anchor_labels, held[0]
    )
    ready = middle(n, rows, row_count, bases, cells, feature, wall)
    late, early_part, grad_feature, loss = convs(
        n, rows, row_count, bases, cells, feature, stat, ready, anchor_labels, box_targets
    )
    gradient = finish(
        n, rows, points, counts, small, stat, first_out, pooled, grad_feature, late, early_part
    )
    *outs, loss_sum, positives = update(gradient, held, loss, stat)
    moment, second, momentum, updated = [x.reshape(weights.shape) for x in outs]
    return (moment, second, momentum, updated, loss_sum, positives)


def solution(mesh):
    split = ("group", "tile")
    in_specs = (
        P(None, None, split), P(split), P(split), P(None, split, None), P(None, split, None),
        P(split), P(split), P(split), P(split),
    )
    out_specs = (P(split), P(split), P(split), P(split), P("group"), P("group"))
    return jax.shard_map(shards, mesh=mesh, in_specs=in_specs, out_specs=out_specs, check_vma=False)
```

```python
import functools
import math

import jax
import jax.numpy as jnp
from jax import lax
from jax.experimental import pallas as pl
from jax.experimental.pallas import tpu as pltpu
from jax.sharding import PartitionSpec as P

MESH = pl.DeviceIdType.MESH
F32 = jnp.float32
BF16 = jnp.bfloat16
HIGH = lax.Precision.HIGHEST

C1, C2, CM, CR1, CR2, CR3, ANCH, ZD = 32, 128, 64, 128, 128, 256, 2, 4
H_SCENE = 200
STEP = 10
LANES = 128
NORM_EPSILON = 1e-05
INNER_RATE = 0.05
FIRST_DECAY = 0.9
SECOND_DECAY = 0.999
ADAM_EPSILON = 1e-08
WEIGHT_DECAY = 0.01
OUTER_RATE = 0.7
OUTER_MOMENT = 0.9
FOCAL_ALPHA = 0.25
HUBER_BETA = 1.0 / 9.0

SMALL = 80
FC_ROW, FC_LANE = 2, 32
BIAS_ROWS = (1795, 2947, 2948, 4100, 4101, 6405, 6406, 6407, 6439)
RUN_A = (2, 32)
RUN_B = (1795, 96)
A_MID = 65
B_ONE, B_TWO, B_THREE, B_HEAD = 0, 1153, 2306, 4612
PAIRS_OF = tuple((a, b) for a in range(7) for b in range(a, 7))
DIAGONAL = tuple(r for r, (a, b) in enumerate(PAIRS_OF) if a == b)
CHUNK = 256


def vmem():
    return pl.BlockSpec(memory_space=pltpu.VMEM)


def anywhere():
    return pl.BlockSpec(memory_space=pl.ANY)


def smem():
    return pl.BlockSpec(memory_space=pltpu.SMEM)


def ceil_to(value, step):
    return (value + step - 1) // step * step


def sigmoid(value):
    return 0.5 * jnp.tanh(0.5 * value) + 0.5


def slope(value):
    s = sigmoid(value)
    return s * (1.0 + value * (1.0 - s))


def half_silu(half):
    return half * (1.0 + jnp.tanh(half))


def half_slope(half):
    t = jnp.tanh(half)
    return (1.0 + t) * (1.0 + half * (1.0 - t))


def nt(a, b, precision=None):
    return lax.dot_general(a, b, (((1,), (1,)), ((), ())), precision=precision, preferred_element_type=F32)


def tn(a, b, precision=None):
    return lax.dot_general(a, b, (((0,), (0,)), ((), ())), precision=precision, preferred_element_type=F32)


def nn(a, b, precision=None):
    return lax.dot_general(a, b, (((1,), (0,)), ((), ())), precision=precision, preferred_element_type=F32)


def lane_of(shape):
    return lax.broadcasted_iota(jnp.int32, shape, len(shape) - 1)


def row_of(shape):
    return lax.broadcasted_iota(jnp.int32, shape, len(shape) - 2)


def enter(n, me, between=None):
    sem = pltpu.get_barrier_semaphore()

    def greet(k, carry):
        pl.semaphore_signal(
            sem, inc=1, device_id={"tile": lax.rem(me + k, n)}, device_id_type=MESH
        )
        return carry

    lax.fori_loop(1, n, greet, 0)
    if between is not None:
        between()
    pl.semaphore_wait(sem, n - 1)


def remote(src, dst, send, recv, peer):
    return pltpu.make_async_remote_copy(
        src_ref=src,
        dst_ref=dst,
        send_sem=send,
        recv_sem=recv,
        device_id={"tile": peer},
        device_id_type=MESH,
    )


def even_first():
    out = row_of((LANES, LANES))
    source = jnp.where(out < 64, 2 * out, 2 * out - 127)
    return lane_of((LANES, LANES)) == source


def first_layer(small_ref):
    turned = jnp.transpose(small_ref[0:LANES_PAD, :])
    columns = [turned[(k % 4) * 32 : (k % 4) * 32 + 32, k // 4 : k // 4 + 1] for k in range(7)]
    return columns, turned[96:128, 1:2], turned[0:32, 2:3]


LANES_PAD = 8


def voxel_rows(small_ref):
    here, after = small_ref[2:74, :], small_ref[3:75, :]
    mixed = jnp.where(lane_of((72, LANES)) >= FC_LANE, here, after)
    return pltpu.roll(mixed, LANES - FC_LANE, axis=1)


def layout(n, row_count):
    first = lax.axis_index("tile") * row_count
    ahead = (first // H_SCENE + 1) * H_SCENE - first
    split = jnp.where(ahead < row_count, 1, 0)
    edge = jnp.where(ahead < row_count, ahead, row_count)
    top = jnp.where(lax.rem(first, H_SCENE) != 0, 1, 0)
    last = first + row_count
    bottom = jnp.where((lax.rem(last, H_SCENE) != 0) & (last < n * row_count), 1, 0)
    return edge, split, top, bottom


def place_ok(place, edge, split, row_count):
    return (place >= 1) & (place <= row_count + split) & ((place != edge + 1) | (split == 0))


def place_row(place, edge, row_count):
    row = jnp.where(place <= edge, place - 1, place - 2)
    return jnp.clip(row, 0, row_count - 1)


PITCH = 136


def voxel_bases(cells, n, row_count, columns):
    edge, split, _, _ = layout(n, row_count)
    local = lax.rem(cells, row_count * columns * ZD)
    row = local // (columns * ZD)
    column = lax.rem(local, columns * ZD) // ZD
    place = row + 1 + jnp.where((row >= edge) & (split == 1), 1, 0)
    return (place - 1) * PITCH + column + 7


def linear_row(wide, points, p):
    value = wide[0] * points[0, pl.ds(p, 1), :]
    for k in range(1, 7):
        value += wide[k] * points[k, pl.ds(p, 1), :]
    return value


def local_moments(points, counts, labels_ref, sums, message):
    slots, voxels = points.shape[1:]
    inside = row_of((slots, voxels)) < counts

    def folded(value):
        total = value[:, 0:LANES]
        for c in range(1, voxels // LANES):
            total = total + value[:, c * LANES : (c + 1) * LANES]
        return jnp.sum(total, axis=0, keepdims=True)

    def whole(row):
        return jnp.sum(row, axis=1, keepdims=True)

    held = whole(folded(inside.astype(F32)))
    masked = [jnp.where(inside, points[k], 0.0) for k in range(7)]
    rows = [folded(value) for value in masked]
    means = [whole(row) / held for row in rows]
    centred = [jnp.where(inside, points[k] - means[k], 0.0) for k in range(7)]
    for r, (a, b) in enumerate(PAIRS_OF):
        sums[0, r : r + 1, :] = folded(centred[a] * centred[b])
        sums[1, r : r + 1, :] = rows[a]
        sums[2, r : r + 1, :] = rows[b]
    spare = len(PAIRS_OF)
    for c in range(3):
        sums[c, spare:LANES, :] = jnp.zeros((LANES - spare, LANES), F32)
    lane = lane_of((LANES, LANES))
    columns = jnp.zeros((LANES, LANES), F32)
    for c in range(3):
        columns = jnp.where(lane == c, jnp.sum(sums[c], axis=1, keepdims=True), columns)
    positives = jnp.zeros((1, 1), F32)
    for a in range(ANCH):
        positives += whole(jnp.sum((labels_ref[a] == 1).astype(F32), axis=0, keepdims=True))
    packed = jnp.transpose(columns)[0:8]
    row = row_of((8, LANES))
    packed = jnp.where(row == 3, held, packed)
    message[...] = jnp.where(row == 4, positives, packed)


def joint_moments(n, messages):
    total = messages[0]
    for d in range(1, n):
        total += messages[d]
    held = total[3:4]
    mean_a, mean_b = total[1:2] / held, total[2:3] / held
    product = total[0:1]
    for d in range(n):
        held_d = messages[d, 3:4, :]
        product += held_d * (messages[d, 1:2, :] / held_d - mean_a) * (messages[d, 2:3, :] / held_d - mean_b)
    return mean_a, product, held, total[4:5]


def channel_statistics(columns, mean_row, product, held):
    lane = lane_of((32, LANES))
    once, twice = jnp.zeros((32, LANES), F32), jnp.zeros((32, LANES), F32)
    for r, (a, b) in enumerate(PAIRS_OF):
        if a == b:
            once = jnp.where(lane == r, columns[a], once)
        twice = jnp.where(lane == r, (1.0 if a == b else 2.0) * columns[a] * columns[b], twice)
    mean = jnp.sum(once * mean_row, axis=1, keepdims=True)
    variance = jnp.sum(twice * (product / held), axis=1, keepdims=True)
    return mean, lax.rsqrt(variance + NORM_EPSILON)


def front_kernel(
    n, points, counts_ref, cells_ref, labels_ref, shard_ref,
    wall, small, stat, first_out, pooled_out, feature, bases,
    own, sums, mine, messages, my_bias, biases,
    sem_small_s, sem_small_r, sem_msg_s, sem_msg_r, sem_b_s, sem_b_r, sem_w_s, sem_w_r, sem_f_s, sem_e_s,
):
    me = lax.axis_index("tile")
    rows = shard_ref.shape[0]
    slots, voxels = points.shape[1:]
    sibling = me + 1 - 2 * lax.rem(me, 2)
    half = n // 2
    counts = counts_ref[...]

    def prepare():
        local_moments(points, counts, labels_ref, sums, mine)
        bases[...] = voxel_bases(cells_ref[...], n, labels_ref.shape[1], labels_ref.shape[2])
        own[...] = jnp.zeros_like(own)
        own[0:rows, :] = shard_ref[...].astype(BF16)
        for a, row in enumerate(BIAS_ROWS):
            owner, place = row // rows, row % rows
            my_bias[a : a + 1, :] = jnp.where(me == owner, shard_ref[place : place + 1, :], 0.0)
        for a in range(len(BIAS_ROWS), 16):
            my_bias[a : a + 1, :] = jnp.zeros((1, LANES), F32)

    enter(n, me, prepare)

    def message(k):
        return remote(mine, messages.at[me], sem_msg_s.at[k], sem_msg_r.at[me], lax.rem(me + k, n))

    def bias_message(k):
        return remote(my_bias, biases.at[me], sem_b_s.at[k], sem_b_r.at[me], lax.rem(me + k, n))

    def small_copy(k):
        return remote(small, small, sem_small_s.at[k], sem_small_r.at[0], lax.rem(me + k, n))

    def shard_copy(k):
        return remote(own, wall.at[me], sem_w_s.at[k], sem_w_r.at[me], lax.rem(me + 2 * k, n))

    for k in range(1, n):
        message(k).start()

    @pl.when(me == 0)
    def _():
        small[...] = shard_ref[0:SMALL, :]

        def send(k, carry):
            small_copy(k).start()
            return carry

        lax.fori_loop(1, n, send, 0)

    for k in range(1, n):
        bias_message(k).start()
    line = me // 2
    if n == 8:
        inner = (line == 1) | (line == 2)
        toward = jnp.where(line == 2, 2, -2)
        turn = jnp.where(line == 0, 2, -2)

        def own_copy(step, k):
            return remote(own, wall.at[me], sem_w_s.at[k], sem_w_r.at[me], me + step)

        @pl.when(inner)
        def _():
            own_copy(-toward, 1).start()
            own_copy(toward, 2).start()

        @pl.when(jnp.logical_not(inner))
        def _():
            own_copy(turn, 1).start()
            own_copy(2 * turn, 2).start()

    else:
        for k in range(1, half):
            shard_copy(k).start()

    def arrived(source):
        remote(own, wall.at[source], sem_w_s.at[0], sem_w_r.at[source], sibling).wait_recv()

    def pass_on(source, k, peer, sem):
        return remote(wall.at[source], wall.at[source], sem.at[k], sem_w_r.at[source], peer)

    def relay(step):
        if n == 8 and step < 2:

            @pl.when(inner)
            def _():
                source = me - (step + 1) * toward
                arrived(source)
                pass_on(source, step, me + toward, sem_e_s).start()
                pass_on(source, step + 1, sibling, sem_f_s).start()

    to_sibling = remote(own, wall.at[me], sem_w_s.at[0], sem_w_r.at[me], sibling)
    to_sibling.start()
    wall[me] = own[...]
    messages[me] = mine[...]
    biases[me] = my_bias[...]

    @pl.when(me > 0)
    def _():
        small_copy(0).wait_recv()

    columns, gamma, beta = first_layer(small)
    order = even_first()
    rows_fc = voxel_rows(small)
    kernel_t = (0.5 * nt(order.astype(BF16), rows_fc[0:64, :].astype(BF16))).astype(BF16)
    bias = 0.5 * jnp.sum(jnp.where(order, rows_fc[64:65, :], 0.0), axis=1, keepdims=True)
    for k in range(1, n):
        sender = lax.rem(me + n - k, n)
        remote(mine, messages.at[sender], sem_msg_s.at[k], sem_msg_r.at[sender], sender).wait_recv()
    mean_row, product, held, positives = joint_moments(n, messages)
    mean, inverse = channel_statistics(columns, mean_row, product, held)
    lane, row = lane_of((32, LANES)), row_of((32, LANES))
    columns_out = jnp.where(lane == 0, mean, 0.0)
    columns_out = jnp.where(lane == 1, inverse, columns_out)
    columns_out = jnp.where(lane == 2, held, columns_out)
    columns_out = jnp.where(lane == 3, positives, columns_out)
    for k, r in enumerate(DIAGONAL):
        columns_out = jnp.where((lane == 4) & (row == k), mean_row[:, r : r + 1], columns_out)
    stat[0:32, :] = columns_out

    half_gamma, half_beta = 0.5 * gamma, 0.5 * beta
    for c in range(voxels // CHUNK):
        part = slice(c * CHUNK, (c + 1) * CHUNK)
        wide = [jnp.broadcast_to(column, (32, CHUNK)) for column in columns]
        held_c = counts[:, part]
        view = points.at[:, :, part]

        def pass_c(p, pooled, wide=wide, held_c=held_c, view=view, part=part):
            half_act = half_gamma * ((linear_row(wide, view, p) - mean) * inverse) + half_beta
            out = jnp.where(p < held_c, half_silu(half_act), 0.0)
            first_out[p, :, part] = out.astype(BF16)
            return pooled + out

        pooled = lax.fori_loop(0, slots, pass_c, jnp.zeros((32, CHUNK), F32), unroll=5)
        pooled = (pooled / held_c.astype(F32)).astype(BF16)
        pooled_out[:, part] = pooled
        fixed = nn(kernel_t[:, 32:64], pooled) + bias

        def pass_d(p, total, fixed=fixed, held_c=held_c, part=part):
            half_inner = nn(kernel_t[:, 0:32], first_out[p, :, part]) + fixed
            return total + jnp.where(p < held_c, half_silu(half_inner), 0.0)

        total = lax.fori_loop(0, slots, pass_d, jnp.zeros((LANES, CHUNK), F32), unroll=7)
        feature[part, :] = jnp.transpose(total / held_c.astype(F32))
        relay(c)

    for step in range(voxels // CHUNK, 2):
        relay(step)
    if n == 8:

        @pl.when(inner)
        def _():
            source = me + toward
            arrived(source)
            pass_on(source, 3, sibling, sem_f_s).start()

        @pl.when(jnp.logical_not(inner))
        def _():
            for k in range(1, 4):
                arrived(me + k * turn)
                pass_on(me + k * turn, k, sibling, sem_f_s).start()

    else:
        for k in range(1, half):
            source = lax.rem(me + n - 2 * k, n)
            arrived(source)
            pass_on(source, k, sibling, sem_f_s).start()
    for k in range(1, n):
        sender = lax.rem(me + n - k, n)
        remote(my_bias, biases.at[sender], sem_b_s.at[k], sem_b_r.at[sender], sender).wait_recv()
    total = biases[0]
    for d in range(1, n):
        total += biases[d]
    stat[32:48, :] = total
    for k in range(half):
        arrived(lax.rem(sibling + n - 2 * k, n))
    for k in range(1, half):
        pass_on(me, k, sibling, sem_f_s).wait_send()
    if n == 8:
        for k in (1, 2):
            own_copy(turn, k).wait_send()

        @pl.when(inner)
        def _():
            for k in range(2):
                pass_on(me, k, sibling, sem_e_s).wait_send()

    else:
        for k in range(1, half):
            shard_copy(k).wait_send()
    to_sibling.wait_send()
    for k in range(1, n):
        message(k).wait_send()
        bias_message(k).wait_send()

    @pl.when(me == 0)
    def _():
        def done(k, carry):
            small_copy(k).wait_send()
            return carry

        lax.fori_loop(1, n, done, 0)


def front(n, points, counts, cells, labels, shard):
    slots, voxels = points.shape[1:]
    rows = shard.shape[0]
    padded = ceil_to(rows, 16)
    shape = jax.ShapeDtypeStruct
    dma = pltpu.SemaphoreType.DMA
    return pl.pallas_call(
        functools.partial(front_kernel, n),
        name="front",
        out_shape=(
            shape((n, padded, LANES), BF16),
            shape((SMALL, LANES), F32),
            shape((48, LANES), F32),
            shape((slots, 32, voxels), BF16),
            shape((32, voxels), BF16),
            shape((voxels, LANES), F32),
            shape((1, voxels), jnp.int32),
        ),
        in_specs=[vmem()] * 5,
        out_specs=(vmem(),) * 7,
        scratch_shapes=[
            pltpu.VMEM((padded, LANES), BF16),
            pltpu.VMEM((3, LANES, LANES), F32),
            pltpu.VMEM((8, LANES), F32),
            pltpu.VMEM((n, 8, LANES), F32),
            pltpu.VMEM((16, LANES), F32),
            pltpu.VMEM((n, 16, LANES), F32),
            dma((n,)), dma((1,)), dma((n,)), dma((n,)), dma((n,)), dma((n,)), dma((n,)), dma((n,)), dma((n,)), dma((2,)),
        ],
        compiler_params=pltpu.CompilerParams(
            collective_id=1, has_side_effects=True, vmem_limit_bytes=56 << 20
        ),
    )(points, counts, cells, labels, shard)


def flat_pieces(rows, slot):
    begin, end = slot * rows, (slot + 1) * rows
    spans = ((0, 67, None, 0), (67, 1795, "a", 2), (1795, 1796, "both", 0), (1796, 6440, "b", 1795), (6440, 1 << 30, None, 0))
    pieces = []
    for low, high, run, shift in spans:
        first, last = max(begin, low), min(end, high)
        if first < last:
            pieces.append((first - begin, last - first, run, first - shift))
    return pieces


def flat_slot(slot, rows, low, high, grad_a, grad_b, out_ref):
    def realigned(ref, start, count, lane):
        here, before = ref[pl.ds(start, count), :], ref[pl.ds(start - 1, count), :]
        mixed = jnp.where(lane_of((count, LANES)) >= LANES - lane, before, here)
        return pltpu.roll(mixed, lane, axis=1)

    for row, count, run, start in flat_pieces(rows, slot):
        first, last = max(row, low), min(row + count, high)
        if first >= last:
            continue
        start, row, count = start + first - row, first, last - first
        if run is None:
            value = jnp.zeros((count, LANES), F32)
        elif run == "a":
            value = realigned(grad_a, start, count, 32)
        elif run == "b":
            value = realigned(grad_b, start, count, 96)
        else:
            lane = lane_of((1, LANES))
            part_a = jnp.where(lane >= 96, grad_a[1792:1793, :], grad_a[1793:1794, :])
            part_b = jnp.where(lane >= 32, 0.0, grad_b[0:1, :])
            part_a = pltpu.roll(jnp.broadcast_to(part_a, (8, LANES)), 32, axis=1)
            part_b = pltpu.roll(jnp.broadcast_to(part_b, (8, LANES)), 96, axis=1)
            value = jnp.where(lane < 96, part_a[0:1], part_b[0:1])
        out_ref[row : row + count, :] = value


class Piece:
    def __init__(self, chip, row, count, stage, order):
        self.chip, self.group, self.side = chip, chip // 2, chip % 2
        self.row, self.count, self.stage, self.order = row, count, stage, order
        self.rows = pl.ds(row, count)


def shard_pieces(n, rows):
    padded = ceil_to(rows, 8)
    pieces = []
    for chip in range(n // 2):
        first = 2 * chip * rows
        cut = min(ceil_to(min(max(1796 - first, 0), rows), 8), padded)
        spans = [(0, cut)] if cut else []
        if cut >= 400:
            marks = [ceil_to(cut * k // 4, 8) for k in range(4)] + [cut]
            spans = list(zip(marks[:-1], marks[1:]))
        for order, (low, high) in enumerate(spans):
            pieces.append(Piece(chip, low, high - low, 3, order))
        if cut < padded:
            begin = first + cut
            stage = 0 if begin >= 4102 else 1 if begin >= 2949 else 2
            pieces.append(Piece(chip, cut, padded - cut, stage, 4))
    return pieces


def z_columns(cells_row):
    z = lax.rem(cells_row, ZD).astype(F32)
    return jnp.transpose(jnp.broadcast_to(z, (8, z.shape[1])))[:, 0:1]


def spread_z(feature, z_column, out_ref):
    for z in range(ZD):
        out_ref[:, z * C2 : (z + 1) * C2] = jnp.where(z_column == z, feature, 0.0).astype(BF16)


def middle_kernel(
    n, rows, row_count,
    bases, cells_row, feature, wall,
    pre, *refs,
):
    outs, kept, (flat, run, spread, parts0, parts1, parts2, sum0, sum1, sum2, sem) = refs[:8], refs[8:16], refs[16:]
    w_mid, f_one, f_two, f_three, d_one, d_two, d_three, head_t = kept
    stores = [pltpu.make_async_copy(kept[a], outs[a], sem.at[a]) for a in range(8)]
    voxels = feature.shape[0]
    columns = LANES
    parts, sums = (parts0, parts1, parts2), (sum0, sum1, sum2)
    for s in range(n):
        flat[s * rows : s * rows + wall.shape[1], :] = wall[s].astype(F32)

    def aligned(begin, start, count):
        row, lane = begin
        here = flat[pl.ds(row + start, count), :]
        after = flat[pl.ds(row + start + 1, count), :]
        mixed = jnp.where(lane_of((count, LANES)) >= lane, here, after)
        return pltpu.roll(mixed, LANES - lane, axis=1)

    def zero_half(ref, row, column, height, width):
        ref[row : row + height, column : column + width] = jnp.zeros((height, width), BF16)

    for begin, f_ref, d_ref in ((B_ONE, f_one, d_one), (B_TWO, f_two, d_two)):
        for j in range(3):
            for e in range(2):
                outside = 3 if e == 0 else 0
                zero_half(f_ref, outside * 384 + j * LANES, e * LANES, LANES, LANES)
                zero_half(d_ref, e * LANES, outside * 384 + j * LANES, LANES, LANES)

        def tap(i, j, begin=begin, f_ref=f_ref, d_ref=d_ref):
            block = aligned(RUN_B, begin + (i * 3 + j) * LANES, LANES).astype(BF16)
            for e in range(2):
                t = i + e
                f_ref[t * 384 + j * LANES : t * 384 + (j + 1) * LANES, e * LANES : (e + 1) * LANES] = block
                t = 2 + e - i
                lane = t * 384 + (2 - j) * LANES
                d_ref[e * LANES : (e + 1) * LANES, lane : lane + LANES] = block

        for i in range(3):
            for j in range(3):
                tap(i, j)
        for a in (1, 4) if begin == B_ONE else (2, 5):
            stores[a].start()
    for j in range(3):
        for e in range(2):
            outside = 3 if e == 0 else 0
            zero_half(d_three, e * LANES, outside * 768 + j * 256, LANES, 256)
    for i in range(3):
        for j in range(3):
            run[...] = aligned(RUN_B, B_THREE + (i * 3 + j) * 256, 256)
            for h in range(2):
                block = run[pl.ds(h, LANES, 2), :].astype(BF16)
                row = (i * 3 + j) * LANES
                f_three[row : row + LANES, h * LANES : (h + 1) * LANES] = block
                for e in range(2):
                    lane = (2 + e - i) * 768 + (2 - j) * 256 + h * LANES
                    d_three[e * LANES : (e + 1) * LANES, lane : lane + LANES] = block
    head_rows = aligned(RUN_B, B_HEAD, 32).astype(BF16)
    chosen = nn(eighths(), head_rows)
    chosen = jnp.where(same_eighth(), chosen, 0.0).astype(BF16)
    head_t[...] = nt(fold16(), chosen).astype(BF16)
    for a in (3, 6, 7):
        stores[a].start()

    low = lane_of((64, LANES)) < 64
    for ij in range(9):
        taps = [aligned(RUN_A, A_MID + (t * 9 + ij) * 64, 64) for t in range(3)]
        turned = [pltpu.roll(tap, 64, axis=1) for tap in taps]
        none = jnp.zeros((64, LANES), F32)
        for z in range(ZD):
            first, second = z + 1, z - 1
            a, a_t = (taps[first], turned[first]) if first < 3 else (none, none)
            b, b_t = (taps[second], turned[second]) if second >= 0 else (none, none)
            lanes = slice(ij * LANES, (ij + 1) * LANES)
            w_mid[z * C2 : z * C2 + 64, lanes] = jnp.where(low, a, b_t).astype(BF16)
            w_mid[z * C2 + 64 : (z + 1) * C2, lanes] = jnp.where(low, a_t, b).astype(BF16)

    stores[0].start()
    spread_z(feature[...], z_columns(cells_row[...]), spread)
    for i in range(3):
        product = nn(spread[...], w_mid[:, i * 384 : (i + 1) * 384])
        for j in range(3):
            parts[i][pl.ds(2 - j, voxels, 4), :] = product[:, j * LANES : (j + 1) * LANES]
        sums[i][...] = jnp.zeros_like(sums[i])

    def add(v, carry):
        base = bases[0, v]
        for i in range(3):
            spot = pl.ds(base + (2 - i) * PITCH, 3)
            sums[i][spot, :] = sums[i][spot, :] + parts[i][pl.ds(4 * v, 3), :]
        return carry

    lax.fori_loop(0, voxels, add, 0, unroll=8)

    def gather(p, carry):
        spot = pl.ds(pl.multiple_of(p * PITCH + 8, 8), columns)
        pre[p] = sum0[spot, :] + sum1[spot, :] + sum2[spot, :]
        return carry

    lax.fori_loop(0, row_count + 5, gather, 0)
    for store in stores:
        store.wait()


def eighths():
    return (row_of((CR3, 32)) // 8 == lane_of((CR3, 32))).astype(F32).astype(BF16)


def same_eighth():
    return lane_of((CR3, LANES)) // 16 == lax.rem(row_of((CR3, LANES)), 8)


def fold16():
    return (lax.rem(lane_of((16, LANES)), 16) == row_of((16, LANES))).astype(F32).astype(BF16)


def middle(n, rows, row_count, bases, cells, feature, wall):
    shape = jax.ShapeDtypeStruct
    voxels = feature.shape[0]
    cells_all = (row_count + 6) * PITCH
    return pl.pallas_call(
        functools.partial(middle_kernel, n, rows, row_count),
        name="middle",
        out_shape=(
            shape((row_count + 5, LANES, LANES), F32),
            shape((512, 1152), BF16),
            shape((1536, 256), BF16),
            shape((1536, 256), BF16),
            shape((1152, 256), BF16),
            shape((256, 1536), BF16),
            shape((256, 1536), BF16),
            shape((256, 3072), BF16),
            shape((16, 256), BF16),
        ),
        in_specs=[smem(), vmem(), vmem(), vmem()],
        out_specs=(vmem(),) + (anywhere(),) * 8,
        scratch_shapes=[
            pltpu.VMEM((512, 1152), BF16),
            pltpu.VMEM((1536, 256), BF16),
            pltpu.VMEM((1536, 256), BF16),
            pltpu.VMEM((1152, 256), BF16),
            pltpu.VMEM((256, 1536), BF16),
            pltpu.VMEM((256, 1536), BF16),
            pltpu.VMEM((256, 3072), BF16),
            pltpu.VMEM((16, 256), BF16),
            pltpu.VMEM((n * rows + 24, LANES), F32),
            pltpu.VMEM((256, LANES), F32),
            pltpu.VMEM((voxels, ZD * C2), BF16),
            pltpu.VMEM((voxels * 4, LANES), F32),
            pltpu.VMEM((voxels * 4, LANES), F32),
            pltpu.VMEM((voxels * 4, LANES), F32),
            pltpu.VMEM((cells_all, LANES), F32),
            pltpu.VMEM((cells_all, LANES), F32),
            pltpu.VMEM((cells_all, LANES), F32),
            pltpu.SemaphoreType.DMA((8,)),
        ],
        compiler_params=pltpu.CompilerParams(vmem_limit_bytes=56 << 20),
    )(bases, cells, feature, wall)


NOTE_A, NOTE_B = 72, 40
PAIRS = 18
QB = 9
STEPS = PAIRS // QB
SPAN = QB * LANES
GRID = PAIRS * LANES
A_ROWS, B_ROWS = 1800, 4656


def conv_kernel(
    n, rows_dev, row_count,
    bases, cells_row, feature, stat, pre_in,
    w_mid_h, f_one_h, f_two_h, f_three_h, d_one_h, d_two_h, d_three_h, head_t_h,
    labels_hbm, boxes_hbm, points_hbm, counts_ref, small, pooled_in, first_hbm,
    gradient, loss_out,
    grad_a, grad_b, slots, core_in, chip_in, far_in, grad_feature,
    mine_a, mine_b, notes_a, notes_b, fc_rows, small_grad,
    f_one, f_two, f_three, d_three, head_t, sem_k,
    x_one, x_two, x_three, pre_mid, pre_one, pre_two, back, spread,
    acc0, acc1, acc2,
    labels, boxes, logit_grads, loss_mine, loss_all,
    up_f, down_f, from_up_f, from_down_f, send_up, send_down, from_up, from_down,
    send_up_w, send_down_w, from_up_w, from_down_w,
    sem_t, sem_fs, sem_fr, sem_s, sem_r, sem_ws, sem_wr, sem_ls, sem_lr, sem_cs, sem_cr, sem_zs, sem_zr,
    sem_gs, sem_gr, sem_p, sem_ns, sem_nar, sem_nbr,
):
    me = lax.axis_index("tile")
    edge, split, top, bottom = layout(n, row_count)
    has_up, has_down = me > 0, me < n - 1
    above, below = jnp.maximum(me - 1, 0), jnp.minimum(me + 1, n - 1)
    loads = [pltpu.make_async_copy(labels_hbm.at[a], labels.at[:, a, :], sem_t.at[a]) for a in range(2)]
    loads += [
        pltpu.make_async_copy(boxes_hbm.at[a], boxes.at[:, 2 + a, :], sem_t.at[2 + a]) for a in range(14)
    ]
    for load in loads:
        load.start()
    kernels = (
        (f_one_h, f_one), (f_two_h, f_two), (f_three_h, f_three), (head_t_h, head_t),
        (d_three_h, d_three),
    )
    kernel_loads = [pltpu.make_async_copy(a, b, sem_k.at[i]) for i, (a, b) in enumerate(kernels)]
    for load in kernel_loads:
        load.start()
    enter(n, me)

    pieces = shard_pieces(n, rows_dev)
    core, side, my_group = lax.rem(me, 2), lax.rem(me // 2, 2), me // 4
    sibling, other = me + 1 - 2 * core, me + 2 - 4 * side

    def collects(piece):
        nearer = jnp.where(my_group > piece.group, 0, 1)
        return side == jnp.where(my_group == piece.group, piece.side, nearer)

    def core_copy(i):
        piece = pieces[i]
        return remote(
            slots.at[2 * piece.chip + 1 - core, piece.rows],
            core_in.at[piece.chip, piece.rows],
            sem_cs.at[i], sem_cr.at[i], sibling,
        )

    def chip_copy(i):
        piece = pieces[i]
        return remote(
            slots.at[2 * piece.chip + core, piece.rows],
            chip_in.at[piece.chip, piece.rows],
            sem_zs.at[i], sem_zr.at[i], other,
        )

    def far_copy(i, sender):
        piece = pieces[i]
        return remote(
            slots.at[2 * piece.chip + core, piece.rows],
            far_in.at[sender, piece.rows],
            sem_gs.at[i], sem_gr.at[5 * sender + piece.order], 2 * piece.chip + core,
        )

    def of_stage(stage):
        return [i for i, piece in enumerate(pieces) if piece.stage == stage]

    def ship(stage):
        for i in of_stage(stage):
            piece = pieces[i]
            for s in (2 * piece.chip, 2 * piece.chip + 1):
                flat_slot(s, rows_dev, piece.row, piece.row + piece.count, grad_a, grad_b, slots.at[s])
            core_copy(i).start()

    def ship_on(stage):
        for i in of_stage(stage):
            piece = pieces[i]
            core_copy(i).wait()
            spot = 2 * piece.chip + core
            slots[spot, piece.rows, :] = slots[spot, piece.rows, :] + core_in[piece.chip, piece.rows, :]

            @pl.when(jnp.logical_not(collects(piece)))
            def _(i=i):
                chip_copy(i).start()

    def ship_far(i):
        piece = pieces[i]

        @pl.when(collects(piece))
        def _():
            chip_copy(i).wait_recv()
            spot = 2 * piece.chip + core
            slots[spot, piece.rows, :] = slots[spot, piece.rows, :] + chip_in[piece.chip, piece.rows, :]

        @pl.when(collects(piece) & (my_group != piece.group))
        def _():
            far_copy(i, my_group).start()

    def ship_end():
        for i, piece in enumerate(pieces):
            count = min(piece.count, rows_dev - piece.row)
            taken = pl.ds(piece.row, count)
            here = collects(piece)

            @pl.when(here & (my_group == piece.group))
            def _(i=i, piece=piece, taken=taken):
                gradient[taken, :] = slots[2 * piece.chip + core, taken, :]
                for k in range(1, n // 4):
                    sender = lax.rem(my_group + n // 4 - k, n // 4)
                    far_copy(i, sender).wait_recv()
                    gradient[taken, :] = gradient[taken, :] + far_in[sender, taken, :]

            @pl.when(here & (my_group != piece.group))
            def _(i=i):
                far_copy(i, my_group).wait_send()

            @pl.when(jnp.logical_not(here))
            def _(i=i):
                chip_copy(i).wait_send()

    late = of_stage(3)

    def ok(place):
        return place_ok(place, edge, split, row_count)

    def halo_copies(s, up_src, down_src, up_dst, down_dst, sem_send, sem_recv):
        up = remote(up_src, down_dst, sem_send.at[2 * s], sem_recv.at[2 * s], above)
        down = remote(down_src, up_dst, sem_send.at[2 * s + 1], sem_recv.at[2 * s + 1], below)
        return up, down

    def halo_start(copies):
        up, down = copies

        @pl.when(has_up)
        def _():
            up.start()

        @pl.when(has_down)
        def _():
            down.start()

    def halo_wait(copies):
        up, down = copies

        @pl.when(has_up)
        def _():
            up.wait_send()
            down.wait_recv()

        @pl.when(has_down)
        def _():
            down.wait_send()
            up.wait_recv()

    def thin(s):
        return halo_copies(
            s, send_up.at[s], send_down.at[s], from_up.at[s], from_down.at[s], sem_s, sem_r
        )

    def pick(condition, a, b):
        return jnp.where(condition, a, b)

    column = row_of((LANES, LANES))

    def shifted(value):
        left = jnp.where(column > 0, pltpu.roll(value, 1, axis=0), 0.0)
        right = jnp.where(column < LANES - 1, pltpu.roll(value, LANES - 1, axis=0), 0.0)
        return left.astype(BF16), value.astype(BF16), right.astype(BF16)

    def put(ref, pair, parity, value, part, parts):
        rows = pl.ds(pl.multiple_of(pair * LANES, LANES), LANES)
        width = 3 * parts * LANES
        for j, shift in enumerate(shifted(value)):
            lane = parity * width + (j * parts + part) * LANES
            ref[rows, lane : lane + LANES] = shift

    def edges(parts, up_halo, down_halo):
        rows = []
        for good, halo in (((top == 1) & has_up, up_halo), ((bottom == 1) & has_down, down_halo)):
            pieces = [shifted(pick(good, halo[:, p * LANES : (p + 1) * LANES].astype(F32), 0.0)) for p in range(parts)]
            rows.append(jnp.concatenate([pieces[p][j] for j in range(3) for p in range(parts)], axis=1))
        return rows

    def put_edges(ref, top_row, bottom_row):
        width = top_row.shape[1]
        ref[0:LANES, 0:width] = top_row
        rows = slice(16 * LANES, 17 * LANES)
        ref[rows, width : 2 * width] = pick(split == 1, ref[rows, width : 2 * width], bottom_row)
        rows = slice(17 * LANES, 18 * LANES)
        ref[rows, 0:width] = pick(split == 1, bottom_row, jnp.zeros_like(bottom_row))

    def add_edges(ref, at_top, at_bottom):
        width = at_top.shape[1]
        ref[0:LANES, 0:width] += at_top
        rows = slice(15 * LANES, 16 * LANES)
        ref[rows, width : 2 * width] += pick(split == 1, 0.0, at_bottom)
        rows = slice(16 * LANES, 17 * LANES)
        ref[rows, 0:width] += pick(split == 1, at_bottom, 0.0)

    up_f[...] = pre_in[0]
    down_f[...] = pick(split == 1, pre_in[row_count + 2], pre_in[row_count + 1])
    copies = halo_copies(0, up_f, down_f, from_up_f, from_down_f, sem_fs, sem_fr)
    halo_start(copies)
    for ref, wide in ((x_one, 768), (x_two, 768), (x_three, 768)):
        ref[0:LANES, 0:384] = jnp.zeros((LANES, 384), BF16)
        ref[18 * LANES : 20 * LANES, :] = jnp.zeros((2 * LANES, wide), BF16)
    spread_z(feature[...], z_columns(cells_row[...]), spread)
    bias_mid = stat[32:33, :]
    b_mid = jnp.concatenate([bias_mid[:, 32:96], bias_mid[:, 32:96]], axis=1)

    def activated(value, x_ref, q, e):
        value = pick(ok(2 * q + 1 + e), value * sigmoid(value), 0.0)
        put(x_ref, q + e, 1 - e, value, 0, 1)

    def mid_step(q, carry):
        rows = pl.ds(pl.multiple_of(q * LANES, LANES), LANES)
        for e in range(2):
            value = pre_in[2 * q + 1 + e] + b_mid
            pre_mid[rows, e * LANES : (e + 1) * LANES] = value
            activated(value, x_one, q, e)
        return carry

    lax.fori_loop(0, PAIRS, mid_step, 0)
    halo_wait(copies)
    at_top = pick((top == 1) & has_up, from_up_f[...], 0.0)
    at_bottom = pick((bottom == 1) & has_down, from_down_f[...], 0.0)
    add_edges(pre_mid, at_top, at_bottom)
    for q, e in ((0, 0), (15, 1), (16, 0)):
        activated(pre_mid[q * LANES : (q + 1) * LANES, e * LANES : (e + 1) * LANES], x_one, q, e)

    def activate(pre_ref, x_ref):
        def step(q, carry):
            rows = pl.ds(pl.multiple_of(q * LANES, LANES), LANES)
            for e in range(2):
                activated(pre_ref[rows, e * LANES : (e + 1) * LANES], x_ref, q, e)
            return carry

        lax.fori_loop(0, PAIRS, step, 0)

    def exchange(x_ref, s):
        send_up[s] = x_ref[0:LANES, 512:640]
        send_down[s] = pick(split == 1, x_ref[16 * LANES : 17 * LANES, 512:640], x_ref[16 * LANES : 17 * LANES, 128:256])
        halo_start(thin(s))

    def banded(x_ref, f_ref, bias, out_ref):
        def step(b, carry):
            start = pl.multiple_of(b * SPAN, LANES)
            total = nn(x_ref[pl.ds(start, SPAN), :], f_ref[0:768, :])
            total += nn(x_ref[pl.ds(start + LANES, SPAN), :], f_ref[768:1536, :])
            out_ref[pl.ds(start, SPAN), :] = total + bias
            return carry

        lax.fori_loop(0, STEPS, step, 0)

    def banded_back(g_ref, d_ref, out_ref):
        width = g_ref.shape[1]

        def step(b, carry):
            start = pl.multiple_of(b * SPAN, LANES)
            total = nt(g_ref[pl.ds(start, SPAN), :], d_ref[:, 0:width])
            total += nt(g_ref[pl.ds(start + LANES, SPAN), :], d_ref[:, width : 2 * width])
            out_ref[pl.ds(start, SPAN), :] = total
            return carry

        lax.fori_loop(0, STEPS, step, 0)

    def bias_row(first, lane):
        mixed = jnp.where(lane_of((1, LANES)) >= lane, stat[first : first + 1, :], stat[first + 1 : first + 2, :])
        return pltpu.roll(jnp.broadcast_to(mixed, (8, LANES)), LANES - lane, axis=1)[0:1, :]

    def twice(row):
        return jnp.concatenate([row, row], axis=1)

    def layer_forward(x_ref, f_ref, bias, out_ref, s):
        exchange(x_ref, s)
        banded(x_ref, f_ref, twice(bias), out_ref)
        halo_wait(thin(s))
        top_row, bottom_row = edges(1, from_up[s], from_down[s])
        put_edges(x_ref, top_row, bottom_row)
        add_edges(out_ref, nn(top_row, f_ref[0:384, 0:LANES]), nn(bottom_row, f_ref[768:1152, 0:LANES]))

    kernel_loads[0].wait()
    layer_forward(x_one, f_one, bias_row(33, 96), pre_one, 0)
    activate(pre_one, x_two)
    for load in kernel_loads[1:]:
        load.wait()
    layer_forward(x_two, f_two, bias_row(35, 96), pre_two, 1)
    activate(pre_two, x_three)

    def weight_grads(g_ref, x_ref, parts, write):
        width, wide = parts * LANES, 3 * parts * LANES
        middle0 = slice(width, 2 * width)
        middle1 = slice(wide + width, wide + 2 * width)
        acc0[0 : 2 * width, :] = jnp.zeros((2 * width, 768), F32)
        acc1[0:width, :] = jnp.zeros((width, 384), F32)
        acc2[0:width, :] = jnp.zeros((width, 384), F32)

        def step(b, carry):
            start = pl.multiple_of(b * SPAN, LANES)
            rows = pl.ds(start, SPAN)
            g0, g1 = g_ref[rows, middle0], g_ref[rows, middle1]
            both = jnp.concatenate([g0, g1], axis=1)
            acc0[0 : 2 * width, :] += tn(both, x_ref[rows, :])
            acc2[0:width, :] += tn(g1, x_ref[pl.ds(start + LANES, SPAN), 0:384])
            after = g_ref[pl.ds(start + LANES, SPAN), middle0]
            acc1[0:width, :] += tn(after, x_ref[rows, 384:768])
            return carry

        lax.fori_loop(0, STEPS, step, 0)
        for i in range(3):
            if i == 0:
                total = acc0[width : 2 * width, 0:384] + acc1[0:width, :]
            elif i == 1:
                total = acc0[0:width, 0:384] + acc0[width : 2 * width, 384:768]
            else:
                total = acc0[0:width, 384:768] + acc2[0:width, :]
            for j in range(3):
                for part in range(parts):
                    block = total[part * LANES : (part + 1) * LANES, j * LANES : (j + 1) * LANES]
                    write(i, j, part, jnp.transpose(block))

    def bias_grads(g_ref, parts):
        width, wide = parts * LANES, 3 * parts * LANES
        ones = jnp.ones((16, SPAN), BF16)

        def step(b, total):
            rows = pl.ds(pl.multiple_of(b * SPAN, LANES), SPAN)
            total += nn(ones, g_ref[rows, width : 2 * width])
            return total + nn(ones, g_ref[rows, wide + width : wide + 2 * width])

        return lax.fori_loop(0, STEPS, step, jnp.zeros((16, width), F32))[0:1, :]

    def last_layers(pre_three, x_head, g_three):
        bias = jnp.concatenate([bias_row(37, 96), bias_row(38, 96)], axis=1)

        def conv_step(b, carry):
            start = pl.multiple_of(b * SPAN, LANES)
            rows, more = pl.ds(start, SPAN), pl.ds(start + LANES, SPAN)
            total = nn(x_ref3[rows, :], f_three[0:768, :]) + nn(x_ref3[more, 0:384], f_three[768:1152, :])
            pre_three[rows, 0:256] = total + bias
            total = nn(x_ref3[rows, 384:768], f_three[0:384, :]) + nn(x_ref3[more, :], f_three[384:1152, :])
            pre_three[rows, 256:512] = total + bias
            return carry

        x_ref3 = x_three
        exchange(x_three, 2)
        lax.fori_loop(0, STEPS, conv_step, 0)
        halo_wait(thin(2))
        top_row, bottom_row = edges(1, from_up[2], from_down[2])
        put_edges(x_three, top_row, bottom_row)
        add_edges(pre_three, nn(top_row, f_three[0:384, :]), nn(bottom_row, f_three[768:1152, :]))

        def head_step(q, carry):
            rows = pl.ds(pl.multiple_of(q * LANES, LANES), LANES)
            value = pre_three[rows, :]
            x_head[rows, :] = (value * sigmoid(value)).astype(BF16)
            return carry

        lax.fori_loop(0, PAIRS, head_step, 0)
        for load in loads:
            load.wait()
        head_row = jnp.broadcast_to(stat[40:41, :], (LANES, LANES))
        b_head = jnp.sum(jnp.where(lane_of((16, LANES)) == row_of((16, LANES)) + 96, head_row[0:16, :], 0.0), axis=1, keepdims=True)
        divisor = jnp.maximum(stat[0:1, 3:4], 1.0)
        inverse = 1.0 / divisor
        row16 = row_of((16, LANES))

        def loss_tile(logits, place):
            row = place_row(place, edge, row_count)
            label = labels[row]
            kind = jnp.concatenate([label, jnp.zeros((14, LANES), jnp.int32)], axis=0)
            is_class = row16 < 2
            anchor0, anchor1 = label[0:1, :] == 1, label[1:2, :] == 1
            box_on = ((row16 < 9) & anchor0) | ((row16 >= 9) & anchor1)
            positive = (kind == 1).astype(F32)
            negative = (kind == 0).astype(F32)
            q = 1.0 / (1.0 + jnp.exp(-logits))
            rest = jnp.log(1.0 + jnp.exp(-jnp.abs(logits)))
            log_q = jnp.minimum(logits, 0.0) - rest
            log_not = jnp.minimum(-logits, 0.0) - rest
            short = 1.0 - q
            focal = -FOCAL_ALPHA * positive * short * short * log_q
            focal -= (1.0 - FOCAL_ALPHA) * negative * q * q * log_not
            slope_p = FOCAL_ALPHA * (2.0 * q * short * short * log_q - short * short * short)
            slope_n = (1.0 - FOCAL_ALPHA) * (q * q * q - 2.0 * q * q * short * log_not)
            residual = logits - boxes[row]
            size = jnp.abs(residual)
            huber = jnp.where(size < HUBER_BETA, (0.5 / HUBER_BETA) * residual * residual, size - 0.5 * HUBER_BETA)
            bent = jnp.clip(residual * (1.0 / HUBER_BETA), -1.0, 1.0)
            value = jnp.where(is_class, focal, jnp.where(box_on, 2.0 * huber, 0.0))
            grad = jnp.where(is_class, positive * slope_p + negative * slope_n, jnp.where(box_on, 2.0 * bent, 0.0))
            good = ok(place)
            return pick(good, value, 0.0), pick(good, grad * inverse, 0.0)

        def loss_step(q, total):
            rows = pl.ds(pl.multiple_of(q * LANES, LANES), LANES)
            for e in range(2):
                logits = nt(head_t[...], x_head[rows, e * 256 : (e + 1) * 256]) + b_head
                value, grad = loss_tile(logits, 2 * q + 1 + e)
                logit_grads[e, :, rows] = grad.astype(BF16)
                total = total + value
            return total

        total = lax.fori_loop(0, PAIRS, loss_step, jnp.zeros((16, LANES), F32), unroll=3)
        total = jnp.sum(jnp.sum(total, axis=1, keepdims=True), axis=0, keepdims=True)
        loss_mine[...] = jnp.broadcast_to(total, (8, LANES))
        for k in range(1, n):
            loss_copy(k).start()
        g_head = jnp.zeros((16, CR3), F32)
        g_bias = jnp.zeros((16, 1), F32)
        for e in range(2):
            g_head += nn(logit_grads[e], x_head[0:GRID, e * 256 : (e + 1) * 256])
            g_bias += jnp.sum(logit_grads[e].astype(F32), axis=1, keepdims=True)
        back_rows = jnp.where(same_eighth(), tn(g_head, fold16().astype(F32), HIGH), 0.0)
        grad_b[B_HEAD : B_HEAD + 32, :] = tn(eighths().astype(F32), back_rows, HIGH)
        spots = (lane_of((16, LANES)) == row_of((16, LANES))).astype(F32)
        grad_b[B_HEAD + 32 : B_HEAD + 33, :] = jnp.sum(spots * g_bias, axis=0, keepdims=True)

        def back_step(q, carry):
            rows = pl.ds(pl.multiple_of(q * LANES, LANES), LANES)
            for e in range(2):
                grad = tn(logit_grads[e, :, rows], head_t[...])
                grad = grad * slope(pre_three[rows, e * 256 : (e + 1) * 256])
                for part in range(2):
                    put(g_three, q + e, 1 - e, grad[:, part * LANES : (part + 1) * LANES], part, 2)
            return carry

        g_three[0:LANES, 0:768] = jnp.zeros((LANES, 768), BF16)
        g_three[18 * LANES : 20 * LANES, :] = jnp.zeros((2 * LANES, 1536), BF16)
        lax.fori_loop(0, PAIRS, back_step, 0)
        last_row = slice(16 * LANES, 17 * LANES)
        send_up_w[...] = g_three[0:LANES, 1024:1280]
        send_down_w[...] = pick(split == 1, g_three[last_row, 1024:1280], g_three[last_row, 256:512])
        copies = halo_copies(0, send_up_w, send_down_w, from_up_w, from_down_w, sem_ws, sem_wr)
        halo_start(copies)

        def write(i, j, part, block):
            start = B_THREE + 2 * (i * 3 + j) * LANES + part
            grad_b[pl.ds(start, LANES, 2), :] = block

        weight_grads(g_three, x_three, 2, write)
        sums = bias_grads(g_three, 2)
        grad_b[B_HEAD - 2 : B_HEAD - 1, :] = sums[:, 0:LANES]
        grad_b[B_HEAD - 1 : B_HEAD, :] = sums[:, LANES : 2 * LANES]
        ship(0)
        banded_back(g_three, d_three, back)
        ship_on(0)
        halo_wait(copies)
        add_back(d_three, *edges(2, from_up_w[...], from_down_w[...]))

    def add_back(d_ref, top_row, bottom_row):
        width = top_row.shape[1]
        add_edges(back, nt(top_row, d_ref[0:LANES, 0:width]), nt(bottom_row, d_ref[0:LANES, 2 * width : 3 * width]))

    def loss_copy(k):
        return remote(loss_mine, loss_all.at[me], sem_ls.at[k], sem_lr.at[me], lax.rem(me + k, n))

    pl.run_scoped(
        last_layers,
        pltpu.VMEM((GRID, 512), F32),
        pltpu.VMEM((GRID, 512), BF16),
        pltpu.VMEM((20 * LANES, 1536), BF16),
    )

    def lower_layers(g_ref, g_map, win0, win1, win2, gathered, d_two, d_one, w_mid):
        lower = ((d_two_h, d_two), (d_one_h, d_one), (w_mid_h, w_mid))
        lower_loads = [pltpu.make_async_copy(a, b, sem_k.at[5 + i]) for i, (a, b) in enumerate(lower)]
        for load in lower_loads:
            load.start()

        def grads_in(pre_ref):
            def step(q, carry):
                rows = pl.ds(pl.multiple_of(q * LANES, LANES), LANES)
                for e in range(2):
                    lanes = slice(e * LANES, (e + 1) * LANES)
                    value = back[rows, lanes] * slope(pre_ref[rows, lanes])
                    put(g_ref, q + e, 1 - e, pick(ok(2 * q + 1 + e), value, 0.0), 0, 1)
                return carry

            lax.fori_loop(0, PAIRS, step, 0)

        def weights_of(x_ref, begin):
            def write(i, j, part, block):
                start = begin + (i * 3 + j) * LANES
                grad_b[start : start + LANES, :] = block

            weight_grads(g_ref, x_ref, 1, write)
            grad_b[begin + 1152 : begin + 1153, :] = bias_grads(g_ref, 1)

        def from_edges(d_ref, s):
            halo_wait(thin(s))
            add_back(d_ref, *edges(1, from_up[s], from_down[s]))

        g_ref[0:LANES, 0:384] = jnp.zeros((LANES, 384), BF16)
        g_ref[18 * LANES : 20 * LANES, :] = jnp.zeros((2 * LANES, 768), BF16)
        grads_in(pre_two)
        exchange(g_ref, 3)
        weights_of(x_two, B_TWO)
        ship(1)
        for load in lower_loads:
            load.wait()
        banded_back(g_ref, d_two, back)
        from_edges(d_two, 3)
        ship_on(1)
        grads_in(pre_one)
        exchange(g_ref, 4)
        banded_back(g_ref, d_one, back)
        for i in of_stage(0):
            ship_far(i)
        from_edges(d_one, 4)

        g_map[...] = jnp.zeros_like(g_map)

        def to_map(q, total):
            rows = pl.ds(pl.multiple_of(q * LANES, LANES), LANES)
            for e in range(2):
                p = 2 * q + 1 + e
                lanes = slice(e * LANES, (e + 1) * LANES)
                value = back[rows, lanes] * slope(pre_mid[rows, lanes])
                value = pick(ok(p), value, 0.0).astype(BF16).astype(F32)
                g_map[pl.ds(pl.multiple_of(p * PITCH + 8, 8), LANES), :] = value
                total += jnp.sum(value, axis=0, keepdims=True)
            return total

        total = lax.fori_loop(0, PAIRS, to_map, jnp.zeros((1, LANES), F32))
        total = total[:, 0:CM] + total[:, CM : 2 * CM]
        grad_a[0:A_MID, :] = jnp.zeros((A_MID, LANES), F32)
        grad_a[A_MID + 1728 : A_ROWS, :] = jnp.zeros((A_ROWS - A_MID - 1728, LANES), F32)
        grad_a[A_MID + 1728 : A_MID + 1729, 0:CM] = total

        def map_row(place):
            return slice(place * PITCH + 8, place * PITCH + 8 + LANES)

        send_up[5] = g_map[map_row(1), :].astype(BF16)
        send_down[5] = pick(split == 1, g_map[map_row(row_count + 1), :], g_map[map_row(row_count), :]).astype(BF16)
        halo_start(thin(5))
        weights_of(x_one, B_ONE)
        ship(2)
        halo_wait(thin(5))
        g_map[map_row(0), :] = pick((top == 1) & has_up, from_up[5].astype(F32), 0.0)
        halo = pick((bottom == 1) & has_down, from_down[5].astype(F32), 0.0)
        g_map[map_row(row_count + 1), :] = pick(split == 1, g_map[map_row(row_count + 1), :], halo)
        g_map[map_row(row_count + 2), :] = pick(split == 1, halo, 0.0)

        wins = (win0, win1, win2)
        voxels = feature.shape[0]

        def fetch(v, carry):
            base = bases[0, v]
            for i in range(3):
                wins[i][pl.ds(4 * v, 3), :] = g_map[pl.ds(base + (2 - i) * PITCH, 3), :]
            return carry

        lax.fori_loop(0, voxels, fetch, 0, unroll=8)
        ship_on(2)
        for i in range(3):
            for j in range(3):
                lanes = slice((i * 3 + j) * LANES, (i * 3 + j + 1) * LANES)
                gathered[:, lanes] = wins[i][pl.ds(2 - j, voxels, 4), :].astype(BF16)
        low = lane_of((64, LANES)) < 64
        for i in range(3):
            block = tn(spread[...], gathered[:, i * 384 : (i + 1) * 384])
            for j in range(3):
                part = block[:, j * LANES : (j + 1) * LANES]
                even = [part[z * LANES : z * LANES + 64] for z in range(ZD)]
                odd = [part[z * LANES + 64 : (z + 1) * LANES] for z in range(ZD)]

                def flip(x):
                    return pltpu.roll(x, 64, axis=1)

                taps = (
                    jnp.where(low, flip(even[1]), odd[1]),
                    jnp.where(low, even[0] + flip(even[2]), flip(odd[0]) + odd[2]),
                    jnp.where(low, even[1] + flip(even[3]), flip(odd[1]) + odd[3]),
                )
                for t in range(3):
                    start = A_MID + (t * 9 + i * 3 + j) * 64
                    grad_a[start : start + 64, :] = taps[t]
        ship(3)
        for i in of_stage(1):
            ship_far(i)
        z_column = z_columns(cells_row[...])
        total = jnp.zeros((voxels, C2), F32)
        for z in range(ZD):
            total += jnp.where(z_column == z, nt(gathered[...], w_mid[z * C2 : (z + 1) * C2, :]), 0.0)
        grad_feature[...] = total

    voxels = feature.shape[0]
    pl.run_scoped(
        lower_layers,
        pltpu.VMEM((20 * LANES, 768), BF16),
        pltpu.VMEM(((row_count + 6) * PITCH, LANES), F32),
        pltpu.VMEM((voxels * 4, LANES), F32),
        pltpu.VMEM((voxels * 4, LANES), F32),
        pltpu.VMEM((voxels * 4, LANES), F32),
        pltpu.VMEM((voxels, 1152), BF16),
        pltpu.VMEM(d_two_h.shape, BF16),
        pltpu.VMEM(d_one_h.shape, BF16),
        pltpu.VMEM(w_mid_h.shape, BF16),
    )
    counts = counts_ref[...]
    slot_count = points_hbm.shape[1]
    columns, gamma, beta = first_layer(small)
    mean, scale, held = stat[0:32, 0:1], stat[0:32, 1:2], stat[0:32, 2:3]
    centre = stat[0:8, 4:5]
    order = even_first()
    rows_fc = voxel_rows(small)
    kernel = rows_fc[0:64, :].astype(BF16)
    kernel_t = (0.5 * nt(order.astype(BF16), kernel)).astype(BF16)
    kernel = nt(kernel, order.astype(BF16)).astype(BF16)
    bias = 0.5 * jnp.sum(jnp.where(order, rows_fc[64:65, :], 0.0), axis=1, keepdims=True)
    half_gamma, half_beta = 0.5 * gamma, 0.5 * beta


    def halves(value):
        high = value.astype(BF16)
        return high, (value - high.astype(F32)).astype(BF16)

    def note(ref, notes, sender, s, received):
        return remote(ref, notes.at[sender], sem_ns.at[s], received.at[sender], 0)

    def send_note(s):
        @pl.when(me > 0)
        def _():
            (note(mine_a, notes_a, me, 0, sem_nar) if s == 0 else note(mine_b, notes_b, me, 1, sem_nbr)).start()

    chunks = voxels // CHUNK

    def after(step):
        last = 3 * chunks - 1
        for place, i in enumerate(late):
            if min(place + 1, last) == step:
                ship_far(i)

    def voxel_layers(points, first, inner_grads, first_out):
        first_load = pltpu.make_async_copy(first_hbm, first_out, sem_p.at[7])
        first_load.start()
        points[...] = jnp.ones_like(points)
        point_loads = [
            pltpu.make_async_copy(points_hbm.at[k], points.at[:, k, :], sem_p.at[k]) for k in range(7)
        ]
        for load in point_loads:
            load.start()
        ship_on(3)
        first_load.wait()
        tail = jnp.where(row_of((16, CHUNK)) == 0, 1.0, 0.0).astype(BF16)
        fc = jnp.zeros((80, LANES), F32)
        pooled_grads = []
        for c in range(chunks):
            part = slice(c * CHUNK, (c + 1) * CHUNK)
            held_c = counts[:, part]
            counts_f = held_c.astype(F32)
            grad_pre = (0.5 * jnp.transpose(grad_feature[part, :])) / counts_f
            pooled_c = pooled_in[:, part]
            fixed = nn(kernel_t[:, 32:64], pooled_c) + bias

            def spot(p):
                return pl.ds(pl.multiple_of(p * CHUNK, LANES), CHUNK)

            def pass_e(p, carry, part=part, held_c=held_c, grad_pre=grad_pre, fixed=fixed):
                half_inner = nn(kernel_t[:, 0:32], first_out[p, :, part]) + fixed
                grad = jnp.where(p < held_c, grad_pre * half_slope(half_inner), 0.0)
                inner_grads[:, spot(p)] = grad.astype(BF16)
                return carry

            lax.fori_loop(0, slot_count, pass_e, 0, unroll=7)
            if c == 0:
                for i in of_stage(2):
                    ship_far(i)
            else:
                after(2 * c)

            def pass_g(p, carry, c=c, part=part, pooled_c=pooled_c):
                fc, pooled = carry
                grad = inner_grads[:, spot(p)]
                fc += nt(jnp.concatenate([first_out[p, :, part], pooled_c, tail], axis=0), grad)
                down = nn(kernel, grad)
                first[c, p] = down[0:32]
                return fc, pooled + down[32:64]

            fc, pooled = lax.fori_loop(0, slot_count, pass_g, (fc, jnp.zeros((32, CHUNK), F32)), unroll=5)
            pooled_grads.append(pooled / counts_f)
            after(2 * c + 1)
        mine_a[...] = fc[0:NOTE_A]
        send_note(0)
        for load in point_loads:
            load.wait()
        moments, g_gamma, centred = jnp.zeros((LANES, 16), F32), jnp.zeros((32, CHUNK), F32), jnp.zeros((8, CHUNK), F32)
        for c in range(chunks):
            part = slice(c * CHUNK, (c + 1) * CHUNK)
            wide = [jnp.broadcast_to(column, (32, CHUNK)) for column in columns]

            def pass_f(p, carry, c=c, part=part, held_c=counts[:, part], pooled=pooled_grads[c], wide=wide):
                moments, g_gamma, centred = carry
                inside = p < held_c
                value = wide[0] * points[p, 0:1, part]
                for k in range(1, 7):
                    value += wide[k] * points[p, k : k + 1, part]
                normed = jnp.where(inside, (value - mean) * scale, 0.0)
                slopes = half_slope(half_gamma * normed + half_beta)
                grad = jnp.where(inside, (0.5 * (first[c, p] + pooled)) * slopes, 0.0)
                off = points[p, :, part] - centre
                off_high, off_low = halves(off)
                grad_high, grad_low = halves(grad)
                norm_high, norm_low = halves(normed)
                left = jnp.concatenate([grad_high, grad_low, norm_high, norm_low], axis=0)
                right = jnp.concatenate([off_high, off_low], axis=0)
                return (
                    moments + nt(left, right),
                    g_gamma + grad * normed,
                    centred + jnp.where(inside, off, 0.0),
                )

            moments, g_gamma, centred = lax.fori_loop(0, slot_count, pass_f, (moments, g_gamma, centred), unroll=5)
            after(2 * chunks + c)
        by_grad = moments[0:32] + moments[32:64]
        by_norm = moments[64:96] + moments[96:128]
        mine_b[...] = jnp.zeros_like(mine_b)
        mine_b[0:32, 0:8] = by_grad[:, 0:8] + by_grad[:, 8:16]
        mine_b[0:32, 8:16] = by_norm[:, 0:8] + by_norm[:, 8:16]
        mine_b[0:32, 16:17] = jnp.sum(g_gamma, axis=1, keepdims=True)
        mine_b[32:40, 0:1] = jnp.sum(centred, axis=1, keepdims=True)
        send_note(1)

    pl.run_scoped(
        voxel_layers,
        pltpu.VMEM((slot_count, 8, voxels), F32),
        pltpu.VMEM((chunks, slot_count, 32, CHUNK), F32),
        pltpu.VMEM((LANES, slot_count * CHUNK), BF16),
        pltpu.VMEM(first_hbm.shape, BF16),
    )
    small_grad[...] = jnp.zeros_like(small_grad)

    @pl.when(me == 0)
    def _():
        notes_a[0] = mine_a[...]
        notes_b[0] = mine_b[...]
        for d in range(1, n):
            note(mine_a, notes_a, d, 0, sem_nar).wait_recv()
        fc_total = notes_a[0]
        for d in range(1, n):
            fc_total += notes_a[d]
        fc_rows[...] = jnp.zeros_like(fc_rows)
        fc_rows[8:80, :] = nn(fc_total, order.astype(F32), HIGH)
        here, before = fc_rows[8:80, :], fc_rows[7:79, :]
        mixed = jnp.where(lane_of((72, LANES)) >= LANES - FC_LANE, before, here)
        small_grad[2:74, :] = pltpu.roll(mixed, FC_LANE, axis=1)
        for d in range(1, n):
            note(mine_b, notes_b, d, 1, sem_nbr).wait_recv()
        total = notes_b[0]
        for d in range(1, n):
            total += notes_b[d]
        by_grad, by_norm = total[0:32, 0:8], total[0:32, 8:16]
        g_gamma, g_beta = total[0:32, 16:17], total[0:32, 7:8]
        off_sums = jnp.transpose(jnp.broadcast_to(total[32:40, 0:1], (8, LANES)))[0:32, 0:8]
        g_vfe = scale * gamma * (
            by_grad - g_beta / held * off_sums - g_gamma / held * by_norm
        )
        tall0 = jnp.concatenate([g_vfe[:, k : k + 1] for k in range(4)], axis=0)
        tall1 = jnp.concatenate([g_vfe[:, 4:5], g_vfe[:, 5:6], g_vfe[:, 6:7], g_gamma], axis=0)
        tall2 = jnp.concatenate([g_beta, jnp.zeros((96, 1), F32)], axis=0)
        lane = lane_of((LANES, LANES))
        tall = jnp.where(lane == 0, tall0, 0.0) + jnp.where(lane == 1, tall1, 0.0) + jnp.where(lane == 2, tall2, 0.0)
        head = jnp.transpose(tall)[0:8]
        small_grad[0:8, :] = small_grad[0:8, :] + head

    ship_end()
    gradient[0:SMALL, :] = gradient[0:SMALL, :] + small_grad[...]

    @pl.when(me > 0)
    def _():
        note(mine_a, notes_a, me, 0, sem_nar).wait_send()
        note(mine_b, notes_b, me, 1, sem_nbr).wait_send()

    for k in range(1, n):
        sender = lax.rem(me + n - k, n)
        remote(loss_mine, loss_all.at[sender], sem_ls.at[k], sem_lr.at[sender], sender).wait_recv()
    loss_all[me] = loss_mine[...]
    total = loss_all[0]
    for d in range(1, n):
        total += loss_all[d]
    loss_out[...] = total
    for k in range(1, n):
        loss_copy(k).wait_send()


def train(n, rows_dev, row_count, bases, cells, feature, stat, middle_out, labels, boxes, points, counts, small, pooled, first_out):
    shape = jax.ShapeDtypeStruct
    dma = pltpu.SemaphoreType.DMA
    voxels = feature.shape[0]
    row = (LANES, LANES)
    padded = ceil_to(rows_dev, 8)
    pieces = len(shard_pieces(n, rows_dev))
    fours = n // 4
    return pl.pallas_call(
        functools.partial(conv_kernel, n, rows_dev, row_count),
        name="train",
        out_shape=(
            shape((rows_dev, LANES), F32),
            shape((8, LANES), F32),
        ),
        in_specs=[smem()] + [vmem()] * 4 + [anywhere()] * 11 + [vmem()] * 3 + [anywhere()],
        out_specs=(vmem(),) * 2,
        scratch_shapes=[
            pltpu.VMEM((A_ROWS, LANES), F32),
            pltpu.VMEM((B_ROWS, LANES), F32),
            pltpu.VMEM((n, padded, LANES), F32),
            pltpu.VMEM((n // 2, padded, LANES), F32),
            pltpu.VMEM((n // 2, padded, LANES), F32),
            pltpu.VMEM((fours, padded, LANES), F32),
            pltpu.VMEM((voxels, LANES), F32),
            pltpu.VMEM((NOTE_A, LANES), F32),
            pltpu.VMEM((NOTE_B, LANES), F32),
            pltpu.VMEM((n, NOTE_A, LANES), F32),
            pltpu.VMEM((n, NOTE_B, LANES), F32),
            pltpu.VMEM((88, LANES), F32),
            pltpu.VMEM((SMALL, LANES), F32),
            *[pltpu.VMEM(middle_out[a].shape, BF16) for a in (2, 3, 4, 7, 8)],
            dma((8,)),
            pltpu.VMEM((20 * LANES, 768), BF16),
            pltpu.VMEM((20 * LANES, 768), BF16),
            pltpu.VMEM((20 * LANES, 768), BF16),
            pltpu.VMEM((GRID, 256), F32),
            pltpu.VMEM((GRID, 256), F32),
            pltpu.VMEM((GRID, 256), F32),
            pltpu.VMEM((GRID, 256), F32),
            pltpu.VMEM((voxels, ZD * C2), BF16),
            pltpu.VMEM((512, 768), F32),
            pltpu.VMEM((256, 384), F32),
            pltpu.VMEM((256, 384), F32),
            pltpu.VMEM((row_count, 2, LANES), jnp.int32),
            pltpu.VMEM((row_count, 16, LANES), F32),
            pltpu.VMEM((2, 16, GRID), BF16),
            pltpu.VMEM((8, LANES), F32),
            pltpu.VMEM((n, 8, LANES), F32),
            pltpu.VMEM(row, F32),
            pltpu.VMEM(row, F32),
            pltpu.VMEM(row, F32),
            pltpu.VMEM(row, F32),
            pltpu.VMEM((6,) + row, BF16),
            pltpu.VMEM((6,) + row, BF16),
            pltpu.VMEM((6,) + row, BF16),
            pltpu.VMEM((6,) + row, BF16),
            pltpu.VMEM((LANES, 256), BF16),
            pltpu.VMEM((LANES, 256), BF16),
            pltpu.VMEM((LANES, 256), BF16),
            pltpu.VMEM((LANES, 256), BF16),
            dma((16,)), dma((2,)), dma((2,)), dma((12,)), dma((12,)), dma((2,)), dma((2,)), dma((n,)), dma((n,)),
            dma((pieces,)), dma((pieces,)), dma((pieces,)), dma((pieces,)),
            dma((pieces,)), dma((5 * fours,)), dma((8,)), dma((2,)), dma((n,)), dma((n,)),
        ],
        compiler_params=pltpu.CompilerParams(
            collective_id=2, has_side_effects=True, vmem_limit_bytes=63 << 20
        ),
    )(bases, cells, feature, stat, *middle_out, labels, boxes, points, counts, small, pooled, first_out)


def adam_outer(gradient, weight, moment, second, momentum):
    moment = FIRST_DECAY * moment + (1.0 - FIRST_DECAY) * gradient
    second = SECOND_DECAY * second + (1.0 - SECOND_DECAY) * gradient * gradient
    moment_fix = moment / (1.0 - FIRST_DECAY**STEP)
    second_fix = second / (1.0 - SECOND_DECAY**STEP)
    inner_weight = weight - INNER_RATE * (
        moment_fix / (jnp.sqrt(second_fix) + ADAM_EPSILON) + WEIGHT_DECAY * weight
    )
    inner_step = weight - inner_weight
    momentum = OUTER_MOMENT * momentum + inner_step
    updated = weight - OUTER_RATE * (inner_step + OUTER_MOMENT * momentum)
    return (moment, second, momentum, updated)


def update_kernel(
    gradient, weight, moment, second, momentum, loss, stat,
    moment_out, second_out, momentum_out, weight_out, loss_out, positives_out,
    grad, held, outs, sem_in, sem_out,
):
    sources = (weight, moment, second, momentum)
    targets = (moment_out, second_out, momentum_out, weight_out)
    rows = grad.shape[0]
    steps = 4
    marks = [s * rows // steps // 8 * 8 for s in range(steps)] + [rows]
    loads, stores = [], []
    for s in range(steps):
        window = pl.ds(marks[s], marks[s + 1] - marks[s])
        loads.append([
            pltpu.make_async_copy(source.at[window], target.at[window], sem_in.at[5 * s + a])
            for a, (source, target) in enumerate(
                [(gradient, grad)] + [(source, held.at[a]) for a, source in enumerate(sources)]
            )
        ])
        for load in loads[-1]:
            load.start()
    loss_out[0] = loss[0, 0]
    positives_out[0] = stat[0, 3]
    for s in range(steps):
        part = slice(marks[s], marks[s + 1])
        window = pl.ds(marks[s], marks[s + 1] - marks[s])
        for load in loads[s]:
            load.wait()
        values = adam_outer(grad[part, :], held[0, part, :], held[1, part, :], held[2, part, :], held[3, part, :])
        for a, value in enumerate(values):
            outs[a, part, :] = value
            store = pltpu.make_async_copy(outs.at[a, window], targets[a].at[window], sem_out.at[4 * s + a])
            store.start()
            stores.append(store)
    for store in stores:
        store.wait()


def update(gradient, held, loss, stat):
    shape = jax.ShapeDtypeStruct
    rows = gradient.shape[0]
    dma = pltpu.SemaphoreType.DMA
    return pl.pallas_call(
        update_kernel,
        name="update",
        out_shape=(shape(gradient.shape, F32),) * 4 + (shape((1,), F32),) * 2,
        in_specs=[anywhere()] * 5 + [vmem()] * 2,
        out_specs=(anywhere(),) * 4 + (smem(),) * 2,
        scratch_shapes=[
            pltpu.VMEM((rows, LANES), F32),
            pltpu.VMEM((4, rows, LANES), F32),
            pltpu.VMEM((4, rows, LANES), F32),
            dma((20,)),
            dma((16,)),
        ],
        compiler_params=pltpu.CompilerParams(vmem_limit_bytes=60 << 20),
    )(gradient, *held, loss, stat)


def shards(
    points, point_counts, voxel_cells, anchor_labels, box_targets, weights, adam_m, adam_v, outer_momentum
):
    n = lax.axis_size("tile")
    rows = weights.shape[0] // LANES
    row_count = anchor_labels.shape[1]
    held = [x.reshape(rows, LANES) for x in (weights, adam_m, adam_v, outer_momentum)]
    counts = point_counts.reshape(1, -1)
    cells = voxel_cells.reshape(1, -1)
    wall, small, stat, first_out, pooled, feature, bases = front(
        n, points, counts, cells, anchor_labels, held[0]
    )
    ready = middle(n, rows, row_count, bases, cells, feature, wall)
    gradient, loss = train(
        n, rows, row_count, bases, cells, feature, stat, ready, anchor_labels, box_targets,
        points, counts, small, pooled, first_out,
    )
    *outs, loss_sum, positives = update(gradient, held, loss, stat)
    moment, second, momentum, updated = [x.reshape(weights.shape) for x in outs]
    return (moment, second, momentum, updated, loss_sum, positives)


def solution(mesh):
    split = ("group", "tile")
    in_specs = (
        P(None, None, split), P(split), P(split), P(None, split, None), P(None, split, None),
        P(split), P(split), P(split), P(split),
    )
    out_specs = (P(split), P(split), P(split), P(split), P("group"), P("group"))
    return jax.shard_map(shards, mesh=mesh, in_specs=in_specs, out_specs=out_specs, check_vma=False)
```

```python
import functools
import math

import jax
import jax.numpy as jnp
from jax import lax
from jax.experimental import pallas as pl
from jax.experimental.pallas import tpu as pltpu
from jax.sharding import PartitionSpec as P

MESH = pl.DeviceIdType.MESH
F32 = jnp.float32
BF16 = jnp.bfloat16
HIGH = lax.Precision.HIGHEST

C1, C2, CM, CR1, CR2, CR3, ANCH, ZD = 32, 128, 64, 128, 128, 256, 2, 4
H_SCENE = 200
STEP = 10
LANES = 128
NORM_EPSILON = 1e-05
INNER_RATE = 0.05
FIRST_DECAY = 0.9
SECOND_DECAY = 0.999
ADAM_EPSILON = 1e-08
WEIGHT_DECAY = 0.01
OUTER_RATE = 0.7
OUTER_MOMENT = 0.9
FOCAL_ALPHA = 0.25
HUBER_BETA = 1.0 / 9.0

SMALL = 80
FC_ROW, FC_LANE = 2, 32
BIAS_ROWS = (1795, 2947, 2948, 4100, 4101, 6405, 6406, 6407, 6439)
RUN_A = (2, 32)
RUN_B = (1795, 96)
A_MID = 65
B_ONE, B_TWO, B_THREE, B_HEAD = 0, 1153, 2306, 4612
PAIRS_OF = tuple((a, b) for a in range(7) for b in range(a, 7))
DIAGONAL = tuple(r for r, (a, b) in enumerate(PAIRS_OF) if a == b)
CHUNK = 256


def vmem():
    return pl.BlockSpec(memory_space=pltpu.VMEM)


def anywhere():
    return pl.BlockSpec(memory_space=pl.ANY)


def smem():
    return pl.BlockSpec(memory_space=pltpu.SMEM)


def ceil_to(value, step):
    return (value + step - 1) // step * step


def sigmoid(value):
    return 0.5 * jnp.tanh(0.5 * value) + 0.5


def slope(value):
    s = sigmoid(value)
    return s * (1.0 + value * (1.0 - s))


def half_silu(half):
    return half * (1.0 + jnp.tanh(half))


def half_slope(half):
    t = jnp.tanh(half)
    return (1.0 + t) * (1.0 + half * (1.0 - t))


def nt(a, b, precision=None):
    return lax.dot_general(a, b, (((1,), (1,)), ((), ())), precision=precision, preferred_element_type=F32)


def tn(a, b, precision=None):
    return lax.dot_general(a, b, (((0,), (0,)), ((), ())), precision=precision, preferred_element_type=F32)


def nn(a, b, precision=None):
    return lax.dot_general(a, b, (((1,), (0,)), ((), ())), precision=precision, preferred_element_type=F32)


def lane_of(shape):
    return lax.broadcasted_iota(jnp.int32, shape, len(shape) - 1)


def row_of(shape):
    return lax.broadcasted_iota(jnp.int32, shape, len(shape) - 2)


def enter(n, me, between=None):
    sem = pltpu.get_barrier_semaphore()

    def greet(k, carry):
        pl.semaphore_signal(
            sem, inc=1, device_id={"tile": lax.rem(me + k, n)}, device_id_type=MESH
        )
        return carry

    lax.fori_loop(1, n, greet, 0)
    if between is not None:
        between()
    pl.semaphore_wait(sem, n - 1)


def remote(src, dst, send, recv, peer):
    return pltpu.make_async_remote_copy(
        src_ref=src,
        dst_ref=dst,
        send_sem=send,
        recv_sem=recv,
        device_id={"tile": peer},
        device_id_type=MESH,
    )


def even_first():
    out = row_of((LANES, LANES))
    source = jnp.where(out < 64, 2 * out, 2 * out - 127)
    return lane_of((LANES, LANES)) == source


def first_layer(small_ref):
    turned = jnp.transpose(small_ref[0:LANES_PAD, :])
    columns = [turned[(k % 4) * 32 : (k % 4) * 32 + 32, k // 4 : k // 4 + 1] for k in range(7)]
    return columns, turned[96:128, 1:2], turned[0:32, 2:3]


LANES_PAD = 8


def voxel_rows(small_ref):
    here, after = small_ref[2:74, :], small_ref[3:75, :]
    mixed = jnp.where(lane_of((72, LANES)) >= FC_LANE, here, after)
    return pltpu.roll(mixed, LANES - FC_LANE, axis=1)


def layout(n, row_count):
    first = lax.axis_index("tile") * row_count
    ahead = (first // H_SCENE + 1) * H_SCENE - first
    split = jnp.where(ahead < row_count, 1, 0)
    edge = jnp.where(ahead < row_count, ahead, row_count)
    top = jnp.where(lax.rem(first, H_SCENE) != 0, 1, 0)
    last = first + row_count
    bottom = jnp.where((lax.rem(last, H_SCENE) != 0) & (last < n * row_count), 1, 0)
    return edge, split, top, bottom


def place_ok(place, edge, split, row_count):
    return (place >= 1) & (place <= row_count + split) & ((place != edge + 1) | (split == 0))


def place_row(place, edge, row_count):
    row = jnp.where(place <= edge, place - 1, place - 2)
    return jnp.clip(row, 0, row_count - 1)


PITCH = 136


def voxel_bases(cells, n, row_count, columns):
    edge, split, _, _ = layout(n, row_count)
    local = lax.rem(cells, row_count * columns * ZD)
    row = local // (columns * ZD)
    column = lax.rem(local, columns * ZD) // ZD
    place = row + 1 + jnp.where((row >= edge) & (split == 1), 1, 0)
    return (place - 1) * PITCH + column + 7


def linear_row(wide, points, p):
    value = wide[0] * points[0, pl.ds(p, 1), :]
    for k in range(1, 7):
        value += wide[k] * points[k, pl.ds(p, 1), :]
    return value


def local_moments(points, counts, labels_ref, sums, message):
    slots, voxels = points.shape[1:]
    inside = row_of((slots, voxels)) < counts

    def folded(value):
        total = value[:, 0:LANES]
        for c in range(1, voxels // LANES):
            total = total + value[:, c * LANES : (c + 1) * LANES]
        return jnp.sum(total, axis=0, keepdims=True)

    def whole(row):
        return jnp.sum(row, axis=1, keepdims=True)

    held = whole(folded(inside.astype(F32)))
    masked = [jnp.where(inside, points[k], 0.0) for k in range(7)]
    rows = [folded(value) for value in masked]
    means = [whole(row) / held for row in rows]
    centred = [jnp.where(inside, points[k] - means[k], 0.0) for k in range(7)]
    for r, (a, b) in enumerate(PAIRS_OF):
        sums[0, r : r + 1, :] = folded(centred[a] * centred[b])
        sums[1, r : r + 1, :] = rows[a]
        sums[2, r : r + 1, :] = rows[b]
    spare = len(PAIRS_OF)
    for c in range(3):
        sums[c, spare:LANES, :] = jnp.zeros((LANES - spare, LANES), F32)
    lane = lane_of((LANES, LANES))
    columns = jnp.zeros((LANES, LANES), F32)
    for c in range(3):
        columns = jnp.where(lane == c, jnp.sum(sums[c], axis=1, keepdims=True), columns)
    positives = jnp.zeros((1, 1), F32)
    for a in range(ANCH):
        positives += whole(jnp.sum((labels_ref[a] == 1).astype(F32), axis=0, keepdims=True))
    packed = jnp.transpose(columns)[0:8]
    row = row_of((8, LANES))
    packed = jnp.where(row == 3, held, packed)
    message[...] = jnp.where(row == 4, positives, packed)


def joint_moments(n, messages):
    total = messages[0]
    for d in range(1, n):
        total += messages[d]
    held = total[3:4]
    mean_a, mean_b = total[1:2] / held, total[2:3] / held
    product = total[0:1]
    for d in range(n):
        held_d = messages[d, 3:4, :]
        product += held_d * (messages[d, 1:2, :] / held_d - mean_a) * (messages[d, 2:3, :] / held_d - mean_b)
    return mean_a, product, held, total[4:5]


def channel_statistics(columns, mean_row, product, held):
    lane = lane_of((32, LANES))
    once, twice = jnp.zeros((32, LANES), F32), jnp.zeros((32, LANES), F32)
    for r, (a, b) in enumerate(PAIRS_OF):
        if a == b:
            once = jnp.where(lane == r, columns[a], once)
        twice = jnp.where(lane == r, (1.0 if a == b else 2.0) * columns[a] * columns[b], twice)
    mean = jnp.sum(once * mean_row, axis=1, keepdims=True)
    variance = jnp.sum(twice * (product / held), axis=1, keepdims=True)
    return mean, lax.rsqrt(variance + NORM_EPSILON)


def front_kernel(
    n, points, counts_ref, cells_ref, labels_ref, shard_ref,
    wall, small, stat, first_out, pooled_out, feature, bases,
    own, sums, mine, messages, my_bias, biases,
    sem_small_s, sem_small_r, sem_msg_s, sem_msg_r, sem_b_s, sem_b_r, sem_w_s, sem_w_r, sem_f_s, sem_e_s,
):
    me = lax.axis_index("tile")
    rows = shard_ref.shape[0]
    slots, voxels = points.shape[1:]
    sibling = me + 1 - 2 * lax.rem(me, 2)
    half = n // 2
    counts = counts_ref[...]

    def prepare():
        local_moments(points, counts, labels_ref, sums, mine)
        bases[...] = voxel_bases(cells_ref[...], n, labels_ref.shape[1], labels_ref.shape[2])
        own[...] = jnp.zeros_like(own)
        own[0:rows, :] = shard_ref[...].astype(BF16)
        for a, row in enumerate(BIAS_ROWS):
            owner, place = row // rows, row % rows
            my_bias[a : a + 1, :] = jnp.where(me == owner, shard_ref[place : place + 1, :], 0.0)
        for a in range(len(BIAS_ROWS), 16):
            my_bias[a : a + 1, :] = jnp.zeros((1, LANES), F32)

    enter(n, me, prepare)

    def message(k):
        return remote(mine, messages.at[me], sem_msg_s.at[k], sem_msg_r.at[me], lax.rem(me + k, n))

    def bias_message(k):
        return remote(my_bias, biases.at[me], sem_b_s.at[k], sem_b_r.at[me], lax.rem(me + k, n))

    def small_copy(k):
        return remote(small, small, sem_small_s.at[k], sem_small_r.at[0], lax.rem(me + k, n))

    def shard_copy(k):
        return remote(own, wall.at[me], sem_w_s.at[k], sem_w_r.at[me], lax.rem(me + 2 * k, n))

    for k in range(1, n):
        message(k).start()

    @pl.when(me == 0)
    def _():
        small[...] = shard_ref[0:SMALL, :]

        def send(k, carry):
            small_copy(k).start()
            return carry

        lax.fori_loop(1, n, send, 0)

    for k in range(1, n):
        bias_message(k).start()
    line = me // 2
    if n == 8:
        inner = (line == 1) | (line == 2)
        toward = jnp.where(line == 2, 2, -2)
        turn = jnp.where(line == 0, 2, -2)

        def own_copy(step, k):
            return remote(own, wall.at[me], sem_w_s.at[k], sem_w_r.at[me], me + step)

        @pl.when(inner)
        def _():
            own_copy(-toward, 1).start()
            own_copy(toward, 2).start()

        @pl.when(jnp.logical_not(inner))
        def _():
            own_copy(turn, 1).start()
            own_copy(2 * turn, 2).start()

    else:
        for k in range(1, half):
            shard_copy(k).start()

    def arrived(source):
        remote(own, wall.at[source], sem_w_s.at[0], sem_w_r.at[source], sibling).wait_recv()

    def pass_on(source, k, peer, sem):
        return remote(wall.at[source], wall.at[source], sem.at[k], sem_w_r.at[source], peer)

    def relay(step):
        if n == 8:

            @pl.when(inner)
            def _():
                source = me - (step + 1) * toward
                arrived(source)
                pass_on(source, step, me + toward, sem_e_s).start()
                pass_on(source, step + 1, sibling, sem_f_s).start()

    to_sibling = remote(own, wall.at[me], sem_w_s.at[0], sem_w_r.at[me], sibling)
    to_sibling.start()
    wall[me] = own[...]
    messages[me] = mine[...]
    biases[me] = my_bias[...]

    @pl.when(me > 0)
    def _():
        small_copy(0).wait_recv()

    columns, gamma, beta = first_layer(small)
    order = even_first()
    rows_fc = voxel_rows(small)
    kernel_t = (0.5 * nt(order.astype(BF16), rows_fc[0:64, :].astype(BF16))).astype(BF16)
    bias = 0.5 * jnp.sum(jnp.where(order, rows_fc[64:65, :], 0.0), axis=1, keepdims=True)
    for k in range(1, n):
        sender = lax.rem(me + n - k, n)
        remote(mine, messages.at[sender], sem_msg_s.at[k], sem_msg_r.at[sender], sender).wait_recv()
    mean_row, product, held, positives = joint_moments(n, messages)
    mean, inverse = channel_statistics(columns, mean_row, product, held)
    lane, row = lane_of((32, LANES)), row_of((32, LANES))
    columns_out = jnp.where(lane == 0, mean, 0.0)
    columns_out = jnp.where(lane == 1, inverse, columns_out)
    columns_out = jnp.where(lane == 2, held, columns_out)
    columns_out = jnp.where(lane == 3, positives, columns_out)
    for k, r in enumerate(DIAGONAL):
        columns_out = jnp.where((lane == 4) & (row == k), mean_row[:, r : r + 1], columns_out)
    stat[0:32, :] = columns_out

    half_gamma, half_beta = 0.5 * gamma, 0.5 * beta
    for c in range(voxels // CHUNK):
        part = slice(c * CHUNK, (c + 1) * CHUNK)
        wide = [jnp.broadcast_to(column, (32, CHUNK)) for column in columns]
        held_c = counts[:, part]
        view = points.at[:, :, part]

        def pass_c(p, pooled, wide=wide, held_c=held_c, view=view, part=part):
            half_act = half_gamma * ((linear_row(wide, view, p) - mean) * inverse) + half_beta
            out = jnp.where(p < held_c, half_silu(half_act), 0.0)
            first_out[p, :, part] = out.astype(BF16)
            return pooled + out

        pooled = lax.fori_loop(0, slots, pass_c, jnp.zeros((32, CHUNK), F32), unroll=5)
        pooled = (pooled / held_c.astype(F32)).astype(BF16)
        pooled_out[:, part] = pooled
        fixed = nn(kernel_t[:, 32:64], pooled) + bias
        if c < 2:
            relay(c)

        def pass_d(p, total, fixed=fixed, held_c=held_c, part=part):
            half_inner = nn(kernel_t[:, 0:32], first_out[p, :, part]) + fixed
            return total + jnp.where(p < held_c, half_silu(half_inner), 0.0)

        total = lax.fori_loop(0, slots, pass_d, jnp.zeros((LANES, CHUNK), F32), unroll=7)
        feature[part, :] = jnp.transpose(total / held_c.astype(F32))

    for step in range(voxels // CHUNK, 2):
        relay(step)
    if n == 8:

        @pl.when(inner)
        def _():
            source = me + toward
            arrived(source)
            pass_on(source, 3, sibling, sem_f_s).start()

        @pl.when(jnp.logical_not(inner))
        def _():
            for k in range(1, 4):
                arrived(me + k * turn)
                pass_on(me + k * turn, k, sibling, sem_f_s).start()

    else:
        for k in range(1, half):
            source = lax.rem(me + n - 2 * k, n)
            arrived(source)
            pass_on(source, k, sibling, sem_f_s).start()
    for k in range(1, n):
        sender = lax.rem(me + n - k, n)
        remote(my_bias, biases.at[sender], sem_b_s.at[k], sem_b_r.at[sender], sender).wait_recv()
    total = biases[0]
    for d in range(1, n):
        total += biases[d]
    stat[32:48, :] = total
    for k in range(half):
        arrived(lax.rem(sibling + n - 2 * k, n))
    for k in range(1, half):
        pass_on(me, k, sibling, sem_f_s).wait_send()
    if n == 8:
        for k in (1, 2):
            own_copy(turn, k).wait_send()

        @pl.when(inner)
        def _():
            for k in range(2):
                pass_on(me, k, sibling, sem_e_s).wait_send()

    else:
        for k in range(1, half):
            shard_copy(k).wait_send()
    to_sibling.wait_send()
    for k in range(1, n):
        message(k).wait_send()
        bias_message(k).wait_send()

    @pl.when(me == 0)
    def _():
        def done(k, carry):
            small_copy(k).wait_send()
            return carry

        lax.fori_loop(1, n, done, 0)


def front(n, points, counts, cells, labels, shard):
    slots, voxels = points.shape[1:]
    rows = shard.shape[0]
    padded = ceil_to(rows, 16)
    shape = jax.ShapeDtypeStruct
    dma = pltpu.SemaphoreType.DMA
    return pl.pallas_call(
        functools.partial(front_kernel, n),
        name="front",
        out_shape=(
            shape((n, padded, LANES), BF16),
            shape((SMALL, LANES), F32),
            shape((48, LANES), F32),
            shape((slots, 32, voxels), BF16),
            shape((32, voxels), BF16),
            shape((voxels, LANES), F32),
            shape((1, voxels), jnp.int32),
        ),
        in_specs=[vmem()] * 5,
        out_specs=(vmem(),) * 7,
        scratch_shapes=[
            pltpu.VMEM((padded, LANES), BF16),
            pltpu.VMEM((3, LANES, LANES), F32),
            pltpu.VMEM((8, LANES), F32),
            pltpu.VMEM((n, 8, LANES), F32),
            pltpu.VMEM((16, LANES), F32),
            pltpu.VMEM((n, 16, LANES), F32),
            dma((n,)), dma((1,)), dma((n,)), dma((n,)), dma((n,)), dma((n,)), dma((n,)), dma((n,)), dma((n,)), dma((2,)),
        ],
        compiler_params=pltpu.CompilerParams(
            collective_id=1, has_side_effects=True, vmem_limit_bytes=56 << 20
        ),
    )(points, counts, cells, labels, shard)


def flat_pieces(rows, slot):
    begin, end = slot * rows, (slot + 1) * rows
    spans = ((0, 67, None, 0), (67, 1795, "a", 2), (1795, 1796, "both", 0), (1796, 6440, "b", 1795), (6440, 1 << 30, None, 0))
    pieces = []
    for low, high, run, shift in spans:
        first, last = max(begin, low), min(end, high)
        if first < last:
            pieces.append((first - begin, last - first, run, first - shift))
    return pieces


def flat_slot(slot, rows, low, high, grad_a, grad_b, out_ref):
    def realigned(ref, start, count, lane):
        here, before = ref[pl.ds(start, count), :], ref[pl.ds(start - 1, count), :]
        mixed = jnp.where(lane_of((count, LANES)) >= LANES - lane, before, here)
        return pltpu.roll(mixed, lane, axis=1)

    for row, count, run, start in flat_pieces(rows, slot):
        first, last = max(row, low), min(row + count, high)
        if first >= last:
            continue
        start, row, count = start + first - row, first, last - first
        if run is None:
            value = jnp.zeros((count, LANES), F32)
        elif run == "a":
            value = realigned(grad_a, start, count, 32)
        elif run == "b":
            value = realigned(grad_b, start, count, 96)
        else:
            lane = lane_of((1, LANES))
            part_a = jnp.where(lane >= 96, grad_a[1792:1793, :], grad_a[1793:1794, :])
            part_b = jnp.where(lane >= 32, 0.0, grad_b[0:1, :])
            part_a = pltpu.roll(jnp.broadcast_to(part_a, (8, LANES)), 32, axis=1)
            part_b = pltpu.roll(jnp.broadcast_to(part_b, (8, LANES)), 96, axis=1)
            value = jnp.where(lane < 96, part_a[0:1], part_b[0:1])
        out_ref[row : row + count, :] = value


class Piece:
    def __init__(self, chip, row, count, stage, order):
        self.chip, self.group, self.side = chip, chip // 2, chip % 2
        self.row, self.count, self.stage, self.order = row, count, stage, order
        self.rows = pl.ds(row, count)


def shard_pieces(n, rows):
    padded = ceil_to(rows, 8)
    pieces = []
    for chip in range(n // 2):
        first = 2 * chip * rows
        cut = min(ceil_to(min(max(1796 - first, 0), rows), 8), padded)
        spans = [(0, cut)] if cut else []
        if cut >= 400:
            marks = [ceil_to(cut * k // 4, 8) for k in range(4)] + [cut]
            spans = list(zip(marks[:-1], marks[1:]))
        for order, (low, high) in enumerate(spans):
            pieces.append(Piece(chip, low, high - low, 3, order))
        if cut < padded:
            begin = first + cut
            stage = 0 if begin >= 4102 else 1 if begin >= 2949 else 2
            pieces.append(Piece(chip, cut, padded - cut, stage, 4))
    return pieces


def z_columns(cells_row):
    z = lax.rem(cells_row, ZD).astype(F32)
    return jnp.transpose(jnp.broadcast_to(z, (8, z.shape[1])))[:, 0:1]


def spread_z(feature, z_column, out_ref):
    for z in range(ZD):
        out_ref[:, z * C2 : (z + 1) * C2] = jnp.where(z_column == z, feature, 0.0).astype(BF16)


def middle_kernel(
    n, rows, row_count,
    bases, cells_row, feature, wall,
    pre, *refs,
):
    outs, kept, (flat, run, spread, parts0, parts1, parts2, sum0, sum1, sum2, sem) = refs[:8], refs[8:16], refs[16:]
    w_mid, f_one, f_two, f_three, d_one, d_two, d_three, head_t = kept
    stores = [pltpu.make_async_copy(kept[a], outs[a], sem.at[a]) for a in range(8)]
    voxels = feature.shape[0]
    columns = LANES
    parts, sums = (parts0, parts1, parts2), (sum0, sum1, sum2)
    for s in range(n):
        flat[s * rows : s * rows + wall.shape[1], :] = wall[s].astype(F32)

    def aligned(begin, start, count):
        row, lane = begin
        here = flat[pl.ds(row + start, count), :]
        after = flat[pl.ds(row + start + 1, count), :]
        mixed = jnp.where(lane_of((count, LANES)) >= lane, here, after)
        return pltpu.roll(mixed, LANES - lane, axis=1)

    def zero_half(ref, row, column, height, width):
        ref[row : row + height, column : column + width] = jnp.zeros((height, width), BF16)

    for begin, f_ref, d_ref in ((B_ONE, f_one, d_one), (B_TWO, f_two, d_two)):
        for j in range(3):
            for e in range(2):
                outside = 3 if e == 0 else 0
                zero_half(f_ref, outside * 384 + j * LANES, e * LANES, LANES, LANES)
                zero_half(d_ref, e * LANES, outside * 384 + j * LANES, LANES, LANES)

        def tap(i, j, begin=begin, f_ref=f_ref, d_ref=d_ref):
            block = aligned(RUN_B, begin + (i * 3 + j) * LANES, LANES).astype(BF16)
            for e in range(2):
                t = i + e
                f_ref[t * 384 + j * LANES : t * 384 + (j + 1) * LANES, e * LANES : (e + 1) * LANES] = block
                t = 2 + e - i
                lane = t * 384 + (2 - j) * LANES
                d_ref[e * LANES : (e + 1) * LANES, lane : lane + LANES] = block

        for i in range(3):
            for j in range(3):
                tap(i, j)
        for a in (1, 4) if begin == B_ONE else (2, 5):
            stores[a].start()
    for j in range(3):
        for e in range(2):
            outside = 3 if e == 0 else 0
            zero_half(d_three, e * LANES, outside * 768 + j * 256, LANES, 256)
    for i in range(3):
        for j in range(3):
            run[...] = aligned(RUN_B, B_THREE + (i * 3 + j) * 256, 256)
            for h in range(2):
                block = run[pl.ds(h, LANES, 2), :].astype(BF16)
                row = (i * 3 + j) * LANES
                f_three[row : row + LANES, h * LANES : (h + 1) * LANES] = block
                for e in range(2):
                    lane = (2 + e - i) * 768 + (2 - j) * 256 + h * LANES
                    d_three[e * LANES : (e + 1) * LANES, lane : lane + LANES] = block
    head_rows = aligned(RUN_B, B_HEAD, 32).astype(BF16)
    chosen = nn(eighths(), head_rows)
    chosen = jnp.where(same_eighth(), chosen, 0.0).astype(BF16)
    head_t[...] = nt(fold16(), chosen).astype(BF16)
    for a in (3, 6, 7):
        stores[a].start()

    low = lane_of((64, LANES)) < 64
    for ij in range(9):
        taps = [aligned(RUN_A, A_MID + (t * 9 + ij) * 64, 64) for t in range(3)]
        turned = [pltpu.roll(tap, 64, axis=1) for tap in taps]
        none = jnp.zeros((64, LANES), F32)
        for z in range(ZD):
            first, second = z + 1, z - 1
            a, a_t = (taps[first], turned[first]) if first < 3 else (none, none)
            b, b_t = (taps[second], turned[second]) if second >= 0 else (none, none)
            lanes = slice(ij * LANES, (ij + 1) * LANES)
            w_mid[z * C2 : z * C2 + 64, lanes] = jnp.where(low, a, b_t).astype(BF16)
            w_mid[z * C2 + 64 : (z + 1) * C2, lanes] = jnp.where(low, a_t, b).astype(BF16)

    stores[0].start()
    spread_z(feature[...], z_columns(cells_row[...]), spread)
    for i in range(3):
        product = nn(spread[...], w_mid[:, i * 384 : (i + 1) * 384])
        for j in range(3):
            parts[i][pl.ds(2 - j, voxels, 4), :] = product[:, j * LANES : (j + 1) * LANES]
        sums[i][...] = jnp.zeros_like(sums[i])

    def add(v, carry):
        base = bases[0, v]
        for i in range(3):
            spot = pl.ds(base + (2 - i) * PITCH, 3)
            sums[i][spot, :] = sums[i][spot, :] + parts[i][pl.ds(4 * v, 3), :]
        return carry

    lax.fori_loop(0, voxels, add, 0, unroll=8)

    def gather(p, carry):
        spot = pl.ds(pl.multiple_of(p * PITCH + 8, 8), columns)
        pre[p] = sum0[spot, :] + sum1[spot, :] + sum2[spot, :]
        return carry

    lax.fori_loop(0, row_count + 5, gather, 0)
    for store in stores:
        store.wait()


def eighths():
    return (row_of((CR3, 32)) // 8 == lane_of((CR3, 32))).astype(F32).astype(BF16)


def same_eighth():
    return lane_of((CR3, LANES)) // 16 == lax.rem(row_of((CR3, LANES)), 8)


def fold16():
    return (lax.rem(lane_of((16, LANES)), 16) == row_of((16, LANES))).astype(F32).astype(BF16)


def middle(n, rows, row_count, bases, cells, feature, wall):
    shape = jax.ShapeDtypeStruct
    voxels = feature.shape[0]
    cells_all = (row_count + 6) * PITCH
    return pl.pallas_call(
        functools.partial(middle_kernel, n, rows, row_count),
        name="middle",
        out_shape=(
            shape((row_count + 5, LANES, LANES), F32),
            shape((512, 1152), BF16),
            shape((1536, 256), BF16),
            shape((1536, 256), BF16),
            shape((1152, 256), BF16),
            shape((256, 1536), BF16),
            shape((256, 1536), BF16),
            shape((256, 3072), BF16),
            shape((16, 256), BF16),
        ),
        in_specs=[smem(), vmem(), vmem(), vmem()],
        out_specs=(vmem(),) + (anywhere(),) * 8,
        scratch_shapes=[
            pltpu.VMEM((512, 1152), BF16),
            pltpu.VMEM((1536, 256), BF16),
            pltpu.VMEM((1536, 256), BF16),
            pltpu.VMEM((1152, 256), BF16),
            pltpu.VMEM((256, 1536), BF16),
            pltpu.VMEM((256, 1536), BF16),
            pltpu.VMEM((256, 3072), BF16),
            pltpu.VMEM((16, 256), BF16),
            pltpu.VMEM((n * rows + 24, LANES), F32),
            pltpu.VMEM((256, LANES), F32),
            pltpu.VMEM((voxels, ZD * C2), BF16),
            pltpu.VMEM((voxels * 4, LANES), F32),
            pltpu.VMEM((voxels * 4, LANES), F32),
            pltpu.VMEM((voxels * 4, LANES), F32),
            pltpu.VMEM((cells_all, LANES), F32),
            pltpu.VMEM((cells_all, LANES), F32),
            pltpu.VMEM((cells_all, LANES), F32),
            pltpu.SemaphoreType.DMA((8,)),
        ],
        compiler_params=pltpu.CompilerParams(vmem_limit_bytes=56 << 20),
    )(bases, cells, feature, wall)


NOTE_A, NOTE_B = 72, 40
PAIRS = 18
QB = 9
STEPS = PAIRS // QB
SPAN = QB * LANES
GRID = PAIRS * LANES
A_ROWS, B_ROWS = 1800, 4656


def conv_kernel(
    n, rows_dev, row_count,
    bases, cells_row, feature, stat, pre_in,
    w_mid_h, f_one_h, f_two_h, f_three_h, d_one_h, d_two_h, d_three_h, head_t_h,
    labels_hbm, boxes_hbm, points_hbm, counts_ref, small, pooled_in, first_hbm,
    gradient, loss_out,
    grad_a, grad_b, slots, core_in, chip_in, far_in, grad_feature,
    mine_a, mine_b, notes_a, notes_b, fc_rows, small_grad,
    f_one, f_two, f_three, d_three, head_t, sem_k,
    x_one, x_two, x_three, pre_mid, pre_one, pre_two, back, spread,
    acc0, acc1, acc2,
    labels, boxes, logit_grads, loss_mine, loss_all,
    up_f, down_f, from_up_f, from_down_f, send_up, send_down, from_up, from_down,
    send_up_w, send_down_w, from_up_w, from_down_w,
    sem_t, sem_fs, sem_fr, sem_s, sem_r, sem_ws, sem_wr, sem_ls, sem_lr, sem_cs, sem_cr, sem_zs, sem_zr,
    sem_gs, sem_gr, sem_p, sem_ns, sem_nar, sem_nbr,
):
    me = lax.axis_index("tile")
    edge, split, top, bottom = layout(n, row_count)
    has_up, has_down = me > 0, me < n - 1
    above, below = jnp.maximum(me - 1, 0), jnp.minimum(me + 1, n - 1)
    loads = [pltpu.make_async_copy(labels_hbm.at[a], labels.at[:, a, :], sem_t.at[a]) for a in range(2)]
    loads += [
        pltpu.make_async_copy(boxes_hbm.at[a], boxes.at[:, 2 + a, :], sem_t.at[2 + a]) for a in range(14)
    ]
    for load in loads:
        load.start()
    kernels = (
        (f_one_h, f_one), (f_two_h, f_two), (f_three_h, f_three), (head_t_h, head_t),
        (d_three_h, d_three),
    )
    kernel_loads = [pltpu.make_async_copy(a, b, sem_k.at[i]) for i, (a, b) in enumerate(kernels)]
    for load in kernel_loads:
        load.start()
    enter(n, me)

    pieces = shard_pieces(n, rows_dev)
    core, side, my_group = lax.rem(me, 2), lax.rem(me // 2, 2), me // 4
    sibling, other = me + 1 - 2 * core, me + 2 - 4 * side

    def collects(piece):
        nearer = jnp.where(my_group > piece.group, 0, 1)
        return side == jnp.where(my_group == piece.group, piece.side, nearer)

    def core_copy(i):
        piece = pieces[i]
        return remote(
            slots.at[2 * piece.chip + 1 - core, piece.rows],
            core_in.at[piece.chip, piece.rows],
            sem_cs.at[i], sem_cr.at[i], sibling,
        )

    def chip_copy(i):
        piece = pieces[i]
        return remote(
            slots.at[2 * piece.chip + core, piece.rows],
            chip_in.at[piece.chip, piece.rows],
            sem_zs.at[i], sem_zr.at[i], other,
        )

    def far_copy(i, sender):
        piece = pieces[i]
        return remote(
            slots.at[2 * piece.chip + core, piece.rows],
            far_in.at[sender, piece.rows],
            sem_gs.at[i], sem_gr.at[5 * sender + piece.order], 2 * piece.chip + core,
        )

    def of_stage(stage):
        return [i for i, piece in enumerate(pieces) if piece.stage == stage]

    def ship(stage):
        for i in of_stage(stage):
            piece = pieces[i]
            for s in (2 * piece.chip, 2 * piece.chip + 1):
                flat_slot(s, rows_dev, piece.row, piece.row + piece.count, grad_a, grad_b, slots.at[s])
            core_copy(i).start()

    def ship_on(stage):
        for i in of_stage(stage):
            piece = pieces[i]
            core_copy(i).wait()
            spot = 2 * piece.chip + core
            slots[spot, piece.rows, :] = slots[spot, piece.rows, :] + core_in[piece.chip, piece.rows, :]

            @pl.when(jnp.logical_not(collects(piece)))
            def _(i=i):
                chip_copy(i).start()

    def ship_far(i):
        piece = pieces[i]

        @pl.when(collects(piece))
        def _():
            chip_copy(i).wait_recv()
            spot = 2 * piece.chip + core
            slots[spot, piece.rows, :] = slots[spot, piece.rows, :] + chip_in[piece.chip, piece.rows, :]

        @pl.when(collects(piece) & (my_group != piece.group))
        def _():
            far_copy(i, my_group).start()

    def ship_end():
        for i, piece in enumerate(pieces):
            count = min(piece.count, rows_dev - piece.row)
            taken = pl.ds(piece.row, count)
            here = collects(piece)

            @pl.when(here & (my_group == piece.group))
            def _(i=i, piece=piece, taken=taken):
                gradient[taken, :] = slots[2 * piece.chip + core, taken, :]
                for k in range(1, n // 4):
                    sender = lax.rem(my_group + n // 4 - k, n // 4)
                    far_copy(i, sender).wait_recv()
                    gradient[taken, :] = gradient[taken, :] + far_in[sender, taken, :]

            @pl.when(here & (my_group != piece.group))
            def _(i=i):
                far_copy(i, my_group).wait_send()

            @pl.when(jnp.logical_not(here))
            def _(i=i):
                chip_copy(i).wait_send()

    late = of_stage(3)

    def ok(place):
        return place_ok(place, edge, split, row_count)

    def halo_copies(s, up_src, down_src, up_dst, down_dst, sem_send, sem_recv):
        up = remote(up_src, down_dst, sem_send.at[2 * s], sem_recv.at[2 * s], above)
        down = remote(down_src, up_dst, sem_send.at[2 * s + 1], sem_recv.at[2 * s + 1], below)
        return up, down

    def halo_start(copies):
        up, down = copies

        @pl.when(has_up)
        def _():
            up.start()

        @pl.when(has_down)
        def _():
            down.start()

    def halo_wait(copies):
        up, down = copies

        @pl.when(has_up)
        def _():
            up.wait_send()
            down.wait_recv()

        @pl.when(has_down)
        def _():
            down.wait_send()
            up.wait_recv()

    def thin(s):
        return halo_copies(
            s, send_up.at[s], send_down.at[s], from_up.at[s], from_down.at[s], sem_s, sem_r
        )

    def pick(condition, a, b):
        return jnp.where(condition, a, b)

    column = row_of((LANES, LANES))

    def shifted(value):
        left = jnp.where(column > 0, pltpu.roll(value, 1, axis=0), 0.0)
        right = jnp.where(column < LANES - 1, pltpu.roll(value, LANES - 1, axis=0), 0.0)
        return left.astype(BF16), value.astype(BF16), right.astype(BF16)

    def put(ref, pair, parity, value, part, parts):
        rows = pl.ds(pl.multiple_of(pair * LANES, LANES), LANES)
        width = 3 * parts * LANES
        for j, shift in enumerate(shifted(value)):
            lane = parity * width + (j * parts + part) * LANES
            ref[rows, lane : lane + LANES] = shift

    def edges(parts, up_halo, down_halo):
        rows = []
        for good, halo in (((top == 1) & has_up, up_halo), ((bottom == 1) & has_down, down_halo)):
            pieces = [shifted(pick(good, halo[:, p * LANES : (p + 1) * LANES].astype(F32), 0.0)) for p in range(parts)]
            rows.append(jnp.concatenate([pieces[p][j] for j in range(3) for p in range(parts)], axis=1))
        return rows

    def put_edges(ref, top_row, bottom_row):
        width = top_row.shape[1]
        ref[0:LANES, 0:width] = top_row
        rows = slice(16 * LANES, 17 * LANES)
        ref[rows, width : 2 * width] = pick(split == 1, ref[rows, width : 2 * width], bottom_row)
        rows = slice(17 * LANES, 18 * LANES)
        ref[rows, 0:width] = pick(split == 1, bottom_row, jnp.zeros_like(bottom_row))

    def add_edges(ref, at_top, at_bottom):
        width = at_top.shape[1]
        ref[0:LANES, 0:width] += at_top
        rows = slice(15 * LANES, 16 * LANES)
        ref[rows, width : 2 * width] += pick(split == 1, 0.0, at_bottom)
        rows = slice(16 * LANES, 17 * LANES)
        ref[rows, 0:width] += pick(split == 1, at_bottom, 0.0)

    up_f[...] = pre_in[0]
    down_f[...] = pick(split == 1, pre_in[row_count + 2], pre_in[row_count + 1])
    copies = halo_copies(0, up_f, down_f, from_up_f, from_down_f, sem_fs, sem_fr)
    halo_start(copies)
    for ref, wide in ((x_one, 768), (x_two, 768), (x_three, 768)):
        ref[0:LANES, 0:384] = jnp.zeros((LANES, 384), BF16)
        ref[18 * LANES : 19 * LANES, :] = jnp.zeros((LANES, wide), BF16)
    spread_z(feature[...], z_columns(cells_row[...]), spread)
    bias_mid = stat[32:33, :]
    b_mid = jnp.concatenate([bias_mid[:, 32:96], bias_mid[:, 32:96]], axis=1)

    def activated(value, x_ref, q, e):
        value = pick(ok(2 * q + 1 + e), half_silu(0.5 * value), 0.0)
        put(x_ref, q + e, 1 - e, value, 0, 1)

    def mid_step(q, carry):
        rows = pl.ds(pl.multiple_of(q * LANES, LANES), LANES)
        for e in range(2):
            value = pre_in[2 * q + 1 + e] + b_mid
            pre_mid[rows, e * LANES : (e + 1) * LANES] = value
            activated(value, x_one, q, e)
        return carry

    lax.fori_loop(0, PAIRS, mid_step, 0)
    halo_wait(copies)
    at_top = pick((top == 1) & has_up, from_up_f[...], 0.0)
    at_bottom = pick((bottom == 1) & has_down, from_down_f[...], 0.0)
    add_edges(pre_mid, at_top, at_bottom)
    for q, e in ((0, 0), (15, 1), (16, 0)):
        activated(pre_mid[q * LANES : (q + 1) * LANES, e * LANES : (e + 1) * LANES], x_one, q, e)

    def exchange(x_ref, s):
        send_up[s] = x_ref[0:LANES, 512:640]
        send_down[s] = pick(split == 1, x_ref[16 * LANES : 17 * LANES, 512:640], x_ref[16 * LANES : 17 * LANES, 128:256])
        halo_start(thin(s))

    def banded_back(g_ref, d_ref, out_ref):
        width = g_ref.shape[1]

        def step(b, carry):
            start = pl.multiple_of(b * SPAN, LANES)
            total = nt(g_ref[pl.ds(start, SPAN), :], d_ref[:, 0:width])
            total += nt(g_ref[pl.ds(start + LANES, SPAN), :], d_ref[:, width : 2 * width])
            out_ref[pl.ds(start, SPAN), :] = total
            return carry

        lax.fori_loop(0, STEPS, step, 0)

    def bias_row(first, lane):
        mixed = jnp.where(lane_of((1, LANES)) >= lane, stat[first : first + 1, :], stat[first + 1 : first + 2, :])
        return pltpu.roll(jnp.broadcast_to(mixed, (8, LANES)), LANES - lane, axis=1)[0:1, :]

    def twice(row):
        return jnp.concatenate([row, row], axis=1)

    def layer_forward(x_ref, f_ref, bias, out_ref, s, x_next):
        exchange(x_ref, s)
        bias = twice(bias)

        def products(b):
            rows, more = pl.ds(b * SPAN, SPAN), pl.ds(b * SPAN + LANES, SPAN)
            total = nn(x_ref[rows, :], f_ref[0:768, :])
            total += nn(x_ref[more, :], f_ref[768:1536, :])
            out_ref[rows, :] = total + bias

        def piece(q, e):
            rows = pl.ds(q * LANES, LANES)
            activated(out_ref[rows, e * LANES : (e + 1) * LANES], x_next, q, e)

        products(0)
        products(1)
        for q in range(QB):
            for e in range(2):
                piece(q, e)

        def step(q, carry):
            rows = pl.ds(pl.multiple_of(q * LANES, LANES), LANES)
            for e in range(2):
                activated(out_ref[rows, e * LANES : (e + 1) * LANES], x_next, q, e)
            return carry

        lax.fori_loop(QB, PAIRS, step, 0)
        halo_wait(thin(s))
        top_row, bottom_row = edges(1, from_up[s], from_down[s])
        put_edges(x_ref, top_row, bottom_row)
        add_edges(out_ref, nn(top_row, f_ref[0:384, 0:LANES]), nn(bottom_row, f_ref[768:1152, 0:LANES]))
        for q, e in ((0, 0), (15, 1), (16, 0)):
            piece(q, e)

    kernel_loads[0].wait()
    layer_forward(x_one, f_one, bias_row(33, 96), pre_one, 0, x_two)
    for load in kernel_loads[1:]:
        load.wait()
    layer_forward(x_two, f_two, bias_row(35, 96), pre_two, 1, x_three)

    def weight_grads(g_ref, x_ref, parts, write):
        width, wide = parts * LANES, 3 * parts * LANES
        middle0 = slice(width, 2 * width)
        middle1 = slice(wide + width, wide + 2 * width)
        acc0[0 : 2 * width, :] = jnp.zeros((2 * width, 768), F32)
        acc1[0:width, :] = jnp.zeros((width, 384), F32)
        acc2[0:width, :] = jnp.zeros((width, 384), F32)

        def step(b, carry):
            start = pl.multiple_of(b * SPAN, LANES)
            rows = pl.ds(start, SPAN)
            g0, g1 = g_ref[rows, middle0], g_ref[rows, middle1]
            both = jnp.concatenate([g0, g1], axis=1)
            acc0[0 : 2 * width, :] += tn(both, x_ref[rows, :])
            acc2[0:width, :] += tn(g1, x_ref[pl.ds(start + LANES, SPAN), 0:384])
            after = g_ref[pl.ds(start + LANES, SPAN), middle0]
            acc1[0:width, :] += tn(after, x_ref[rows, 384:768])
            return carry

        lax.fori_loop(0, STEPS, step, 0)
        for i in range(3):
            if i == 0:
                total = acc0[width : 2 * width, 0:384] + acc1[0:width, :]
            elif i == 1:
                total = acc0[0:width, 0:384] + acc0[width : 2 * width, 384:768]
            else:
                total = acc0[0:width, 384:768] + acc2[0:width, :]
            for j in range(3):
                for part in range(parts):
                    block = total[part * LANES : (part + 1) * LANES, j * LANES : (j + 1) * LANES]
                    write(i, j, part, jnp.transpose(block))

    def bias_grads(g_ref, parts):
        width, wide = parts * LANES, 3 * parts * LANES
        ones = jnp.ones((16, SPAN), BF16)

        def step(b, total):
            rows = pl.ds(pl.multiple_of(b * SPAN, LANES), SPAN)
            total += nn(ones, g_ref[rows, width : 2 * width])
            return total + nn(ones, g_ref[rows, wide + width : wide + 2 * width])

        return lax.fori_loop(0, STEPS, step, jnp.zeros((16, width), F32))[0:1, :]

    def last_layers(pre_three, x_head, g_three):
        bias = jnp.concatenate([bias_row(37, 96), bias_row(38, 96)], axis=1)

        def products(b):
            rows, more = pl.ds(b * SPAN, SPAN), pl.ds(b * SPAN + LANES, SPAN)
            total = nn(x_three[rows, :], f_three[0:768, :]) + nn(x_three[more, 0:384], f_three[768:1152, :])
            pre_three[rows, 0:256] = total + bias
            total = nn(x_three[rows, 384:768], f_three[0:384, :]) + nn(x_three[more, :], f_three[384:1152, :])
            pre_three[rows, 256:512] = total + bias

        def head_rows(rows):
            x_head[rows, :] = half_silu(0.5 * pre_three[rows, :]).astype(BF16)

        def head_step(q, carry):
            head_rows(pl.ds(pl.multiple_of(q * LANES, LANES), LANES))
            return carry

        exchange(x_three, 2)
        products(0)
        products(1)
        for q in range(QB):
            head_rows(pl.ds(q * LANES, LANES))
        lax.fori_loop(QB, PAIRS, head_step, 0)
        halo_wait(thin(2))
        top_row, bottom_row = edges(1, from_up[2], from_down[2])
        put_edges(x_three, top_row, bottom_row)
        add_edges(pre_three, nn(top_row, f_three[0:384, :]), nn(bottom_row, f_three[768:1152, :]))
        for q in (0, 15, 16):
            head_rows(pl.ds(q * LANES, LANES))
        for load in loads:
            load.wait()
        head_row = jnp.broadcast_to(stat[40:41, :], (LANES, LANES))
        b_head = jnp.sum(jnp.where(lane_of((16, LANES)) == row_of((16, LANES)) + 96, head_row[0:16, :], 0.0), axis=1, keepdims=True)
        divisor = jnp.maximum(stat[0:1, 3:4], 1.0)
        inverse = 1.0 / divisor
        row16 = row_of((16, LANES))

        def loss_tile(logits, place):
            row = place_row(place, edge, row_count)
            label = labels[row]
            kind = jnp.concatenate([label, jnp.zeros((14, LANES), jnp.int32)], axis=0)
            is_class = row16 < 2
            anchor0, anchor1 = label[0:1, :] == 1, label[1:2, :] == 1
            box_on = ((row16 < 9) & anchor0) | ((row16 >= 9) & anchor1)
            positive = (kind == 1).astype(F32)
            negative = (kind == 0).astype(F32)
            q = 1.0 / (1.0 + jnp.exp(-logits))
            rest = jnp.log(1.0 + jnp.exp(-jnp.abs(logits)))
            log_q = jnp.minimum(logits, 0.0) - rest
            log_not = jnp.minimum(-logits, 0.0) - rest
            short = 1.0 - q
            focal = -FOCAL_ALPHA * positive * short * short * log_q
            focal -= (1.0 - FOCAL_ALPHA) * negative * q * q * log_not
            slope_p = FOCAL_ALPHA * (2.0 * q * short * short * log_q - short * short * short)
            slope_n = (1.0 - FOCAL_ALPHA) * (q * q * q - 2.0 * q * q * short * log_not)
            residual = logits - boxes[row]
            size = jnp.abs(residual)
            huber = jnp.where(size < HUBER_BETA, (0.5 / HUBER_BETA) * residual * residual, size - 0.5 * HUBER_BETA)
            bent = jnp.clip(residual * (1.0 / HUBER_BETA), -1.0, 1.0)
            value = jnp.where(is_class, focal, jnp.where(box_on, 2.0 * huber, 0.0))
            grad = jnp.where(is_class, positive * slope_p + negative * slope_n, jnp.where(box_on, 2.0 * bent, 0.0))
            good = ok(place)
            return pick(good, value, 0.0), pick(good, grad * inverse, 0.0)

        def loss_step(q, total):
            rows = pl.ds(pl.multiple_of(q * LANES, LANES), LANES)
            for e in range(2):
                logits = nt(head_t[...], x_head[rows, e * 256 : (e + 1) * 256]) + b_head
                value, grad = loss_tile(logits, 2 * q + 1 + e)
                logit_grads[e, :, rows] = grad.astype(BF16)
                total = total + value
            return total

        total = lax.fori_loop(0, PAIRS, loss_step, jnp.zeros((16, LANES), F32), unroll=3)
        total = jnp.sum(jnp.sum(total, axis=1, keepdims=True), axis=0, keepdims=True)
        loss_mine[...] = jnp.broadcast_to(total, (8, LANES))
        for k in range(1, n):
            loss_copy(k).start()
        g_head = jnp.zeros((16, CR3), F32)
        g_bias = jnp.zeros((16, 1), F32)
        for e in range(2):
            g_head += nn(logit_grads[e], x_head[0:GRID, e * 256 : (e + 1) * 256])
            g_bias += jnp.sum(logit_grads[e].astype(F32), axis=1, keepdims=True)
        back_rows = jnp.where(same_eighth(), tn(g_head, fold16().astype(F32), HIGH), 0.0)
        grad_b[B_HEAD : B_HEAD + 32, :] = tn(eighths().astype(F32), back_rows, HIGH)
        spots = (lane_of((16, LANES)) == row_of((16, LANES))).astype(F32)
        grad_b[B_HEAD + 32 : B_HEAD + 33, :] = jnp.sum(spots * g_bias, axis=0, keepdims=True)

        def back_step(q, carry):
            rows = pl.ds(pl.multiple_of(q * LANES, LANES), LANES)
            for e in range(2):
                grad = tn(logit_grads[e, :, rows], head_t[...])
                grad = grad * slope(pre_three[rows, e * 256 : (e + 1) * 256])
                for part in range(2):
                    put(g_three, q + e, 1 - e, grad[:, part * LANES : (part + 1) * LANES], part, 2)
            return carry

        g_three[0:LANES, 0:768] = jnp.zeros((LANES, 768), BF16)
        g_three[18 * LANES : 19 * LANES, :] = jnp.zeros((LANES, 1536), BF16)
        lax.fori_loop(0, PAIRS, back_step, 0)
        last_row = slice(16 * LANES, 17 * LANES)
        send_up_w[...] = g_three[0:LANES, 1024:1280]
        send_down_w[...] = pick(split == 1, g_three[last_row, 1024:1280], g_three[last_row, 256:512])
        copies = halo_copies(0, send_up_w, send_down_w, from_up_w, from_down_w, sem_ws, sem_wr)
        halo_start(copies)

        def write(i, j, part, block):
            start = B_THREE + 2 * (i * 3 + j) * LANES + part
            grad_b[pl.ds(start, LANES, 2), :] = block

        weight_grads(g_three, x_three, 2, write)
        sums = bias_grads(g_three, 2)
        grad_b[B_HEAD - 2 : B_HEAD - 1, :] = sums[:, 0:LANES]
        grad_b[B_HEAD - 1 : B_HEAD, :] = sums[:, LANES : 2 * LANES]
        ship(0)
        banded_back(g_three, d_three, back)
        ship_on(0)
        halo_wait(copies)
        add_back(d_three, *edges(2, from_up_w[...], from_down_w[...]))

    def add_back(d_ref, top_row, bottom_row):
        width = top_row.shape[1]
        add_edges(back, nt(top_row, d_ref[0:LANES, 0:width]), nt(bottom_row, d_ref[0:LANES, 2 * width : 3 * width]))

    def loss_copy(k):
        return remote(loss_mine, loss_all.at[me], sem_ls.at[k], sem_lr.at[me], lax.rem(me + k, n))

    pl.run_scoped(
        last_layers,
        pltpu.VMEM((GRID, 512), F32),
        pltpu.VMEM((GRID, 512), BF16),
        pltpu.VMEM((19 * LANES, 1536), BF16),
    )

    def lower_layers(g_ref, g_map, win0, win1, win2, gathered, d_two, d_one, w_mid):
        lower = ((d_two_h, d_two), (d_one_h, d_one), (w_mid_h, w_mid))
        lower_loads = [pltpu.make_async_copy(a, b, sem_k.at[5 + i]) for i, (a, b) in enumerate(lower)]
        for load in lower_loads:
            load.start()

        def piece_in(pre_ref, rows, q, e):
            lanes = slice(e * LANES, (e + 1) * LANES)
            value = (0.5 * back[rows, lanes]) * half_slope(0.5 * pre_ref[rows, lanes])
            put(g_ref, q + e, 1 - e, pick(ok(2 * q + 1 + e), value, 0.0), 0, 1)

        def all_pieces(first, take):
            def step(q, carry):
                rows = pl.ds(pl.multiple_of(q * LANES, LANES), LANES)
                for e in range(2):
                    take(rows, q, e)
                return carry

            lax.fori_loop(first, PAIRS, step, 0)

        def back_and_on(d_ref, s, take, between):
            for b in range(STEPS):
                total = nt(g_ref[b * SPAN : (b + 1) * SPAN, :], d_ref[:, 0:768])
                total += nt(g_ref[b * SPAN + LANES : (b + 1) * SPAN + LANES, :], d_ref[:, 768:1536])
                back[b * SPAN : (b + 1) * SPAN, :] = total
            for q in range(QB):
                for e in range(2):
                    take(pl.ds(q * LANES, LANES), q, e)
            all_pieces(QB, take)
            between()
            from_edges(d_ref, s)
            for q, e in ((0, 0), (15, 1), (16, 0)):
                take(pl.ds(q * LANES, LANES), q, e)

        def weights_of(x_ref, begin):
            def write(i, j, part, block):
                start = begin + (i * 3 + j) * LANES
                grad_b[start : start + LANES, :] = block

            weight_grads(g_ref, x_ref, 1, write)
            grad_b[begin + 1152 : begin + 1153, :] = bias_grads(g_ref, 1)

        def from_edges(d_ref, s):
            halo_wait(thin(s))
            add_back(d_ref, *edges(1, from_up[s], from_down[s]))

        g_ref[0:LANES, 0:384] = jnp.zeros((LANES, 384), BF16)
        g_ref[18 * LANES : 19 * LANES, :] = jnp.zeros((LANES, 768), BF16)
        all_pieces(0, functools.partial(piece_in, pre_two))
        exchange(g_ref, 3)
        weights_of(x_two, B_TWO)
        ship(1)
        for load in lower_loads:
            load.wait()
        back_and_on(d_two, 3, functools.partial(piece_in, pre_one), lambda: ship_on(1))
        exchange(g_ref, 4)

        g_map[...] = jnp.zeros_like(g_map)

        def piece_to_map(rows, q, e):
            p = 2 * q + 1 + e
            lanes = slice(e * LANES, (e + 1) * LANES)
            value = (0.5 * back[rows, lanes]) * half_slope(0.5 * pre_mid[rows, lanes])
            value = pick(ok(p), value, 0.0).astype(BF16).astype(F32)
            spot = p * PITCH + 8
            g_map[pl.ds(spot if isinstance(q, int) else pl.multiple_of(spot, 8), LANES), :] = value

        def far_zero():
            for i in of_stage(0):
                ship_far(i)

        back_and_on(d_one, 4, piece_to_map, far_zero)

        def map_sum(p, total):
            return total + g_map[pl.ds(pl.multiple_of(p * PITCH + 8, 8), LANES), :]

        total = lax.fori_loop(1, 2 * PAIRS + 1, map_sum, jnp.zeros((LANES, LANES), F32))
        total = jnp.sum(total, axis=0, keepdims=True)
        total = total[:, 0:CM] + total[:, CM : 2 * CM]
        grad_a[0:A_MID, :] = jnp.zeros((A_MID, LANES), F32)
        grad_a[A_MID + 1728 : A_ROWS, :] = jnp.zeros((A_ROWS - A_MID - 1728, LANES), F32)
        grad_a[A_MID + 1728 : A_MID + 1729, 0:CM] = total

        def map_row(place):
            return slice(place * PITCH + 8, place * PITCH + 8 + LANES)

        send_up[5] = g_map[map_row(1), :].astype(BF16)
        send_down[5] = pick(split == 1, g_map[map_row(row_count + 1), :], g_map[map_row(row_count), :]).astype(BF16)
        halo_start(thin(5))
        weights_of(x_one, B_ONE)
        ship(2)
        halo_wait(thin(5))
        g_map[map_row(0), :] = pick((top == 1) & has_up, from_up[5].astype(F32), 0.0)
        halo = pick((bottom == 1) & has_down, from_down[5].astype(F32), 0.0)
        g_map[map_row(row_count + 1), :] = pick(split == 1, g_map[map_row(row_count + 1), :], halo)
        g_map[map_row(row_count + 2), :] = pick(split == 1, halo, 0.0)

        wins = (win0, win1, win2)
        voxels = feature.shape[0]

        def fetch(v, carry):
            base = bases[0, v]
            for i in range(3):
                wins[i][pl.ds(4 * v, 3), :] = g_map[pl.ds(base + (2 - i) * PITCH, 3), :]
            return carry

        lax.fori_loop(0, voxels, fetch, 0, unroll=8)
        ship_on(2)
        for i in range(3):
            for j in range(3):
                lanes = slice((i * 3 + j) * LANES, (i * 3 + j + 1) * LANES)
                gathered[:, lanes] = wins[i][pl.ds(2 - j, voxels, 4), :].astype(BF16)
        low = lane_of((64, LANES)) < 64
        for i in range(3):
            block = tn(spread[...], gathered[:, i * 384 : (i + 1) * 384])
            for j in range(3):
                part = block[:, j * LANES : (j + 1) * LANES]
                even = [part[z * LANES : z * LANES + 64] for z in range(ZD)]
                odd = [part[z * LANES + 64 : (z + 1) * LANES] for z in range(ZD)]

                def flip(x):
                    return pltpu.roll(x, 64, axis=1)

                taps = (
                    jnp.where(low, flip(even[1]), odd[1]),
                    jnp.where(low, even[0] + flip(even[2]), flip(odd[0]) + odd[2]),
                    jnp.where(low, even[1] + flip(even[3]), flip(odd[1]) + odd[3]),
                )
                for t in range(3):
                    start = A_MID + (t * 9 + i * 3 + j) * 64
                    grad_a[start : start + 64, :] = taps[t]
        ship(3)
        for i in of_stage(1):
            ship_far(i)
        z_column = z_columns(cells_row[...])
        total = jnp.zeros((voxels, C2), F32)
        for z in range(ZD):
            total += jnp.where(z_column == z, nt(gathered[...], w_mid[z * C2 : (z + 1) * C2, :]), 0.0)
        grad_feature[...] = total

    voxels = feature.shape[0]
    pl.run_scoped(
        lower_layers,
        pltpu.VMEM((19 * LANES, 768), BF16),
        pltpu.VMEM(((row_count + 6) * PITCH, LANES), F32),
        pltpu.VMEM((voxels * 4, LANES), F32),
        pltpu.VMEM((voxels * 4, LANES), F32),
        pltpu.VMEM((voxels * 4, LANES), F32),
        pltpu.VMEM((voxels, 1152), BF16),
        pltpu.VMEM(d_two_h.shape, BF16),
        pltpu.VMEM(d_one_h.shape, BF16),
        pltpu.VMEM(w_mid_h.shape, BF16),
    )
    counts = counts_ref[...]
    slot_count = points_hbm.shape[1]
    columns, gamma, beta = first_layer(small)
    mean, scale, held = stat[0:32, 0:1], stat[0:32, 1:2], stat[0:32, 2:3]
    centre = stat[0:8, 4:5]
    order = even_first()
    rows_fc = voxel_rows(small)
    kernel = rows_fc[0:64, :].astype(BF16)
    kernel_t = (0.5 * nt(order.astype(BF16), kernel)).astype(BF16)
    kernel = nt(kernel, order.astype(BF16)).astype(BF16)
    bias = 0.5 * jnp.sum(jnp.where(order, rows_fc[64:65, :], 0.0), axis=1, keepdims=True)
    half_gamma, half_beta = 0.5 * gamma, 0.5 * beta


    def halves(value):
        high = value.astype(BF16)
        return high, (value - high.astype(F32)).astype(BF16)

    def note(s, sender, target):
        mine, notes, received = ((mine_a, notes_a, sem_nar), (mine_b, notes_b, sem_nbr))[s]
        spot = sender // 2
        return remote(mine, notes.at[spot], sem_ns.at[s], received.at[spot], target)

    def send_note(s):
        mine, notes = ((mine_a, notes_a), (mine_b, notes_b))[s]

        @pl.when(core == 1)
        def _():
            note(s, me, sibling).start()

        @pl.when(core == 0)
        def _():
            note(s, me + 1, sibling).wait_recv()
            mine[...] = mine[...] + notes[me // 2]

        @pl.when((core == 0) & (me > 0))
        def _():
            note(s, me, 0).start()

    chunks = voxels // CHUNK

    def after(step):
        last = 3 * chunks - 1
        for place, i in enumerate(late):
            if min(place + 1, last) == step:
                ship_far(i)

    def voxel_layers(points, first, inner_grads, first_out):
        first_load = pltpu.make_async_copy(first_hbm, first_out, sem_p.at[7])
        first_load.start()
        points[...] = jnp.ones_like(points)
        point_loads = [
            pltpu.make_async_copy(points_hbm.at[k], points.at[:, k, :], sem_p.at[k]) for k in range(7)
        ]
        for load in point_loads:
            load.start()
        ship_on(3)
        first_load.wait()
        tail = jnp.where(row_of((16, CHUNK)) == 0, 1.0, 0.0).astype(BF16)
        fc = jnp.zeros((80, LANES), F32)
        pooled_grads = []
        for c in range(chunks):
            part = slice(c * CHUNK, (c + 1) * CHUNK)
            held_c = counts[:, part]
            counts_f = held_c.astype(F32)
            grad_pre = (0.5 * jnp.transpose(grad_feature[part, :])) / counts_f
            pooled_c = pooled_in[:, part]
            fixed = nn(kernel_t[:, 32:64], pooled_c) + bias

            def spot(p):
                return pl.ds(pl.multiple_of(p * CHUNK, LANES), CHUNK)

            def pass_e(p, carry, part=part, held_c=held_c, grad_pre=grad_pre, fixed=fixed):
                half_inner = nn(kernel_t[:, 0:32], first_out[p, :, part]) + fixed
                grad = jnp.where(p < held_c, grad_pre * half_slope(half_inner), 0.0)
                inner_grads[:, spot(p)] = grad.astype(BF16)
                return carry

            lax.fori_loop(0, slot_count, pass_e, 0, unroll=7)
            if c == 0:
                for i in of_stage(2):
                    ship_far(i)
            else:
                after(2 * c)

            def pass_g(p, carry, c=c, part=part, pooled_c=pooled_c):
                fc, pooled = carry
                grad = inner_grads[:, spot(p)]
                fc += nt(jnp.concatenate([first_out[p, :, part], pooled_c, tail], axis=0), grad)
                down = nn(kernel, grad)
                first[c, p] = down[0:32]
                return fc, pooled + down[32:64]

            fc, pooled = lax.fori_loop(0, slot_count, pass_g, (fc, jnp.zeros((32, CHUNK), F32)), unroll=5)
            pooled_grads.append(pooled / counts_f)
            after(2 * c + 1)
        mine_a[...] = fc[0:NOTE_A]
        send_note(0)
        for load in point_loads:
            load.wait()
        moments, g_gamma, centred = jnp.zeros((LANES, 16), F32), jnp.zeros((32, CHUNK), F32), jnp.zeros((8, CHUNK), F32)
        for c in range(chunks):
            part = slice(c * CHUNK, (c + 1) * CHUNK)
            wide = [jnp.broadcast_to(column, (32, CHUNK)) for column in columns]

            def pass_f(p, carry, c=c, part=part, held_c=counts[:, part], pooled=pooled_grads[c], wide=wide):
                moments, g_gamma, centred = carry
                inside = p < held_c
                value = wide[0] * points[p, 0:1, part]
                for k in range(1, 7):
                    value += wide[k] * points[p, k : k + 1, part]
                normed = jnp.where(inside, (value - mean) * scale, 0.0)
                slopes = half_slope(half_gamma * normed + half_beta)
                grad = jnp.where(inside, (0.5 * (first[c, p] + pooled)) * slopes, 0.0)
                off = points[p, :, part] - centre
                off_high, off_low = halves(off)
                grad_high, grad_low = halves(grad)
                norm_high, norm_low = halves(normed)
                left = jnp.concatenate([grad_high, grad_low, norm_high, norm_low], axis=0)
                right = jnp.concatenate([off_high, off_low], axis=0)
                return (
                    moments + nt(left, right),
                    g_gamma + grad * normed,
                    centred + jnp.where(inside, off, 0.0),
                )

            moments, g_gamma, centred = lax.fori_loop(0, slot_count, pass_f, (moments, g_gamma, centred), unroll=5)
            after(2 * chunks + c)
        by_grad = moments[0:32] + moments[32:64]
        by_norm = moments[64:96] + moments[96:128]
        mine_b[...] = jnp.zeros_like(mine_b)
        mine_b[0:32, 0:8] = by_grad[:, 0:8] + by_grad[:, 8:16]
        mine_b[0:32, 8:16] = by_norm[:, 0:8] + by_norm[:, 8:16]
        mine_b[0:32, 16:17] = jnp.sum(g_gamma, axis=1, keepdims=True)
        mine_b[32:40, 0:1] = jnp.sum(centred, axis=1, keepdims=True)
        send_note(1)

    pl.run_scoped(
        voxel_layers,
        pltpu.VMEM((slot_count, 8, voxels), F32),
        pltpu.VMEM((chunks, slot_count, 32, CHUNK), F32),
        pltpu.VMEM((LANES, slot_count * CHUNK), BF16),
        pltpu.VMEM(first_hbm.shape, BF16),
    )
    small_grad[...] = jnp.zeros_like(small_grad)

    @pl.when(me == 0)
    def _():
        fc_total = mine_a[...]
        for d in range(2, n, 2):
            note(0, d, sibling).wait_recv()
            fc_total += notes_a[d // 2]
        fc_rows[...] = jnp.zeros_like(fc_rows)
        fc_rows[8:80, :] = nn(fc_total, order.astype(F32), HIGH)
        here, before = fc_rows[8:80, :], fc_rows[7:79, :]
        mixed = jnp.where(lane_of((72, LANES)) >= LANES - FC_LANE, before, here)
        small_grad[2:74, :] = pltpu.roll(mixed, FC_LANE, axis=1)
        total = mine_b[...]
        for d in range(2, n, 2):
            note(1, d, sibling).wait_recv()
            total += notes_b[d // 2]
        by_grad, by_norm = total[0:32, 0:8], total[0:32, 8:16]
        g_gamma, g_beta = total[0:32, 16:17], total[0:32, 7:8]
        off_sums = jnp.transpose(jnp.broadcast_to(total[32:40, 0:1], (8, LANES)))[0:32, 0:8]
        g_vfe = scale * gamma * (
            by_grad - g_beta / held * off_sums - g_gamma / held * by_norm
        )
        tall0 = jnp.concatenate([g_vfe[:, k : k + 1] for k in range(4)], axis=0)
        tall1 = jnp.concatenate([g_vfe[:, 4:5], g_vfe[:, 5:6], g_vfe[:, 6:7], g_gamma], axis=0)
        tall2 = jnp.concatenate([g_beta, jnp.zeros((96, 1), F32)], axis=0)
        lane = lane_of((LANES, LANES))
        tall = jnp.where(lane == 0, tall0, 0.0) + jnp.where(lane == 1, tall1, 0.0) + jnp.where(lane == 2, tall2, 0.0)
        head = jnp.transpose(tall)[0:8]
        small_grad[0:8, :] = small_grad[0:8, :] + head

    ship_end()
    gradient[0:SMALL, :] = gradient[0:SMALL, :] + small_grad[...]

    @pl.when(me > 0)
    def _():
        for s in range(2):
            note(s, me, sibling).wait_send()

    for k in range(1, n):
        sender = lax.rem(me + n - k, n)
        remote(loss_mine, loss_all.at[sender], sem_ls.at[k], sem_lr.at[sender], sender).wait_recv()
    loss_all[me] = loss_mine[...]
    total = loss_all[0]
    for d in range(1, n):
        total += loss_all[d]
    loss_out[...] = total
    for k in range(1, n):
        loss_copy(k).wait_send()


def train(n, rows_dev, row_count, bases, cells, feature, stat, middle_out, labels, boxes, points, counts, small, pooled, first_out):
    shape = jax.ShapeDtypeStruct
    dma = pltpu.SemaphoreType.DMA
    voxels = feature.shape[0]
    row = (LANES, LANES)
    padded = ceil_to(rows_dev, 8)
    pieces = len(shard_pieces(n, rows_dev))
    fours = n // 4
    return pl.pallas_call(
        functools.partial(conv_kernel, n, rows_dev, row_count),
        name="train",
        out_shape=(
            shape((rows_dev, LANES), F32),
            shape((8, LANES), F32),
        ),
        in_specs=[smem()] + [vmem()] * 4 + [anywhere()] * 11 + [vmem()] * 3 + [anywhere()],
        out_specs=(vmem(),) * 2,
        scratch_shapes=[
            pltpu.VMEM((A_ROWS, LANES), F32),
            pltpu.VMEM((B_ROWS, LANES), F32),
            pltpu.VMEM((n, padded, LANES), F32),
            pltpu.VMEM((n // 2, padded, LANES), F32),
            pltpu.VMEM((n // 2, padded, LANES), F32),
            pltpu.VMEM((fours, padded, LANES), F32),
            pltpu.VMEM((voxels, LANES), F32),
            pltpu.VMEM((NOTE_A, LANES), F32),
            pltpu.VMEM((NOTE_B, LANES), F32),
            pltpu.VMEM((n // 2, NOTE_A, LANES), F32),
            pltpu.VMEM((n // 2, NOTE_B, LANES), F32),
            pltpu.VMEM((88, LANES), F32),
            pltpu.VMEM((SMALL, LANES), F32),
            *[pltpu.VMEM(middle_out[a].shape, BF16) for a in (2, 3, 4, 7, 8)],
            dma((8,)),
            pltpu.VMEM((19 * LANES, 768), BF16),
            pltpu.VMEM((19 * LANES, 768), BF16),
            pltpu.VMEM((19 * LANES, 768), BF16),
            pltpu.VMEM((GRID, 256), F32),
            pltpu.VMEM((GRID, 256), F32),
            pltpu.VMEM((GRID, 256), F32),
            pltpu.VMEM((GRID, 256), F32),
            pltpu.VMEM((voxels, ZD * C2), BF16),
            pltpu.VMEM((512, 768), F32),
            pltpu.VMEM((256, 384), F32),
            pltpu.VMEM((256, 384), F32),
            pltpu.VMEM((row_count, 2, LANES), jnp.int32),
            pltpu.VMEM((row_count, 16, LANES), F32),
            pltpu.VMEM((2, 16, GRID), BF16),
            pltpu.VMEM((8, LANES), F32),
            pltpu.VMEM((n, 8, LANES), F32),
            pltpu.VMEM(row, F32),
            pltpu.VMEM(row, F32),
            pltpu.VMEM(row, F32),
            pltpu.VMEM(row, F32),
            pltpu.VMEM((6,) + row, BF16),
            pltpu.VMEM((6,) + row, BF16),
            pltpu.VMEM((6,) + row, BF16),
            pltpu.VMEM((6,) + row, BF16),
            pltpu.VMEM((LANES, 256), BF16),
            pltpu.VMEM((LANES, 256), BF16),
            pltpu.VMEM((LANES, 256), BF16),
            pltpu.VMEM((LANES, 256), BF16),
            dma((16,)), dma((2,)), dma((2,)), dma((12,)), dma((12,)), dma((2,)), dma((2,)), dma((n,)), dma((n,)),
            dma((pieces,)), dma((pieces,)), dma((pieces,)), dma((pieces,)),
            dma((pieces,)), dma((5 * fours,)), dma((8,)), dma((2,)), dma((n // 2,)), dma((n // 2,)),
        ],
        compiler_params=pltpu.CompilerParams(
            collective_id=2, has_side_effects=True, vmem_limit_bytes=63 << 20
        ),
    )(bases, cells, feature, stat, *middle_out, labels, boxes, points, counts, small, pooled, first_out)


def adam_outer(gradient, weight, moment, second, momentum):
    moment = FIRST_DECAY * moment + (1.0 - FIRST_DECAY) * gradient
    second = SECOND_DECAY * second + (1.0 - SECOND_DECAY) * gradient * gradient
    moment_fix = moment / (1.0 - FIRST_DECAY**STEP)
    second_fix = second / (1.0 - SECOND_DECAY**STEP)
    inner_weight = weight - INNER_RATE * (
        moment_fix / (jnp.sqrt(second_fix) + ADAM_EPSILON) + WEIGHT_DECAY * weight
    )
    inner_step = weight - inner_weight
    momentum = OUTER_MOMENT * momentum + inner_step
    updated = weight - OUTER_RATE * (inner_step + OUTER_MOMENT * momentum)
    return (moment, second, momentum, updated)


def update_kernel(
    gradient, weight, moment, second, momentum, loss, stat,
    moment_out, second_out, momentum_out, weight_out, loss_out, positives_out,
    grad, held, outs, sem_in, sem_out,
):
    sources = (weight, moment, second, momentum)
    targets = (moment_out, second_out, momentum_out, weight_out)
    rows = grad.shape[0]
    steps = 4
    marks = [s * rows // steps // 8 * 8 for s in range(steps)] + [rows]
    loads, stores = [], []
    for s in range(steps):
        window = pl.ds(marks[s], marks[s + 1] - marks[s])
        loads.append([
            pltpu.make_async_copy(source.at[window], target.at[window], sem_in.at[5 * s + a])
            for a, (source, target) in enumerate(
                [(gradient, grad)] + [(source, held.at[a]) for a, source in enumerate(sources)]
            )
        ])
        for load in loads[-1]:
            load.start()
    loss_out[0] = loss[0, 0]
    positives_out[0] = stat[0, 3]
    for s in range(steps):
        part = slice(marks[s], marks[s + 1])
        window = pl.ds(marks[s], marks[s + 1] - marks[s])
        for load in loads[s]:
            load.wait()
        values = adam_outer(grad[part, :], held[0, part, :], held[1, part, :], held[2, part, :], held[3, part, :])
        for a, value in enumerate(values):
            outs[a, part, :] = value
            store = pltpu.make_async_copy(outs.at[a, window], targets[a].at[window], sem_out.at[4 * s + a])
            store.start()
            stores.append(store)
    for store in stores:
        store.wait()


def update(gradient, held, loss, stat):
    shape = jax.ShapeDtypeStruct
    rows = gradient.shape[0]
    dma = pltpu.SemaphoreType.DMA
    return pl.pallas_call(
        update_kernel,
        name="update",
        out_shape=(shape(gradient.shape, F32),) * 4 + (shape((1,), F32),) * 2,
        in_specs=[anywhere()] * 5 + [vmem()] * 2,
        out_specs=(anywhere(),) * 4 + (smem(),) * 2,
        scratch_shapes=[
            pltpu.VMEM((rows, LANES), F32),
            pltpu.VMEM((4, rows, LANES), F32),
            pltpu.VMEM((4, rows, LANES), F32),
            dma((20,)),
            dma((16,)),
        ],
        compiler_params=pltpu.CompilerParams(vmem_limit_bytes=60 << 20),
    )(gradient, *held, loss, stat)


def shards(
    points, point_counts, voxel_cells, anchor_labels, box_targets, weights, adam_m, adam_v, outer_momentum
):
    n = lax.axis_size("tile")
    rows = weights.shape[0] // LANES
    row_count = anchor_labels.shape[1]
    held = [x.reshape(rows, LANES) for x in (weights, adam_m, adam_v, outer_momentum)]
    counts = point_counts.reshape(1, -1)
    cells = voxel_cells.reshape(1, -1)
    wall, small, stat, first_out, pooled, feature, bases = front(
        n, points, counts, cells, anchor_labels, held[0]
    )
    ready = middle(n, rows, row_count, bases, cells, feature, wall)
    gradient, loss = train(
        n, rows, row_count, bases, cells, feature, stat, ready, anchor_labels, box_targets,
        points, counts, small, pooled, first_out,
    )
    *outs, loss_sum, positives = update(gradient, held, loss, stat)
    moment, second, momentum, updated = [x.reshape(weights.shape) for x in outs]
    return (moment, second, momentum, updated, loss_sum, positives)


def solution(mesh):
    split = ("group", "tile")
    in_specs = (
        P(None, None, split), P(split), P(split), P(None, split, None), P(None, split, None),
        P(split), P(split), P(split), P(split),
    )
    out_specs = (P(split), P(split), P(split), P(split), P("group"), P("group"))
    return jax.shard_map(shards, mesh=mesh, in_specs=in_specs, out_specs=out_specs, check_vma=False)
```

```python
import functools
import math

import jax
import jax.numpy as jnp
from jax import lax
from jax.experimental import pallas as pl
from jax.experimental.pallas import tpu as pltpu
from jax.sharding import PartitionSpec as P

MESH = pl.DeviceIdType.MESH
F32 = jnp.float32
BF16 = jnp.bfloat16
HIGH = lax.Precision.HIGHEST

C1, C2, CM, CR1, CR2, CR3, ANCH, ZD = 32, 128, 64, 128, 128, 256, 2, 4
H_SCENE = 200
STEP = 10
LANES = 128
NORM_EPSILON = 1e-05
INNER_RATE = 0.05
FIRST_DECAY = 0.9
SECOND_DECAY = 0.999
ADAM_EPSILON = 1e-08
WEIGHT_DECAY = 0.01
OUTER_RATE = 0.7
OUTER_MOMENT = 0.9
FOCAL_ALPHA = 0.25
HUBER_BETA = 1.0 / 9.0

SMALL = 80
FC_ROW, FC_LANE = 2, 32
BIAS_ROWS = (1795, 2947, 2948, 4100, 4101, 6405, 6406, 6407, 6439)
RUN_A = (2, 32)
RUN_B = (1795, 96)
A_MID = 65
B_ONE, B_TWO, B_THREE, B_HEAD = 0, 1153, 2306, 4612
PAIRS_OF = tuple((a, b) for a in range(7) for b in range(a, 7))
DIAGONAL = tuple(r for r, (a, b) in enumerate(PAIRS_OF) if a == b)
CHUNK = 256


def vmem():
    return pl.BlockSpec(memory_space=pltpu.VMEM)


def anywhere():
    return pl.BlockSpec(memory_space=pl.ANY)


def smem():
    return pl.BlockSpec(memory_space=pltpu.SMEM)


def ceil_to(value, step):
    return (value + step - 1) // step * step


def sigmoid(value):
    return 0.5 * jnp.tanh(0.5 * value) + 0.5


def slope(value):
    s = sigmoid(value)
    return s * (1.0 + value * (1.0 - s))


def half_silu(half):
    return half * (1.0 + jnp.tanh(half))


def half_slope(half):
    t = jnp.tanh(half)
    return (1.0 + t) * (1.0 + half * (1.0 - t))


def nt(a, b, precision=None):
    return lax.dot_general(a, b, (((1,), (1,)), ((), ())), precision=precision, preferred_element_type=F32)


def tn(a, b, precision=None):
    return lax.dot_general(a, b, (((0,), (0,)), ((), ())), precision=precision, preferred_element_type=F32)


def nn(a, b, precision=None):
    return lax.dot_general(a, b, (((1,), (0,)), ((), ())), precision=precision, preferred_element_type=F32)


def lane_of(shape):
    return lax.broadcasted_iota(jnp.int32, shape, len(shape) - 1)


def row_of(shape):
    return lax.broadcasted_iota(jnp.int32, shape, len(shape) - 2)


def enter(n, me, between=None):
    sem = pltpu.get_barrier_semaphore()

    def greet(k, carry):
        pl.semaphore_signal(
            sem, inc=1, device_id={"tile": lax.rem(me + k, n)}, device_id_type=MESH
        )
        return carry

    lax.fori_loop(1, n, greet, 0)
    if between is not None:
        between()
    pl.semaphore_wait(sem, n - 1)


def remote(src, dst, send, recv, peer):
    return pltpu.make_async_remote_copy(
        src_ref=src,
        dst_ref=dst,
        send_sem=send,
        recv_sem=recv,
        device_id={"tile": peer},
        device_id_type=MESH,
    )


def even_first():
    out = row_of((LANES, LANES))
    source = jnp.where(out < 64, 2 * out, 2 * out - 127)
    return lane_of((LANES, LANES)) == source


def first_layer(small_ref):
    turned = jnp.transpose(small_ref[0:LANES_PAD, :])
    columns = [turned[(k % 4) * 32 : (k % 4) * 32 + 32, k // 4 : k // 4 + 1] for k in range(7)]
    return columns, turned[96:128, 1:2], turned[0:32, 2:3]


LANES_PAD = 8


def voxel_rows(small_ref):
    here, after = small_ref[2:74, :], small_ref[3:75, :]
    mixed = jnp.where(lane_of((72, LANES)) >= FC_LANE, here, after)
    return pltpu.roll(mixed, LANES - FC_LANE, axis=1)


def layout(n, row_count):
    first = lax.axis_index("tile") * row_count
    ahead = (first // H_SCENE + 1) * H_SCENE - first
    split = jnp.where(ahead < row_count, 1, 0)
    edge = jnp.where(ahead < row_count, ahead, row_count)
    top = jnp.where(lax.rem(first, H_SCENE) != 0, 1, 0)
    last = first + row_count
    bottom = jnp.where((lax.rem(last, H_SCENE) != 0) & (last < n * row_count), 1, 0)
    return edge, split, top, bottom


def place_ok(place, edge, split, row_count):
    return (place >= 1) & (place <= row_count + split) & ((place != edge + 1) | (split == 0))


def place_row(place, edge, row_count):
    row = jnp.where(place <= edge, place - 1, place - 2)
    return jnp.clip(row, 0, row_count - 1)


PITCH = 136


def voxel_bases(cells, n, row_count, columns):
    edge, split, _, _ = layout(n, row_count)
    local = lax.rem(cells, row_count * columns * ZD)
    row = local // (columns * ZD)
    column = lax.rem(local, columns * ZD) // ZD
    place = row + 1 + jnp.where((row >= edge) & (split == 1), 1, 0)
    return (place - 1) * PITCH + column + 7


def linear_row(wide, points, p):
    value = wide[0] * points[0, pl.ds(p, 1), :]
    for k in range(1, 7):
        value += wide[k] * points[k, pl.ds(p, 1), :]
    return value


def local_moments(points, counts, labels_ref, sums, message):
    slots, voxels = points.shape[1:]
    inside = row_of((slots, voxels)) < counts

    def folded(value):
        total = value[:, 0:LANES]
        for c in range(1, voxels // LANES):
            total = total + value[:, c * LANES : (c + 1) * LANES]
        return jnp.sum(total, axis=0, keepdims=True)

    def whole(row):
        return jnp.sum(row, axis=1, keepdims=True)

    held = whole(folded(inside.astype(F32)))
    masked = [jnp.where(inside, points[k], 0.0) for k in range(7)]
    rows = [folded(value) for value in masked]
    means = [whole(row) / held for row in rows]
    centred = [jnp.where(inside, points[k] - means[k], 0.0) for k in range(7)]
    for r, (a, b) in enumerate(PAIRS_OF):
        sums[0, r : r + 1, :] = folded(centred[a] * centred[b])
        sums[1, r : r + 1, :] = rows[a]
        sums[2, r : r + 1, :] = rows[b]
    spare = len(PAIRS_OF)
    for c in range(3):
        sums[c, spare:LANES, :] = jnp.zeros((LANES - spare, LANES), F32)
    lane = lane_of((LANES, LANES))
    columns = jnp.zeros((LANES, LANES), F32)
    for c in range(3):
        columns = jnp.where(lane == c, jnp.sum(sums[c], axis=1, keepdims=True), columns)
    positives = jnp.zeros((1, 1), F32)
    for a in range(ANCH):
        positives += whole(jnp.sum((labels_ref[a] == 1).astype(F32), axis=0, keepdims=True))
    packed = jnp.transpose(columns)[0:8]
    row = row_of((8, LANES))
    packed = jnp.where(row == 3, held, packed)
    message[...] = jnp.where(row == 4, positives, packed)


def joint_moments(n, messages):
    total = messages[0]
    for d in range(1, n):
        total += messages[d]
    held = total[3:4]
    mean_a, mean_b = total[1:2] / held, total[2:3] / held
    product = total[0:1]
    for d in range(n):
        held_d = messages[d, 3:4, :]
        product += held_d * (messages[d, 1:2, :] / held_d - mean_a) * (messages[d, 2:3, :] / held_d - mean_b)
    return mean_a, product, held, total[4:5]


def channel_statistics(columns, mean_row, product, held):
    lane = lane_of((32, LANES))
    once, twice = jnp.zeros((32, LANES), F32), jnp.zeros((32, LANES), F32)
    for r, (a, b) in enumerate(PAIRS_OF):
        if a == b:
            once = jnp.where(lane == r, columns[a], once)
        twice = jnp.where(lane == r, (1.0 if a == b else 2.0) * columns[a] * columns[b], twice)
    mean = jnp.sum(once * mean_row, axis=1, keepdims=True)
    variance = jnp.sum(twice * (product / held), axis=1, keepdims=True)
    return mean, lax.rsqrt(variance + NORM_EPSILON)


def front_kernel(
    n, points, counts_ref, cells_ref, labels_ref, shard_ref,
    wall, small, stat, first_out, pooled_out, feature, bases,
    own, sums, mine, messages, my_bias, biases,
    sem_small_s, sem_small_r, sem_msg_s, sem_msg_r, sem_b_s, sem_b_r, sem_w_s, sem_w_r, sem_f_s, sem_e_s,
):
    me = lax.axis_index("tile")
    rows = shard_ref.shape[0]
    slots, voxels = points.shape[1:]
    sibling = me + 1 - 2 * lax.rem(me, 2)
    half = n // 2
    counts = counts_ref[...]

    def prepare():
        local_moments(points, counts, labels_ref, sums, mine)
        bases[...] = voxel_bases(cells_ref[...], n, labels_ref.shape[1], labels_ref.shape[2])
        own[...] = jnp.zeros_like(own)
        own[0:rows, :] = shard_ref[...].astype(BF16)
        for a, row in enumerate(BIAS_ROWS):
            owner, place = row // rows, row % rows
            my_bias[a : a + 1, :] = jnp.where(me == owner, shard_ref[place : place + 1, :], 0.0)
        for a in range(len(BIAS_ROWS), 16):
            my_bias[a : a + 1, :] = jnp.zeros((1, LANES), F32)

    enter(n, me, prepare)

    def message(k):
        return remote(mine, messages.at[me], sem_msg_s.at[k], sem_msg_r.at[me], lax.rem(me + k, n))

    def bias_message(k):
        return remote(my_bias, biases.at[me], sem_b_s.at[k], sem_b_r.at[me], lax.rem(me + k, n))

    def small_copy(k):
        return remote(small, small, sem_small_s.at[k], sem_small_r.at[0], lax.rem(me + k, n))

    def shard_copy(k):
        return remote(own, wall.at[me], sem_w_s.at[k], sem_w_r.at[me], lax.rem(me + 2 * k, n))

    for k in range(1, n):
        message(k).start()

    @pl.when(me == 0)
    def _():
        small[...] = shard_ref[0:SMALL, :]

        def send(k, carry):
            small_copy(k).start()
            return carry

        lax.fori_loop(1, n, send, 0)

    for k in range(1, n):
        bias_message(k).start()
    line = me // 2
    if n == 8:
        inner = (line == 1) | (line == 2)
        toward = jnp.where(line == 2, 2, -2)
        turn = jnp.where(line == 0, 2, -2)

        def own_copy(step, k):
            return remote(own, wall.at[me], sem_w_s.at[k], sem_w_r.at[me], me + step)

        @pl.when(inner)
        def _():
            own_copy(-toward, 1).start()
            own_copy(toward, 2).start()

        @pl.when(jnp.logical_not(inner))
        def _():
            own_copy(turn, 1).start()
            own_copy(2 * turn, 2).start()

    else:
        for k in range(1, half):
            shard_copy(k).start()

    def arrived(source):
        remote(own, wall.at[source], sem_w_s.at[0], sem_w_r.at[source], sibling).wait_recv()

    def pass_on(source, k, peer, sem):
        return remote(wall.at[source], wall.at[source], sem.at[k], sem_w_r.at[source], peer)

    def relay(step):
        if n == 8:

            @pl.when(inner)
            def _():
                source = me - (step + 1) * toward
                arrived(source)
                pass_on(source, step, me + toward, sem_e_s).start()
                pass_on(source, step + 1, sibling, sem_f_s).start()

    to_sibling = remote(own, wall.at[me], sem_w_s.at[0], sem_w_r.at[me], sibling)
    to_sibling.start()
    wall[me] = own[...]
    messages[me] = mine[...]
    biases[me] = my_bias[...]

    @pl.when(me > 0)
    def _():
        small_copy(0).wait_recv()

    columns, gamma, beta = first_layer(small)
    order = even_first()
    rows_fc = voxel_rows(small)
    kernel_t = (0.5 * nt(order.astype(BF16), rows_fc[0:64, :].astype(BF16))).astype(BF16)
    bias = 0.5 * jnp.sum(jnp.where(order, rows_fc[64:65, :], 0.0), axis=1, keepdims=True)
    for k in range(1, n):
        sender = lax.rem(me + n - k, n)
        remote(mine, messages.at[sender], sem_msg_s.at[k], sem_msg_r.at[sender], sender).wait_recv()
    mean_row, product, held, positives = joint_moments(n, messages)
    mean, inverse = channel_statistics(columns, mean_row, product, held)
    lane, row = lane_of((32, LANES)), row_of((32, LANES))
    columns_out = jnp.where(lane == 0, mean, 0.0)
    columns_out = jnp.where(lane == 1, inverse, columns_out)
    columns_out = jnp.where(lane == 2, held, columns_out)
    columns_out = jnp.where(lane == 3, positives, columns_out)
    for k, r in enumerate(DIAGONAL):
        columns_out = jnp.where((lane == 4) & (row == k), mean_row[:, r : r + 1], columns_out)
    stat[0:32, :] = columns_out

    half_gamma, half_beta = 0.5 * gamma, 0.5 * beta
    for c in range(voxels // CHUNK):
        part = slice(c * CHUNK, (c + 1) * CHUNK)
        wide = [jnp.broadcast_to(column, (32, CHUNK)) for column in columns]
        held_c = counts[:, part]
        view = points.at[:, :, part]

        def pass_c(p, pooled, wide=wide, held_c=held_c, view=view, part=part):
            half_act = half_gamma * ((linear_row(wide, view, p) - mean) * inverse) + half_beta
            out = jnp.where(p < held_c, half_silu(half_act), 0.0)
            first_out[p, :, part] = out.astype(BF16)
            return pooled + out

        pooled = lax.fori_loop(0, slots, pass_c, jnp.zeros((32, CHUNK), F32), unroll=5)
        pooled = (pooled / held_c.astype(F32)).astype(BF16)
        pooled_out[:, part] = pooled
        fixed = nn(kernel_t[:, 32:64], pooled) + bias
        if c < 2:
            relay(c)

        def pass_d(p, total, fixed=fixed, held_c=held_c, part=part):
            half_inner = nn(kernel_t[:, 0:32], first_out[p, :, part]) + fixed
            return total + jnp.where(p < held_c, half_silu(half_inner), 0.0)

        total = lax.fori_loop(0, slots, pass_d, jnp.zeros((LANES, CHUNK), F32), unroll=7)
        feature[part, :] = jnp.transpose(total / held_c.astype(F32))

    for step in range(voxels // CHUNK, 2):
        relay(step)
    if n == 8:

        @pl.when(inner)
        def _():
            source = me + toward
            arrived(source)
            pass_on(source, 3, sibling, sem_f_s).start()

        @pl.when(jnp.logical_not(inner))
        def _():
            for k in range(1, 4):
                arrived(me + k * turn)
                pass_on(me + k * turn, k, sibling, sem_f_s).start()

    else:
        for k in range(1, half):
            source = lax.rem(me + n - 2 * k, n)
            arrived(source)
            pass_on(source, k, sibling, sem_f_s).start()
    for k in range(1, n):
        sender = lax.rem(me + n - k, n)
        remote(my_bias, biases.at[sender], sem_b_s.at[k], sem_b_r.at[sender], sender).wait_recv()
    total = biases[0]
    for d in range(1, n):
        total += biases[d]
    stat[32:48, :] = total
    for k in range(half):
        arrived(lax.rem(sibling + n - 2 * k, n))
    for k in range(1, half):
        pass_on(me, k, sibling, sem_f_s).wait_send()
    if n == 8:
        for k in (1, 2):
            own_copy(turn, k).wait_send()

        @pl.when(inner)
        def _():
            for k in range(2):
                pass_on(me, k, sibling, sem_e_s).wait_send()

    else:
        for k in range(1, half):
            shard_copy(k).wait_send()
    to_sibling.wait_send()
    for k in range(1, n):
        message(k).wait_send()
        bias_message(k).wait_send()

    @pl.when(me == 0)
    def _():
        def done(k, carry):
            small_copy(k).wait_send()
            return carry

        lax.fori_loop(1, n, done, 0)


def front(n, points, counts, cells, labels, shard):
    slots, voxels = points.shape[1:]
    rows = shard.shape[0]
    padded = ceil_to(rows, 16)
    shape = jax.ShapeDtypeStruct
    dma = pltpu.SemaphoreType.DMA
    return pl.pallas_call(
        functools.partial(front_kernel, n),
        name="front",
        out_shape=(
            shape((n, padded, LANES), BF16),
            shape((SMALL, LANES), F32),
            shape((48, LANES), F32),
            shape((slots, 32, voxels), BF16),
            shape((32, voxels), BF16),
            shape((voxels, LANES), F32),
            shape((1, voxels), jnp.int32),
        ),
        in_specs=[vmem()] * 5,
        out_specs=(vmem(),) * 7,
        scratch_shapes=[
            pltpu.VMEM((padded, LANES), BF16),
            pltpu.VMEM((3, LANES, LANES), F32),
            pltpu.VMEM((8, LANES), F32),
            pltpu.VMEM((n, 8, LANES), F32),
            pltpu.VMEM((16, LANES), F32),
            pltpu.VMEM((n, 16, LANES), F32),
            dma((n,)), dma((1,)), dma((n,)), dma((n,)), dma((n,)), dma((n,)), dma((n,)), dma((n,)), dma((n,)), dma((2,)),
        ],
        compiler_params=pltpu.CompilerParams(
            collective_id=1, has_side_effects=True, vmem_limit_bytes=56 << 20
        ),
    )(points, counts, cells, labels, shard)


def flat_pieces(rows, slot):
    begin, end = slot * rows, (slot + 1) * rows
    spans = ((0, 67, None, 0), (67, 1795, "a", 2), (1795, 1796, "both", 0), (1796, 6440, "b", 1795), (6440, 1 << 30, None, 0))
    pieces = []
    for low, high, run, shift in spans:
        first, last = max(begin, low), min(end, high)
        if first < last:
            pieces.append((first - begin, last - first, run, first - shift))
    return pieces


def flat_slot(slot, rows, low, high, grad_a, grad_b, out_ref):
    def realigned(ref, start, count, lane):
        here, before = ref[pl.ds(start, count), :], ref[pl.ds(start - 1, count), :]
        mixed = jnp.where(lane_of((count, LANES)) >= LANES - lane, before, here)
        return pltpu.roll(mixed, lane, axis=1)

    for row, count, run, start in flat_pieces(rows, slot):
        first, last = max(row, low), min(row + count, high)
        if first >= last:
            continue
        start, row, count = start + first - row, first, last - first
        if run is None:
            value = jnp.zeros((count, LANES), F32)
        elif run == "a":
            value = realigned(grad_a, start, count, 32)
        elif run == "b":
            value = realigned(grad_b, start, count, 96)
        else:
            lane = lane_of((1, LANES))
            part_a = jnp.where(lane >= 96, grad_a[1792:1793, :], grad_a[1793:1794, :])
            part_b = jnp.where(lane >= 32, 0.0, grad_b[0:1, :])
            part_a = pltpu.roll(jnp.broadcast_to(part_a, (8, LANES)), 32, axis=1)
            part_b = pltpu.roll(jnp.broadcast_to(part_b, (8, LANES)), 96, axis=1)
            value = jnp.where(lane < 96, part_a[0:1], part_b[0:1])
        out_ref[row : row + count, :] = value


class Piece:
    def __init__(self, chip, row, count, stage, order):
        self.chip, self.group, self.side = chip, chip // 2, chip % 2
        self.row, self.count, self.stage, self.order = row, count, stage, order
        self.rows = pl.ds(row, count)


def shard_pieces(n, rows):
    padded = ceil_to(rows, 8)
    pieces = []
    for chip in range(n // 2):
        first = 2 * chip * rows
        cut = min(ceil_to(min(max(1796 - first, 0), rows), 8), padded)
        spans = [(0, cut)] if cut else []
        if cut >= 400:
            marks = [ceil_to(cut * k // 4, 8) for k in range(4)] + [cut]
            spans = list(zip(marks[:-1], marks[1:]))
        for order, (low, high) in enumerate(spans):
            pieces.append(Piece(chip, low, high - low, 3, order))
        if cut < padded:
            begin = first + cut
            stage = 0 if begin >= 4102 else 1 if begin >= 2949 else 2
            pieces.append(Piece(chip, cut, padded - cut, stage, 4))
    return pieces


def z_columns(cells_row):
    z = lax.rem(cells_row, ZD).astype(F32)
    return jnp.transpose(jnp.broadcast_to(z, (8, z.shape[1])))[:, 0:1]


def spread_z(feature, z_column, out_ref):
    for z in range(ZD):
        out_ref[:, z * C2 : (z + 1) * C2] = jnp.where(z_column == z, feature, 0.0).astype(BF16)


def middle_kernel(
    n, rows, row_count,
    bases, cells_row, feature, wall,
    pre, *refs,
):
    outs, kept, (flat, run, spread, parts0, parts1, parts2, sum0, sum1, sum2, sem) = refs[:8], refs[8:16], refs[16:]
    w_mid, f_one, f_two, f_three, d_one, d_two, d_three, head_t = kept
    stores = [pltpu.make_async_copy(kept[a], outs[a], sem.at[a]) for a in range(8)]
    voxels = feature.shape[0]
    columns = LANES
    parts, sums = (parts0, parts1, parts2), (sum0, sum1, sum2)
    for s in range(n):
        flat[s * rows : s * rows + wall.shape[1], :] = wall[s].astype(F32)

    def aligned(begin, start, count):
        row, lane = begin
        here = flat[pl.ds(row + start, count), :]
        after = flat[pl.ds(row + start + 1, count), :]
        mixed = jnp.where(lane_of((count, LANES)) >= lane, here, after)
        return pltpu.roll(mixed, LANES - lane, axis=1)

    def zero_half(ref, row, column, height, width):
        ref[row : row + height, column : column + width] = jnp.zeros((height, width), BF16)

    for begin, f_ref, d_ref in ((B_ONE, f_one, d_one), (B_TWO, f_two, d_two)):
        for j in range(3):
            for e in range(2):
                outside = 3 if e == 0 else 0
                zero_half(f_ref, outside * 384 + j * LANES, e * LANES, LANES, LANES)
                zero_half(d_ref, e * LANES, outside * 384 + j * LANES, LANES, LANES)

        def tap(i, j, begin=begin, f_ref=f_ref, d_ref=d_ref):
            block = aligned(RUN_B, begin + (i * 3 + j) * LANES, LANES).astype(BF16)
            for e in range(2):
                t = i + e
                f_ref[t * 384 + j * LANES : t * 384 + (j + 1) * LANES, e * LANES : (e + 1) * LANES] = block
                t = 2 + e - i
                lane = t * 384 + (2 - j) * LANES
                d_ref[e * LANES : (e + 1) * LANES, lane : lane + LANES] = block

        for i in range(3):
            for j in range(3):
                tap(i, j)
        for a in (1, 4) if begin == B_ONE else (2, 5):
            stores[a].start()
    for j in range(3):
        for e in range(2):
            outside = 3 if e == 0 else 0
            zero_half(d_three, e * LANES, outside * 768 + j * 256, LANES, 256)
    for i in range(3):
        for j in range(3):
            run[...] = aligned(RUN_B, B_THREE + (i * 3 + j) * 256, 256)
            for h in range(2):
                block = run[pl.ds(h, LANES, 2), :].astype(BF16)
                row = (i * 3 + j) * LANES
                f_three[row : row + LANES, h * LANES : (h + 1) * LANES] = block
                for e in range(2):
                    lane = (2 + e - i) * 768 + (2 - j) * 256 + h * LANES
                    d_three[e * LANES : (e + 1) * LANES, lane : lane + LANES] = block
    head_rows = aligned(RUN_B, B_HEAD, 32).astype(BF16)
    chosen = nn(eighths(), head_rows)
    chosen = jnp.where(same_eighth(), chosen, 0.0).astype(BF16)
    head_t[...] = nt(fold16(), chosen).astype(BF16)
    for a in (3, 6, 7):
        stores[a].start()

    low = lane_of((64, LANES)) < 64
    for ij in range(9):
        taps = [aligned(RUN_A, A_MID + (t * 9 + ij) * 64, 64) for t in range(3)]
        turned = [pltpu.roll(tap, 64, axis=1) for tap in taps]
        none = jnp.zeros((64, LANES), F32)
        for z in range(ZD):
            first, second = z + 1, z - 1
            a, a_t = (taps[first], turned[first]) if first < 3 else (none, none)
            b, b_t = (taps[second], turned[second]) if second >= 0 else (none, none)
            lanes = slice(ij * LANES, (ij + 1) * LANES)
            w_mid[z * C2 : z * C2 + 64, lanes] = jnp.where(low, a, b_t).astype(BF16)
            w_mid[z * C2 + 64 : (z + 1) * C2, lanes] = jnp.where(low, a_t, b).astype(BF16)

    stores[0].start()
    spread_z(feature[...], z_columns(cells_row[...]), spread)
    for i in range(3):
        product = nn(spread[...], w_mid[:, i * 384 : (i + 1) * 384])
        for j in range(3):
            parts[i][pl.ds(2 - j, voxels, 4), :] = product[:, j * LANES : (j + 1) * LANES]
        sums[i][...] = jnp.zeros_like(sums[i])

    def add(v, carry):
        base = bases[0, v]
        for i in range(3):
            spot = pl.ds(base + (2 - i) * PITCH, 3)
            sums[i][spot, :] = sums[i][spot, :] + parts[i][pl.ds(4 * v, 3), :]
        return carry

    lax.fori_loop(0, voxels, add, 0, unroll=8)

    def gather(p, carry):
        spot = pl.ds(pl.multiple_of(p * PITCH + 8, 8), columns)
        pre[p] = sum0[spot, :] + sum1[spot, :] + sum2[spot, :]
        return carry

    lax.fori_loop(0, row_count + 5, gather, 0)
    for store in stores:
        store.wait()


def eighths():
    return (row_of((CR3, 32)) // 8 == lane_of((CR3, 32))).astype(F32).astype(BF16)


def same_eighth():
    return lane_of((CR3, LANES)) // 16 == lax.rem(row_of((CR3, LANES)), 8)


def fold16():
    return (lax.rem(lane_of((16, LANES)), 16) == row_of((16, LANES))).astype(F32).astype(BF16)


def middle(n, rows, row_count, bases, cells, feature, wall):
    shape = jax.ShapeDtypeStruct
    voxels = feature.shape[0]
    cells_all = (row_count + 6) * PITCH
    return pl.pallas_call(
        functools.partial(middle_kernel, n, rows, row_count),
        name="middle",
        out_shape=(
            shape((row_count + 5, LANES, LANES), F32),
            shape((512, 1152), BF16),
            shape((1536, 256), BF16),
            shape((1536, 256), BF16),
            shape((1152, 256), BF16),
            shape((256, 1536), BF16),
            shape((256, 1536), BF16),
            shape((256, 3072), BF16),
            shape((16, 256), BF16),
        ),
        in_specs=[smem(), vmem(), vmem(), vmem()],
        out_specs=(vmem(),) + (anywhere(),) * 8,
        scratch_shapes=[
            pltpu.VMEM((512, 1152), BF16),
            pltpu.VMEM((1536, 256), BF16),
            pltpu.VMEM((1536, 256), BF16),
            pltpu.VMEM((1152, 256), BF16),
            pltpu.VMEM((256, 1536), BF16),
            pltpu.VMEM((256, 1536), BF16),
            pltpu.VMEM((256, 3072), BF16),
            pltpu.VMEM((16, 256), BF16),
            pltpu.VMEM((n * rows + 24, LANES), F32),
            pltpu.VMEM((256, LANES), F32),
            pltpu.VMEM((voxels, ZD * C2), BF16),
            pltpu.VMEM((voxels * 4, LANES), F32),
            pltpu.VMEM((voxels * 4, LANES), F32),
            pltpu.VMEM((voxels * 4, LANES), F32),
            pltpu.VMEM((cells_all, LANES), F32),
            pltpu.VMEM((cells_all, LANES), F32),
            pltpu.VMEM((cells_all, LANES), F32),
            pltpu.SemaphoreType.DMA((8,)),
        ],
        compiler_params=pltpu.CompilerParams(vmem_limit_bytes=56 << 20),
    )(bases, cells, feature, wall)


NOTE_A, NOTE_B = 72, 40
PAIRS = 18
QB = 9
STEPS = PAIRS // QB
SPAN = QB * LANES
GRID = PAIRS * LANES
A_ROWS, B_ROWS = 1800, 4656


def conv_kernel(
    n, rows_dev, row_count,
    bases, cells_row, feature, stat, pre_in,
    w_mid_h, f_one_h, f_two_h, f_three_h, d_one_h, d_two_h, d_three_h, head_t_h,
    labels_hbm, boxes_hbm, points_hbm, counts_ref, small, pooled_in, first_hbm,
    gradient, loss_out,
    grad_a, grad_b, slots, core_in, chip_in, far_in, grad_feature,
    mine_a, mine_b, notes_a, notes_b, fc_rows, small_grad,
    f_one, f_two, f_three, d_three, head_t, sem_k,
    x_one, x_two, x_three, pre_mid, pre_one, pre_two, back, spread,
    acc0, acc1, acc2,
    labels, boxes, logit_grads, loss_mine, loss_all,
    up_f, down_f, from_up_f, from_down_f, send_up, send_down, from_up, from_down,
    send_up_w, send_down_w, from_up_w, from_down_w,
    sem_t, sem_fs, sem_fr, sem_s, sem_r, sem_ws, sem_wr, sem_ls, sem_lr, sem_cs, sem_cr, sem_zs, sem_zr,
    sem_gs, sem_gr, sem_p, sem_ns, sem_nar, sem_nbr,
):
    me = lax.axis_index("tile")
    edge, split, top, bottom = layout(n, row_count)
    has_up, has_down = me > 0, me < n - 1
    above, below = jnp.maximum(me - 1, 0), jnp.minimum(me + 1, n - 1)
    loads = [pltpu.make_async_copy(labels_hbm.at[a], labels.at[:, a, :], sem_t.at[a]) for a in range(2)]
    loads += [
        pltpu.make_async_copy(boxes_hbm.at[a], boxes.at[:, 2 + a, :], sem_t.at[2 + a]) for a in range(14)
    ]
    for load in loads:
        load.start()
    kernels = (
        (f_one_h, f_one), (f_two_h, f_two), (f_three_h, f_three), (head_t_h, head_t),
        (d_three_h, d_three),
    )
    kernel_loads = [pltpu.make_async_copy(a, b, sem_k.at[i]) for i, (a, b) in enumerate(kernels)]
    for load in kernel_loads:
        load.start()
    enter(n, me)

    pieces = shard_pieces(n, rows_dev)
    core, side, my_group = lax.rem(me, 2), lax.rem(me // 2, 2), me // 4
    sibling, other = me + 1 - 2 * core, me + 2 - 4 * side

    def collects(piece):
        nearer = jnp.where(my_group > piece.group, 0, 1)
        return side == jnp.where(my_group == piece.group, piece.side, nearer)

    def core_copy(i):
        piece = pieces[i]
        return remote(
            slots.at[2 * piece.chip + 1 - core, piece.rows],
            core_in.at[piece.chip, piece.rows],
            sem_cs.at[i], sem_cr.at[i], sibling,
        )

    def chip_copy(i):
        piece = pieces[i]
        return remote(
            slots.at[2 * piece.chip + core, piece.rows],
            chip_in.at[piece.chip, piece.rows],
            sem_zs.at[i], sem_zr.at[i], other,
        )

    def far_copy(i, sender):
        piece = pieces[i]
        return remote(
            slots.at[2 * piece.chip + core, piece.rows],
            far_in.at[sender, piece.rows],
            sem_gs.at[i], sem_gr.at[5 * sender + piece.order], 2 * piece.chip + core,
        )

    def of_stage(stage):
        return [i for i, piece in enumerate(pieces) if piece.stage == stage]

    def ship(stage):
        for i in of_stage(stage):
            piece = pieces[i]
            for s in (2 * piece.chip, 2 * piece.chip + 1):
                flat_slot(s, rows_dev, piece.row, piece.row + piece.count, grad_a, grad_b, slots.at[s])
            core_copy(i).start()

    def ship_on(stage):
        for i in of_stage(stage):
            piece = pieces[i]
            core_copy(i).wait()
            spot = 2 * piece.chip + core
            slots[spot, piece.rows, :] = slots[spot, piece.rows, :] + core_in[piece.chip, piece.rows, :]

            @pl.when(jnp.logical_not(collects(piece)))
            def _(i=i):
                chip_copy(i).start()

    def ship_far(i):
        piece = pieces[i]

        @pl.when(collects(piece))
        def _():
            chip_copy(i).wait_recv()
            spot = 2 * piece.chip + core
            slots[spot, piece.rows, :] = slots[spot, piece.rows, :] + chip_in[piece.chip, piece.rows, :]

        @pl.when(collects(piece) & (my_group != piece.group))
        def _():
            far_copy(i, my_group).start()

    def ship_end():
        for i, piece in enumerate(pieces):
            count = min(piece.count, rows_dev - piece.row)
            taken = pl.ds(piece.row, count)
            here = collects(piece)

            @pl.when(here & (my_group == piece.group))
            def _(i=i, piece=piece, taken=taken):
                gradient[taken, :] = slots[2 * piece.chip + core, taken, :]
                for k in range(1, n // 4):
                    sender = lax.rem(my_group + n // 4 - k, n // 4)
                    far_copy(i, sender).wait_recv()
                    gradient[taken, :] = gradient[taken, :] + far_in[sender, taken, :]

            @pl.when(here & (my_group != piece.group))
            def _(i=i):
                far_copy(i, my_group).wait_send()

            @pl.when(jnp.logical_not(here))
            def _(i=i):
                chip_copy(i).wait_send()

    late = of_stage(3)

    def ok(place):
        return place_ok(place, edge, split, row_count)

    def halo_copies(s, up_src, down_src, up_dst, down_dst, sem_send, sem_recv):
        up = remote(up_src, down_dst, sem_send.at[2 * s], sem_recv.at[2 * s], above)
        down = remote(down_src, up_dst, sem_send.at[2 * s + 1], sem_recv.at[2 * s + 1], below)
        return up, down

    def halo_start(copies):
        up, down = copies

        @pl.when(has_up)
        def _():
            up.start()

        @pl.when(has_down)
        def _():
            down.start()

    def halo_wait(copies):
        up, down = copies

        @pl.when(has_up)
        def _():
            up.wait_send()
            down.wait_recv()

        @pl.when(has_down)
        def _():
            down.wait_send()
            up.wait_recv()

    def thin(s):
        return halo_copies(
            s, send_up.at[s], send_down.at[s], from_up.at[s], from_down.at[s], sem_s, sem_r
        )

    def pick(condition, a, b):
        return jnp.where(condition, a, b)

    column = row_of((LANES, LANES))

    def shifted(value):
        left = jnp.where(column > 0, pltpu.roll(value, 1, axis=0), 0.0)
        right = jnp.where(column < LANES - 1, pltpu.roll(value, LANES - 1, axis=0), 0.0)
        return left.astype(BF16), value.astype(BF16), right.astype(BF16)

    def put(ref, pair, parity, value, part, parts):
        rows = pl.ds(pl.multiple_of(pair * LANES, LANES), LANES)
        width = 3 * parts * LANES
        for j, shift in enumerate(shifted(value)):
            lane = parity * width + (j * parts + part) * LANES
            ref[rows, lane : lane + LANES] = shift

    def edges(parts, up_halo, down_halo):
        rows = []
        for good, halo in (((top == 1) & has_up, up_halo), ((bottom == 1) & has_down, down_halo)):
            pieces = [shifted(pick(good, halo[:, p * LANES : (p + 1) * LANES].astype(F32), 0.0)) for p in range(parts)]
            rows.append(jnp.concatenate([pieces[p][j] for j in range(3) for p in range(parts)], axis=1))
        return rows

    def put_edges(ref, top_row, bottom_row):
        width = top_row.shape[1]
        ref[0:LANES, 0:width] = top_row
        rows = slice(16 * LANES, 17 * LANES)
        ref[rows, width : 2 * width] = pick(split == 1, ref[rows, width : 2 * width], bottom_row)
        rows = slice(17 * LANES, 18 * LANES)
        ref[rows, 0:width] = pick(split == 1, bottom_row, jnp.zeros_like(bottom_row))

    def add_edges(ref, at_top, at_bottom):
        width = at_top.shape[1]
        ref[0:LANES, 0:width] += at_top
        rows = slice(15 * LANES, 16 * LANES)
        ref[rows, width : 2 * width] += pick(split == 1, 0.0, at_bottom)
        rows = slice(16 * LANES, 17 * LANES)
        ref[rows, 0:width] += pick(split == 1, at_bottom, 0.0)

    up_f[...] = pre_in[0]
    down_f[...] = pick(split == 1, pre_in[row_count + 2], pre_in[row_count + 1])
    copies = halo_copies(0, up_f, down_f, from_up_f, from_down_f, sem_fs, sem_fr)
    halo_start(copies)
    for ref, wide in ((x_one, 768), (x_two, 768), (x_three, 768)):
        ref[0:LANES, 0:384] = jnp.zeros((LANES, 384), BF16)
        ref[18 * LANES : 19 * LANES, :] = jnp.zeros((LANES, wide), BF16)
    spread_z(feature[...], z_columns(cells_row[...]), spread)
    bias_mid = stat[32:33, :]
    b_mid = jnp.concatenate([bias_mid[:, 32:96], bias_mid[:, 32:96]], axis=1)

    def activated(value, x_ref, q, e):
        value = pick(ok(2 * q + 1 + e), half_silu(0.5 * value), 0.0)
        put(x_ref, q + e, 1 - e, value, 0, 1)

    def mid_step(q, carry):
        rows = pl.ds(pl.multiple_of(q * LANES, LANES), LANES)
        for e in range(2):
            value = pre_in[2 * q + 1 + e] + b_mid
            pre_mid[rows, e * LANES : (e + 1) * LANES] = value
            activated(value, x_one, q, e)
        return carry

    lax.fori_loop(0, PAIRS, mid_step, 0)
    halo_wait(copies)
    at_top = pick((top == 1) & has_up, from_up_f[...], 0.0)
    at_bottom = pick((bottom == 1) & has_down, from_down_f[...], 0.0)
    add_edges(pre_mid, at_top, at_bottom)
    for q, e in ((0, 0), (15, 1), (16, 0)):
        activated(pre_mid[q * LANES : (q + 1) * LANES, e * LANES : (e + 1) * LANES], x_one, q, e)

    def exchange(x_ref, s):
        send_up[s] = x_ref[0:LANES, 512:640]
        send_down[s] = pick(split == 1, x_ref[16 * LANES : 17 * LANES, 512:640], x_ref[16 * LANES : 17 * LANES, 128:256])
        halo_start(thin(s))

    def banded_back(g_ref, d_ref, out_ref):
        width = g_ref.shape[1]

        def step(b, carry):
            start = pl.multiple_of(b * SPAN, LANES)
            total = nt(g_ref[pl.ds(start, SPAN), :], d_ref[:, 0:width])
            total += nt(g_ref[pl.ds(start + LANES, SPAN), :], d_ref[:, width : 2 * width])
            out_ref[pl.ds(start, SPAN), :] = total
            return carry

        lax.fori_loop(0, STEPS, step, 0)

    def bias_row(first, lane):
        mixed = jnp.where(lane_of((1, LANES)) >= lane, stat[first : first + 1, :], stat[first + 1 : first + 2, :])
        return pltpu.roll(jnp.broadcast_to(mixed, (8, LANES)), LANES - lane, axis=1)[0:1, :]

    def twice(row):
        return jnp.concatenate([row, row], axis=1)

    def layer_forward(x_ref, f_ref, bias, out_ref, s, x_next):
        exchange(x_ref, s)
        bias = twice(bias)

        def products(b):
            rows, more = pl.ds(b * SPAN, SPAN), pl.ds(b * SPAN + LANES, SPAN)
            total = nn(x_ref[rows, :], f_ref[0:768, :])
            total += nn(x_ref[more, :], f_ref[768:1536, :])
            out_ref[rows, :] = total + bias

        def piece(q, e):
            rows = pl.ds(q * LANES, LANES)
            activated(out_ref[rows, e * LANES : (e + 1) * LANES], x_next, q, e)

        products(0)
        products(1)
        for q in range(QB):
            for e in range(2):
                piece(q, e)

        def step(q, carry):
            rows = pl.ds(pl.multiple_of(q * LANES, LANES), LANES)
            for e in range(2):
                activated(out_ref[rows, e * LANES : (e + 1) * LANES], x_next, q, e)
            return carry

        lax.fori_loop(QB, PAIRS, step, 0)
        halo_wait(thin(s))
        top_row, bottom_row = edges(1, from_up[s], from_down[s])
        put_edges(x_ref, top_row, bottom_row)
        add_edges(out_ref, nn(top_row, f_ref[0:384, 0:LANES]), nn(bottom_row, f_ref[768:1152, 0:LANES]))
        for q, e in ((0, 0), (15, 1), (16, 0)):
            piece(q, e)

    kernel_loads[0].wait()
    layer_forward(x_one, f_one, bias_row(33, 96), pre_one, 0, x_two)
    for load in kernel_loads[1:]:
        load.wait()
    layer_forward(x_two, f_two, bias_row(35, 96), pre_two, 1, x_three)

    def weight_grads(g_ref, x_ref, parts, write):
        width, wide = parts * LANES, 3 * parts * LANES
        middle0 = slice(width, 2 * width)
        middle1 = slice(wide + width, wide + 2 * width)
        acc0[0 : 2 * width, :] = jnp.zeros((2 * width, 768), F32)
        acc1[0:width, :] = jnp.zeros((width, 384), F32)
        acc2[0:width, :] = jnp.zeros((width, 384), F32)

        def step(b, carry):
            start = pl.multiple_of(b * SPAN, LANES)
            rows = pl.ds(start, SPAN)
            g0, g1 = g_ref[rows, middle0], g_ref[rows, middle1]
            both = jnp.concatenate([g0, g1], axis=1)
            sums = both.astype(F32).reshape(SPAN // 8, 8, 2 * width)
            carry = carry + jnp.sum(sums, axis=0)
            acc0[0 : 2 * width, :] += tn(both, x_ref[rows, :])
            acc2[0:width, :] += tn(g1, x_ref[pl.ds(start + LANES, SPAN), 0:384])
            after = g_ref[pl.ds(start + LANES, SPAN), middle0]
            acc1[0:width, :] += tn(after, x_ref[rows, 384:768])
            return carry

        sums = lax.fori_loop(0, STEPS, step, jnp.zeros((8, 2 * width), F32))
        sums = jnp.sum(sums, axis=0, keepdims=True)
        for i in range(3):
            if i == 0:
                total = acc0[width : 2 * width, 0:384] + acc1[0:width, :]
            elif i == 1:
                total = acc0[0:width, 0:384] + acc0[width : 2 * width, 384:768]
            else:
                total = acc0[0:width, 384:768] + acc2[0:width, :]
            for j in range(3):
                for part in range(parts):
                    block = total[part * LANES : (part + 1) * LANES, j * LANES : (j + 1) * LANES]
                    write(i, j, part, jnp.transpose(block))
        return sums[:, 0:width] + sums[:, width : 2 * width]

    def last_layers(pre_three, x_head, g_three):
        bias = jnp.concatenate([bias_row(37, 96), bias_row(38, 96)], axis=1)

        def products(b):
            rows, more = pl.ds(b * SPAN, SPAN), pl.ds(b * SPAN + LANES, SPAN)
            total = nn(x_three[rows, :], f_three[0:768, :]) + nn(x_three[more, 0:384], f_three[768:1152, :])
            pre_three[rows, 0:256] = total + bias
            total = nn(x_three[rows, 384:768], f_three[0:384, :]) + nn(x_three[more, :], f_three[384:1152, :])
            pre_three[rows, 256:512] = total + bias

        def head_rows(rows):
            x_head[rows, :] = half_silu(0.5 * pre_three[rows, :]).astype(BF16)

        def head_step(q, carry):
            head_rows(pl.ds(pl.multiple_of(q * LANES, LANES), LANES))
            return carry

        exchange(x_three, 2)
        products(0)
        products(1)
        for q in range(QB):
            head_rows(pl.ds(q * LANES, LANES))
        lax.fori_loop(QB, PAIRS, head_step, 0)
        halo_wait(thin(2))
        top_row, bottom_row = edges(1, from_up[2], from_down[2])
        put_edges(x_three, top_row, bottom_row)
        add_edges(pre_three, nn(top_row, f_three[0:384, :]), nn(bottom_row, f_three[768:1152, :]))
        for q in (0, 15, 16):
            head_rows(pl.ds(q * LANES, LANES))
        for load in loads:
            load.wait()
        head_row = jnp.broadcast_to(stat[40:41, :], (LANES, LANES))
        b_head = jnp.sum(jnp.where(lane_of((16, LANES)) == row_of((16, LANES)) + 96, head_row[0:16, :], 0.0), axis=1, keepdims=True)
        divisor = jnp.maximum(stat[0:1, 3:4], 1.0)
        inverse = 1.0 / divisor
        row16 = row_of((16, LANES))

        def loss_tile(logits, place):
            row = place_row(place, edge, row_count)
            label = labels[row]
            kind = jnp.concatenate([label, jnp.zeros((14, LANES), jnp.int32)], axis=0)
            is_class = row16 < 2
            anchor0, anchor1 = label[0:1, :] == 1, label[1:2, :] == 1
            box_on = ((row16 < 9) & anchor0) | ((row16 >= 9) & anchor1)
            positive = (kind == 1).astype(F32)
            negative = (kind == 0).astype(F32)
            q = 1.0 / (1.0 + jnp.exp(-logits))
            rest = jnp.log(1.0 + jnp.exp(-jnp.abs(logits)))
            log_q = jnp.minimum(logits, 0.0) - rest
            log_not = jnp.minimum(-logits, 0.0) - rest
            short = 1.0 - q
            focal = -FOCAL_ALPHA * positive * short * short * log_q
            focal -= (1.0 - FOCAL_ALPHA) * negative * q * q * log_not
            slope_p = FOCAL_ALPHA * (2.0 * q * short * short * log_q - short * short * short)
            slope_n = (1.0 - FOCAL_ALPHA) * (q * q * q - 2.0 * q * q * short * log_not)
            residual = logits - boxes[row]
            size = jnp.abs(residual)
            huber = jnp.where(size < HUBER_BETA, (0.5 / HUBER_BETA) * residual * residual, size - 0.5 * HUBER_BETA)
            bent = jnp.clip(residual * (1.0 / HUBER_BETA), -1.0, 1.0)
            value = jnp.where(is_class, focal, jnp.where(box_on, 2.0 * huber, 0.0))
            grad = jnp.where(is_class, positive * slope_p + negative * slope_n, jnp.where(box_on, 2.0 * bent, 0.0))
            good = ok(place)
            return pick(good, value, 0.0), pick(good, grad * inverse, 0.0)

        def loss_step(q, total):
            rows = pl.ds(pl.multiple_of(q * LANES, LANES), LANES)
            for e in range(2):
                logits = nt(head_t[...], x_head[rows, e * 256 : (e + 1) * 256]) + b_head
                value, grad = loss_tile(logits, 2 * q + 1 + e)
                logit_grads[e, :, rows] = grad.astype(BF16)
                total = total + value
            return total

        total = lax.fori_loop(0, PAIRS, loss_step, jnp.zeros((16, LANES), F32), unroll=3)
        total = jnp.sum(jnp.sum(total, axis=1, keepdims=True), axis=0, keepdims=True)
        loss_mine[...] = jnp.broadcast_to(total, (8, LANES))
        for k in range(1, n):
            loss_copy(k).start()
        g_head = jnp.zeros((16, CR3), F32)
        g_bias = jnp.zeros((16, 1), F32)
        for e in range(2):
            g_head += nn(logit_grads[e], x_head[0:GRID, e * 256 : (e + 1) * 256])
            g_bias += jnp.sum(logit_grads[e].astype(F32), axis=1, keepdims=True)
        back_rows = jnp.where(same_eighth(), tn(g_head, fold16().astype(F32), HIGH), 0.0)
        grad_b[B_HEAD : B_HEAD + 32, :] = tn(eighths().astype(F32), back_rows, HIGH)
        spots = (lane_of((16, LANES)) == row_of((16, LANES))).astype(F32)
        grad_b[B_HEAD + 32 : B_HEAD + 33, :] = jnp.sum(spots * g_bias, axis=0, keepdims=True)

        def back_step(q, carry):
            rows = pl.ds(pl.multiple_of(q * LANES, LANES), LANES)
            for e in range(2):
                grad = tn(logit_grads[e, :, rows], head_t[...])
                grad = grad * slope(pre_three[rows, e * 256 : (e + 1) * 256])
                for part in range(2):
                    put(g_three, q + e, 1 - e, grad[:, part * LANES : (part + 1) * LANES], part, 2)
            return carry

        g_three[0:LANES, 0:768] = jnp.zeros((LANES, 768), BF16)
        g_three[18 * LANES : 19 * LANES, :] = jnp.zeros((LANES, 1536), BF16)
        lax.fori_loop(0, PAIRS, back_step, 0)
        last_row = slice(16 * LANES, 17 * LANES)
        send_up_w[...] = g_three[0:LANES, 1024:1280]
        send_down_w[...] = pick(split == 1, g_three[last_row, 1024:1280], g_three[last_row, 256:512])
        copies = halo_copies(0, send_up_w, send_down_w, from_up_w, from_down_w, sem_ws, sem_wr)
        halo_start(copies)

        def write(i, j, part, block):
            start = B_THREE + 2 * (i * 3 + j) * LANES + part
            grad_b[pl.ds(start, LANES, 2), :] = block

        sums = weight_grads(g_three, x_three, 2, write)
        grad_b[B_HEAD - 2 : B_HEAD - 1, :] = sums[:, 0:LANES]
        grad_b[B_HEAD - 1 : B_HEAD, :] = sums[:, LANES : 2 * LANES]
        ship(0)
        banded_back(g_three, d_three, back)
        ship_on(0)
        halo_wait(copies)
        add_back(d_three, *edges(2, from_up_w[...], from_down_w[...]))

    def add_back(d_ref, top_row, bottom_row):
        width = top_row.shape[1]
        add_edges(back, nt(top_row, d_ref[0:LANES, 0:width]), nt(bottom_row, d_ref[0:LANES, 2 * width : 3 * width]))

    def loss_copy(k):
        return remote(loss_mine, loss_all.at[me], sem_ls.at[k], sem_lr.at[me], lax.rem(me + k, n))

    pl.run_scoped(
        last_layers,
        pltpu.VMEM((GRID, 512), F32),
        pltpu.VMEM((GRID, 512), BF16),
        pltpu.VMEM((19 * LANES, 1536), BF16),
    )

    def lower_layers(g_ref, g_map, win0, win1, win2, gathered, d_two, d_one, w_mid):
        lower = ((d_two_h, d_two), (d_one_h, d_one), (w_mid_h, w_mid))
        lower_loads = [pltpu.make_async_copy(a, b, sem_k.at[5 + i]) for i, (a, b) in enumerate(lower)]
        for load in lower_loads:
            load.start()

        def piece_in(pre_ref, rows, q, e):
            lanes = slice(e * LANES, (e + 1) * LANES)
            value = (0.5 * back[rows, lanes]) * half_slope(0.5 * pre_ref[rows, lanes])
            put(g_ref, q + e, 1 - e, pick(ok(2 * q + 1 + e), value, 0.0), 0, 1)

        def all_pieces(first, take):
            def step(q, carry):
                rows = pl.ds(pl.multiple_of(q * LANES, LANES), LANES)
                for e in range(2):
                    take(rows, q, e)
                return carry

            lax.fori_loop(first, PAIRS, step, 0)

        def back_and_on(d_ref, s, take, between):
            for b in range(STEPS):
                total = nt(g_ref[b * SPAN : (b + 1) * SPAN, :], d_ref[:, 0:768])
                total += nt(g_ref[b * SPAN + LANES : (b + 1) * SPAN + LANES, :], d_ref[:, 768:1536])
                back[b * SPAN : (b + 1) * SPAN, :] = total
            for q in range(QB):
                for e in range(2):
                    take(pl.ds(q * LANES, LANES), q, e)
            all_pieces(QB, take)
            between()
            from_edges(d_ref, s)
            for q, e in ((0, 0), (15, 1), (16, 0)):
                take(pl.ds(q * LANES, LANES), q, e)

        def weights_of(x_ref, begin):
            def write(i, j, part, block):
                start = begin + (i * 3 + j) * LANES
                grad_b[start : start + LANES, :] = block

            grad_b[begin + 1152 : begin + 1153, :] = weight_grads(g_ref, x_ref, 1, write)

        def from_edges(d_ref, s):
            halo_wait(thin(s))
            add_back(d_ref, *edges(1, from_up[s], from_down[s]))

        g_ref[0:LANES, 0:384] = jnp.zeros((LANES, 384), BF16)
        g_ref[18 * LANES : 19 * LANES, :] = jnp.zeros((LANES, 768), BF16)
        all_pieces(0, functools.partial(piece_in, pre_two))
        exchange(g_ref, 3)
        weights_of(x_two, B_TWO)
        ship(1)
        for load in lower_loads:
            load.wait()
        ship_on(1)
        back_and_on(d_two, 3, functools.partial(piece_in, pre_one), lambda: None)
        exchange(g_ref, 4)

        g_map[...] = jnp.zeros_like(g_map)

        def piece_to_map(rows, q, e):
            p = 2 * q + 1 + e
            lanes = slice(e * LANES, (e + 1) * LANES)
            value = (0.5 * back[rows, lanes]) * half_slope(0.5 * pre_mid[rows, lanes])
            value = pick(ok(p), value, 0.0).astype(BF16).astype(F32)
            spot = p * PITCH + 8
            g_map[pl.ds(spot if isinstance(q, int) else pl.multiple_of(spot, 8), LANES), :] = value

        def far_zero():
            for i in of_stage(0):
                ship_far(i)

        back_and_on(d_one, 4, piece_to_map, far_zero)

        def map_row(place):
            return slice(place * PITCH + 8, place * PITCH + 8 + LANES)

        send_up[5] = g_map[map_row(1), :].astype(BF16)
        send_down[5] = pick(split == 1, g_map[map_row(row_count + 1), :], g_map[map_row(row_count), :]).astype(BF16)
        halo_start(thin(5))

        def map_sum(p, total):
            return total + g_map[pl.ds(pl.multiple_of(p * PITCH + 8, 8), LANES), :]

        total = lax.fori_loop(1, 2 * PAIRS + 1, map_sum, jnp.zeros((LANES, LANES), F32))
        total = jnp.sum(total, axis=0, keepdims=True)
        total = total[:, 0:CM] + total[:, CM : 2 * CM]
        grad_a[0:A_MID, :] = jnp.zeros((A_MID, LANES), F32)
        grad_a[A_MID + 1728 : A_ROWS, :] = jnp.zeros((A_ROWS - A_MID - 1728, LANES), F32)
        grad_a[A_MID + 1728 : A_MID + 1729, 0:CM] = total
        weights_of(x_one, B_ONE)
        ship(2)
        halo_wait(thin(5))
        g_map[map_row(0), :] = pick((top == 1) & has_up, from_up[5].astype(F32), 0.0)
        halo = pick((bottom == 1) & has_down, from_down[5].astype(F32), 0.0)
        g_map[map_row(row_count + 1), :] = pick(split == 1, g_map[map_row(row_count + 1), :], halo)
        g_map[map_row(row_count + 2), :] = pick(split == 1, halo, 0.0)

        wins = (win0, win1, win2)
        voxels = feature.shape[0]

        def fetch(v, carry):
            base = bases[0, v]
            for i in range(3):
                wins[i][pl.ds(4 * v, 3), :] = g_map[pl.ds(base + (2 - i) * PITCH, 3), :]
            return carry

        lax.fori_loop(0, voxels, fetch, 0, unroll=8)
        ship_on(2)
        for i in range(3):
            for j in range(3):
                lanes = slice((i * 3 + j) * LANES, (i * 3 + j + 1) * LANES)
                gathered[:, lanes] = wins[i][pl.ds(2 - j, voxels, 4), :].astype(BF16)
        low = lane_of((64, LANES)) < 64
        for i in range(3):
            block = tn(spread[...], gathered[:, i * 384 : (i + 1) * 384])
            for j in range(3):
                part = block[:, j * LANES : (j + 1) * LANES]
                even = [part[z * LANES : z * LANES + 64] for z in range(ZD)]
                odd = [part[z * LANES + 64 : (z + 1) * LANES] for z in range(ZD)]

                def flip(x):
                    return pltpu.roll(x, 64, axis=1)

                taps = (
                    jnp.where(low, flip(even[1]), odd[1]),
                    jnp.where(low, even[0] + flip(even[2]), flip(odd[0]) + odd[2]),
                    jnp.where(low, even[1] + flip(even[3]), flip(odd[1]) + odd[3]),
                )
                for t in range(3):
                    start = A_MID + (t * 9 + i * 3 + j) * 64
                    grad_a[start : start + 64, :] = taps[t]
        ship(3)
        for i in of_stage(1):
            ship_far(i)
        z_column = z_columns(cells_row[...])
        total = jnp.zeros((voxels, C2), F32)
        for z in range(ZD):
            total += jnp.where(z_column == z, nt(gathered[...], w_mid[z * C2 : (z + 1) * C2, :]), 0.0)
        grad_feature[...] = total

    voxels = feature.shape[0]
    pl.run_scoped(
        lower_layers,
        pltpu.VMEM((19 * LANES, 768), BF16),
        pltpu.VMEM(((row_count + 6) * PITCH, LANES), F32),
        pltpu.VMEM((voxels * 4, LANES), F32),
        pltpu.VMEM((voxels * 4, LANES), F32),
        pltpu.VMEM((voxels * 4, LANES), F32),
        pltpu.VMEM((voxels, 1152), BF16),
        pltpu.VMEM(d_two_h.shape, BF16),
        pltpu.VMEM(d_one_h.shape, BF16),
        pltpu.VMEM(w_mid_h.shape, BF16),
    )
    counts = counts_ref[...]
    slot_count = points_hbm.shape[1]
    columns, gamma, beta = first_layer(small)
    mean, scale, held = stat[0:32, 0:1], stat[0:32, 1:2], stat[0:32, 2:3]
    centre = stat[0:8, 4:5]
    order = even_first()
    rows_fc = voxel_rows(small)
    kernel = rows_fc[0:64, :].astype(BF16)
    kernel_t = (0.5 * nt(order.astype(BF16), kernel)).astype(BF16)
    kernel = nt(kernel, order.astype(BF16)).astype(BF16)
    bias = 0.5 * jnp.sum(jnp.where(order, rows_fc[64:65, :], 0.0), axis=1, keepdims=True)
    half_gamma, half_beta = 0.5 * gamma, 0.5 * beta


    def halves(value):
        high = value.astype(BF16)
        return high, (value - high.astype(F32)).astype(BF16)

    def note(s, sender, target):
        mine, notes, received = ((mine_a, notes_a, sem_nar), (mine_b, notes_b, sem_nbr))[s]
        spot = sender // 2
        return remote(mine, notes.at[spot], sem_ns.at[s], received.at[spot], target)

    def send_note(s):
        mine, notes = ((mine_a, notes_a), (mine_b, notes_b))[s]

        @pl.when(core == 1)
        def _():
            note(s, me, sibling).start()

        @pl.when(core == 0)
        def _():
            note(s, me + 1, sibling).wait_recv()
            mine[...] = mine[...] + notes[me // 2]

        @pl.when((core == 0) & (me > 0))
        def _():
            note(s, me, 0).start()

    chunks = voxels // CHUNK

    def after(step):
        last = 3 * chunks - 1
        for place, i in enumerate(late):
            if min(place + 1, last) == step:
                ship_far(i)

    def voxel_layers(points, first, inner_grads, first_out):
        first_load = pltpu.make_async_copy(first_hbm, first_out, sem_p.at[7])
        first_load.start()
        points[...] = jnp.ones_like(points)
        point_loads = [
            pltpu.make_async_copy(points_hbm.at[k], points.at[:, k, :], sem_p.at[k]) for k in range(7)
        ]
        for load in point_loads:
            load.start()
        ship_on(3)
        first_load.wait()
        tail = jnp.where(row_of((16, CHUNK)) == 0, 1.0, 0.0).astype(BF16)
        fc = jnp.zeros((80, LANES), F32)
        pooled_grads = []
        for c in range(chunks):
            part = slice(c * CHUNK, (c + 1) * CHUNK)
            held_c = counts[:, part]
            counts_f = held_c.astype(F32)
            grad_pre = (0.5 * jnp.transpose(grad_feature[part, :])) / counts_f
            pooled_c = pooled_in[:, part]
            fixed = nn(kernel_t[:, 32:64], pooled_c) + bias

            def spot(p):
                return pl.ds(pl.multiple_of(p * CHUNK, LANES), CHUNK)

            def pass_e(p, carry, part=part, held_c=held_c, grad_pre=grad_pre, fixed=fixed):
                half_inner = nn(kernel_t[:, 0:32], first_out[p, :, part]) + fixed
                grad = jnp.where(p < held_c, grad_pre * half_slope(half_inner), 0.0)
                inner_grads[:, spot(p)] = grad.astype(BF16)
                return carry

            lax.fori_loop(0, slot_count, pass_e, 0, unroll=7)
            if c == 0:
                for i in of_stage(2):
                    ship_far(i)
            else:
                after(2 * c)

            def pass_g(p, carry, c=c, part=part, pooled_c=pooled_c):
                fc, pooled = carry
                grad = inner_grads[:, spot(p)]
                fc += nt(jnp.concatenate([first_out[p, :, part], pooled_c, tail], axis=0), grad)
                down = nn(kernel, grad)
                first[c, p] = down[0:32]
                return fc, pooled + down[32:64]

            fc, pooled = lax.fori_loop(0, slot_count, pass_g, (fc, jnp.zeros((32, CHUNK), F32)), unroll=5)
            pooled_grads.append(pooled / counts_f)
            after(2 * c + 1)
        mine_a[...] = fc[0:NOTE_A]
        send_note(0)
        for load in point_loads:
            load.wait()
        moments, g_gamma, centred = jnp.zeros((LANES, 16), F32), jnp.zeros((32, CHUNK), F32), jnp.zeros((8, CHUNK), F32)
        for c in range(chunks):
            part = slice(c * CHUNK, (c + 1) * CHUNK)
            wide = [jnp.broadcast_to(column, (32, CHUNK)) for column in columns]

            def pass_f(p, carry, c=c, part=part, held_c=counts[:, part], pooled=pooled_grads[c], wide=wide):
                moments, g_gamma, centred = carry
                inside = p < held_c
                value = wide[0] * points[p, 0:1, part]
                for k in range(1, 7):
                    value += wide[k] * points[p, k : k + 1, part]
                normed = jnp.where(inside, (value - mean) * scale, 0.0)
                slopes = half_slope(half_gamma * normed + half_beta)
                grad = jnp.where(inside, (0.5 * (first[c, p] + pooled)) * slopes, 0.0)
                off = points[p, :, part] - centre
                off_high, off_low = halves(off)
                grad_high, grad_low = halves(grad)
                norm_high, norm_low = halves(normed)
                left = jnp.concatenate([grad_high, grad_low, norm_high, norm_low], axis=0)
                right = jnp.concatenate([off_high, off_low], axis=0)
                return (
                    moments + nt(left, right),
                    g_gamma + grad * normed,
                    centred + jnp.where(inside, off, 0.0),
                )

            moments, g_gamma, centred = lax.fori_loop(0, slot_count, pass_f, (moments, g_gamma, centred), unroll=5)
            after(2 * chunks + c)
        by_grad = moments[0:32] + moments[32:64]
        by_norm = moments[64:96] + moments[96:128]
        mine_b[...] = jnp.zeros_like(mine_b)
        mine_b[0:32, 0:8] = by_grad[:, 0:8] + by_grad[:, 8:16]
        mine_b[0:32, 8:16] = by_norm[:, 0:8] + by_norm[:, 8:16]
        mine_b[0:32, 16:17] = jnp.sum(g_gamma, axis=1, keepdims=True)
        mine_b[32:40, 0:1] = jnp.sum(centred, axis=1, keepdims=True)
        send_note(1)

    pl.run_scoped(
        voxel_layers,
        pltpu.VMEM((slot_count, 8, voxels), F32),
        pltpu.VMEM((chunks, slot_count, 32, CHUNK), F32),
        pltpu.VMEM((LANES, slot_count * CHUNK), BF16),
        pltpu.VMEM(first_hbm.shape, BF16),
    )
    small_grad[...] = jnp.zeros_like(small_grad)

    @pl.when(me == 0)
    def _():
        fc_total = mine_a[...]
        for d in range(2, n, 2):
            note(0, d, sibling).wait_recv()
            fc_total += notes_a[d // 2]
        fc_rows[...] = jnp.zeros_like(fc_rows)
        fc_rows[8:80, :] = nn(fc_total, order.astype(F32), HIGH)
        here, before = fc_rows[8:80, :], fc_rows[7:79, :]
        mixed = jnp.where(lane_of((72, LANES)) >= LANES - FC_LANE, before, here)
        small_grad[2:74, :] = pltpu.roll(mixed, FC_LANE, axis=1)
        total = mine_b[...]
        for d in range(2, n, 2):
            note(1, d, sibling).wait_recv()
            total += notes_b[d // 2]
        by_grad, by_norm = total[0:32, 0:8], total[0:32, 8:16]
        g_gamma, g_beta = total[0:32, 16:17], total[0:32, 7:8]
        off_sums = jnp.transpose(jnp.broadcast_to(total[32:40, 0:1], (8, LANES)))[0:32, 0:8]
        g_vfe = scale * gamma * (
            by_grad - g_beta / held * off_sums - g_gamma / held * by_norm
        )
        tall0 = jnp.concatenate([g_vfe[:, k : k + 1] for k in range(4)], axis=0)
        tall1 = jnp.concatenate([g_vfe[:, 4:5], g_vfe[:, 5:6], g_vfe[:, 6:7], g_gamma], axis=0)
        tall2 = jnp.concatenate([g_beta, jnp.zeros((96, 1), F32)], axis=0)
        lane = lane_of((LANES, LANES))
        tall = jnp.where(lane == 0, tall0, 0.0) + jnp.where(lane == 1, tall1, 0.0) + jnp.where(lane == 2, tall2, 0.0)
        head = jnp.transpose(tall)[0:8]
        small_grad[0:8, :] = small_grad[0:8, :] + head

    ship_end()
    gradient[0:SMALL, :] = gradient[0:SMALL, :] + small_grad[...]

    @pl.when(me > 0)
    def _():
        for s in range(2):
            note(s, me, sibling).wait_send()

    for k in range(1, n):
        sender = lax.rem(me + n - k, n)
        remote(loss_mine, loss_all.at[sender], sem_ls.at[k], sem_lr.at[sender], sender).wait_recv()
    loss_all[me] = loss_mine[...]
    total = loss_all[0]
    for d in range(1, n):
        total += loss_all[d]
    loss_out[...] = total
    for k in range(1, n):
        loss_copy(k).wait_send()


def train(n, rows_dev, row_count, bases, cells, feature, stat, middle_out, labels, boxes, points, counts, small, pooled, first_out):
    shape = jax.ShapeDtypeStruct
    dma = pltpu.SemaphoreType.DMA
    voxels = feature.shape[0]
    row = (LANES, LANES)
    padded = ceil_to(rows_dev, 8)
    pieces = len(shard_pieces(n, rows_dev))
    fours = n // 4
    return pl.pallas_call(
        functools.partial(conv_kernel, n, rows_dev, row_count),
        name="train",
        out_shape=(
            shape((rows_dev, LANES), F32),
            shape((8, LANES), F32),
        ),
        in_specs=[smem()] + [vmem()] * 4 + [anywhere()] * 11 + [vmem()] * 3 + [anywhere()],
        out_specs=(vmem(),) * 2,
        scratch_shapes=[
            pltpu.VMEM((A_ROWS, LANES), F32),
            pltpu.VMEM((B_ROWS, LANES), F32),
            pltpu.VMEM((n, padded, LANES), F32),
            pltpu.VMEM((n // 2, padded, LANES), F32),
            pltpu.VMEM((n // 2, padded, LANES), F32),
            pltpu.VMEM((fours, padded, LANES), F32),
            pltpu.VMEM((voxels, LANES), F32),
            pltpu.VMEM((NOTE_A, LANES), F32),
            pltpu.VMEM((NOTE_B, LANES), F32),
            pltpu.VMEM((n // 2, NOTE_A, LANES), F32),
            pltpu.VMEM((n // 2, NOTE_B, LANES), F32),
            pltpu.VMEM((88, LANES), F32),
            pltpu.VMEM((SMALL, LANES), F32),
            *[pltpu.VMEM(middle_out[a].shape, BF16) for a in (2, 3, 4, 7, 8)],
            dma((8,)),
            pltpu.VMEM((19 * LANES, 768), BF16),
            pltpu.VMEM((19 * LANES, 768), BF16),
            pltpu.VMEM((19 * LANES, 768), BF16),
            pltpu.VMEM((GRID, 256), F32),
            pltpu.VMEM((GRID, 256), F32),
            pltpu.VMEM((GRID, 256), F32),
            pltpu.VMEM((GRID, 256), F32),
            pltpu.VMEM((voxels, ZD * C2), BF16),
            pltpu.VMEM((512, 768), F32),
            pltpu.VMEM((256, 384), F32),
            pltpu.VMEM((256, 384), F32),
            pltpu.VMEM((row_count, 2, LANES), jnp.int32),
            pltpu.VMEM((row_count, 16, LANES), F32),
            pltpu.VMEM((2, 16, GRID), BF16),
            pltpu.VMEM((8, LANES), F32),
            pltpu.VMEM((n, 8, LANES), F32),
            pltpu.VMEM(row, F32),
            pltpu.VMEM(row, F32),
            pltpu.VMEM(row, F32),
            pltpu.VMEM(row, F32),
            pltpu.VMEM((6,) + row, BF16),
            pltpu.VMEM((6,) + row, BF16),
            pltpu.VMEM((6,) + row, BF16),
            pltpu.VMEM((6,) + row, BF16),
            pltpu.VMEM((LANES, 256), BF16),
            pltpu.VMEM((LANES, 256), BF16),
            pltpu.VMEM((LANES, 256), BF16),
            pltpu.VMEM((LANES, 256), BF16),
            dma((16,)), dma((2,)), dma((2,)), dma((12,)), dma((12,)), dma((2,)), dma((2,)), dma((n,)), dma((n,)),
            dma((pieces,)), dma((pieces,)), dma((pieces,)), dma((pieces,)),
            dma((pieces,)), dma((5 * fours,)), dma((8,)), dma((2,)), dma((n // 2,)), dma((n // 2,)),
        ],
        compiler_params=pltpu.CompilerParams(
            collective_id=2, has_side_effects=True, vmem_limit_bytes=63 << 20
        ),
    )(bases, cells, feature, stat, *middle_out, labels, boxes, points, counts, small, pooled, first_out)


def adam_outer(gradient, weight, moment, second, momentum):
    moment = FIRST_DECAY * moment + (1.0 - FIRST_DECAY) * gradient
    second = SECOND_DECAY * second + (1.0 - SECOND_DECAY) * gradient * gradient
    moment_fix = moment / (1.0 - FIRST_DECAY**STEP)
    second_fix = second / (1.0 - SECOND_DECAY**STEP)
    inner_weight = weight - INNER_RATE * (
        moment_fix / (jnp.sqrt(second_fix) + ADAM_EPSILON) + WEIGHT_DECAY * weight
    )
    inner_step = weight - inner_weight
    momentum = OUTER_MOMENT * momentum + inner_step
    updated = weight - OUTER_RATE * (inner_step + OUTER_MOMENT * momentum)
    return (moment, second, momentum, updated)


def update_kernel(
    gradient, weight, moment, second, momentum, loss, stat,
    moment_out, second_out, momentum_out, weight_out, loss_out, positives_out,
    grad, held, outs, sem_in, sem_out,
):
    sources = (weight, moment, second, momentum)
    targets = (moment_out, second_out, momentum_out, weight_out)
    rows = grad.shape[0]
    steps = 4
    marks = [s * rows // steps // 8 * 8 for s in range(steps)] + [rows]
    loads, stores = [], []
    for s in range(steps):
        window = pl.ds(marks[s], marks[s + 1] - marks[s])
        loads.append([
            pltpu.make_async_copy(source.at[window], target.at[window], sem_in.at[5 * s + a])
            for a, (source, target) in enumerate(
                [(gradient, grad)] + [(source, held.at[a]) for a, source in enumerate(sources)]
            )
        ])
        for load in loads[-1]:
            load.start()
    loss_out[0] = loss[0, 0]
    positives_out[0] = stat[0, 3]
    for s in range(steps):
        part = slice(marks[s], marks[s + 1])
        window = pl.ds(marks[s], marks[s + 1] - marks[s])
        for load in loads[s]:
            load.wait()
        values = adam_outer(grad[part, :], held[0, part, :], held[1, part, :], held[2, part, :], held[3, part, :])
        for a, value in enumerate(values):
            outs[a, part, :] = value
            store = pltpu.make_async_copy(outs.at[a, window], targets[a].at[window], sem_out.at[4 * s + a])
            store.start()
            stores.append(store)
    for store in stores:
        store.wait()


def update(gradient, held, loss, stat):
    shape = jax.ShapeDtypeStruct
    rows = gradient.shape[0]
    dma = pltpu.SemaphoreType.DMA
    return pl.pallas_call(
        update_kernel,
        name="update",
        out_shape=(shape(gradient.shape, F32),) * 4 + (shape((1,), F32),) * 2,
        in_specs=[anywhere()] * 5 + [vmem()] * 2,
        out_specs=(anywhere(),) * 4 + (smem(),) * 2,
        scratch_shapes=[
            pltpu.VMEM((rows, LANES), F32),
            pltpu.VMEM((4, rows, LANES), F32),
            pltpu.VMEM((4, rows, LANES), F32),
            dma((20,)),
            dma((16,)),
        ],
        compiler_params=pltpu.CompilerParams(vmem_limit_bytes=60 << 20),
    )(gradient, *held, loss, stat)


def shards(
    points, point_counts, voxel_cells, anchor_labels, box_targets, weights, adam_m, adam_v, outer_momentum
):
    n = lax.axis_size("tile")
    rows = weights.shape[0] // LANES
    row_count = anchor_labels.shape[1]
    held = [x.reshape(rows, LANES) for x in (weights, adam_m, adam_v, outer_momentum)]
    counts = point_counts.reshape(1, -1)
    cells = voxel_cells.reshape(1, -1)
    wall, small, stat, first_out, pooled, feature, bases = front(
        n, points, counts, cells, anchor_labels, held[0]
    )
    ready = middle(n, rows, row_count, bases, cells, feature, wall)
    gradient, loss = train(
        n, rows, row_count, bases, cells, feature, stat, ready, anchor_labels, box_targets,
        points, counts, small, pooled, first_out,
    )
    *outs, loss_sum, positives = update(gradient, held, loss, stat)
    moment, second, momentum, updated = [x.reshape(weights.shape) for x in outs]
    return (moment, second, momentum, updated, loss_sum, positives)


def solution(mesh):
    split = ("group", "tile")
    in_specs = (
        P(None, None, split), P(split), P(split), P(None, split, None), P(None, split, None),
        P(split), P(split), P(split), P(split),
    )
    out_specs = (P(split), P(split), P(split), P(split), P("group"), P("group"))
    return jax.shard_map(shards, mesh=mesh, in_specs=in_specs, out_specs=out_specs, check_vma=False)
```

```python
import functools
import math

import jax
import jax.numpy as jnp
from jax import lax
from jax.experimental import pallas as pl
from jax.experimental.pallas import tpu as pltpu
from jax.sharding import PartitionSpec as P

MESH = pl.DeviceIdType.MESH
F32 = jnp.float32
BF16 = jnp.bfloat16
HIGH = lax.Precision.HIGHEST

C1, C2, CM, CR1, CR2, CR3, ANCH, ZD = 32, 128, 64, 128, 128, 256, 2, 4
H_SCENE = 200
STEP = 10
LANES = 128
NORM_EPSILON = 1e-05
INNER_RATE = 0.05
FIRST_DECAY = 0.9
SECOND_DECAY = 0.999
ADAM_EPSILON = 1e-08
WEIGHT_DECAY = 0.01
OUTER_RATE = 0.7
OUTER_MOMENT = 0.9
FOCAL_ALPHA = 0.25
HUBER_BETA = 1.0 / 9.0

SMALL = 80
FC_ROW, FC_LANE = 2, 32
BIAS_ROWS = (1795, 2947, 2948, 4100, 4101, 6405, 6406, 6407, 6439)
RUN_A = (2, 32)
RUN_B = (1795, 96)
A_MID = 65
B_ONE, B_TWO, B_THREE, B_HEAD = 0, 1153, 2306, 4612
PAIRS_OF = tuple((a, b) for a in range(7) for b in range(a, 7))
DIAGONAL = tuple(r for r, (a, b) in enumerate(PAIRS_OF) if a == b)
CHUNK = 256


def vmem():
    return pl.BlockSpec(memory_space=pltpu.VMEM)


def anywhere():
    return pl.BlockSpec(memory_space=pl.ANY)


def smem():
    return pl.BlockSpec(memory_space=pltpu.SMEM)


def ceil_to(value, step):
    return (value + step - 1) // step * step


def sigmoid(value):
    return 0.5 * jnp.tanh(0.5 * value) + 0.5


def slope(value):
    s = sigmoid(value)
    return s * (1.0 + value * (1.0 - s))


def half_silu(half):
    return half * (1.0 + jnp.tanh(half))


def half_slope(half):
    t = jnp.tanh(half)
    return (1.0 + t) * (1.0 + half * (1.0 - t))


def nt(a, b, precision=None):
    return lax.dot_general(a, b, (((1,), (1,)), ((), ())), precision=precision, preferred_element_type=F32)


def tn(a, b, precision=None):
    return lax.dot_general(a, b, (((0,), (0,)), ((), ())), precision=precision, preferred_element_type=F32)


def nn(a, b, precision=None):
    return lax.dot_general(a, b, (((1,), (0,)), ((), ())), precision=precision, preferred_element_type=F32)


def lane_of(shape):
    return lax.broadcasted_iota(jnp.int32, shape, len(shape) - 1)


def row_of(shape):
    return lax.broadcasted_iota(jnp.int32, shape, len(shape) - 2)


def enter(n, me, between=None):
    sem = pltpu.get_barrier_semaphore()

    def greet(k, carry):
        pl.semaphore_signal(
            sem, inc=1, device_id={"tile": lax.rem(me + k, n)}, device_id_type=MESH
        )
        return carry

    lax.fori_loop(1, n, greet, 0)
    if between is not None:
        between()
    pl.semaphore_wait(sem, n - 1)


def remote(src, dst, send, recv, peer):
    return pltpu.make_async_remote_copy(
        src_ref=src,
        dst_ref=dst,
        send_sem=send,
        recv_sem=recv,
        device_id={"tile": peer},
        device_id_type=MESH,
    )


def even_first():
    out = row_of((LANES, LANES))
    source = jnp.where(out < 64, 2 * out, 2 * out - 127)
    return lane_of((LANES, LANES)) == source


def first_layer(small_ref):
    turned = jnp.transpose(small_ref[0:LANES_PAD, :])
    columns = [turned[(k % 4) * 32 : (k % 4) * 32 + 32, k // 4 : k // 4 + 1] for k in range(7)]
    return columns, turned[96:128, 1:2], turned[0:32, 2:3]


LANES_PAD = 8


def voxel_rows(small_ref):
    here, after = small_ref[2:74, :], small_ref[3:75, :]
    mixed = jnp.where(lane_of((72, LANES)) >= FC_LANE, here, after)
    return pltpu.roll(mixed, LANES - FC_LANE, axis=1)


def layout(n, row_count):
    first = lax.axis_index("tile") * row_count
    ahead = (first // H_SCENE + 1) * H_SCENE - first
    split = jnp.where(ahead < row_count, 1, 0)
    edge = jnp.where(ahead < row_count, ahead, row_count)
    top = jnp.where(lax.rem(first, H_SCENE) != 0, 1, 0)
    last = first + row_count
    bottom = jnp.where((lax.rem(last, H_SCENE) != 0) & (last < n * row_count), 1, 0)
    return edge, split, top, bottom


def place_ok(place, edge, split, row_count):
    return (place >= 1) & (place <= row_count + split) & ((place != edge + 1) | (split == 0))


def place_row(place, edge, row_count):
    row = jnp.where(place <= edge, place - 1, place - 2)
    return jnp.clip(row, 0, row_count - 1)


PITCH = 136


def voxel_bases(cells, n, row_count, columns):
    edge, split, _, _ = layout(n, row_count)
    local = lax.rem(cells, row_count * columns * ZD)
    row = local // (columns * ZD)
    column = lax.rem(local, columns * ZD) // ZD
    place = row + 1 + jnp.where((row >= edge) & (split == 1), 1, 0)
    return (place - 1) * PITCH + column + 7


def linear_row(wide, points, p):
    value = wide[0] * points[0, pl.ds(p, 1), :]
    for k in range(1, 7):
        value += wide[k] * points[k, pl.ds(p, 1), :]
    return value


def local_moments(points, counts, labels_ref, sums, message):
    slots, voxels = points.shape[1:]
    inside = row_of((slots, voxels)) < counts

    def folded(value):
        total = value[:, 0:LANES]
        for c in range(1, voxels // LANES):
            total = total + value[:, c * LANES : (c + 1) * LANES]
        return jnp.sum(total, axis=0, keepdims=True)

    def whole(row):
        return jnp.sum(row, axis=1, keepdims=True)

    held = whole(folded(inside.astype(F32)))
    masked = [jnp.where(inside, points[k], 0.0) for k in range(7)]
    rows = [folded(value) for value in masked]
    means = [whole(row) / held for row in rows]
    centred = [jnp.where(inside, points[k] - means[k], 0.0) for k in range(7)]
    for r, (a, b) in enumerate(PAIRS_OF):
        sums[0, r : r + 1, :] = folded(centred[a] * centred[b])
        sums[1, r : r + 1, :] = rows[a]
        sums[2, r : r + 1, :] = rows[b]
    spare = len(PAIRS_OF)
    for c in range(3):
        sums[c, spare:LANES, :] = jnp.zeros((LANES - spare, LANES), F32)
    lane = lane_of((LANES, LANES))
    columns = jnp.zeros((LANES, LANES), F32)
    for c in range(3):
        columns = jnp.where(lane == c, jnp.sum(sums[c], axis=1, keepdims=True), columns)
    positives = jnp.zeros((1, 1), F32)
    for a in range(ANCH):
        positives += whole(jnp.sum((labels_ref[a] == 1).astype(F32), axis=0, keepdims=True))
    packed = jnp.transpose(columns)[0:8]
    row = row_of((8, LANES))
    packed = jnp.where(row == 3, held, packed)
    message[...] = jnp.where(row == 4, positives, packed)


def joint_moments(n, messages):
    total = messages[0]
    for d in range(1, n):
        total += messages[d]
    held = total[3:4]
    mean_a, mean_b = total[1:2] / held, total[2:3] / held
    product = total[0:1]
    for d in range(n):
        held_d = messages[d, 3:4, :]
        product += held_d * (messages[d, 1:2, :] / held_d - mean_a) * (messages[d, 2:3, :] / held_d - mean_b)
    return mean_a, product, held, total[4:5]


def channel_statistics(columns, mean_row, product, held):
    lane = lane_of((32, LANES))
    once, twice = jnp.zeros((32, LANES), F32), jnp.zeros((32, LANES), F32)
    for r, (a, b) in enumerate(PAIRS_OF):
        if a == b:
            once = jnp.where(lane == r, columns[a], once)
        twice = jnp.where(lane == r, (1.0 if a == b else 2.0) * columns[a] * columns[b], twice)
    mean = jnp.sum(once * mean_row, axis=1, keepdims=True)
    variance = jnp.sum(twice * (product / held), axis=1, keepdims=True)
    return mean, lax.rsqrt(variance + NORM_EPSILON)


def front_kernel(
    n, points, counts_ref, cells_ref, labels_ref, shard_ref,
    wall, small, stat, first_out, pooled_out, feature, bases,
    own, sums, mine, messages, my_bias, biases,
    sem_small_s, sem_small_r, sem_msg_s, sem_msg_r, sem_b_s, sem_b_r, sem_w_s, sem_w_r, sem_f_s, sem_e_s,
):
    me = lax.axis_index("tile")
    rows = shard_ref.shape[0]
    slots, voxels = points.shape[1:]
    sibling = me + 1 - 2 * lax.rem(me, 2)
    half = n // 2
    counts = counts_ref[...]

    def prepare():
        local_moments(points, counts, labels_ref, sums, mine)
        bases[...] = voxel_bases(cells_ref[...], n, labels_ref.shape[1], labels_ref.shape[2])
        own[...] = jnp.zeros_like(own)
        own[0:rows, :] = shard_ref[...].astype(BF16)
        for a, row in enumerate(BIAS_ROWS):
            owner, place = row // rows, row % rows
            my_bias[a : a + 1, :] = jnp.where(me == owner, shard_ref[place : place + 1, :], 0.0)
        for a in range(len(BIAS_ROWS), 16):
            my_bias[a : a + 1, :] = jnp.zeros((1, LANES), F32)

    enter(n, me, prepare)

    def message(k):
        return remote(mine, messages.at[me], sem_msg_s.at[k], sem_msg_r.at[me], lax.rem(me + k, n))

    def bias_message(k):
        return remote(my_bias, biases.at[me], sem_b_s.at[k], sem_b_r.at[me], lax.rem(me + k, n))

    def small_copy(k):
        return remote(small, small, sem_small_s.at[k], sem_small_r.at[0], lax.rem(me + k, n))

    def shard_copy(k):
        return remote(own, wall.at[me], sem_w_s.at[k], sem_w_r.at[me], lax.rem(me + 2 * k, n))

    for k in range(1, n):
        message(k).start()

    @pl.when(me == 0)
    def _():
        small[...] = shard_ref[0:SMALL, :]

        def send(k, carry):
            small_copy(k).start()
            return carry

        lax.fori_loop(1, n, send, 0)

    for k in range(1, n):
        bias_message(k).start()
    line = me // 2
    if n == 8:
        inner = (line == 1) | (line == 2)
        toward = jnp.where(line == 2, 2, -2)
        turn = jnp.where(line == 0, 2, -2)

        def own_copy(step, k):
            return remote(own, wall.at[me], sem_w_s.at[k], sem_w_r.at[me], me + step)

        @pl.when(inner)
        def _():
            own_copy(-toward, 1).start()
            own_copy(toward, 2).start()

        @pl.when(jnp.logical_not(inner))
        def _():
            own_copy(turn, 1).start()
            own_copy(2 * turn, 2).start()

    else:
        for k in range(1, half):
            shard_copy(k).start()

    def arrived(source):
        remote(own, wall.at[source], sem_w_s.at[0], sem_w_r.at[source], sibling).wait_recv()

    def pass_on(source, k, peer, sem):
        return remote(wall.at[source], wall.at[source], sem.at[k], sem_w_r.at[source], peer)

    def relay(step):
        if n == 8:

            @pl.when(inner)
            def _():
                source = me - (step + 1) * toward
                arrived(source)
                pass_on(source, step, me + toward, sem_e_s).start()
                pass_on(source, step + 1, sibling, sem_f_s).start()

    to_sibling = remote(own, wall.at[me], sem_w_s.at[0], sem_w_r.at[me], sibling)
    to_sibling.start()
    wall[me] = own[...]
    messages[me] = mine[...]
    biases[me] = my_bias[...]

    @pl.when(me > 0)
    def _():
        small_copy(0).wait_recv()

    columns, gamma, beta = first_layer(small)
    order = even_first()
    rows_fc = voxel_rows(small)
    kernel_t = (0.5 * nt(order.astype(BF16), rows_fc[0:64, :].astype(BF16))).astype(BF16)
    bias = 0.5 * jnp.sum(jnp.where(order, rows_fc[64:65, :], 0.0), axis=1, keepdims=True)
    for k in range(1, n):
        sender = lax.rem(me + n - k, n)
        remote(mine, messages.at[sender], sem_msg_s.at[k], sem_msg_r.at[sender], sender).wait_recv()
    mean_row, product, held, positives = joint_moments(n, messages)
    mean, inverse = channel_statistics(columns, mean_row, product, held)
    lane, row = lane_of((32, LANES)), row_of((32, LANES))
    columns_out = jnp.where(lane == 0, mean, 0.0)
    columns_out = jnp.where(lane == 1, inverse, columns_out)
    columns_out = jnp.where(lane == 2, held, columns_out)
    columns_out = jnp.where(lane == 3, positives, columns_out)
    for k, r in enumerate(DIAGONAL):
        columns_out = jnp.where((lane == 4) & (row == k), mean_row[:, r : r + 1], columns_out)
    stat[0:32, :] = columns_out

    half_gamma, half_beta = 0.5 * gamma, 0.5 * beta
    for c in range(voxels // CHUNK):
        part = slice(c * CHUNK, (c + 1) * CHUNK)
        wide = [jnp.broadcast_to(column, (32, CHUNK)) for column in columns]
        held_c = counts[:, part]
        view = points.at[:, :, part]

        def pass_c(p, pooled, wide=wide, held_c=held_c, view=view, part=part):
            half_act = half_gamma * ((linear_row(wide, view, p) - mean) * inverse) + half_beta
            out = jnp.where(p < held_c, half_silu(half_act), 0.0)
            first_out[p, :, part] = out.astype(BF16)
            return pooled + out

        pooled = lax.fori_loop(0, slots, pass_c, jnp.zeros((32, CHUNK), F32), unroll=5)
        pooled = (pooled / held_c.astype(F32)).astype(BF16)
        pooled_out[:, part] = pooled
        fixed = nn(kernel_t[:, 32:64], pooled) + bias
        if c < 2:
            relay(c)

        def pass_d(p, total, fixed=fixed, held_c=held_c, part=part):
            half_inner = nn(kernel_t[:, 0:32], first_out[p, :, part]) + fixed
            return total + jnp.where(p < held_c, half_silu(half_inner), 0.0)

        total = lax.fori_loop(0, slots, pass_d, jnp.zeros((LANES, CHUNK), F32), unroll=7)
        feature[part, :] = jnp.transpose(total / held_c.astype(F32))

    for step in range(voxels // CHUNK, 2):
        relay(step)
    if n == 8:

        @pl.when(inner)
        def _():
            source = me + toward
            arrived(source)
            pass_on(source, 3, sibling, sem_f_s).start()

        @pl.when(jnp.logical_not(inner))
        def _():
            for k in range(1, 4):
                arrived(me + k * turn)
                pass_on(me + k * turn, k, sibling, sem_f_s).start()

    else:
        for k in range(1, half):
            source = lax.rem(me + n - 2 * k, n)
            arrived(source)
            pass_on(source, k, sibling, sem_f_s).start()
    for k in range(1, n):
        sender = lax.rem(me + n - k, n)
        remote(my_bias, biases.at[sender], sem_b_s.at[k], sem_b_r.at[sender], sender).wait_recv()
    total = biases[0]
    for d in range(1, n):
        total += biases[d]
    stat[32:48, :] = total
    for k in range(half):
        arrived(lax.rem(sibling + n - 2 * k, n))
    for k in range(1, half):
        pass_on(me, k, sibling, sem_f_s).wait_send()
    if n == 8:
        for k in (1, 2):
            own_copy(turn, k).wait_send()

        @pl.when(inner)
        def _():
            for k in range(2):
                pass_on(me, k, sibling, sem_e_s).wait_send()

    else:
        for k in range(1, half):
            shard_copy(k).wait_send()
    to_sibling.wait_send()
    for k in range(1, n):
        message(k).wait_send()
        bias_message(k).wait_send()

    @pl.when(me == 0)
    def _():
        def done(k, carry):
            small_copy(k).wait_send()
            return carry

        lax.fori_loop(1, n, done, 0)


def front(n, points, counts, cells, labels, shard):
    slots, voxels = points.shape[1:]
    rows = shard.shape[0]
    padded = ceil_to(rows, 16)
    shape = jax.ShapeDtypeStruct
    dma = pltpu.SemaphoreType.DMA
    return pl.pallas_call(
        functools.partial(front_kernel, n),
        name="front",
        out_shape=(
            shape((n, padded, LANES), BF16),
            shape((SMALL, LANES), F32),
            shape((48, LANES), F32),
            shape((slots, 32, voxels), BF16),
            shape((32, voxels), BF16),
            shape((voxels, LANES), F32),
            shape((1, voxels), jnp.int32),
        ),
        in_specs=[vmem()] * 5,
        out_specs=(vmem(),) * 7,
        scratch_shapes=[
            pltpu.VMEM((padded, LANES), BF16),
            pltpu.VMEM((3, LANES, LANES), F32),
            pltpu.VMEM((8, LANES), F32),
            pltpu.VMEM((n, 8, LANES), F32),
            pltpu.VMEM((16, LANES), F32),
            pltpu.VMEM((n, 16, LANES), F32),
            dma((n,)), dma((1,)), dma((n,)), dma((n,)), dma((n,)), dma((n,)), dma((n,)), dma((n,)), dma((n,)), dma((2,)),
        ],
        compiler_params=pltpu.CompilerParams(
            collective_id=1, has_side_effects=True, vmem_limit_bytes=56 << 20
        ),
    )(points, counts, cells, labels, shard)


def flat_pieces(rows, slot):
    begin, end = slot * rows, (slot + 1) * rows
    spans = ((0, 67, None, 0), (67, 1795, "a", 2), (1795, 1796, "both", 0), (1796, 6440, "b", 1795), (6440, 1 << 30, None, 0))
    pieces = []
    for low, high, run, shift in spans:
        first, last = max(begin, low), min(end, high)
        if first < last:
            pieces.append((first - begin, last - first, run, first - shift))
    return pieces


def flat_slot(slot, rows, low, high, grad_a, grad_b, out_ref):
    def realigned(ref, start, count, lane):
        here, before = ref[pl.ds(start, count), :], ref[pl.ds(start - 1, count), :]
        mixed = jnp.where(lane_of((count, LANES)) >= LANES - lane, before, here)
        return pltpu.roll(mixed, lane, axis=1)

    for row, count, run, start in flat_pieces(rows, slot):
        first, last = max(row, low), min(row + count, high)
        if first >= last:
            continue
        start, row, count = start + first - row, first, last - first
        if run is None:
            value = jnp.zeros((count, LANES), F32)
        elif run == "a":
            value = realigned(grad_a, start, count, 32)
        elif run == "b":
            value = realigned(grad_b, start, count, 96)
        else:
            lane = lane_of((1, LANES))
            part_a = jnp.where(lane >= 96, grad_a[1792:1793, :], grad_a[1793:1794, :])
            part_b = jnp.where(lane >= 32, 0.0, grad_b[0:1, :])
            part_a = pltpu.roll(jnp.broadcast_to(part_a, (8, LANES)), 32, axis=1)
            part_b = pltpu.roll(jnp.broadcast_to(part_b, (8, LANES)), 96, axis=1)
            value = jnp.where(lane < 96, part_a[0:1], part_b[0:1])
        out_ref[row : row + count, :] = value


class Piece:
    def __init__(self, chip, row, count, stage, order):
        self.chip, self.group, self.side = chip, chip // 2, chip % 2
        self.row, self.count, self.stage, self.order = row, count, stage, order
        self.rows = pl.ds(row, count)


def shard_pieces(n, rows):
    padded = ceil_to(rows, 8)
    pieces = []
    for chip in range(n // 2):
        first = 2 * chip * rows
        cut = min(ceil_to(min(max(1796 - first, 0), rows), 8), padded)
        spans = [(0, cut)] if cut else []
        if cut >= 400:
            marks = [ceil_to(cut * k // 4, 8) for k in range(4)] + [cut]
            spans = list(zip(marks[:-1], marks[1:]))
        for order, (low, high) in enumerate(spans):
            pieces.append(Piece(chip, low, high - low, 3, order))
        if cut < padded:
            begin = first + cut
            stage = 0 if begin >= 4102 else 1 if begin >= 2949 else 2
            pieces.append(Piece(chip, cut, padded - cut, stage, 4))
    return pieces


def z_columns(cells_row):
    z = lax.rem(cells_row, ZD).astype(F32)
    return jnp.transpose(jnp.broadcast_to(z, (8, z.shape[1])))[:, 0:1]


def spread_z(feature, z_column, out_ref):
    for z in range(ZD):
        out_ref[:, z * C2 : (z + 1) * C2] = jnp.where(z_column == z, feature, 0.0).astype(BF16)


def middle_kernel(
    n, rows, row_count,
    bases, cells_row, feature, wall,
    pre, *refs,
):
    outs, kept, (flat, run, spread, parts0, parts1, parts2, sum0, sum1, sum2, sem) = refs[:8], refs[8:16], refs[16:]
    w_mid, f_one, f_two, f_three, d_one, d_two, d_three, head_t = kept
    stores = [pltpu.make_async_copy(kept[a], outs[a], sem.at[a]) for a in range(8)]
    voxels = feature.shape[0]
    columns = LANES
    parts, sums = (parts0, parts1, parts2), (sum0, sum1, sum2)
    for s in range(n):
        flat[s * rows : s * rows + wall.shape[1], :] = wall[s].astype(F32)

    def aligned(begin, start, count):
        row, lane = begin
        here = flat[pl.ds(row + start, count), :]
        after = flat[pl.ds(row + start + 1, count), :]
        mixed = jnp.where(lane_of((count, LANES)) >= lane, here, after)
        return pltpu.roll(mixed, LANES - lane, axis=1)

    def zero_half(ref, row, column, height, width):
        ref[row : row + height, column : column + width] = jnp.zeros((height, width), BF16)

    for begin, f_ref, d_ref in ((B_ONE, f_one, d_one), (B_TWO, f_two, d_two)):
        for j in range(3):
            for e in range(2):
                outside = 3 if e == 0 else 0
                zero_half(f_ref, outside * 384 + j * LANES, e * LANES, LANES, LANES)
                zero_half(d_ref, e * LANES, outside * 384 + j * LANES, LANES, LANES)

        def tap(i, j, begin=begin, f_ref=f_ref, d_ref=d_ref):
            block = aligned(RUN_B, begin + (i * 3 + j) * LANES, LANES).astype(BF16)
            for e in range(2):
                t = i + e
                f_ref[t * 384 + j * LANES : t * 384 + (j + 1) * LANES, e * LANES : (e + 1) * LANES] = block
                t = 2 + e - i
                lane = t * 384 + (2 - j) * LANES
                d_ref[e * LANES : (e + 1) * LANES, lane : lane + LANES] = block

        for i in range(3):
            for j in range(3):
                tap(i, j)
        for a in (1, 4) if begin == B_ONE else (2, 5):
            stores[a].start()
    for j in range(3):
        for e in range(2):
            outside = 3 if e == 0 else 0
            zero_half(d_three, e * LANES, outside * 768 + j * 256, LANES, 256)
    for i in range(3):
        for j in range(3):
            run[...] = aligned(RUN_B, B_THREE + (i * 3 + j) * 256, 256)
            for h in range(2):
                block = run[pl.ds(h, LANES, 2), :].astype(BF16)
                row = (i * 3 + j) * LANES
                f_three[row : row + LANES, h * LANES : (h + 1) * LANES] = block
                for e in range(2):
                    lane = (2 + e - i) * 768 + (2 - j) * 256 + h * LANES
                    d_three[e * LANES : (e + 1) * LANES, lane : lane + LANES] = block
    head_rows = aligned(RUN_B, B_HEAD, 32).astype(BF16)
    chosen = nn(eighths(), head_rows)
    chosen = jnp.where(same_eighth(), chosen, 0.0).astype(BF16)
    head_t[...] = nt(fold16(), chosen).astype(BF16)
    for a in (3, 6, 7):
        stores[a].start()

    low = lane_of((64, LANES)) < 64
    for ij in range(9):
        taps = [aligned(RUN_A, A_MID + (t * 9 + ij) * 64, 64) for t in range(3)]
        turned = [pltpu.roll(tap, 64, axis=1) for tap in taps]
        none = jnp.zeros((64, LANES), F32)
        for z in range(ZD):
            first, second = z + 1, z - 1
            a, a_t = (taps[first], turned[first]) if first < 3 else (none, none)
            b, b_t = (taps[second], turned[second]) if second >= 0 else (none, none)
            lanes = slice(ij * LANES, (ij + 1) * LANES)
            w_mid[z * C2 : z * C2 + 64, lanes] = jnp.where(low, a, b_t).astype(BF16)
            w_mid[z * C2 + 64 : (z + 1) * C2, lanes] = jnp.where(low, a_t, b).astype(BF16)

    stores[0].start()
    spread_z(feature[...], z_columns(cells_row[...]), spread)
    for i in range(3):
        product = nn(spread[...], w_mid[:, i * 384 : (i + 1) * 384])
        for j in range(3):
            parts[i][pl.ds(2 - j, voxels, 4), :] = product[:, j * LANES : (j + 1) * LANES]
        sums[i][...] = jnp.zeros_like(sums[i])

    def add(v, carry):
        base = bases[0, v]
        for i in range(3):
            spot = pl.ds(base + (2 - i) * PITCH, 3)
            sums[i][spot, :] = sums[i][spot, :] + parts[i][pl.ds(4 * v, 3), :]
        return carry

    lax.fori_loop(0, voxels, add, 0, unroll=8)

    def gather(p, carry):
        spot = pl.ds(pl.multiple_of(p * PITCH + 8, 8), columns)
        pre[p] = sum0[spot, :] + sum1[spot, :] + sum2[spot, :]
        return carry

    lax.fori_loop(0, row_count + 5, gather, 0)
    for store in stores:
        store.wait()


def eighths():
    return (row_of((CR3, 32)) // 8 == lane_of((CR3, 32))).astype(F32).astype(BF16)


def same_eighth():
    return lane_of((CR3, LANES)) // 16 == lax.rem(row_of((CR3, LANES)), 8)


def fold16():
    return (lax.rem(lane_of((16, LANES)), 16) == row_of((16, LANES))).astype(F32).astype(BF16)


def middle(n, rows, row_count, bases, cells, feature, wall):
    shape = jax.ShapeDtypeStruct
    voxels = feature.shape[0]
    cells_all = (row_count + 6) * PITCH
    return pl.pallas_call(
        functools.partial(middle_kernel, n, rows, row_count),
        name="middle",
        out_shape=(
            shape((row_count + 5, LANES, LANES), F32),
            shape((512, 1152), BF16),
            shape((1536, 256), BF16),
            shape((1536, 256), BF16),
            shape((1152, 256), BF16),
            shape((256, 1536), BF16),
            shape((256, 1536), BF16),
            shape((256, 3072), BF16),
            shape((16, 256), BF16),
        ),
        in_specs=[smem(), vmem(), vmem(), vmem()],
        out_specs=(vmem(),) + (anywhere(),) * 8,
        scratch_shapes=[
            pltpu.VMEM((512, 1152), BF16),
            pltpu.VMEM((1536, 256), BF16),
            pltpu.VMEM((1536, 256), BF16),
            pltpu.VMEM((1152, 256), BF16),
            pltpu.VMEM((256, 1536), BF16),
            pltpu.VMEM((256, 1536), BF16),
            pltpu.VMEM((256, 3072), BF16),
            pltpu.VMEM((16, 256), BF16),
            pltpu.VMEM((n * rows + 24, LANES), F32),
            pltpu.VMEM((256, LANES), F32),
            pltpu.VMEM((voxels, ZD * C2), BF16),
            pltpu.VMEM((voxels * 4, LANES), F32),
            pltpu.VMEM((voxels * 4, LANES), F32),
            pltpu.VMEM((voxels * 4, LANES), F32),
            pltpu.VMEM((cells_all, LANES), F32),
            pltpu.VMEM((cells_all, LANES), F32),
            pltpu.VMEM((cells_all, LANES), F32),
            pltpu.SemaphoreType.DMA((8,)),
        ],
        compiler_params=pltpu.CompilerParams(vmem_limit_bytes=56 << 20),
    )(bases, cells, feature, wall)


NOTE_A, NOTE_B = 72, 40
PAIRS = 18
QB = 9
STEPS = PAIRS // QB
SPAN = QB * LANES
GRID = PAIRS * LANES
A_ROWS, B_ROWS = 1800, 4656


def conv_kernel(
    n, rows_dev, row_count,
    bases, cells_row, feature, stat, pre_in,
    w_mid_h, f_one_h, f_two_h, f_three_h, d_one_h, d_two_h, d_three_h, head_t_h,
    labels_hbm, boxes_hbm, points_hbm, counts_ref, small, pooled_in, first_hbm,
    gradient, loss_out,
    grad_a, grad_b, slots, core_in, chip_in, far_in, grad_feature,
    mine_a, mine_b, notes_a, notes_b, fc_rows, small_grad,
    f_one, f_two, f_three, d_three, head_t, sem_k,
    x_one, x_two, x_three, pre_mid, pre_one, pre_two, back, spread,
    acc0, acc1, acc2,
    labels, boxes, logit_grads, loss_mine, loss_all,
    up_f, down_f, from_up_f, from_down_f, send_up, send_down, from_up, from_down,
    send_up_w, send_down_w, from_up_w, from_down_w,
    sem_t, sem_fs, sem_fr, sem_s, sem_r, sem_ws, sem_wr, sem_ls, sem_lr, sem_cs, sem_cr, sem_zs, sem_zr,
    sem_gs, sem_gr, sem_p, sem_ns, sem_nar, sem_nbr,
):
    me = lax.axis_index("tile")
    edge, split, top, bottom = layout(n, row_count)
    has_up, has_down = me > 0, me < n - 1
    above, below = jnp.maximum(me - 1, 0), jnp.minimum(me + 1, n - 1)
    loads = [pltpu.make_async_copy(labels_hbm.at[a], labels.at[:, a, :], sem_t.at[a]) for a in range(2)]
    loads += [
        pltpu.make_async_copy(boxes_hbm.at[a], boxes.at[:, 2 + a, :], sem_t.at[2 + a]) for a in range(14)
    ]
    for load in loads:
        load.start()
    kernels = (
        (f_one_h, f_one), (f_two_h, f_two), (f_three_h, f_three), (head_t_h, head_t),
        (d_three_h, d_three),
    )
    kernel_loads = [pltpu.make_async_copy(a, b, sem_k.at[i]) for i, (a, b) in enumerate(kernels)]
    for load in kernel_loads:
        load.start()
    enter(n, me)

    pieces = shard_pieces(n, rows_dev)
    core, side, my_group = lax.rem(me, 2), lax.rem(me // 2, 2), me // 4
    sibling, other = me + 1 - 2 * core, me + 2 - 4 * side

    def collects(piece):
        nearer = jnp.where(my_group > piece.group, 0, 1)
        return side == jnp.where(my_group == piece.group, piece.side, nearer)

    def core_copy(i):
        piece = pieces[i]
        return remote(
            slots.at[2 * piece.chip + 1 - core, piece.rows],
            core_in.at[piece.chip, piece.rows],
            sem_cs.at[i], sem_cr.at[i], sibling,
        )

    def chip_copy(i):
        piece = pieces[i]
        return remote(
            slots.at[2 * piece.chip + core, piece.rows],
            chip_in.at[piece.chip, piece.rows],
            sem_zs.at[i], sem_zr.at[i], other,
        )

    def far_copy(i, sender):
        piece = pieces[i]
        return remote(
            slots.at[2 * piece.chip + core, piece.rows],
            far_in.at[sender, piece.rows],
            sem_gs.at[i], sem_gr.at[5 * sender + piece.order], 2 * piece.chip + core,
        )

    def of_stage(stage):
        return [i for i, piece in enumerate(pieces) if piece.stage == stage]

    def ship(stage):
        for i in of_stage(stage):
            piece = pieces[i]
            for s in (2 * piece.chip, 2 * piece.chip + 1):
                flat_slot(s, rows_dev, piece.row, piece.row + piece.count, grad_a, grad_b, slots.at[s])
            core_copy(i).start()

    def ship_on(stage):
        for i in of_stage(stage):
            piece = pieces[i]
            core_copy(i).wait()
            spot = 2 * piece.chip + core
            slots[spot, piece.rows, :] = slots[spot, piece.rows, :] + core_in[piece.chip, piece.rows, :]

            @pl.when(jnp.logical_not(collects(piece)))
            def _(i=i):
                chip_copy(i).start()

    def ship_far(i):
        piece = pieces[i]

        @pl.when(collects(piece))
        def _():
            chip_copy(i).wait_recv()
            spot = 2 * piece.chip + core
            slots[spot, piece.rows, :] = slots[spot, piece.rows, :] + chip_in[piece.chip, piece.rows, :]

        @pl.when(collects(piece) & (my_group != piece.group))
        def _():
            far_copy(i, my_group).start()

    def ship_end():
        for i, piece in enumerate(pieces):
            count = min(piece.count, rows_dev - piece.row)
            taken = pl.ds(piece.row, count)
            here = collects(piece)

            @pl.when(here & (my_group == piece.group))
            def _(i=i, piece=piece, taken=taken):
                gradient[taken, :] = slots[2 * piece.chip + core, taken, :]
                for k in range(1, n // 4):
                    sender = lax.rem(my_group + n // 4 - k, n // 4)
                    far_copy(i, sender).wait_recv()
                    gradient[taken, :] = gradient[taken, :] + far_in[sender, taken, :]

            @pl.when(here & (my_group != piece.group))
            def _(i=i):
                far_copy(i, my_group).wait_send()

            @pl.when(jnp.logical_not(here))
            def _(i=i):
                chip_copy(i).wait_send()

    late = of_stage(3)

    def ok(place):
        return place_ok(place, edge, split, row_count)

    def halo_copies(s, up_src, down_src, up_dst, down_dst, sem_send, sem_recv):
        up = remote(up_src, down_dst, sem_send.at[2 * s], sem_recv.at[2 * s], above)
        down = remote(down_src, up_dst, sem_send.at[2 * s + 1], sem_recv.at[2 * s + 1], below)
        return up, down

    def halo_start(copies):
        up, down = copies

        @pl.when(has_up)
        def _():
            up.start()

        @pl.when(has_down)
        def _():
            down.start()

    def halo_wait(copies):
        up, down = copies

        @pl.when(has_up)
        def _():
            up.wait_send()
            down.wait_recv()

        @pl.when(has_down)
        def _():
            down.wait_send()
            up.wait_recv()

    def thin(s):
        return halo_copies(
            s, send_up.at[s], send_down.at[s], from_up.at[s], from_down.at[s], sem_s, sem_r
        )

    def pick(condition, a, b):
        return jnp.where(condition, a, b)

    column = row_of((LANES, LANES))

    def shifted(value):
        left = jnp.where(column > 0, pltpu.roll(value, 1, axis=0), 0.0)
        right = jnp.where(column < LANES - 1, pltpu.roll(value, LANES - 1, axis=0), 0.0)
        return left.astype(BF16), value.astype(BF16), right.astype(BF16)

    def put(ref, pair, parity, value, part, parts):
        rows = pl.ds(pl.multiple_of(pair * LANES, LANES), LANES)
        width = 3 * parts * LANES
        for j, shift in enumerate(shifted(value)):
            lane = parity * width + (j * parts + part) * LANES
            ref[rows, lane : lane + LANES] = shift

    def edges(parts, up_halo, down_halo):
        rows = []
        for good, halo in (((top == 1) & has_up, up_halo), ((bottom == 1) & has_down, down_halo)):
            pieces = [shifted(pick(good, halo[:, p * LANES : (p + 1) * LANES].astype(F32), 0.0)) for p in range(parts)]
            rows.append(jnp.concatenate([pieces[p][j] for j in range(3) for p in range(parts)], axis=1))
        return rows

    def put_edges(ref, top_row, bottom_row):
        width = top_row.shape[1]
        ref[0:LANES, 0:width] = top_row
        rows = slice(16 * LANES, 17 * LANES)
        ref[rows, width : 2 * width] = pick(split == 1, ref[rows, width : 2 * width], bottom_row)
        rows = slice(17 * LANES, 18 * LANES)
        ref[rows, 0:width] = pick(split == 1, bottom_row, jnp.zeros_like(bottom_row))

    def add_edges(ref, at_top, at_bottom):
        width = at_top.shape[1]
        ref[0:LANES, 0:width] += at_top
        rows = slice(15 * LANES, 16 * LANES)
        ref[rows, width : 2 * width] += pick(split == 1, 0.0, at_bottom)
        rows = slice(16 * LANES, 17 * LANES)
        ref[rows, 0:width] += pick(split == 1, at_bottom, 0.0)

    up_f[...] = pre_in[0]
    down_f[...] = pick(split == 1, pre_in[row_count + 2], pre_in[row_count + 1])
    copies = halo_copies(0, up_f, down_f, from_up_f, from_down_f, sem_fs, sem_fr)
    halo_start(copies)
    for ref, wide in ((x_one, 768), (x_two, 768), (x_three, 768)):
        ref[0:LANES, 0:384] = jnp.zeros((LANES, 384), BF16)
        ref[18 * LANES : 19 * LANES, :] = jnp.zeros((LANES, wide), BF16)
    spread_z(feature[...], z_columns(cells_row[...]), spread)
    bias_mid = stat[32:33, :]
    b_mid = jnp.concatenate([bias_mid[:, 32:96], bias_mid[:, 32:96]], axis=1)

    def activated(value, x_ref, q, e):
        value = pick(ok(2 * q + 1 + e), half_silu(0.5 * value), 0.0)
        put(x_ref, q + e, 1 - e, value, 0, 1)

    def mid_step(q, carry):
        rows = pl.ds(pl.multiple_of(q * LANES, LANES), LANES)
        for e in range(2):
            value = pre_in[2 * q + 1 + e] + b_mid
            pre_mid[rows, e * LANES : (e + 1) * LANES] = value
            activated(value, x_one, q, e)
        return carry

    lax.fori_loop(0, PAIRS, mid_step, 0, unroll=2)
    halo_wait(copies)
    at_top = pick((top == 1) & has_up, from_up_f[...], 0.0)
    at_bottom = pick((bottom == 1) & has_down, from_down_f[...], 0.0)
    add_edges(pre_mid, at_top, at_bottom)
    for q, e in ((0, 0), (15, 1), (16, 0)):
        activated(pre_mid[q * LANES : (q + 1) * LANES, e * LANES : (e + 1) * LANES], x_one, q, e)

    def exchange(x_ref, s):
        send_up[s] = x_ref[0:LANES, 512:640]
        send_down[s] = pick(split == 1, x_ref[16 * LANES : 17 * LANES, 512:640], x_ref[16 * LANES : 17 * LANES, 128:256])
        halo_start(thin(s))

    def banded_back(g_ref, d_ref, out_ref):
        width = g_ref.shape[1]

        def step(b, carry):
            start = pl.multiple_of(b * SPAN, LANES)
            total = nt(g_ref[pl.ds(start, SPAN), :], d_ref[:, 0:width])
            total += nt(g_ref[pl.ds(start + LANES, SPAN), :], d_ref[:, width : 2 * width])
            out_ref[pl.ds(start, SPAN), :] = total
            return carry

        lax.fori_loop(0, STEPS, step, 0)

    def bias_row(first, lane):
        mixed = jnp.where(lane_of((1, LANES)) >= lane, stat[first : first + 1, :], stat[first + 1 : first + 2, :])
        return pltpu.roll(jnp.broadcast_to(mixed, (8, LANES)), LANES - lane, axis=1)[0:1, :]

    def twice(row):
        return jnp.concatenate([row, row], axis=1)

    def layer_forward(x_ref, f_ref, bias, out_ref, s, x_next):
        exchange(x_ref, s)
        bias = twice(bias)

        def products(b):
            rows, more = pl.ds(b * SPAN, SPAN), pl.ds(b * SPAN + LANES, SPAN)
            total = nn(x_ref[rows, :], f_ref[0:768, :])
            total += nn(x_ref[more, :], f_ref[768:1536, :])
            out_ref[rows, :] = total + bias

        def piece(q, e):
            rows = pl.ds(q * LANES, LANES)
            activated(out_ref[rows, e * LANES : (e + 1) * LANES], x_next, q, e)

        products(0)
        products(1)
        for q in range(QB):
            for e in range(2):
                piece(q, e)

        def step(q, carry):
            rows = pl.ds(pl.multiple_of(q * LANES, LANES), LANES)
            for e in range(2):
                activated(out_ref[rows, e * LANES : (e + 1) * LANES], x_next, q, e)
            return carry

        lax.fori_loop(QB, PAIRS, step, 0)
        halo_wait(thin(s))
        top_row, bottom_row = edges(1, from_up[s], from_down[s])
        put_edges(x_ref, top_row, bottom_row)
        add_edges(out_ref, nn(top_row, f_ref[0:384, 0:LANES]), nn(bottom_row, f_ref[768:1152, 0:LANES]))
        for q, e in ((0, 0), (15, 1), (16, 0)):
            piece(q, e)

    kernel_loads[0].wait()
    layer_forward(x_one, f_one, bias_row(33, 96), pre_one, 0, x_two)
    for load in kernel_loads[1:]:
        load.wait()
    layer_forward(x_two, f_two, bias_row(35, 96), pre_two, 1, x_three)

    def weight_grads(g_ref, x_ref, parts, write):
        width, wide = parts * LANES, 3 * parts * LANES
        middle0 = slice(width, 2 * width)
        middle1 = slice(wide + width, wide + 2 * width)
        acc0[0 : 2 * width, :] = jnp.zeros((2 * width, 768), F32)
        acc1[0:width, :] = jnp.zeros((width, 384), F32)
        acc2[0:width, :] = jnp.zeros((width, 384), F32)

        def step(b, carry):
            start = pl.multiple_of(b * SPAN, LANES)
            rows = pl.ds(start, SPAN)
            g0, g1 = g_ref[rows, middle0], g_ref[rows, middle1]
            both = jnp.concatenate([g0, g1], axis=1)
            sums = both.astype(F32).reshape(SPAN // 8, 8, 2 * width)
            carry = carry + jnp.sum(sums, axis=0)
            acc0[0 : 2 * width, :] += tn(both, x_ref[rows, :])
            acc2[0:width, :] += tn(g1, x_ref[pl.ds(start + LANES, SPAN), 0:384])
            after = g_ref[pl.ds(start + LANES, SPAN), middle0]
            acc1[0:width, :] += tn(after, x_ref[rows, 384:768])
            return carry

        sums = lax.fori_loop(0, STEPS, step, jnp.zeros((8, 2 * width), F32))
        sums = jnp.sum(sums, axis=0, keepdims=True)
        for i in range(3):
            if i == 0:
                total = acc0[width : 2 * width, 0:384] + acc1[0:width, :]
            elif i == 1:
                total = acc0[0:width, 0:384] + acc0[width : 2 * width, 384:768]
            else:
                total = acc0[0:width, 384:768] + acc2[0:width, :]
            for j in range(3):
                for part in range(parts):
                    block = total[part * LANES : (part + 1) * LANES, j * LANES : (j + 1) * LANES]
                    write(i, j, part, jnp.transpose(block))
        return sums[:, 0:width] + sums[:, width : 2 * width]

    def last_layers(pre_three, x_head, g_three):
        bias = jnp.concatenate([bias_row(37, 96), bias_row(38, 96)], axis=1)

        def products(b):
            rows, more = pl.ds(b * SPAN, SPAN), pl.ds(b * SPAN + LANES, SPAN)
            total = nn(x_three[rows, :], f_three[0:768, :]) + nn(x_three[more, 0:384], f_three[768:1152, :])
            pre_three[rows, 0:256] = total + bias
            total = nn(x_three[rows, 384:768], f_three[0:384, :]) + nn(x_three[more, :], f_three[384:1152, :])
            pre_three[rows, 256:512] = total + bias

        def head_rows(rows):
            x_head[rows, :] = half_silu(0.5 * pre_three[rows, :]).astype(BF16)

        def head_step(q, carry):
            head_rows(pl.ds(pl.multiple_of(q * LANES, LANES), LANES))
            return carry

        exchange(x_three, 2)
        products(0)
        products(1)
        for q in range(QB):
            head_rows(pl.ds(q * LANES, LANES))
        lax.fori_loop(QB, PAIRS, head_step, 0)
        halo_wait(thin(2))
        top_row, bottom_row = edges(1, from_up[2], from_down[2])
        put_edges(x_three, top_row, bottom_row)
        add_edges(pre_three, nn(top_row, f_three[0:384, :]), nn(bottom_row, f_three[768:1152, :]))
        for q in (0, 15, 16):
            head_rows(pl.ds(q * LANES, LANES))
        for load in loads:
            load.wait()
        head_row = jnp.broadcast_to(stat[40:41, :], (LANES, LANES))
        b_head = jnp.sum(jnp.where(lane_of((16, LANES)) == row_of((16, LANES)) + 96, head_row[0:16, :], 0.0), axis=1, keepdims=True)
        divisor = jnp.maximum(stat[0:1, 3:4], 1.0)
        inverse = 1.0 / divisor
        row16 = row_of((16, LANES))

        def loss_tile(logits, place):
            row = place_row(place, edge, row_count)
            label = labels[row]
            kind = jnp.concatenate([label, jnp.zeros((14, LANES), jnp.int32)], axis=0)
            is_class = row16 < 2
            anchor0, anchor1 = label[0:1, :] == 1, label[1:2, :] == 1
            box_on = ((row16 < 9) & anchor0) | ((row16 >= 9) & anchor1)
            positive = (kind == 1).astype(F32)
            negative = (kind == 0).astype(F32)
            q = 1.0 / (1.0 + jnp.exp(-logits))
            rest = jnp.log(1.0 + jnp.exp(-jnp.abs(logits)))
            log_q = jnp.minimum(logits, 0.0) - rest
            log_not = jnp.minimum(-logits, 0.0) - rest
            short = 1.0 - q
            focal = -FOCAL_ALPHA * positive * short * short * log_q
            focal -= (1.0 - FOCAL_ALPHA) * negative * q * q * log_not
            slope_p = FOCAL_ALPHA * (2.0 * q * short * short * log_q - short * short * short)
            slope_n = (1.0 - FOCAL_ALPHA) * (q * q * q - 2.0 * q * q * short * log_not)
            residual = logits - boxes[row]
            size = jnp.abs(residual)
            huber = jnp.where(size < HUBER_BETA, (0.5 / HUBER_BETA) * residual * residual, size - 0.5 * HUBER_BETA)
            bent = jnp.clip(residual * (1.0 / HUBER_BETA), -1.0, 1.0)
            value = jnp.where(is_class, focal, jnp.where(box_on, 2.0 * huber, 0.0))
            grad = jnp.where(is_class, positive * slope_p + negative * slope_n, jnp.where(box_on, 2.0 * bent, 0.0))
            good = ok(place)
            return pick(good, value, 0.0), pick(good, grad * inverse, 0.0)

        def loss_step(q, total):
            rows = pl.ds(pl.multiple_of(q * LANES, LANES), LANES)
            for e in range(2):
                logits = nt(head_t[...], x_head[rows, e * 256 : (e + 1) * 256]) + b_head
                value, grad = loss_tile(logits, 2 * q + 1 + e)
                logit_grads[e, :, rows] = grad.astype(BF16)
                total = total + value
            return total

        total = lax.fori_loop(0, PAIRS, loss_step, jnp.zeros((16, LANES), F32), unroll=3)
        total = jnp.sum(jnp.sum(total, axis=1, keepdims=True), axis=0, keepdims=True)
        loss_mine[...] = jnp.broadcast_to(total, (8, LANES))
        for k in range(1, n):
            loss_copy(k).start()
        g_head = jnp.zeros((16, CR3), F32)
        g_bias = jnp.zeros((16, 1), F32)
        for e in range(2):
            g_head += nn(logit_grads[e], x_head[0:GRID, e * 256 : (e + 1) * 256])
            g_bias += jnp.sum(logit_grads[e].astype(F32), axis=1, keepdims=True)
        back_rows = jnp.where(same_eighth(), tn(g_head, fold16().astype(F32), HIGH), 0.0)
        grad_b[B_HEAD : B_HEAD + 32, :] = tn(eighths().astype(F32), back_rows, HIGH)
        spots = (lane_of((16, LANES)) == row_of((16, LANES))).astype(F32)
        grad_b[B_HEAD + 32 : B_HEAD + 33, :] = jnp.sum(spots * g_bias, axis=0, keepdims=True)

        def back_step(q, carry):
            rows = pl.ds(pl.multiple_of(q * LANES, LANES), LANES)
            for e in range(2):
                grad = tn(logit_grads[e, :, rows], head_t[...])
                grad = (0.5 * grad) * half_slope(0.5 * pre_three[rows, e * 256 : (e + 1) * 256])
                for part in range(2):
                    put(g_three, q + e, 1 - e, grad[:, part * LANES : (part + 1) * LANES], part, 2)
            return carry

        g_three[0:LANES, 0:768] = jnp.zeros((LANES, 768), BF16)
        g_three[18 * LANES : 19 * LANES, :] = jnp.zeros((LANES, 1536), BF16)
        lax.fori_loop(0, PAIRS, back_step, 0, unroll=2)
        last_row = slice(16 * LANES, 17 * LANES)
        send_up_w[...] = g_three[0:LANES, 1024:1280]
        send_down_w[...] = pick(split == 1, g_three[last_row, 1024:1280], g_three[last_row, 256:512])
        copies = halo_copies(0, send_up_w, send_down_w, from_up_w, from_down_w, sem_ws, sem_wr)
        halo_start(copies)

        def write(i, j, part, block):
            start = B_THREE + 2 * (i * 3 + j) * LANES + part
            grad_b[pl.ds(start, LANES, 2), :] = block

        sums = weight_grads(g_three, x_three, 2, write)
        grad_b[B_HEAD - 2 : B_HEAD - 1, :] = sums[:, 0:LANES]
        grad_b[B_HEAD - 1 : B_HEAD, :] = sums[:, LANES : 2 * LANES]
        ship(0)
        banded_back(g_three, d_three, back)
        ship_on(0)
        halo_wait(copies)
        add_back(d_three, *edges(2, from_up_w[...], from_down_w[...]))

    def add_back(d_ref, top_row, bottom_row):
        width = top_row.shape[1]
        add_edges(back, nt(top_row, d_ref[0:LANES, 0:width]), nt(bottom_row, d_ref[0:LANES, 2 * width : 3 * width]))

    def loss_copy(k):
        return remote(loss_mine, loss_all.at[me], sem_ls.at[k], sem_lr.at[me], lax.rem(me + k, n))

    pl.run_scoped(
        last_layers,
        pltpu.VMEM((GRID, 512), F32),
        pltpu.VMEM((GRID, 512), BF16),
        pltpu.VMEM((19 * LANES, 1536), BF16),
    )

    def lower_layers(g_ref, g_map, win0, win1, win2, gathered, d_two, d_one, w_mid):
        lower = ((d_two_h, d_two), (d_one_h, d_one), (w_mid_h, w_mid))
        lower_loads = [pltpu.make_async_copy(a, b, sem_k.at[5 + i]) for i, (a, b) in enumerate(lower)]
        for load in lower_loads:
            load.start()

        def piece_in(pre_ref, rows, q, e):
            lanes = slice(e * LANES, (e + 1) * LANES)
            value = (0.5 * back[rows, lanes]) * half_slope(0.5 * pre_ref[rows, lanes])
            put(g_ref, q + e, 1 - e, pick(ok(2 * q + 1 + e), value, 0.0), 0, 1)

        def all_pieces(first, take):
            def step(q, carry):
                rows = pl.ds(pl.multiple_of(q * LANES, LANES), LANES)
                for e in range(2):
                    take(rows, q, e)
                return carry

            lax.fori_loop(first, PAIRS, step, 0)

        def back_and_on(d_ref, s, take, between):
            for b in range(STEPS):
                total = nt(g_ref[b * SPAN : (b + 1) * SPAN, :], d_ref[:, 0:768])
                total += nt(g_ref[b * SPAN + LANES : (b + 1) * SPAN + LANES, :], d_ref[:, 768:1536])
                back[b * SPAN : (b + 1) * SPAN, :] = total
            for q in range(QB):
                for e in range(2):
                    take(pl.ds(q * LANES, LANES), q, e)
            all_pieces(QB, take)
            between()
            from_edges(d_ref, s)
            for q, e in ((0, 0), (15, 1), (16, 0)):
                take(pl.ds(q * LANES, LANES), q, e)

        def weights_of(x_ref, begin):
            def write(i, j, part, block):
                start = begin + (i * 3 + j) * LANES
                grad_b[start : start + LANES, :] = block

            grad_b[begin + 1152 : begin + 1153, :] = weight_grads(g_ref, x_ref, 1, write)

        def from_edges(d_ref, s):
            halo_wait(thin(s))
            add_back(d_ref, *edges(1, from_up[s], from_down[s]))

        g_ref[0:LANES, 0:384] = jnp.zeros((LANES, 384), BF16)
        g_ref[18 * LANES : 19 * LANES, :] = jnp.zeros((LANES, 768), BF16)
        all_pieces(0, functools.partial(piece_in, pre_two))
        exchange(g_ref, 3)
        weights_of(x_two, B_TWO)
        ship(1)
        for load in lower_loads:
            load.wait()
        ship_on(1)
        back_and_on(d_two, 3, functools.partial(piece_in, pre_one), lambda: None)
        exchange(g_ref, 4)

        g_map[...] = jnp.zeros_like(g_map)

        def piece_to_map(rows, q, e):
            p = 2 * q + 1 + e
            lanes = slice(e * LANES, (e + 1) * LANES)
            value = (0.5 * back[rows, lanes]) * half_slope(0.5 * pre_mid[rows, lanes])
            value = pick(ok(p), value, 0.0).astype(BF16).astype(F32)
            spot = p * PITCH + 8
            g_map[pl.ds(spot if isinstance(q, int) else pl.multiple_of(spot, 8), LANES), :] = value

        def far_zero():
            for i in of_stage(0):
                ship_far(i)

        back_and_on(d_one, 4, piece_to_map, far_zero)

        def map_row(place):
            return slice(place * PITCH + 8, place * PITCH + 8 + LANES)

        send_up[5] = g_map[map_row(1), :].astype(BF16)
        send_down[5] = pick(split == 1, g_map[map_row(row_count + 1), :], g_map[map_row(row_count), :]).astype(BF16)
        halo_start(thin(5))

        def map_sum(p, total):
            return total + g_map[pl.ds(pl.multiple_of(p * PITCH + 8, 8), LANES), :]

        total = lax.fori_loop(1, 2 * PAIRS + 1, map_sum, jnp.zeros((LANES, LANES), F32))
        total = jnp.sum(total, axis=0, keepdims=True)
        total = total[:, 0:CM] + total[:, CM : 2 * CM]
        grad_a[0:A_MID, :] = jnp.zeros((A_MID, LANES), F32)
        grad_a[A_MID + 1728 : A_ROWS, :] = jnp.zeros((A_ROWS - A_MID - 1728, LANES), F32)
        grad_a[A_MID + 1728 : A_MID + 1729, 0:CM] = total
        weights_of(x_one, B_ONE)
        ship(2)
        halo_wait(thin(5))
        g_map[map_row(0), :] = pick((top == 1) & has_up, from_up[5].astype(F32), 0.0)
        halo = pick((bottom == 1) & has_down, from_down[5].astype(F32), 0.0)
        g_map[map_row(row_count + 1), :] = pick(split == 1, g_map[map_row(row_count + 1), :], halo)
        g_map[map_row(row_count + 2), :] = pick(split == 1, halo, 0.0)

        wins = (win0, win1, win2)
        voxels = feature.shape[0]

        def fetch(v, carry):
            base = bases[0, v]
            for i in range(3):
                wins[i][pl.ds(4 * v, 3), :] = g_map[pl.ds(base + (2 - i) * PITCH, 3), :]
            return carry

        lax.fori_loop(0, voxels, fetch, 0, unroll=8)
        ship_on(2)
        for i in range(3):
            for j in range(3):
                lanes = slice((i * 3 + j) * LANES, (i * 3 + j + 1) * LANES)
                gathered[:, lanes] = wins[i][pl.ds(2 - j, voxels, 4), :].astype(BF16)
        low = lane_of((64, LANES)) < 64
        for i in range(3):
            block = tn(spread[...], gathered[:, i * 384 : (i + 1) * 384])
            for j in range(3):
                part = block[:, j * LANES : (j + 1) * LANES]
                even = [part[z * LANES : z * LANES + 64] for z in range(ZD)]
                odd = [part[z * LANES + 64 : (z + 1) * LANES] for z in range(ZD)]

                def flip(x):
                    return pltpu.roll(x, 64, axis=1)

                taps = (
                    jnp.where(low, flip(even[1]), odd[1]),
                    jnp.where(low, even[0] + flip(even[2]), flip(odd[0]) + odd[2]),
                    jnp.where(low, even[1] + flip(even[3]), flip(odd[1]) + odd[3]),
                )
                for t in range(3):
                    start = A_MID + (t * 9 + i * 3 + j) * 64
                    grad_a[start : start + 64, :] = taps[t]
        ship(3)
        for i in of_stage(1):
            ship_far(i)
        z_column = z_columns(cells_row[...])
        total = jnp.zeros((voxels, C2), F32)
        for z in range(ZD):
            total += jnp.where(z_column == z, nt(gathered[...], w_mid[z * C2 : (z + 1) * C2, :]), 0.0)
        grad_feature[...] = total

    voxels = feature.shape[0]
    pl.run_scoped(
        lower_layers,
        pltpu.VMEM((19 * LANES, 768), BF16),
        pltpu.VMEM(((row_count + 6) * PITCH, LANES), F32),
        pltpu.VMEM((voxels * 4, LANES), F32),
        pltpu.VMEM((voxels * 4, LANES), F32),
        pltpu.VMEM((voxels * 4, LANES), F32),
        pltpu.VMEM((voxels, 1152), BF16),
        pltpu.VMEM(d_two_h.shape, BF16),
        pltpu.VMEM(d_one_h.shape, BF16),
        pltpu.VMEM(w_mid_h.shape, BF16),
    )
    counts = counts_ref[...]
    slot_count = points_hbm.shape[1]
    columns, gamma, beta = first_layer(small)
    mean, scale, held = stat[0:32, 0:1], stat[0:32, 1:2], stat[0:32, 2:3]
    centre = stat[0:8, 4:5]
    order = even_first()
    rows_fc = voxel_rows(small)
    kernel = rows_fc[0:64, :].astype(BF16)
    kernel_t = (0.5 * nt(order.astype(BF16), kernel)).astype(BF16)
    kernel = nt(kernel, order.astype(BF16)).astype(BF16)
    bias = 0.5 * jnp.sum(jnp.where(order, rows_fc[64:65, :], 0.0), axis=1, keepdims=True)
    half_gamma, half_beta = 0.5 * gamma, 0.5 * beta


    def halves(value):
        high = value.astype(BF16)
        return high, (value - high.astype(F32)).astype(BF16)

    def note(s, sender, target):
        mine, notes, received = ((mine_a, notes_a, sem_nar), (mine_b, notes_b, sem_nbr))[s]
        spot = sender // 2
        return remote(mine, notes.at[spot], sem_ns.at[s], received.at[spot], target)

    def send_note(s):
        mine, notes = ((mine_a, notes_a), (mine_b, notes_b))[s]

        @pl.when(core == 1)
        def _():
            note(s, me, sibling).start()

        @pl.when(core == 0)
        def _():
            note(s, me + 1, sibling).wait_recv()
            mine[...] = mine[...] + notes[me // 2]

        @pl.when((core == 0) & (me > 0))
        def _():
            note(s, me, 0).start()

    chunks = voxels // CHUNK

    def after(step):
        last = 3 * chunks - 1
        for place, i in enumerate(late):
            if min(place + 1, last) == step:
                ship_far(i)

    def voxel_layers(points, first, inner_grads, first_out):
        first_load = pltpu.make_async_copy(first_hbm, first_out, sem_p.at[7])
        first_load.start()
        points[...] = jnp.ones_like(points)
        point_loads = [
            pltpu.make_async_copy(points_hbm.at[k], points.at[:, k, :], sem_p.at[k]) for k in range(7)
        ]
        for load in point_loads:
            load.start()
        ship_on(3)
        first_load.wait()
        tail = jnp.where(row_of((16, CHUNK)) == 0, 1.0, 0.0).astype(BF16)
        fc = jnp.zeros((80, LANES), F32)
        pooled_grads = []
        for c in range(chunks):
            part = slice(c * CHUNK, (c + 1) * CHUNK)
            held_c = counts[:, part]
            counts_f = held_c.astype(F32)
            grad_pre = (0.5 * jnp.transpose(grad_feature[part, :])) / counts_f
            pooled_c = pooled_in[:, part]
            fixed = nn(kernel_t[:, 32:64], pooled_c) + bias

            def spot(p):
                return pl.ds(pl.multiple_of(p * CHUNK, LANES), CHUNK)

            def pass_e(p, carry, part=part, held_c=held_c, grad_pre=grad_pre, fixed=fixed):
                half_inner = nn(kernel_t[:, 0:32], first_out[p, :, part]) + fixed
                grad = jnp.where(p < held_c, grad_pre * half_slope(half_inner), 0.0)
                inner_grads[:, spot(p)] = grad.astype(BF16)
                return carry

            lax.fori_loop(0, slot_count, pass_e, 0, unroll=7)
            if c == 0:
                for i in of_stage(2):
                    ship_far(i)
            else:
                after(2 * c)

            def pass_g(p, carry, c=c, part=part, pooled_c=pooled_c):
                fc, pooled = carry
                grad = inner_grads[:, spot(p)]
                fc += nt(jnp.concatenate([first_out[p, :, part], pooled_c, tail], axis=0), grad)
                down = nn(kernel, grad)
                first[c, p] = down[0:32]
                return fc, pooled + down[32:64]

            fc, pooled = lax.fori_loop(0, slot_count, pass_g, (fc, jnp.zeros((32, CHUNK), F32)), unroll=5)
            pooled_grads.append(pooled / counts_f)
            after(2 * c + 1)
        mine_a[...] = fc[0:NOTE_A]
        send_note(0)
        for load in point_loads:
            load.wait()
        moments, g_gamma, centred = jnp.zeros((LANES, 16), F32), jnp.zeros((32, CHUNK), F32), jnp.zeros((8, CHUNK), F32)
        for c in range(chunks):
            part = slice(c * CHUNK, (c + 1) * CHUNK)
            wide = [jnp.broadcast_to(column, (32, CHUNK)) for column in columns]

            def pass_f(p, carry, c=c, part=part, held_c=counts[:, part], pooled=pooled_grads[c], wide=wide):
                moments, g_gamma, centred = carry
                inside = p < held_c
                value = wide[0] * points[p, 0:1, part]
                for k in range(1, 7):
                    value += wide[k] * points[p, k : k + 1, part]
                normed = jnp.where(inside, (value - mean) * scale, 0.0)
                slopes = half_slope(half_gamma * normed + half_beta)
                grad = jnp.where(inside, (0.5 * (first[c, p] + pooled)) * slopes, 0.0)
                off = points[p, :, part] - centre
                off_high, off_low = halves(off)
                grad_high, grad_low = halves(grad)
                norm_high, norm_low = halves(normed)
                left = jnp.concatenate([grad_high, grad_low, norm_high, norm_low], axis=0)
                right = jnp.concatenate([off_high, off_low], axis=0)
                return (
                    moments + nt(left, right),
                    g_gamma + grad * normed,
                    centred + jnp.where(inside, off, 0.0),
                )

            moments, g_gamma, centred = lax.fori_loop(0, slot_count, pass_f, (moments, g_gamma, centred), unroll=5)
            after(2 * chunks + c)
        by_grad = moments[0:32] + moments[32:64]
        by_norm = moments[64:96] + moments[96:128]
        mine_b[...] = jnp.zeros_like(mine_b)
        mine_b[0:32, 0:8] = by_grad[:, 0:8] + by_grad[:, 8:16]
        mine_b[0:32, 8:16] = by_norm[:, 0:8] + by_norm[:, 8:16]
        mine_b[0:32, 16:17] = jnp.sum(g_gamma, axis=1, keepdims=True)
        mine_b[32:40, 0:1] = jnp.sum(centred, axis=1, keepdims=True)
        send_note(1)

    pl.run_scoped(
        voxel_layers,
        pltpu.VMEM((slot_count, 8, voxels), F32),
        pltpu.VMEM((chunks, slot_count, 32, CHUNK), F32),
        pltpu.VMEM((LANES, slot_count * CHUNK), BF16),
        pltpu.VMEM(first_hbm.shape, BF16),
    )
    small_grad[...] = jnp.zeros_like(small_grad)

    @pl.when(me == 0)
    def _():
        fc_total = mine_a[...]
        for d in range(2, n, 2):
            note(0, d, sibling).wait_recv()
            fc_total += notes_a[d // 2]
        fc_rows[...] = jnp.zeros_like(fc_rows)
        fc_rows[8:80, :] = nn(fc_total, order.astype(F32), HIGH)
        here, before = fc_rows[8:80, :], fc_rows[7:79, :]
        mixed = jnp.where(lane_of((72, LANES)) >= LANES - FC_LANE, before, here)
        small_grad[2:74, :] = pltpu.roll(mixed, FC_LANE, axis=1)
        total = mine_b[...]
        for d in range(2, n, 2):
            note(1, d, sibling).wait_recv()
            total += notes_b[d // 2]
        by_grad, by_norm = total[0:32, 0:8], total[0:32, 8:16]
        g_gamma, g_beta = total[0:32, 16:17], total[0:32, 7:8]
        off_sums = jnp.transpose(jnp.broadcast_to(total[32:40, 0:1], (8, LANES)))[0:32, 0:8]
        g_vfe = scale * gamma * (
            by_grad - g_beta / held * off_sums - g_gamma / held * by_norm
        )
        tall0 = jnp.concatenate([g_vfe[:, k : k + 1] for k in range(4)], axis=0)
        tall1 = jnp.concatenate([g_vfe[:, 4:5], g_vfe[:, 5:6], g_vfe[:, 6:7], g_gamma], axis=0)
        tall2 = jnp.concatenate([g_beta, jnp.zeros((96, 1), F32)], axis=0)
        lane = lane_of((LANES, LANES))
        tall = jnp.where(lane == 0, tall0, 0.0) + jnp.where(lane == 1, tall1, 0.0) + jnp.where(lane == 2, tall2, 0.0)
        head = jnp.transpose(tall)[0:8]
        small_grad[0:8, :] = small_grad[0:8, :] + head

    ship_end()
    gradient[0:SMALL, :] = gradient[0:SMALL, :] + small_grad[...]

    @pl.when(me > 0)
    def _():
        for s in range(2):
            note(s, me, sibling).wait_send()

    for k in range(1, n):
        sender = lax.rem(me + n - k, n)
        remote(loss_mine, loss_all.at[sender], sem_ls.at[k], sem_lr.at[sender], sender).wait_recv()
    loss_all[me] = loss_mine[...]
    total = loss_all[0]
    for d in range(1, n):
        total += loss_all[d]
    loss_out[...] = total
    for k in range(1, n):
        loss_copy(k).wait_send()


def train(n, rows_dev, row_count, bases, cells, feature, stat, middle_out, labels, boxes, points, counts, small, pooled, first_out):
    shape = jax.ShapeDtypeStruct
    dma = pltpu.SemaphoreType.DMA
    voxels = feature.shape[0]
    row = (LANES, LANES)
    padded = ceil_to(rows_dev, 8)
    pieces = len(shard_pieces(n, rows_dev))
    fours = n // 4
    return pl.pallas_call(
        functools.partial(conv_kernel, n, rows_dev, row_count),
        name="train",
        out_shape=(
            shape((rows_dev, LANES), F32),
            shape((8, LANES), F32),
        ),
        in_specs=[smem()] + [vmem()] * 4 + [anywhere()] * 11 + [vmem()] * 3 + [anywhere()],
        out_specs=(vmem(),) * 2,
        scratch_shapes=[
            pltpu.VMEM((A_ROWS, LANES), F32),
            pltpu.VMEM((B_ROWS, LANES), F32),
            pltpu.VMEM((n, padded, LANES), F32),
            pltpu.VMEM((n // 2, padded, LANES), F32),
            pltpu.VMEM((n // 2, padded, LANES), F32),
            pltpu.VMEM((fours, padded, LANES), F32),
            pltpu.VMEM((voxels, LANES), F32),
            pltpu.VMEM((NOTE_A, LANES), F32),
            pltpu.VMEM((NOTE_B, LANES), F32),
            pltpu.VMEM((n // 2, NOTE_A, LANES), F32),
            pltpu.VMEM((n // 2, NOTE_B, LANES), F32),
            pltpu.VMEM((88, LANES), F32),
            pltpu.VMEM((SMALL, LANES), F32),
            *[pltpu.VMEM(middle_out[a].shape, BF16) for a in (2, 3, 4, 7, 8)],
            dma((8,)),
            pltpu.VMEM((19 * LANES, 768), BF16),
            pltpu.VMEM((19 * LANES, 768), BF16),
            pltpu.VMEM((19 * LANES, 768), BF16),
            pltpu.VMEM((GRID, 256), F32),
            pltpu.VMEM((GRID, 256), F32),
            pltpu.VMEM((GRID, 256), F32),
            pltpu.VMEM((GRID, 256), F32),
            pltpu.VMEM((voxels, ZD * C2), BF16),
            pltpu.VMEM((512, 768), F32),
            pltpu.VMEM((256, 384), F32),
            pltpu.VMEM((256, 384), F32),
            pltpu.VMEM((row_count, 2, LANES), jnp.int32),
            pltpu.VMEM((row_count, 16, LANES), F32),
            pltpu.VMEM((2, 16, GRID), BF16),
            pltpu.VMEM((8, LANES), F32),
            pltpu.VMEM((n, 8, LANES), F32),
            pltpu.VMEM(row, F32),
            pltpu.VMEM(row, F32),
            pltpu.VMEM(row, F32),
            pltpu.VMEM(row, F32),
            pltpu.VMEM((6,) + row, BF16),
            pltpu.VMEM((6,) + row, BF16),
            pltpu.VMEM((6,) + row, BF16),
            pltpu.VMEM((6,) + row, BF16),
            pltpu.VMEM((LANES, 256), BF16),
            pltpu.VMEM((LANES, 256), BF16),
            pltpu.VMEM((LANES, 256), BF16),
            pltpu.VMEM((LANES, 256), BF16),
            dma((16,)), dma((2,)), dma((2,)), dma((12,)), dma((12,)), dma((2,)), dma((2,)), dma((n,)), dma((n,)),
            dma((pieces,)), dma((pieces,)), dma((pieces,)), dma((pieces,)),
            dma((pieces,)), dma((5 * fours,)), dma((8,)), dma((2,)), dma((n // 2,)), dma((n // 2,)),
        ],
        compiler_params=pltpu.CompilerParams(
            collective_id=2, has_side_effects=True, vmem_limit_bytes=63 << 20
        ),
    )(bases, cells, feature, stat, *middle_out, labels, boxes, points, counts, small, pooled, first_out)


def adam_outer(gradient, weight, moment, second, momentum):
    moment = FIRST_DECAY * moment + (1.0 - FIRST_DECAY) * gradient
    second = SECOND_DECAY * second + (1.0 - SECOND_DECAY) * gradient * gradient
    moment_fix = moment / (1.0 - FIRST_DECAY**STEP)
    second_fix = second / (1.0 - SECOND_DECAY**STEP)
    inner_weight = weight - INNER_RATE * (
        moment_fix / (jnp.sqrt(second_fix) + ADAM_EPSILON) + WEIGHT_DECAY * weight
    )
    inner_step = weight - inner_weight
    momentum = OUTER_MOMENT * momentum + inner_step
    updated = weight - OUTER_RATE * (inner_step + OUTER_MOMENT * momentum)
    return (moment, second, momentum, updated)


def update_kernel(
    gradient, weight, moment, second, momentum, loss, stat,
    moment_out, second_out, momentum_out, weight_out, loss_out, positives_out,
    grad, held, outs, sem_in, sem_out,
):
    sources = (weight, moment, second, momentum)
    targets = (moment_out, second_out, momentum_out, weight_out)
    rows = grad.shape[0]
    steps = 4
    marks = [s * rows // steps // 8 * 8 for s in range(steps)] + [rows]
    loads, stores = [], []
    for s in range(steps):
        window = pl.ds(marks[s], marks[s + 1] - marks[s])
        loads.append([
            pltpu.make_async_copy(source.at[window], target.at[window], sem_in.at[5 * s + a])
            for a, (source, target) in enumerate(
                [(gradient, grad)] + [(source, held.at[a]) for a, source in enumerate(sources)]
            )
        ])
        for load in loads[-1]:
            load.start()
    loss_out[0] = loss[0, 0]
    positives_out[0] = stat[0, 3]
    for s in range(steps):
        part = slice(marks[s], marks[s + 1])
        window = pl.ds(marks[s], marks[s + 1] - marks[s])
        for load in loads[s]:
            load.wait()
        values = adam_outer(grad[part, :], held[0, part, :], held[1, part, :], held[2, part, :], held[3, part, :])
        for a, value in enumerate(values):
            outs[a, part, :] = value
            store = pltpu.make_async_copy(outs.at[a, window], targets[a].at[window], sem_out.at[4 * s + a])
            store.start()
            stores.append(store)
    for store in stores:
        store.wait()


def update(gradient, held, loss, stat):
    shape = jax.ShapeDtypeStruct
    rows = gradient.shape[0]
    dma = pltpu.SemaphoreType.DMA
    return pl.pallas_call(
        update_kernel,
        name="update",
        out_shape=(shape(gradient.shape, F32),) * 4 + (shape((1,), F32),) * 2,
        in_specs=[anywhere()] * 5 + [vmem()] * 2,
        out_specs=(anywhere(),) * 4 + (smem(),) * 2,
        scratch_shapes=[
            pltpu.VMEM((rows, LANES), F32),
            pltpu.VMEM((4, rows, LANES), F32),
            pltpu.VMEM((4, rows, LANES), F32),
            dma((20,)),
            dma((16,)),
        ],
        compiler_params=pltpu.CompilerParams(vmem_limit_bytes=60 << 20),
    )(gradient, *held, loss, stat)


def shards(
    points, point_counts, voxel_cells, anchor_labels, box_targets, weights, adam_m, adam_v, outer_momentum
):
    n = lax.axis_size("tile")
    rows = weights.shape[0] // LANES
    row_count = anchor_labels.shape[1]
    held = [x.reshape(rows, LANES) for x in (weights, adam_m, adam_v, outer_momentum)]
    counts = point_counts.reshape(1, -1)
    cells = voxel_cells.reshape(1, -1)
    wall, small, stat, first_out, pooled, feature, bases = front(
        n, points, counts, cells, anchor_labels, held[0]
    )
    ready = middle(n, rows, row_count, bases, cells, feature, wall)
    gradient, loss = train(
        n, rows, row_count, bases, cells, feature, stat, ready, anchor_labels, box_targets,
        points, counts, small, pooled, first_out,
    )
    *outs, loss_sum, positives = update(gradient, held, loss, stat)
    moment, second, momentum, updated = [x.reshape(weights.shape) for x in outs]
    return (moment, second, momentum, updated, loss_sum, positives)


def solution(mesh):
    split = ("group", "tile")
    in_specs = (
        P(None, None, split), P(split), P(split), P(None, split, None), P(None, split, None),
        P(split), P(split), P(split), P(split),
    )
    out_specs = (P(split), P(split), P(split), P(split), P("group"), P("group"))
    return jax.shard_map(shards, mesh=mesh, in_specs=in_specs, out_specs=out_specs, check_vma=False)
```
